32 devices in a mesh: batch: 4 (over y, x), rows: 8 (over z, core).
Axes of the slice: x: 2, y: 2, z: 4, core: 2. Of those that a mesh axis runs over, the one named last changes fastest.
Arguments:
- image_in: float32 [4, 128, 16, 512], P('batch', 'rows'), may hold values from -40 to 40
- cotangent: float32 [4, 128, 16, 512], P('batch', 'rows'), may hold values from -6 to 6
- slot_rows: int32 [6144], replicated, may hold values from 0 to 6143, as said below
- master: float32 [6144, 512], P(('batch', 'rows')), may hold values from -2 to 2
- first_moment: float32 [6144, 512], P(('batch', 'rows')), may hold values from -1025 to 1025
- second_moment: float32 [6144, 512], P(('batch', 'rows')), may hold values from 0 to 8192, as said below
Outputs:
- block_out: float32 [4, 128, 16, 512], P('batch', 'rows')
- grad_in: float32 [4, 128, 16, 512], P('batch', 'rows')
- grad_slots: float32 [6144, 512], P(('batch', 'rows'))
- new_first: float32 [6144, 512], P(('batch', 'rows'))
- new_second: float32 [6144, 512], P(('batch', 'rows'))
- new_master: float32 [6144, 512], P(('batch', 'rows'))
- new_copy: bfloat16 [6144, 512], P(('batch', 'rows'))
The draws below stay inside these ranges and needn't reach their ends.
Inputs may be any that keep to these rules, and one draw needn't show every extreme that they name: `slot_rows`: A permutation: each table row is held by exactly one owner slot; slot s is on device s // 192 of batch+rows (batch slowest). `second_moment`: Positive.
All inputs are finite; a program needn't handle non-finite values.
Results may differ from the reference program's by a relative error of at most 0.012.
Values may be sent and summed in bfloat16 or wider, within the bound.
A program may use at most 192 MiB of HBM per device.

```python
import math
import jax
import jax.numpy as jnp
from jax import lax

C = 512
FF = 2048
KL = 31
KS = 5
IMG_W = 16
STEP = 10
IMG_H = 128
BATCHES = 4
ROWS_ALL = 128
IMAGES = 4
PIXELS = 8192
BLOCKS = 6144


def slot_order(key):
    return jax.random.permutation(jax.random.fold_in(key, 11), BLOCKS).astype(jnp.int32)


def grad_scale(row_ids):
    bound_two = 2 * C
    bound_three = 2 * C + FF
    bound_four = 2 * C + 2 * FF
    bound_six = bound_four + KL * KL + KS * KS
    bound_seven = bound_six + 10
    bound_nine = bound_seven + 2 * (FF // C)
    factor = jnp.where(row_ids < bound_two, 1.0, jnp.where(row_ids < bound_three, 0.3, jnp.where(row_ids < bound_four, 0.6, jnp.where(row_ids < bound_six, 0.7, jnp.where(row_ids < bound_seven, 1.0, jnp.where(row_ids < bound_nine, 0.3, 1.0))))))
    return factor.astype(jnp.float32) * math.sqrt(float(PIXELS))


def draw_slot_rows(key, part):
    return slot_order(key)


def draw_master(key, part):
    row_ids = slot_order(key)[:, None]
    noise_vals = jax.random.truncated_normal(jax.random.fold_in(key, 21), -4.0, 4.0, (BLOCKS, C), jnp.float32)
    bound_three = 2 * C + FF
    bound_four = 2 * C + 2 * FF
    bound_five = bound_four + KL * KL
    bound_six = bound_five + KS * KS
    bound_seven = bound_six + 10
    bound_eight = bound_seven + FF // C
    bound_nine = bound_eight + FF // C
    scale_vals = jnp.where(row_ids < bound_three, C ** (-0.5), jnp.where(row_ids < bound_four, FF ** (-0.5), jnp.where(row_ids < bound_five, 1.0 / KL, jnp.where(row_ids < bound_six, 1.0 / KS, 0.5))))
    is_gain = (row_ids >= bound_six) & (row_ids < bound_seven) & ((row_ids - bound_six) % 2 == 0) | (row_ids >= bound_seven) & (row_ids < bound_eight)
    is_bias = (row_ids >= bound_six) & (row_ids < bound_nine) & jnp.logical_not(is_gain)
    values = jnp.where(is_gain, 1.0 + 0.1 * noise_vals, jnp.where(is_bias, 0.2 * noise_vals, scale_vals * noise_vals))
    return values.astype(jnp.float32)


def draw_first_moment(key, part):
    row_ids = slot_order(key)[:, None]
    noise_vals = jax.random.truncated_normal(jax.random.fold_in(key, 31), -3.0, 3.0, (BLOCKS, C), jnp.float32)
    return (grad_scale(row_ids) * noise_vals / 9.0).astype(jnp.float32)


def draw_second_moment(key, part):
    row_ids = slot_order(key)[:, None]
    spread_vals = jnp.exp(jax.random.uniform(jax.random.fold_in(key, 41), (BLOCKS, C), jnp.float32, 0.0, math.log(4.0)))
    level_vals = grad_scale(row_ids)
    return (0.001 * level_vals * level_vals * spread_vals).astype(jnp.float32)


def draw_image_in(key, part):
    shape_all = (BATCHES, ROWS_ALL, IMG_W, C)
    noise_vals = jax.random.truncated_normal(jax.random.fold_in(key, 52), -4.0, 4.0, shape_all, jnp.float32)
    rise_base = 3.0
    offsets = 0.5 * jax.random.truncated_normal(jax.random.fold_in(key, 53), -4.0, 4.0, (C,), jnp.float32)
    batch_frac = lax_iota(shape_all, 0) / max(BATCHES - 1, 1)
    row_frac = lax_iota(shape_all, 1) / max(ROWS_ALL - 1, 1)
    factor = rise_base ** (batch_frac + row_frac - 1.0)
    return (factor * (noise_vals + offsets)).astype(jnp.float32)


def lax_iota(shape_all, axis_num):
    return jax.lax.broadcasted_iota(jnp.int32, shape_all, axis_num).astype(jnp.float32)


def shard_levels(key, shape, split, least, high):
    factor_of, own = 1.0, jax.random.fold_in(key, 6)
    for axis_at, parts in split:
        heights = jnp.exp(jax.random.uniform(jax.random.fold_in(own, axis_at), (parts,), jnp.float32, least / len(split), high / len(split)))
        factor_of = factor_of * jnp.repeat(heights, shape[axis_at] // parts).reshape([-1 if axis == axis_at else 1 for axis in range(len(shape))])
    return factor_of


def centred(rng, dims, deviation, most, shards=(), kind=jnp.bfloat16):
    level = shard_levels(rng, dims, shards, -0.22, 0.18) if shards else 1.0
    values = jax.random.normal(rng, dims, jnp.float32) * deviation * level
    return jnp.minimum(jnp.maximum(values, -most), most).astype(kind)


def setup_inputs(seed: int = 0) -> dict:
    seeds = jax.random.split(jax.random.key(seed), 7)
    return {
        "image_in": draw_image_in(jax.random.fold_in(seeds[6], 71), 0),
        "cotangent": centred(seeds[1], (BATCHES, ROWS_ALL, IMG_W, C), 1.0, 6.0, ((0, 4), (1, 8)), jnp.float32),
        "slot_rows": draw_slot_rows(jax.random.fold_in(seeds[6], 71), 0),
        "master": draw_master(jax.random.fold_in(seeds[6], 71), 0),
        "first_moment": draw_first_moment(jax.random.fold_in(seeds[6], 71), 0),
        "second_moment": draw_second_moment(jax.random.fold_in(seeds[6], 71), 0),
    }


@jax.custom_vjp
def low(v):
    return lax.optimization_barrier(v.astype(jnp.bfloat16)).astype(jnp.float32)

@jax.custom_vjp
def low_back(v):
    return v

def low_keep(v):
    return (low(v), None)

def low_pass(kept, grad):
    return (grad,)

def back_keep(v):
    return (v, None)

def back_low(kept, grad):
    return (low(grad),)
low.defvjp(low_keep, low_pass)
low_back.defvjp(back_keep, back_low)
norm_eps = 1e-05
highest = lax.Precision.HIGHEST

def unpack(table):
    offset = 2 * C + 2 * FF
    w_in = table[0:C]
    w_out = table[C:2 * C]
    w_up = table[2 * C:2 * C + FF].reshape(C, FF)
    w_down = table[2 * C + FF:offset]
    k_large = table[offset:offset + KL * KL].reshape(KL, KL, C)
    offset = offset + KL * KL
    k_small = table[offset:offset + KS * KS].reshape(KS, KS, C)
    offset = offset + KS * KS
    norm_rows = table[offset:offset + 10]
    offset = offset + 10
    mid_gain = table[offset:offset + FF // C].reshape(FF)
    mid_bias = table[offset + FF // C:offset + 2 * (FF // C)].reshape(FF)
    return (w_in, w_out, w_up, w_down, k_large, k_small, norm_rows, mid_gain, mid_bias)

def pack(grads, total_rows):
    g_in, g_out, g_up, g_down, g_large, g_small, g_norms, g_mgain, g_mbias = grads
    pieces = jnp.concatenate([g_in, g_out, g_up.reshape(FF, C), g_down, g_large.reshape(KL * KL, C), g_small.reshape(KS * KS, C), g_norms, g_mgain.reshape(FF // C, C), g_mbias.reshape(FF // C, C)], axis=0)
    return jnp.pad(pieces, ((0, total_rows - pieces.shape[0]), (0, 0)))

def normalize(values, gain_row, bias_row):
    centre = lax.optimization_barrier(jnp.mean(values, axis=(0, 1, 2)))
    shifted = values - centre
    spread = lax.optimization_barrier(jnp.mean(shifted * shifted, axis=(0, 1, 2)))
    return shifted * lax.rsqrt(spread + norm_eps) * gain_row + bias_row

def mix(values, matrix):
    return jnp.einsum('nhwc,cd->nhwd', values, matrix, precision=highest)

def conv_pair(image, spec_large, spec_small):
    reach = (KL - 1) // 2
    shape_full = (IMG_H + KL - 1, IMG_W + KL - 1)
    spectrum = jnp.fft.rfft2(image, s=shape_full, axes=(0, 1))
    large_out = jnp.fft.irfft2(spectrum * spec_large, s=shape_full, axes=(0, 1))[reach:reach + IMG_H, reach:reach + IMG_W]
    small_out = jnp.fft.irfft2(spectrum * spec_small, s=shape_full, axes=(0, 1))[reach:reach + IMG_H, reach:reach + IMG_W]
    return (large_out, small_out)
conv_saved = jax.checkpoint(conv_pair)

def depthwise(u_val, k_large, k_small):
    shape_full = (IMG_H + KL - 1, IMG_W + KL - 1)
    margin = (KL - KS) // 2
    k_embed = jnp.pad(k_small, ((margin, margin), (margin, margin), (0, 0)))
    spec_large = jnp.fft.rfft2(k_large[::-1, ::-1], s=shape_full, axes=(0, 1))
    spec_small = jnp.fft.rfft2(k_embed[::-1, ::-1], s=shape_full, axes=(0, 1))
    return lax.map(lambda image: conv_saved(image, spec_large, spec_small), u_val)

def hidden_stats(hidden):
    centre = lax.optimization_barrier(jnp.mean(hidden, axis=(0, 1, 2)))
    shifted = hidden - centre
    spread = lax.optimization_barrier(jnp.mean(shifted * shifted, axis=(0, 1, 2)))
    return (centre, lax.rsqrt(spread + norm_eps))

def tail(block, centre, inv_std, gain_row, bias_row, w_down):
    normed = (block - centre) * inv_std * gain_row + bias_row
    return jnp.einsum('hwf,fc->hwc', low(jax.nn.gelu(normed)), w_down, precision=highest)
tail_saved = jax.checkpoint(tail)

def forward(images, params):
    w_in, w_out, w_up, w_down, k_large, k_small, norm_rows, mid_gain, mid_bias = params
    pre = normalize(images, norm_rows[0], norm_rows[1])
    z_first = low_back(mix(low(pre), w_in))
    u_val = low(jax.nn.gelu(z_first))
    large_out, small_out = depthwise(u_val, k_large, k_small)
    s_val = normalize(large_out, norm_rows[2], norm_rows[3]) + normalize(small_out, norm_rows[4], norm_rows[5])
    p_val = low_back(mix(low(jax.nn.gelu(s_val)), w_out))
    mid_sum = images + normalize(p_val, norm_rows[6], norm_rows[7])
    hidden = low_back(mix(low(normalize(mid_sum, norm_rows[8], norm_rows[9])), w_up))
    centre, inv_std = jax.checkpoint(hidden_stats)(hidden)
    branch = lax.map(lambda block: tail_saved(block, centre, inv_std, mid_gain, mid_bias, w_down), hidden)
    return mid_sum + low_back(branch)

def reference(image_in, cotangent, slot_rows, master, first_moment, second_moment):
    copy_vals = master.astype(jnp.bfloat16).astype(jnp.float32)
    table = jnp.zeros_like(copy_vals).at[slot_rows].set(copy_vals)
    params = unpack(table)
    images = image_in.reshape(IMAGES, IMG_H, IMG_W, C)
    result, pullback = jax.vjp(forward, images, params)
    grad_images, grad_params = pullback(cotangent.reshape(IMAGES, IMG_H, IMG_W, C))
    grad_table = pack(grad_params, table.shape[0])
    grad_slots = grad_table[slot_rows]
    norm_start = 2 * C + 2 * FF + KL * KL + KS * KS
    rates = jnp.where(slot_rows >= norm_start, 0.5, 0.05)[:, None]
    new_first = 0.9 * first_moment + 0.1 * grad_slots
    new_second = 0.999 * second_moment + 0.001 * grad_slots * grad_slots
    first_hat = new_first / (1.0 - 0.9 ** STEP)
    second_hat = new_second / (1.0 - 0.999 ** STEP)
    new_master = master - rates * (first_hat / (jnp.sqrt(second_hat) + 1e-08) + 0.05 * master)
    new_copy = new_master.astype(jnp.bfloat16)
    return (result.reshape(image_in.shape), grad_images.reshape(image_in.shape), grad_slots, new_first, new_second, new_master, new_copy)
```

```python
import functools

import jax
import jax.numpy as jnp
import numpy as np
from jax import lax
from jax.sharding import PartitionSpec as P

C = 512
FF = 2048
KL = 31
KS = 5
STEP = 10

norm_eps = 1e-05
beta_one = 0.9
beta_two = 0.999
adam_eps = 1e-08
decay_rate = 0.05
matrix_rate = 0.05
norm_rate = 0.5

TH = 16
TW = 16
NY = 47
NX = 31
NF = 768
REACH = (KL - 1) // 2
AXES = ("batch", "rows")
f32 = jnp.float32
bf16 = jnp.bfloat16


@functools.lru_cache(None)
def tables():
    freqs = [(ky, 0) for ky in range((NY + 1) // 2)]
    freqs += [(ky, kx) for kx in range(1, (NX + 1) // 2) for ky in range(NY)]
    ky = np.array([f[0] for f in freqs], np.int64)[:, None]
    kx = np.array([f[1] for f in freqs], np.int64)[:, None]
    pad = NF - len(freqs)

    def angle(rows, cols):
        ty = (ky * rows.reshape(1, -1)) % NY
        tx = (kx * cols.reshape(1, -1)) % NX
        return 2 * np.pi * (ty / NY + tx / NX)

    def grid(rows, cols):
        r, c = np.meshgrid(rows, cols, indexing="ij")
        return r.reshape(-1), c.reshape(-1)

    def stack(re, im):
        z = np.zeros((pad, re.shape[1]))
        return np.concatenate([re, z, im, z], axis=0)

    r, c = grid(np.arange(-TH, 2 * TH), np.arange(TW))
    used = ((r + REACH >= 0) & (r + REACH < NY - 1)).astype(np.float64)[None]
    t = angle(r + REACH, c)
    a = stack(np.cos(t) * used, -np.sin(t) * used)
    i, j = grid(np.arange(KL), np.arange(KL))
    t = angle(i, j - REACH)
    b = stack(np.cos(t), -np.sin(t))
    lead = REACH - (KS - 1) // 2
    small = ((i >= lead) & (i < lead + KS) & (j >= lead) & (j < lead + KS)).nonzero()[0]
    bs = b[:, small]
    y, x = grid(np.arange(TH), np.arange(TW))
    t = angle(y, x)
    w = np.full((len(freqs), 1), 2.0)
    w[0] = 1.0
    w /= NY * NX
    c = stack(w * np.cos(t), -w * np.sin(t)).T

    def split(m):
        hi = m.astype(np.float32).astype(bf16)
        lo = (m - hi.astype(np.float64)).astype(np.float32).astype(bf16)
        return hi, lo

    return tuple(split(m) for m in (a, b, bs, c))


def dot(a, b, dims=(1, 0)):
    return lax.dot_general(a, b, (((dims[0],), (dims[1],)), ((), ())), preferred_element_type=f32)


def split(v):
    hi = v.astype(bf16)
    lo = (v - hi.astype(f32)).astype(bf16)
    return hi, lo


def dot_exact(pair, low, dims=(1, 0)):
    return dot(pair[0], low, dims) + dot(pair[1], low, dims)


def dot_pair(pair, v, dims=(1, 0)):
    hi, lo = split(v)
    return dot(pair[0], hi, dims) + dot(pair[1], hi, dims) + dot(pair[0], lo, dims)


def times_conj(u, k):
    ur, ui, kr, ki = u[:NF], u[NF:], k[:NF], k[NF:]
    return jnp.concatenate([ur * kr + ui * ki, ui * kr - ur * ki], axis=0)


def times(g, k):
    gr, gi, kr, ki = g[:NF], g[NF:], k[:NF], k[NF:]
    return jnp.concatenate([gr * kr - gi * ki, gr * ki + gi * kr], axis=0)


def exchange(rows):
    return lax.all_gather(jnp.stack(rows), AXES, axis=0)


def local_stats(v):
    m = jnp.mean(v, axis=0)
    d = v - m
    return m, jnp.sum(d * d, axis=0)


def combine(means, seconds, n):
    m = jnp.mean(means, axis=0)
    d = means - m
    total = jnp.sum(seconds, axis=0) + n * jnp.sum(d * d, axis=0)
    return m, total / (n * means.shape[0])


def combine_cross(means_a, means_b, cross, n):
    da = means_a - jnp.mean(means_a, axis=0)
    db = means_b - jnp.mean(means_b, axis=0)
    return (jnp.sum(cross, axis=0) + n * jnp.sum(da * db, axis=0)) / (n * cross.shape[0])


def gelu_grad(v):
    a = np.float32(np.sqrt(2 / np.pi))
    t = jnp.tanh(a * (v + 0.044715 * (v * v * v)))
    return 0.5 * (1 + t) + 0.5 * v * (1 - t * t) * (a * (1 + 3 * 0.044715 * v * v))


def gelu(v):
    a = np.float32(np.sqrt(2 / np.pi))
    return 0.5 * v * (1 + jnp.tanh(a * (v + 0.044715 * (v * v * v))))


def body(image_in, cotangent, slot_rows, master, first_moment, second_moment):
    n = image_in.shape[0] * image_in.shape[1] * image_in.shape[2]
    devices = lax.axis_size("batch") * lax.axis_size("rows")
    every = n * devices
    ta, tb, tbs, tc = tables()
    own_copy = master.astype(bf16)
    gathered = lax.all_gather(own_copy, AXES, axis=0, tiled=True)
    ordered = jnp.zeros_like(gathered).at[slot_rows].set(gathered)
    w_in = ordered[0:C]
    w_out = ordered[C : 2 * C]
    w_up = ordered[2 * C : 2 * C + FF].reshape(C, FF)
    w_down = ordered[2 * C + FF : 2 * C + 2 * FF]
    offset = 2 * C + 2 * FF
    k_large = ordered[offset : offset + KL * KL]
    offset = offset + KL * KL
    k_small = ordered[offset : offset + KS * KS]
    offset = offset + KS * KS
    norm_start = offset
    rows = ordered[offset : offset + 10].astype(f32)
    offset = offset + 10
    mid_gain = ordered[offset : offset + FF // C].astype(f32).reshape(FF)
    mid_bias = ordered[offset + FF // C : offset + 2 * (FF // C)].astype(f32).reshape(FF)

    x = image_in.reshape(n, C)
    cot = cotangent.reshape(n, C)
    all_one = exchange(local_stats(x))
    m_x, q_x = combine(all_one[:, 0], all_one[:, 1], n)
    inv_x = lax.rsqrt(q_x + norm_eps)
    pre_hat = (x - m_x) * inv_x
    pre_low = (pre_hat * rows[0] + rows[1]).astype(bf16)
    z = dot(pre_low, w_in)
    u_low = gelu(z).astype(bf16)
    count = lax.axis_size("rows")
    above = lax.ppermute(u_low, "rows", [(i, i + 1) for i in range(count - 1)])
    below = lax.ppermute(u_low, "rows", [(i + 1, i) for i in range(count - 1)])
    wide = jnp.concatenate([above, u_low, below], axis=0)
    spec_l = dot_exact(tb, k_large)
    spec_s = dot_exact(tbs, k_small)
    spec_u = dot_exact(ta, wide)
    d_l = dot_pair(tc, times_conj(spec_u, spec_l))
    d_s = dot_pair(tc, times_conj(spec_u, spec_s))
    all_two = exchange(local_stats(d_l) + local_stats(d_s))
    m_l, q_l = combine(all_two[:, 0], all_two[:, 1], n)
    m_s, q_s = combine(all_two[:, 2], all_two[:, 3], n)
    inv_l, inv_s = lax.rsqrt(q_l + norm_eps), lax.rsqrt(q_s + norm_eps)
    hat_l, hat_s = (d_l - m_l) * inv_l, (d_s - m_s) * inv_s
    s_val = hat_l * rows[2] + rows[3] + hat_s * rows[4] + rows[5]
    t_low = gelu(s_val).astype(bf16)
    p = dot(t_low, w_out)
    mean_p, second_p = local_stats(p)
    cross = jnp.sum((p - mean_p) * (x - jnp.mean(x, axis=0)), axis=0)
    all_three = exchange((mean_p, second_p, cross))
    m_p, q_p = combine(all_three[:, 0], all_three[:, 1], n)
    cov = combine_cross(all_one[:, 0], all_three[:, 0], all_three[:, 2], n)
    inv_p = lax.rsqrt(q_p + norm_eps)
    proj_hat = (p - m_p) * inv_p
    mid = x + (proj_hat * rows[6] + rows[7])
    slope = rows[6] * inv_p
    m_f = m_x + rows[7]
    q_f = jnp.maximum(q_x + 2 * slope * cov + slope * slope * q_p, 0.0)
    inv_f = lax.rsqrt(q_f + norm_eps)
    ffn_hat = (mid - m_f) * inv_f
    hats = inv_f * inv_p * (cov + slope * q_p)
    c_low = (ffn_hat * rows[8] + rows[9]).astype(bf16)
    hidden = dot(c_low, w_up)
    all_four = exchange(local_stats(hidden))
    m_h, q_h = combine(all_four[:, 0], all_four[:, 1], n)
    inv_h = lax.rsqrt(q_h + norm_eps)
    hid_hat = (hidden - m_h) * inv_h
    hid_out = hid_hat * mid_gain + mid_bias
    a_low = gelu(hid_out).astype(bf16)
    result = mid + dot(a_low, w_down)

    gy_low = cot.astype(bf16)
    g_down = dot(a_low, gy_low, (0, 0))
    g_hid = dot(gy_low, w_down, (1, 1)) * gelu_grad(hid_out)
    b_mid, g_mid_gain = jnp.sum(g_hid, axis=0), jnp.sum(g_hid * hid_hat, axis=0)
    tot = jnp.sum(exchange((b_mid, g_mid_gain)), axis=0) / every
    gh_low = (mid_gain * inv_h * (g_hid - tot[0] - hid_hat * tot[1])).astype(bf16)
    g_up = dot(c_low, gh_low, (0, 0))
    g_ffn = dot(gh_low, w_up, (1, 1))
    b_ffn, g_ffn_gain = jnp.sum(g_ffn, axis=0), jnp.sum(g_ffn * ffn_hat, axis=0)
    tot = jnp.sum(
        exchange((b_ffn, g_ffn_gain, jnp.sum(g_ffn * proj_hat, axis=0), jnp.sum(cot, axis=0), jnp.sum(cot * proj_hat, axis=0))),
        axis=0,
    ) / every
    scale_f = rows[8] * inv_f
    g_mid = cot + scale_f * (g_ffn - tot[0] - ffn_hat * tot[1])
    mean_mid = tot[3]
    mean_mid_hat = tot[4] + scale_f * (tot[2] - tot[1] * hats)
    b_proj, g_proj = jnp.sum(g_mid, axis=0), jnp.sum(g_mid * proj_hat, axis=0)
    gp_low = (slope * (g_mid - mean_mid - proj_hat * mean_mid_hat)).astype(bf16)
    g_out = dot(t_low, gp_low, (0, 0))
    g_s = dot(gp_low, w_out, (1, 1)) * gelu_grad(s_val)
    b_pair, g_l_gain, g_s_gain = jnp.sum(g_s, axis=0), jnp.sum(g_s * hat_l, axis=0), jnp.sum(g_s * hat_s, axis=0)
    tot = jnp.sum(exchange((b_pair, g_l_gain, g_s_gain)), axis=0) / every
    gl = rows[2] * inv_l * (g_s - tot[0] - hat_l * tot[1])
    gs = rows[4] * inv_s * (g_s - tot[0] - hat_s * tot[2])
    spec_gl = dot_pair(tc, gl, (0, 0))
    spec_gs = dot_pair(tc, gs, (0, 0))
    grad_wide = dot_pair(ta, times(spec_gl, spec_l) + times(spec_gs, spec_s), (0, 0))
    from_below = lax.ppermute(grad_wide[:n].astype(bf16), "rows", [(i + 1, i) for i in range(count - 1)])
    from_above = lax.ppermute(grad_wide[2 * n :].astype(bf16), "rows", [(i, i + 1) for i in range(count - 1)])
    g_u = grad_wide[n : 2 * n] + from_below.astype(f32) + from_above.astype(f32)
    flip = times_conj(spec_u, spec_gl)
    g_k_l = dot_pair(tb, flip, (0, 0))
    flip = times_conj(spec_u, spec_gs)
    g_k_s = dot_pair(tbs, flip, (0, 0))
    gz_low = (g_u * gelu_grad(z)).astype(bf16)
    g_in = dot(pre_low, gz_low, (0, 0))
    g_pre = dot(gz_low, w_in, (1, 1))
    b_pre, g_pre_gain = jnp.sum(g_pre, axis=0), jnp.sum(g_pre * pre_hat, axis=0)
    tot = jnp.sum(exchange((b_pre, g_pre_gain)), axis=0) / every
    grad_x = g_mid + rows[0] * inv_x * (g_pre - tot[0] - pre_hat * tot[1])

    norm_grads = jnp.stack(
        [g_pre_gain, b_pre, g_l_gain, b_pair, g_s_gain, b_pair, g_proj, b_proj, g_ffn_gain, b_ffn]
    )
    grads = jnp.concatenate(
        [
            g_in,
            g_out,
            g_up.reshape(FF, C),
            g_down,
            g_k_l,
            g_k_s,
            norm_grads,
            g_mid_gain.reshape(FF // C, C),
            b_mid.reshape(FF // C, C),
        ],
        axis=0,
    )
    grads = jnp.pad(grads, ((0, gathered.shape[0] - grads.shape[0]), (0, 0)))
    slot_grads = grads[slot_rows]
    reduced = lax.psum_scatter(slot_grads, AXES, scatter_dimension=0, tiled=True)
    own_count = master.shape[0]
    place = lax.axis_index("batch") * lax.axis_size("rows") + lax.axis_index("rows")
    own_rows = lax.dynamic_slice_in_dim(slot_rows, place * own_count, own_count)
    rates = jnp.where(own_rows >= norm_start, norm_rate, matrix_rate)[:, None]
    new_first = beta_one * first_moment + (1.0 - beta_one) * reduced
    new_second = beta_two * second_moment + (1.0 - beta_two) * reduced * reduced
    first_hat = new_first / (1.0 - beta_one**STEP)
    second_hat = new_second / (1.0 - beta_two**STEP)
    new_master = master - rates * (
        first_hat / (jnp.sqrt(second_hat) + adam_eps) + decay_rate * master
    )
    return (
        result.reshape(image_in.shape),
        grad_x.reshape(image_in.shape),
        reduced,
        new_first,
        new_second,
        new_master,
        new_master.astype(bf16),
    )


def solution(mesh):
    image = P("batch", "rows", None, None)
    owner = P(AXES, None)
    return jax.shard_map(
        body,
        mesh=mesh,
        in_specs=(image, image, P(), owner, owner, owner),
        out_specs=(image, image, owner, owner, owner, owner, owner),
        check_vma=False,
    )
```

```python
import functools

import jax
import jax.numpy as jnp
import numpy as np
from jax import lax
from jax.experimental import pallas as pl
from jax.experimental.pallas import tpu as pltpu
from jax.sharding import PartitionSpec as P

C = 512
FF = 2048
KL = 31
KS = 5
STEP = 10

norm_eps = 1e-05
beta_one = 0.9
beta_two = 0.999
adam_eps = 1e-08
decay_rate = 0.05
matrix_rate = 0.05
norm_rate = 0.5

TH = 16
TW = 16
NY = 47
NX = 31
NF = 768
REACH = (KL - 1) // 2
AXES = ("batch", "rows")
f32 = jnp.float32
bf16 = jnp.bfloat16


@functools.lru_cache(None)
def tables():
    freqs = [(ky, 0) for ky in range((NY + 1) // 2)]
    freqs += [(ky, kx) for kx in range(1, (NX + 1) // 2) for ky in range(NY)]
    ky = np.array([f[0] for f in freqs], np.int64)[:, None]
    kx = np.array([f[1] for f in freqs], np.int64)[:, None]
    pad = NF - len(freqs)

    def angle(rows, cols):
        ty = (ky * rows.reshape(1, -1)) % NY
        tx = (kx * cols.reshape(1, -1)) % NX
        return 2 * np.pi * (ty / NY + tx / NX)

    def grid(rows, cols):
        r, c = np.meshgrid(rows, cols, indexing="ij")
        return r.reshape(-1), c.reshape(-1)

    def stack(re, im):
        z = np.zeros((pad, re.shape[1]))
        return np.concatenate([re, z, im, z], axis=0)

    r, c = grid(np.arange(-TH, 2 * TH), np.arange(TW))
    used = ((r + REACH >= 0) & (r + REACH < NY - 1)).astype(np.float64)[None]
    t = angle(r + REACH, c)
    a = stack(np.cos(t) * used, -np.sin(t) * used)
    i, j = grid(np.arange(KL), np.arange(KL))
    t = angle(i, j - REACH)
    b = stack(np.cos(t), -np.sin(t))
    lead = REACH - (KS - 1) // 2
    small = ((i >= lead) & (i < lead + KS) & (j >= lead) & (j < lead + KS)).nonzero()[0]
    bs = np.pad(b[:, small], ((0, 0), (0, 32 - KS * KS)))
    b = np.pad(b, ((0, 0), (0, 2 * C - KL * KL)))
    y, x = grid(np.arange(TH), np.arange(TW))
    t = angle(y, x)
    w = np.full((len(freqs), 1), 2.0)
    w[0] = 1.0
    w /= NY * NX
    ct = stack(w * np.cos(t), -w * np.sin(t))
    return tuple(m.astype(np.float32).astype(bf16) for m in (a, a.T, b, b.T, bs, bs.T, ct.T, ct))


def dot(a, b, dims=(1, 0)):
    return lax.dot_general(a, b, (((dims[0],), (dims[1],)), ((), ())), preferred_element_type=f32)


def exchange_kernel(nb, nr, x_ref, o_ref, send_sem, recv_sem):
    nd = nb * nr
    me = lax.axis_index("batch") * nr + lax.axis_index("rows")

    def peer(k):
        other = lax.rem(me + k, nd)
        return (other // nr, lax.rem(other, nr))

    barrier = pltpu.get_barrier_semaphore()

    @pl.loop(1, nd)
    def _(k):
        pl.semaphore_signal(barrier, inc=1, device_id=peer(k), device_id_type=pl.DeviceIdType.MESH)

    o_ref[me] = x_ref[...]
    pl.semaphore_wait(barrier, nd - 1)

    @pl.loop(1, nd)
    def _(k):
        pltpu.make_async_remote_copy(
            o_ref.at[me], o_ref.at[me], send_sem, recv_sem, device_id=peer(k), device_id_type=pl.DeviceIdType.MESH
        ).start()

    others = o_ref.at[pl.ds(0, nd - 1)]
    pltpu.make_async_copy(others, others, recv_sem).wait()
    pltpu.make_async_copy(others, others, send_sem).wait()


def exchange(rows):
    x = jnp.stack(rows)
    nb, nr = lax.axis_size("batch"), lax.axis_size("rows")
    return pl.pallas_call(
        functools.partial(exchange_kernel, nb, nr),
        out_shape=jax.ShapeDtypeStruct((nb * nr,) + x.shape, f32),
        in_specs=[pl.BlockSpec(memory_space=pltpu.VMEM)],
        out_specs=pl.BlockSpec(memory_space=pltpu.VMEM),
        scratch_shapes=[pltpu.SemaphoreType.DMA, pltpu.SemaphoreType.DMA],
        compiler_params=pltpu.CompilerParams(
            collective_id=x.shape[0] + 8 * (x.shape[1] != C), has_side_effects=True, vmem_limit_bytes=32 * 2**20
        ),
    )(x)


MESH = pl.DeviceIdType.MESH
WIDTHS = (4, 3, 8, 8, 5, 3, 2)


def chunks(n, fn, init=()):
    return lax.fori_loop(0, n // 32, lambda i, c: fn(pl.ds(pl.multiple_of(i * 32, 32), 32), c), init)


def fold(v):
    return jnp.sum(v.reshape(v.shape[0] // 8, 8, v.shape[1]), axis=0)


def close(v):
    return jnp.sum(v, axis=0, keepdims=True)


def gelu_both(v):
    a = np.float32(np.sqrt(2 / np.pi))
    sq = v * v
    t = jnp.tanh(a * (v + 0.044715 * (sq * v)))
    half = 0.5 * (1 + t)
    return v * half, half + 0.5 * v * (1 - t * t) * (a * (1 + 3 * 0.044715 * sq))


def core_kernel(
    nb, nr, x_ref, cot_ref, sx_ref, tab_hbm, a_hbm, at_hbm, b_hbm, bt_hbm, bs_ref, bst_ref, c_hbm, ct_hbm,
    out_ref, gin_ref, grad_hbm,
    tab, ta, tat, tb, tbt, tc, tct, pre_low, wide, dz, spec_u, spec_l, spec_s, prod_l, prod_s, prod_k,
    d_l, d_s, s_val, t_low, p_val, mid, c_low, gy_low, hid, gact, a_low, gh_low, g_f, acc, stage0, stage1, halo_out, halo_in,
    *rest,
):
    first = rest[: len(WIDTHS)]
    second = rest[len(WIDTHS) : 2 * len(WIDTHS)]
    send_sem, recv_sem, halo_send, halo_recv, load_sem, store_sem = rest[2 * len(WIDTHS) :]
    n = x_ref.shape[0]
    every = float(n * nb * nr)
    b = lax.axis_index("batch")
    r = lax.axis_index("rows")

    barrier = pltpu.get_barrier_semaphore()
    for k in range(1, nr):
        pl.semaphore_signal(barrier, inc=1, device_id=(b, lax.rem(r + k, nr)), device_id_type=MESH)
    for k in range(1, nb):
        pl.semaphore_signal(barrier, inc=1, device_id=(lax.rem(b + k, nb), r), device_id_type=MESH)

    pieces = [pl.ds(0, 2 * C), pl.ds(2 * C + 2 * FF, 2 * C), pl.ds(2 * C, 2 * FF)]
    moves = [(tab_hbm.at[p], tab.at[p]) for p in pieces]
    order = [moves[0], moves[1], (b_hbm, tb), (a_hbm, ta), (c_hbm, tc), moves[2], (ct_hbm, tct), (at_hbm, tat), (bt_hbm, tbt)]
    loads = [pltpu.make_async_copy(s, d, load_sem.at[i]) for i, (s, d) in enumerate(order)]
    for c in loads:
        c.start()
    ld_w, ld_k, ld_b, ld_a, ld_c, ld_f, ld_ct, ld_at, ld_bt = loads

    def share(e, v, merge, work=lambda: None):
        count = n
        for stage, (buf, mine, axis, size) in enumerate(((first[e], r, "rows", nr), (second[e], b, "batch", nb))):
            buf[mine] = v
            for k in range(1, size):
                other = lax.rem(mine + k, size)
                where = (b, other) if axis == "rows" else (other, r)
                pltpu.make_async_remote_copy(
                    buf.at[mine], buf.at[mine], send_sem.at[e, stage], recv_sem.at[e, stage],
                    device_id=where, device_id_type=MESH,
                ).start()
            if stage == 0:
                work()
            got = buf.at[pl.ds(0, size - 1)]
            pltpu.make_async_copy(got, got, recv_sem.at[e, stage]).wait()
            v = merge(buf, size, float(count))
            count = count * size
        return v

    def merge_sum(buf, size, count):
        return jnp.sum(buf[...], axis=0)

    def merge_stats(h):
        def merge(buf, size, count):
            v = buf[...]
            means = v[:, :h]
            m = jnp.sum(means, axis=0) * (1.0 / size)
            d = means - m
            parts = [m, jnp.sum(v[:, h : 2 * h], axis=0) + count * jnp.sum(d * d, axis=0)]
            if v.shape[1] > 2 * h:
                parts.append(jnp.sum(v[:, 2 * h :], axis=0))
            return jnp.concatenate(parts, axis=0)

        return merge

    zero = jnp.zeros((8, C), f32)

    m_x, q_x = sx_ref[0:1, :], sx_ref[1:2, :]
    inv_x = lax.rsqrt(q_x + norm_eps)
    ld_w.wait()
    ld_k.wait()
    small = tab[pl.ds(2 * C + 2 * FF + 976, 48), :].astype(f32)
    row = lambda i: small[32 + i : 33 + i, :]
    mid_gain = lambda j: small[42 + j : 43 + j, :]
    mid_bias = lambda j: small[25 + j : 26 + j, :]

    def pre(s, sx):
        d = x_ref[s, :] - m_x
        pre_low[s, :] = (d * (inv_x * row(0)) + row(1)).astype(bf16)
        return sx + fold(d)

    sum_x = close(chunks(n, pre, zero))
    dz[...] = dot(pre_low[...], tab[pl.ds(0, C), :])

    def act(s, c):
        u, d = gelu_both(dz[s, :])
        dz[s, :] = d
        wide[pl.ds(pl.multiple_of(n + s.start, 32), 32), :] = u.astype(bf16)
        return c

    chunks(n, act)

    pl.semaphore_wait(barrier, nr - 1 + nb - 1)
    mine = wide.at[pl.ds(n, n)]
    up = pltpu.make_async_remote_copy(
        mine, wide.at[pl.ds(2 * n, n)], halo_send.at[0], halo_recv.at[0], device_id=(b, lax.rem(r + nr - 1, nr)), device_id_type=MESH
    )
    down = pltpu.make_async_remote_copy(
        mine, wide.at[pl.ds(0, n)], halo_send.at[1], halo_recv.at[1], device_id=(b, lax.rem(r + 1, nr)), device_id_type=MESH
    )
    has_above, has_below = r > 0, r < nr - 1

    @pl.when(has_above)
    def _():
        up.start()

    @pl.when(has_below)
    def _():
        down.start()

    ld_b.wait()
    kernel_rows = pl.ds(2 * C + 2 * FF, 2 * C)
    small_rows = pl.ds(2 * C + 2 * FF + 976, 32)

    @pl.loop(0, 2 * NF // 256)
    def _(t):
        s = pl.ds(pl.multiple_of(t * 256, 256), 256)
        spec_l[s, :] = dot(tb[s, :], tab[kernel_rows, :])
        spec_s[s, :] = dot(bs_ref[s, :], tab[small_rows, :])

    @pl.when(has_below)
    def _():
        up.wait_recv()
        down.wait_send()

    @pl.when(has_above)
    def _():
        down.wait_recv()
        up.wait_send()

    @pl.when(jnp.logical_not(has_above))
    def _():
        wide[pl.ds(0, n), :] = jnp.zeros((n, C), bf16)

    @pl.when(jnp.logical_not(has_below))
    def _():
        wide[pl.ds(2 * n, n), :] = jnp.zeros((n, C), bf16)

    ld_a.wait()

    @pl.loop(0, 2 * NF // 256)
    def _(t):
        s = pl.ds(pl.multiple_of(t * 256, 256), 256)
        spec_u[s, :] = dot(ta[s, :], wide[...])

    def halves(i):
        return pl.ds(pl.multiple_of(i * 32, 32), 32), pl.ds(pl.multiple_of(NF + i * 32, 32), 32)

    @pl.loop(0, NF // 32)
    def _(i):
        re, im = halves(i)
        ur, ui = spec_u[re, :], spec_u[im, :]
        for k, p in ((spec_l, prod_l), (spec_s, prod_s)):
            kr, ki = k[re, :], k[im, :]
            p[re, :] = (ur * kr + ui * ki).astype(bf16)
            p[im, :] = (ui * kr - ur * ki).astype(bf16)

    ld_c.wait()
    d_l[...] = dot(tc[...], prod_l[...])
    d_s[...] = dot(tc[...], prod_s[...])

    def local(ref):
        m = close(chunks(n, lambda s, c: c + fold(ref[s, :]), zero)) * (1.0 / n)

        def sq(s, c):
            d = ref[s, :] - m
            return c + fold(d * d)

        return m, close(chunks(n, sq, zero))

    m_l, v_l = local(d_l)
    m_s, v_s = local(d_s)

    def early():
        def low(s, c):
            gy_low[s, :] = cot_ref[s, :].astype(bf16)
            return c

        chunks(n, low)

    tot = share(0, jnp.concatenate([m_l, m_s, v_l, v_s], axis=0), merge_stats(2), early)
    m_l, m_s = tot[0:1], tot[1:2]
    inv_l, inv_s = lax.rsqrt(tot[2:3] / every + norm_eps), lax.rsqrt(tot[3:4] / every + norm_eps)

    def pair(s, c):
        hl = (d_l[s, :] - m_l) * inv_l
        hs = (d_s[s, :] - m_s) * inv_s
        d_l[s, :] = hl
        d_s[s, :] = hs
        t, d = gelu_both(hl * row(2) + row(3) + hs * row(4) + row(5))
        s_val[s, :] = d
        t_low[s, :] = t.astype(bf16)
        return c

    chunks(n, pair)
    p_val[...] = dot(t_low[...], tab[pl.ds(C, C), :])
    m_p = close(chunks(n, lambda s, c: c + fold(p_val[s, :]), zero)) * (1.0 / n)

    def proj(s, c):
        d = p_val[s, :] - m_p
        return c[0] + fold(d * d), c[1] + fold(d * (x_ref[s, :] - m_x))

    v_p, cross = chunks(n, proj, (zero, zero))
    tot = share(1, jnp.concatenate([m_p, close(v_p), close(cross) + m_p * sum_x], axis=0), merge_stats(1))
    m_p, q_p, cov = tot[0:1], tot[1:2] / every, tot[2:3] / every
    inv_p = lax.rsqrt(q_p + norm_eps)
    slope = row(6) * inv_p
    m_f = m_x + row(7)
    q_f = jnp.maximum(q_x + 2 * slope * cov + slope * slope * q_p, 0.0)
    inv_f = lax.rsqrt(q_f + norm_eps)
    hats = inv_f * inv_p * (cov + slope * q_p)

    def ffn(s, c):
        ph = (p_val[s, :] - m_p) * inv_p
        p_val[s, :] = ph
        m = x_ref[s, :] + (ph * row(6) + row(7))
        mid[s, :] = m
        c_low[s, :] = ((m - m_f) * (inv_f * row(8)) + row(9)).astype(bf16)
        g = cot_ref[s, :]
        return c[0] + fold(g), c[1] + fold(g * ph)

    sum_c, sum_ch = chunks(n, ffn, (zero, zero))
    sum_c, sum_ch = close(sum_c), close(sum_ch)
    ld_f.wait()
    up_rows = lambda j: pl.ds(pl.multiple_of(2 * C + j * C, C), C)
    down_rows = lambda j: pl.ds(pl.multiple_of(2 * C + FF + j * C, C), C)
    blocks = FF // C
    for j in range(blocks):
        hid[j] = dot(c_low[...], tab[up_rows(j), :])
    st = [local(hid.at[j]) for j in range(blocks)]

    def back_first():
        for j in range(blocks):
            gact[j] = dot(gy_low[...], tab[down_rows(j), :], (1, 1))

    tot = share(2, jnp.concatenate([s[0] for s in st] + [s[1] for s in st], axis=0), merge_stats(blocks), back_first)
    m_h = tot[:blocks]
    inv_h = lax.rsqrt(tot[blocks:] / every + norm_eps)
    sums = []
    for j in range(blocks):
        mj, ij, gj, bj = m_h[j : j + 1], inv_h[j : j + 1], mid_gain(j), mid_bias(j)

        def hidden(s, c, j=j, mj=mj, ij=ij, gj=gj, bj=bj):
            hat = (hid[j, s, :] - mj) * ij
            hid[j, s, :] = hat
            a, d = gelu_both(hat * gj + bj)
            a_low[j, s, :] = a.astype(bf16)
            g = gact[j, s, :] * d
            gact[j, s, :] = g
            return c[0] + fold(g), c[1] + fold(g * hat)

        sums.append(tuple(close(v) for v in chunks(n, hidden, (zero, zero))))
    mid_rows = jnp.concatenate([s[0] for s in sums] + [s[1] for s in sums], axis=0)

    def half_cols(h):
        return pl.ds(pl.multiple_of(h * 256, 256), 256)

    def outputs():
        out_ref[...] = mid[...]
        for j in range(blocks):
            out_ref[...] += dot(a_low[j], tab[down_rows(j), :])
            for h in range(C // 256):
                stage0[pl.ds(j * C + h * 256, 256), :] = dot(a_low[j, :, half_cols(h)], gy_low[...], (0, 0))

    tot = share(3, mid_rows, merge_sum, outputs) * (1.0 / every)
    st_down = pltpu.make_async_copy(stage0, grad_hbm.at[pl.ds(2 * C + FF, FF)], store_sem.at[0])
    st_down.start()
    for j in range(blocks):
        tb_, tg_, sc = tot[j : j + 1], tot[blocks + j : blocks + j + 1], mid_gain(j) * inv_h[j : j + 1]

        def grad_h(s, c, j=j, tb_=tb_, tg_=tg_, sc=sc):
            gh_low[j, s, :] = (sc * (gact[j, s, :] - tb_ - hid[j, s, :] * tg_)).astype(bf16)
            return c

        chunks(n, grad_h)
    g_f[...] = dot(gh_low[0], tab[up_rows(0), :], (1, 1))
    for j in range(1, blocks):
        g_f[...] += dot(gh_low[j], tab[up_rows(j), :], (1, 1))

    def ffn_sums(s, c):
        g = g_f[s, :]
        hat = (mid[s, :] - m_f) * inv_f
        return c[0] + fold(g), c[1] + fold(g * hat), c[2] + fold(g * p_val[s, :])

    b_ffn, g_ffn, g_fp = (close(v) for v in chunks(n, ffn_sums, (zero, zero, zero)))

    def grad_up():
        for j in range(blocks):
            for h in range(C // 256):
                stage1[pl.ds(j * C + h * 256, 256), :] = dot(c_low[:, half_cols(h)], gh_low[j], (0, 0))

    tot = share(4, jnp.concatenate([b_ffn, g_ffn, g_fp, sum_c, sum_ch], axis=0), merge_sum, grad_up) * (1.0 / every)
    st_up = pltpu.make_async_copy(stage1, grad_hbm.at[pl.ds(2 * C, FF)], store_sem.at[1])
    st_up.start()
    scale_f = row(8) * inv_f
    mean_hat = tot[4:5] + scale_f * (tot[2:3] - tot[1:2] * hats)

    def grad_mid(s, c):
        hat = (mid[s, :] - m_f) * inv_f
        g = cot_ref[s, :] + scale_f * (g_f[s, :] - tot[0:1] - hat * tot[1:2])
        g_f[s, :] = g
        ph = p_val[s, :]
        pre_p = slope * (g - tot[3:4] - ph * mean_hat)
        gh_low[0, s, :] = pre_p.astype(bf16)
        return c[0] + fold(g), c[1] + fold(g * ph)

    b_proj, g_proj = (close(v) for v in chunks(n, grad_mid, (zero, zero)))
    p_val[...] = dot(gh_low[0], tab[pl.ds(C, C), :], (1, 1))

    def grad_s(s, c):
        g = p_val[s, :] * s_val[s, :]
        p_val[s, :] = g
        return c[0] + fold(g), c[1] + fold(g * d_l[s, :]), c[2] + fold(g * d_s[s, :])

    b_pair, g_lg, g_sg = (close(v) for v in chunks(n, grad_s, (zero, zero, zero)))
    st_down.wait()

    def grad_out():
        for h in range(C // 256):
            stage0[pl.ds(C + h * 256, 256), :] = dot(t_low[:, half_cols(h)], gh_low[0], (0, 0))

    tot = share(5, jnp.concatenate([b_pair, g_lg, g_sg], axis=0), merge_sum, grad_out) * (1.0 / every)
    sc_l, sc_s = row(2) * inv_l, row(4) * inv_s

    def grad_pair(s, c):
        g = p_val[s, :] - tot[0:1]
        t_low[s, :] = (sc_l * (g - d_l[s, :] * tot[1:2])).astype(bf16)
        gh_low[1, s, :] = (sc_s * (g - d_s[s, :] * tot[2:3])).astype(bf16)
        return c

    chunks(n, grad_pair)
    ld_ct.wait()

    @pl.loop(0, NF // 256)
    def _(t):
        re, im = pl.ds(pl.multiple_of(t * 256, 256), 256), pl.ds(pl.multiple_of(NF + t * 256, 256), 256)
        acc[0] = dot(tct[re, :], t_low[...])
        acc[1] = dot(tct[im, :], t_low[...])
        acc[2] = dot(tct[re, :], gh_low[1])
        acc[3] = dot(tct[im, :], gh_low[1])

        @pl.loop(0, 8)
        def _(i):
            s = pl.ds(pl.multiple_of(i * 32, 32), 32)
            re = pl.ds(pl.multiple_of(t * 256 + i * 32, 32), 32)
            im = pl.ds(pl.multiple_of(NF + t * 256 + i * 32, 32), 32)
            lr, li, sr, si = acc[0, s, :], acc[1, s, :], acc[2, s, :], acc[3, s, :]
            kr, ki = spec_l[re, :], spec_l[im, :]
            hr, hi = spec_s[re, :], spec_s[im, :]
            prod_k[re, :] = (lr * kr - li * ki + sr * hr - si * hi).astype(bf16)
            prod_k[im, :] = (lr * ki + li * kr + sr * hi + si * hr).astype(bf16)
            ur, ui = spec_u[re, :], spec_u[im, :]
            prod_l[re, :] = (lr * ur + li * ui).astype(bf16)
            prod_l[im, :] = (lr * ui - li * ur).astype(bf16)
            prod_s[re, :] = (sr * ur + si * ui).astype(bf16)
            prod_s[im, :] = (sr * ui - si * ur).astype(bf16)

    ld_at.wait()
    halo_out[0] = dot(tat[pl.ds(0, n), :], prod_k[...]).astype(bf16)
    halo_out[1] = dot(tat[pl.ds(2 * n, n), :], prod_k[...]).astype(bf16)
    up2 = pltpu.make_async_remote_copy(
        halo_out.at[0], halo_in.at[1], halo_send.at[2], halo_recv.at[2], device_id=(b, lax.rem(r + nr - 1, nr)), device_id_type=MESH
    )
    down2 = pltpu.make_async_remote_copy(
        halo_out.at[1], halo_in.at[0], halo_send.at[3], halo_recv.at[3], device_id=(b, lax.rem(r + 1, nr)), device_id_type=MESH
    )

    @pl.when(has_above)
    def _():
        up2.start()

    @pl.when(has_below)
    def _():
        down2.start()

    p_val[...] = dot(tat[pl.ds(n, n), :], prod_k[...])
    ld_bt.wait()

    @pl.loop(0, 4)
    def _(t):
        s = pl.ds(pl.multiple_of(t * 256, 256), 256)
        stage0[pl.ds(pl.multiple_of(2 * C + t * 256, 256), 256), :] = dot(tbt[s, :], prod_l[...])

    stage0[pl.ds(2 * C + 976, 32), :] = dot(bst_ref[...], prod_s[...])

    @pl.when(has_below)
    def _():
        up2.wait_recv()
        down2.wait_send()

    @pl.when(has_above)
    def _():
        down2.wait_recv()
        up2.wait_send()

    @pl.when(jnp.logical_not(has_above))
    def _():
        halo_in[0] = jnp.zeros((n, C), bf16)

    @pl.when(jnp.logical_not(has_below))
    def _():
        halo_in[1] = jnp.zeros((n, C), bf16)

    def grad_z(s, c):
        g = p_val[s, :] + halo_in[0, s, :].astype(f32) + halo_in[1, s, :].astype(f32)
        t_low[s, :] = (g * dz[s, :]).astype(bf16)
        return c

    chunks(n, grad_z)
    p_val[...] = dot(t_low[...], tab[pl.ds(0, C), :], (1, 1))

    def pre_sums(s, c):
        g = p_val[s, :]
        return c[0] + fold(g), c[1] + fold(g * ((x_ref[s, :] - m_x) * inv_x))

    b_pre, g_pre = (close(v) for v in chunks(n, pre_sums, (zero, zero)))

    def grad_in():
        for h in range(C // 256):
            stage0[pl.ds(h * 256, 256), :] = dot(pre_low[:, half_cols(h)], t_low[...], (0, 0))

    tot = share(6, jnp.concatenate([b_pre, g_pre], axis=0), merge_sum, grad_in) * (1.0 / every)
    scale_x = row(0) * inv_x
    norms = [g_pre, b_pre, g_lg, b_pair, g_sg, b_pair, g_proj, b_proj, g_ffn, b_ffn]
    norms += [mid_rows[blocks + j : blocks + j + 1] for j in range(blocks)]
    base = 2 * C + 976
    stage0[pl.ds(base + 32, 16), :] = jnp.concatenate(norms + [jnp.zeros((2, C), f32)], axis=0)
    for j in range(blocks):
        stage0[pl.ds(base + 25 + j, 1), :] = mid_rows[j : j + 1]
    stores = [
        pltpu.make_async_copy(stage0.at[pl.ds(0, 2 * C)], grad_hbm.at[pl.ds(0, 2 * C)], store_sem.at[2]),
        pltpu.make_async_copy(stage0.at[pl.ds(2 * C, 2 * C)], grad_hbm.at[pl.ds(2 * C + 2 * FF, 2 * C)], store_sem.at[3]),
    ]
    for c in stores:
        c.start()

    def last(s, c):
        hat = (x_ref[s, :] - m_x) * inv_x
        gin_ref[s, :] = g_f[s, :] + scale_x * (p_val[s, :] - tot[0:1] - hat * tot[1:2])
        return c

    chunks(n, last)
    for e in range(len(WIDTHS)):
        for stage, (buf, size) in enumerate(((first[e], nr), (second[e], nb))):
            sent = buf.at[pl.ds(0, size - 1)]
            pltpu.make_async_copy(sent, sent, send_sem.at[e, stage]).wait()
    st_up.wait()
    for c in stores:
        c.wait()


def core(x, cot, sx, tab, nb, nr):
    (a, at, b, bt, bs, bst, c, ct) = tables()
    n = x.shape[0]
    vm = lambda shape, dtype=f32: pltpu.VMEM(shape, dtype)
    pix = vm((n, C))
    low = vm((n, C), bf16)
    wide_spec = vm((2 * NF, C))
    low_spec = vm((2 * NF, C), bf16)
    vmem = pl.BlockSpec(memory_space=pltpu.VMEM)
    anywhere = pl.BlockSpec(memory_space=pl.ANY)
    scratch = [vm(tab.shape, bf16)] + [vm(m.shape, bf16) for m in (a, at, b, bt, c, ct)]
    scratch += [low, vm((3 * n, C), bf16), pix, wide_spec, wide_spec, wide_spec, low_spec, low_spec, low_spec]
    scratch += [pix, pix, pix, low, pix, pix, low, low]
    scratch += [vm((FF // C, n, C)), vm((FF // C, n, C)), vm((FF // C, n, C), bf16), vm((FF // C, n, C), bf16), pix, vm((4, 256, C))]
    scratch += [vm((FF, C)), vm((FF, C)), vm((2, n, C), bf16), vm((2, n, C), bf16)]
    scratch += [vm((nr, w, C)) for w in WIDTHS] + [vm((nb, w, C)) for w in WIDTHS]
    dma = pltpu.SemaphoreType.DMA
    scratch += [dma((len(WIDTHS), 2)), dma((len(WIDTHS), 2)), dma((4,)), dma((4,)), dma((9,)), dma((4,))]
    return pl.pallas_call(
        functools.partial(core_kernel, nb, nr),
        out_shape=[
            jax.ShapeDtypeStruct((n, C), f32),
            jax.ShapeDtypeStruct((n, C), f32),
            jax.ShapeDtypeStruct(tab.shape, f32),
        ],
        in_specs=[vmem] * 3 + [anywhere] * 5 + [vmem] * 2 + [anywhere] * 2,
        out_specs=[vmem, vmem, anywhere],
        scratch_shapes=scratch,
        compiler_params=pltpu.CompilerParams(collective_id=1, has_side_effects=True, vmem_limit_bytes=62 * 2**20),
    )(x, cot, sx, tab, a, at, b, bt, bs, bst, c, ct)


def table_place(t):
    start = 2 * C + 2 * FF
    k_end = start + KL * KL
    s_end = k_end + KS * KS
    m_gain = s_end + 10
    m_bias = m_gain + FF // C
    m_end = m_bias + FF // C
    up = t - 2 * C
    up = 2 * C + up % (FF // C) * C + up // (FF // C)
    base = start + 976
    unused = t - m_end
    unused = jnp.where(unused < 15, k_end + unused, jnp.where(unused < 18, base + 29 + unused - 15, base + 46 + unused - 18))
    p = jnp.where((t >= 2 * C) & (t < 2 * C + FF), up, t)
    p = jnp.where(t >= k_end, t - k_end + base, p)
    p = jnp.where(t >= s_end, t - s_end + base + 32, p)
    p = jnp.where(t >= m_bias, t - m_bias + base + 25, p)
    return jnp.where(t >= m_end, unused, p)


def body(image_in, cotangent, slot_rows, master, first_moment, second_moment):
    n = image_in.shape[0] * image_in.shape[1] * image_in.shape[2]
    nb, nr = lax.axis_size("batch"), lax.axis_size("rows")
    norm_start = 2 * C + 2 * FF + KL * KL + KS * KS
    places = table_place(slot_rows)
    own_copy = master.astype(bf16)
    gathered = lax.all_gather(own_copy, AXES, axis=0, tiled=True)
    ordered = jnp.zeros_like(gathered).at[places].set(gathered)
    x = image_in.reshape(n, C)
    cot = cotangent.reshape(n, C)
    m = jnp.mean(x, axis=0)
    d = x - m
    all_one = exchange((m, jnp.sum(d * d, axis=0)))
    m_x = jnp.mean(all_one[:, 0], axis=0)
    d = all_one[:, 0] - m_x
    q_x = (jnp.sum(all_one[:, 1], axis=0) + n * jnp.sum(d * d, axis=0)) / (n * nb * nr)
    result, grad_x, grads = core(x, cot, jnp.stack([m_x, q_x]), ordered, nb, nr)
    slot_grads = grads[places]
    reduced = lax.psum_scatter(slot_grads, AXES, scatter_dimension=0, tiled=True)
    own_count = master.shape[0]
    place = lax.axis_index("batch") * nr + lax.axis_index("rows")
    own_rows = lax.dynamic_slice_in_dim(slot_rows, place * own_count, own_count)
    rates = jnp.where(own_rows >= norm_start, norm_rate, matrix_rate)[:, None]
    new_first = beta_one * first_moment + (1.0 - beta_one) * reduced
    new_second = beta_two * second_moment + (1.0 - beta_two) * reduced * reduced
    first_hat = new_first / (1.0 - beta_one**STEP)
    second_hat = new_second / (1.0 - beta_two**STEP)
    new_master = master - rates * (
        first_hat / (jnp.sqrt(second_hat) + adam_eps) + decay_rate * master
    )
    return (
        result.reshape(image_in.shape),
        grad_x.reshape(image_in.shape),
        reduced,
        new_first,
        new_second,
        new_master,
        new_master.astype(bf16),
    )


def solution(mesh):
    image = P("batch", "rows", None, None)
    owner = P(AXES, None)
    return jax.shard_map(
        body,
        mesh=mesh,
        in_specs=(image, image, P(), owner, owner, owner),
        out_specs=(image, image, owner, owner, owner, owner, owner),
        check_vma=False,
    )
```

```python
import functools

import jax
import jax.numpy as jnp
import numpy as np
from jax import lax
from jax.experimental import pallas as pl
from jax.experimental.pallas import tpu as pltpu
from jax.sharding import PartitionSpec as P

C = 512
FF = 2048
KL = 31
KS = 5
STEP = 10

norm_eps = 1e-05
beta_one = 0.9
beta_two = 0.999
adam_eps = 1e-08
decay_rate = 0.05
matrix_rate = 0.05
norm_rate = 0.5

TH = 16
TW = 16
NY = 47
NX = 31
NF = 768
REACH = (KL - 1) // 2
AXES = ("batch", "rows")
f32 = jnp.float32
bf16 = jnp.bfloat16


@functools.lru_cache(None)
def tables():
    freqs = [(ky, 0) for ky in range((NY + 1) // 2)]
    freqs += [(ky, kx) for kx in range(1, (NX + 1) // 2) for ky in range(NY)]
    ky = np.array([f[0] for f in freqs], np.int64)[:, None]
    kx = np.array([f[1] for f in freqs], np.int64)[:, None]
    pad = NF - len(freqs)

    def angle(rows, cols):
        ty = (ky * rows.reshape(1, -1)) % NY
        tx = (kx * cols.reshape(1, -1)) % NX
        return 2 * np.pi * (ty / NY + tx / NX)

    def grid(rows, cols):
        r, c = np.meshgrid(rows, cols, indexing="ij")
        return r.reshape(-1), c.reshape(-1)

    def stack(re, im):
        z = np.zeros((pad, re.shape[1]))
        return np.concatenate([re, z, im, z], axis=0)

    r, c = grid(np.arange(-TH, 2 * TH), np.arange(TW))
    used = ((r + REACH >= 0) & (r + REACH < NY - 1)).astype(np.float64)[None]
    t = angle(r + REACH, c)
    a = stack(np.cos(t) * used, -np.sin(t) * used)
    i, j = grid(np.arange(KL), np.arange(KL))
    t = angle(i, j - REACH)
    b = stack(np.cos(t), -np.sin(t))
    lead = REACH - (KS - 1) // 2
    small = ((i >= lead) & (i < lead + KS) & (j >= lead) & (j < lead + KS)).nonzero()[0]
    bs = np.pad(b[:, small], ((0, 0), (0, 32 - KS * KS)))
    b = np.pad(b, ((0, 0), (0, 2 * C - KL * KL)))
    y, x = grid(np.arange(TH), np.arange(TW))
    t = angle(y, x)
    w = np.full((len(freqs), 1), 2.0)
    w[0] = 1.0
    w /= NY * NX
    ct = stack(w * np.cos(t), -w * np.sin(t))
    return tuple(m.astype(np.float32).astype(bf16) for m in (a, a.T, b, b.T, bs, bs.T, ct.T, ct))


def dot(a, b, dims=(1, 0)):
    return lax.dot_general(a, b, (((dims[0],), (dims[1],)), ((), ())), preferred_element_type=f32)


def exchange_kernel(nb, nr, x_ref, o_ref, send_sem, recv_sem):
    nd = nb * nr
    me = lax.axis_index("batch") * nr + lax.axis_index("rows")

    def peer(k):
        other = lax.rem(me + k, nd)
        return (other // nr, lax.rem(other, nr))

    barrier = pltpu.get_barrier_semaphore()

    @pl.loop(1, nd)
    def _(k):
        pl.semaphore_signal(barrier, inc=1, device_id=peer(k), device_id_type=pl.DeviceIdType.MESH)

    o_ref[me] = x_ref[...]
    pl.semaphore_wait(barrier, nd - 1)

    @pl.loop(1, nd)
    def _(k):
        pltpu.make_async_remote_copy(
            o_ref.at[me], o_ref.at[me], send_sem, recv_sem, device_id=peer(k), device_id_type=pl.DeviceIdType.MESH
        ).start()

    others = o_ref.at[pl.ds(0, nd - 1)]
    pltpu.make_async_copy(others, others, recv_sem).wait()
    pltpu.make_async_copy(others, others, send_sem).wait()


def exchange(rows):
    x = jnp.stack(rows)
    nb, nr = lax.axis_size("batch"), lax.axis_size("rows")
    return pl.pallas_call(
        functools.partial(exchange_kernel, nb, nr),
        out_shape=jax.ShapeDtypeStruct((nb * nr,) + x.shape, f32),
        in_specs=[pl.BlockSpec(memory_space=pltpu.VMEM)],
        out_specs=pl.BlockSpec(memory_space=pltpu.VMEM),
        scratch_shapes=[pltpu.SemaphoreType.DMA, pltpu.SemaphoreType.DMA],
        compiler_params=pltpu.CompilerParams(
            collective_id=0, has_side_effects=True, vmem_limit_bytes=32 * 2**20
        ),
    )(x)


MESH = pl.DeviceIdType.MESH
WIDTHS = (4, 3, 8, 8, 5, 3, 2)


def chunks(n, fn, init=()):
    return lax.fori_loop(0, n // 32, lambda i, c: fn(pl.ds(pl.multiple_of(i * 32, 32), 32), c), init)


def fold(v):
    return jnp.sum(v.reshape(v.shape[0] // 8, 8, v.shape[1]), axis=0)


def close(v):
    return jnp.sum(v, axis=0, keepdims=True)


def put(ref, start, v):
    for j in range(4):
        ref[pl.ds(start * 4 + j, v.shape[0], stride=4), :] = v[:, j * 128 : (j + 1) * 128]


def gelu_both(v):
    a = np.float32(np.sqrt(2 / np.pi))
    sq = v * v
    t = jnp.tanh(a * (v + 0.044715 * (sq * v)))
    half = 0.5 * (1 + t)
    return v * half, half + 0.5 * v * (1 - t * t) * (a * (1 + 3 * 0.044715 * sq))


def core_kernel(
    nb, nr, x_ref, cot_ref, sx_ref, tab_hbm, a_hbm, at_hbm, b_hbm, bt_hbm, bs_ref, bst_ref, c_hbm, ct_hbm,
    out_ref, gin_ref, grad_hbm,
    tab, ta, tat, tb, tbt, tc, tct, pre_low, wide, dz, spec_u, spec_l, spec_s, prod_l, prod_s, prod_k,
    d_l, d_s, s_val, t_low, p_val, mid, c_low, gy_low, hid, gact, a_low, gh_low, g_f, acc, stage0, stage1, halo_out, halo_in,
    *rest,
):
    first = rest[: len(WIDTHS)]
    second = rest[len(WIDTHS) : 2 * len(WIDTHS)]
    send_sem, recv_sem, halo_send, halo_recv, load_sem, store_sem = rest[2 * len(WIDTHS) :]
    n = x_ref.shape[0]
    every = float(n * nb * nr)
    b = lax.axis_index("batch")
    r = lax.axis_index("rows")

    barrier = pltpu.get_barrier_semaphore()
    for k in range(1, nr):
        pl.semaphore_signal(barrier, inc=1, device_id=(b, lax.rem(r + k, nr)), device_id_type=MESH)
    for k in range(1, nb):
        pl.semaphore_signal(barrier, inc=1, device_id=(lax.rem(b + k, nb), r), device_id_type=MESH)

    pieces = [pl.ds(0, 2 * C), pl.ds(2 * C + 2 * FF, 2 * C), pl.ds(2 * C, 2 * FF)]
    moves = [(tab_hbm.at[p], tab.at[p]) for p in pieces]
    order = [moves[0], moves[1], (b_hbm, tb), (a_hbm, ta), (c_hbm, tc), moves[2], (ct_hbm, tct), (at_hbm, tat), (bt_hbm, tbt)]
    loads = [pltpu.make_async_copy(s, d, load_sem.at[i]) for i, (s, d) in enumerate(order)]
    for c in loads:
        c.start()
    ld_w, ld_k, ld_b, ld_a, ld_c, ld_f, ld_ct, ld_at, ld_bt = loads

    def share(e, v, merge, work=lambda: None):
        count = n
        for stage, (buf, mine, axis, size) in enumerate(((first[e], r, "rows", nr), (second[e], b, "batch", nb))):
            buf[mine] = v
            for k in range(1, size):
                other = lax.rem(mine + k, size)
                where = (b, other) if axis == "rows" else (other, r)
                pltpu.make_async_remote_copy(
                    buf.at[mine], buf.at[mine], send_sem.at[e, stage], recv_sem.at[e, stage],
                    device_id=where, device_id_type=MESH,
                ).start()
            if stage == 0:
                work()
            got = buf.at[pl.ds(0, size - 1)]
            pltpu.make_async_copy(got, got, recv_sem.at[e, stage]).wait()
            v = merge(buf, size, float(count))
            count = count * size
        return v

    def merge_sum(buf, size, count):
        return jnp.sum(buf[...], axis=0)

    def merge_stats(h):
        def merge(buf, size, count):
            v = buf[...]
            means = v[:, :h]
            m = jnp.sum(means, axis=0) * (1.0 / size)
            d = means - m
            parts = [m, jnp.sum(v[:, h : 2 * h], axis=0) + count * jnp.sum(d * d, axis=0)]
            if v.shape[1] > 2 * h:
                parts.append(jnp.sum(v[:, 2 * h :], axis=0))
            return jnp.concatenate(parts, axis=0)

        return merge

    zero = jnp.zeros((8, C), f32)

    m_x, q_x = sx_ref[0:1, :], sx_ref[1:2, :]
    inv_x = lax.rsqrt(q_x + norm_eps)
    ld_w.wait()
    ld_k.wait()
    small = tab[pl.ds(2 * C + 2 * FF + 976, 48), :].astype(f32)
    row = lambda i: small[32 + i : 33 + i, :]
    mid_gain = lambda j: small[42 + j : 43 + j, :]
    mid_bias = lambda j: small[25 + j : 26 + j, :]

    def pre(s, sx):
        d = x_ref[s, :] - m_x
        pre_low[s, :] = (d * (inv_x * row(0)) + row(1)).astype(bf16)
        return sx + fold(d)

    sum_x = close(chunks(n, pre, zero))
    dz[...] = dot(pre_low[...], tab[pl.ds(0, C), :])

    def act(s, c):
        u, d = gelu_both(dz[s, :])
        dz[s, :] = d
        wide[pl.ds(pl.multiple_of(n + s.start, 32), 32), :] = u.astype(bf16)
        return c

    chunks(n, act)

    pl.semaphore_wait(barrier, nr - 1 + nb - 1)
    mine = wide.at[pl.ds(n, n)]
    up = pltpu.make_async_remote_copy(
        mine, wide.at[pl.ds(2 * n, n)], halo_send.at[0], halo_recv.at[0], device_id=(b, lax.rem(r + nr - 1, nr)), device_id_type=MESH
    )
    down = pltpu.make_async_remote_copy(
        mine, wide.at[pl.ds(0, n)], halo_send.at[1], halo_recv.at[1], device_id=(b, lax.rem(r + 1, nr)), device_id_type=MESH
    )
    has_above, has_below = r > 0, r < nr - 1

    @pl.when(has_above)
    def _():
        up.start()

    @pl.when(has_below)
    def _():
        down.start()

    ld_b.wait()
    kernel_rows = pl.ds(2 * C + 2 * FF, 2 * C)
    small_rows = pl.ds(2 * C + 2 * FF + 976, 32)

    @pl.loop(0, 2 * NF // 256)
    def _(t):
        s = pl.ds(pl.multiple_of(t * 256, 256), 256)
        spec_l[s, :] = dot(tb[s, :], tab[kernel_rows, :])
        spec_s[s, :] = dot(bs_ref[s, :], tab[small_rows, :])

    @pl.when(has_below)
    def _():
        up.wait_recv()
        down.wait_send()

    @pl.when(has_above)
    def _():
        down.wait_recv()
        up.wait_send()

    @pl.when(jnp.logical_not(has_above))
    def _():
        wide[pl.ds(0, n), :] = jnp.zeros((n, C), bf16)

    @pl.when(jnp.logical_not(has_below))
    def _():
        wide[pl.ds(2 * n, n), :] = jnp.zeros((n, C), bf16)

    ld_a.wait()

    @pl.loop(0, 2 * NF // 256)
    def _(t):
        s = pl.ds(pl.multiple_of(t * 256, 256), 256)
        spec_u[s, :] = dot(ta[s, :], wide[...])

    def halves(i):
        return pl.ds(pl.multiple_of(i * 32, 32), 32), pl.ds(pl.multiple_of(NF + i * 32, 32), 32)

    @pl.loop(0, NF // 32)
    def _(i):
        re, im = halves(i)
        ur, ui = spec_u[re, :], spec_u[im, :]
        for k, p in ((spec_l, prod_l), (spec_s, prod_s)):
            kr, ki = k[re, :], k[im, :]
            p[re, :] = (ur * kr + ui * ki).astype(bf16)
            p[im, :] = (ui * kr - ur * ki).astype(bf16)

    ld_c.wait()
    d_l[...] = dot(tc[...], prod_l[...])
    d_s[...] = dot(tc[...], prod_s[...])

    def local(ref):
        m = close(chunks(n, lambda s, c: c + fold(ref[s, :]), zero)) * (1.0 / n)

        def sq(s, c):
            d = ref[s, :] - m
            return c + fold(d * d)

        return m, close(chunks(n, sq, zero))

    m_l, v_l = local(d_l)
    m_s, v_s = local(d_s)

    def early():
        def low(s, c):
            gy_low[s, :] = cot_ref[s, :].astype(bf16)
            return c

        chunks(n, low)

    tot = share(0, jnp.concatenate([m_l, m_s, v_l, v_s], axis=0), merge_stats(2), early)
    m_l, m_s = tot[0:1], tot[1:2]
    inv_l, inv_s = lax.rsqrt(tot[2:3] / every + norm_eps), lax.rsqrt(tot[3:4] / every + norm_eps)

    def pair(s, c):
        hl = (d_l[s, :] - m_l) * inv_l
        hs = (d_s[s, :] - m_s) * inv_s
        d_l[s, :] = hl
        d_s[s, :] = hs
        t, d = gelu_both(hl * row(2) + row(3) + hs * row(4) + row(5))
        s_val[s, :] = d
        t_low[s, :] = t.astype(bf16)
        return c

    chunks(n, pair)
    p_val[...] = dot(t_low[...], tab[pl.ds(C, C), :])
    m_p = close(chunks(n, lambda s, c: c + fold(p_val[s, :]), zero)) * (1.0 / n)

    def proj(s, c):
        d = p_val[s, :] - m_p
        return c[0] + fold(d * d), c[1] + fold(d * (x_ref[s, :] - m_x))

    v_p, cross = chunks(n, proj, (zero, zero))
    tot = share(1, jnp.concatenate([m_p, close(v_p), close(cross) + m_p * sum_x], axis=0), merge_stats(1))
    m_p, q_p, cov = tot[0:1], tot[1:2] / every, tot[2:3] / every
    inv_p = lax.rsqrt(q_p + norm_eps)
    slope = row(6) * inv_p
    m_f = m_x + row(7)
    q_f = jnp.maximum(q_x + 2 * slope * cov + slope * slope * q_p, 0.0)
    inv_f = lax.rsqrt(q_f + norm_eps)
    hats = inv_f * inv_p * (cov + slope * q_p)

    def ffn(s, c):
        ph = (p_val[s, :] - m_p) * inv_p
        p_val[s, :] = ph
        m = x_ref[s, :] + (ph * row(6) + row(7))
        mid[s, :] = m
        c_low[s, :] = ((m - m_f) * (inv_f * row(8)) + row(9)).astype(bf16)
        g = cot_ref[s, :]
        return c[0] + fold(g), c[1] + fold(g * ph)

    sum_c, sum_ch = chunks(n, ffn, (zero, zero))
    sum_c, sum_ch = close(sum_c), close(sum_ch)
    ld_f.wait()
    up_rows = lambda j: pl.ds(pl.multiple_of(2 * C + j * C, C), C)
    down_rows = lambda j: pl.ds(pl.multiple_of(2 * C + FF + j * C, C), C)
    blocks = FF // C
    for j in range(blocks):
        hid[j] = dot(c_low[...], tab[up_rows(j), :])
    st = [local(hid.at[j]) for j in range(blocks)]

    def back_first():
        for j in range(blocks):
            gact[j] = dot(gy_low[...], tab[down_rows(j), :], (1, 1))

    tot = share(2, jnp.concatenate([s[0] for s in st] + [s[1] for s in st], axis=0), merge_stats(blocks), back_first)
    m_h = tot[:blocks]
    inv_h = lax.rsqrt(tot[blocks:] / every + norm_eps)
    sums = []
    for j in range(blocks):
        mj, ij, gj, bj = m_h[j : j + 1], inv_h[j : j + 1], mid_gain(j), mid_bias(j)

        def hidden(s, c, j=j, mj=mj, ij=ij, gj=gj, bj=bj):
            hat = (hid[j, s, :] - mj) * ij
            hid[j, s, :] = hat
            a, d = gelu_both(hat * gj + bj)
            a_low[j, s, :] = a.astype(bf16)
            g = gact[j, s, :] * d
            gact[j, s, :] = g
            return c[0] + fold(g), c[1] + fold(g * hat)

        sums.append(tuple(close(v) for v in chunks(n, hidden, (zero, zero))))
    mid_rows = jnp.concatenate([s[0] for s in sums] + [s[1] for s in sums], axis=0)

    def half_cols(h):
        return pl.ds(pl.multiple_of(h * 256, 256), 256)

    def outputs():
        out_ref[...] = mid[...]
        for j in range(blocks):
            out_ref[...] += dot(a_low[j], tab[down_rows(j), :])
            for h in range(C // 256):
                put(stage0, j * C + h * 256, dot(a_low[j, :, half_cols(h)], gy_low[...], (0, 0)))

    tot = share(3, mid_rows, merge_sum, outputs) * (1.0 / every)
    st_down = pltpu.make_async_copy(stage0, grad_hbm.at[pl.ds(4 * (2 * C + FF), 4 * FF)], store_sem.at[0])
    st_down.start()
    for j in range(blocks):
        tb_, tg_, sc = tot[j : j + 1], tot[blocks + j : blocks + j + 1], mid_gain(j) * inv_h[j : j + 1]

        def grad_h(s, c, j=j, tb_=tb_, tg_=tg_, sc=sc):
            gh_low[j, s, :] = (sc * (gact[j, s, :] - tb_ - hid[j, s, :] * tg_)).astype(bf16)
            return c

        chunks(n, grad_h)
    g_f[...] = dot(gh_low[0], tab[up_rows(0), :], (1, 1))
    for j in range(1, blocks):
        g_f[...] += dot(gh_low[j], tab[up_rows(j), :], (1, 1))

    def ffn_sums(s, c):
        g = g_f[s, :]
        hat = (mid[s, :] - m_f) * inv_f
        return c[0] + fold(g), c[1] + fold(g * hat), c[2] + fold(g * p_val[s, :])

    b_ffn, g_ffn, g_fp = (close(v) for v in chunks(n, ffn_sums, (zero, zero, zero)))

    def grad_up():
        for j in range(blocks):
            for h in range(C // 256):
                put(stage1, j * C + h * 256, dot(c_low[:, half_cols(h)], gh_low[j], (0, 0)))

    tot = share(4, jnp.concatenate([b_ffn, g_ffn, g_fp, sum_c, sum_ch], axis=0), merge_sum, grad_up) * (1.0 / every)
    st_up = pltpu.make_async_copy(stage1, grad_hbm.at[pl.ds(4 * 2 * C, 4 * FF)], store_sem.at[1])
    st_up.start()
    scale_f = row(8) * inv_f
    mean_hat = tot[4:5] + scale_f * (tot[2:3] - tot[1:2] * hats)

    def grad_mid(s, c):
        hat = (mid[s, :] - m_f) * inv_f
        g = cot_ref[s, :] + scale_f * (g_f[s, :] - tot[0:1] - hat * tot[1:2])
        g_f[s, :] = g
        ph = p_val[s, :]
        pre_p = slope * (g - tot[3:4] - ph * mean_hat)
        gh_low[0, s, :] = pre_p.astype(bf16)
        return c[0] + fold(g), c[1] + fold(g * ph)

    b_proj, g_proj = (close(v) for v in chunks(n, grad_mid, (zero, zero)))
    p_val[...] = dot(gh_low[0], tab[pl.ds(C, C), :], (1, 1))

    def grad_s(s, c):
        g = p_val[s, :] * s_val[s, :]
        p_val[s, :] = g
        return c[0] + fold(g), c[1] + fold(g * d_l[s, :]), c[2] + fold(g * d_s[s, :])

    b_pair, g_lg, g_sg = (close(v) for v in chunks(n, grad_s, (zero, zero, zero)))
    st_down.wait()

    def grad_out():
        for h in range(C // 256):
            put(stage0, C + h * 256, dot(t_low[:, half_cols(h)], gh_low[0], (0, 0)))

    tot = share(5, jnp.concatenate([b_pair, g_lg, g_sg], axis=0), merge_sum, grad_out) * (1.0 / every)
    sc_l, sc_s = row(2) * inv_l, row(4) * inv_s

    def grad_pair(s, c):
        g = p_val[s, :] - tot[0:1]
        t_low[s, :] = (sc_l * (g - d_l[s, :] * tot[1:2])).astype(bf16)
        gh_low[1, s, :] = (sc_s * (g - d_s[s, :] * tot[2:3])).astype(bf16)
        return c

    chunks(n, grad_pair)
    ld_ct.wait()

    @pl.loop(0, NF // 256)
    def _(t):
        re, im = pl.ds(pl.multiple_of(t * 256, 256), 256), pl.ds(pl.multiple_of(NF + t * 256, 256), 256)
        acc[0] = dot(tct[re, :], t_low[...])
        acc[1] = dot(tct[im, :], t_low[...])
        acc[2] = dot(tct[re, :], gh_low[1])
        acc[3] = dot(tct[im, :], gh_low[1])

        @pl.loop(0, 8)
        def _(i):
            s = pl.ds(pl.multiple_of(i * 32, 32), 32)
            re = pl.ds(pl.multiple_of(t * 256 + i * 32, 32), 32)
            im = pl.ds(pl.multiple_of(NF + t * 256 + i * 32, 32), 32)
            lr, li, sr, si = acc[0, s, :], acc[1, s, :], acc[2, s, :], acc[3, s, :]
            kr, ki = spec_l[re, :], spec_l[im, :]
            hr, hi = spec_s[re, :], spec_s[im, :]
            prod_k[re, :] = (lr * kr - li * ki + sr * hr - si * hi).astype(bf16)
            prod_k[im, :] = (lr * ki + li * kr + sr * hi + si * hr).astype(bf16)
            ur, ui = spec_u[re, :], spec_u[im, :]
            prod_l[re, :] = (lr * ur + li * ui).astype(bf16)
            prod_l[im, :] = (lr * ui - li * ur).astype(bf16)
            prod_s[re, :] = (sr * ur + si * ui).astype(bf16)
            prod_s[im, :] = (sr * ui - si * ur).astype(bf16)

    ld_at.wait()
    halo_out[0] = dot(tat[pl.ds(0, n), :], prod_k[...]).astype(bf16)
    halo_out[1] = dot(tat[pl.ds(2 * n, n), :], prod_k[...]).astype(bf16)
    up2 = pltpu.make_async_remote_copy(
        halo_out.at[0], halo_in.at[1], halo_send.at[2], halo_recv.at[2], device_id=(b, lax.rem(r + nr - 1, nr)), device_id_type=MESH
    )
    down2 = pltpu.make_async_remote_copy(
        halo_out.at[1], halo_in.at[0], halo_send.at[3], halo_recv.at[3], device_id=(b, lax.rem(r + 1, nr)), device_id_type=MESH
    )

    @pl.when(has_above)
    def _():
        up2.start()

    @pl.when(has_below)
    def _():
        down2.start()

    p_val[...] = dot(tat[pl.ds(n, n), :], prod_k[...])
    ld_bt.wait()

    @pl.loop(0, 4)
    def _(t):
        s = pl.ds(pl.multiple_of(t * 256, 256), 256)
        put(stage0, 2 * C + t * 256, dot(tbt[s, :], prod_l[...]))

    put(stage0, 2 * C + 976, dot(bst_ref[...], prod_s[...]))

    @pl.when(has_below)
    def _():
        up2.wait_recv()
        down2.wait_send()

    @pl.when(has_above)
    def _():
        down2.wait_recv()
        up2.wait_send()

    @pl.when(jnp.logical_not(has_above))
    def _():
        halo_in[0] = jnp.zeros((n, C), bf16)

    @pl.when(jnp.logical_not(has_below))
    def _():
        halo_in[1] = jnp.zeros((n, C), bf16)

    def grad_z(s, c):
        g = p_val[s, :] + halo_in[0, s, :].astype(f32) + halo_in[1, s, :].astype(f32)
        t_low[s, :] = (g * dz[s, :]).astype(bf16)
        return c

    chunks(n, grad_z)
    p_val[...] = dot(t_low[...], tab[pl.ds(0, C), :], (1, 1))

    def pre_sums(s, c):
        g = p_val[s, :]
        return c[0] + fold(g), c[1] + fold(g * ((x_ref[s, :] - m_x) * inv_x))

    b_pre, g_pre = (close(v) for v in chunks(n, pre_sums, (zero, zero)))

    def grad_in():
        for h in range(C // 256):
            put(stage0, h * 256, dot(pre_low[:, half_cols(h)], t_low[...], (0, 0)))

    tot = share(6, jnp.concatenate([b_pre, g_pre], axis=0), merge_sum, grad_in) * (1.0 / every)
    scale_x = row(0) * inv_x
    norms = [g_pre, b_pre, g_lg, b_pair, g_sg, b_pair, g_proj, b_proj, g_ffn, b_ffn]
    norms += [mid_rows[blocks + j : blocks + j + 1] for j in range(blocks)]
    base = 2 * C + 976
    put(stage0, base + 32, jnp.concatenate(norms + [jnp.zeros((2, C), f32)], axis=0))
    for j in range(blocks):
        for k in range(4):
            stage0[pl.ds((base + 25 + j) * 4 + k, 1), :] = mid_rows[j : j + 1, k * 128 : (k + 1) * 128]
    stores = [
        pltpu.make_async_copy(stage0.at[pl.ds(0, 8 * C)], grad_hbm.at[pl.ds(0, 8 * C)], store_sem.at[2]),
        pltpu.make_async_copy(stage0.at[pl.ds(8 * C, 8 * C)], grad_hbm.at[pl.ds(4 * (2 * C + 2 * FF), 8 * C)], store_sem.at[3]),
    ]
    for c in stores:
        c.start()

    def last(s, c):
        hat = (x_ref[s, :] - m_x) * inv_x
        gin_ref[s, :] = g_f[s, :] + scale_x * (p_val[s, :] - tot[0:1] - hat * tot[1:2])
        return c

    chunks(n, last)
    for e in range(len(WIDTHS)):
        for stage, (buf, size) in enumerate(((first[e], nr), (second[e], nb))):
            sent = buf.at[pl.ds(0, size - 1)]
            pltpu.make_async_copy(sent, sent, send_sem.at[e, stage]).wait()
    st_up.wait()
    for c in stores:
        c.wait()


def core(x, cot, sx, tab, nb, nr):
    (a, at, b, bt, bs, bst, c, ct) = tables()
    n = x.shape[0]
    vm = lambda shape, dtype=f32: pltpu.VMEM(shape, dtype)
    pix = vm((n, C))
    low = vm((n, C), bf16)
    wide_spec = vm((2 * NF, C))
    low_spec = vm((2 * NF, C), bf16)
    vmem = pl.BlockSpec(memory_space=pltpu.VMEM)
    anywhere = pl.BlockSpec(memory_space=pl.ANY)
    scratch = [vm(tab.shape, bf16)] + [vm(m.shape, bf16) for m in (a, at, b, bt, c, ct)]
    scratch += [low, vm((3 * n, C), bf16), pix, wide_spec, wide_spec, wide_spec, low_spec, low_spec, low_spec]
    scratch += [pix, pix, pix, low, pix, pix, low, low]
    scratch += [vm((FF // C, n, C)), vm((FF // C, n, C)), vm((FF // C, n, C), bf16), vm((FF // C, n, C), bf16), pix, vm((4, 256, C))]
    scratch += [vm((4 * FF, 128)), vm((4 * FF, 128)), vm((2, n, C), bf16), vm((2, n, C), bf16)]
    scratch += [vm((nr, w, C)) for w in WIDTHS] + [vm((nb, w, C)) for w in WIDTHS]
    dma = pltpu.SemaphoreType.DMA
    scratch += [dma((len(WIDTHS), 2)), dma((len(WIDTHS), 2)), dma((4,)), dma((4,)), dma((9,)), dma((4,))]
    return pl.pallas_call(
        functools.partial(core_kernel, nb, nr),
        out_shape=[
            jax.ShapeDtypeStruct((n, C), f32),
            jax.ShapeDtypeStruct((n, C), f32),
            jax.ShapeDtypeStruct((4 * tab.shape[0], 128), f32),
        ],
        in_specs=[vmem] * 3 + [anywhere] * 5 + [vmem] * 2 + [anywhere] * 2,
        out_specs=[vmem, vmem, anywhere],
        scratch_shapes=scratch,
        compiler_params=pltpu.CompilerParams(collective_id=1, has_side_effects=True, vmem_limit_bytes=62 * 2**20),
    )(x, cot, sx, tab, a, at, b, bt, bs, bst, c, ct)


def flip(b, m):
    k = 0
    while m >> k:
        if (m >> k) & 1:
            b = b + (1 - 2 * lax.rem(b // 2**k, 2)) * 2**k
        k += 1
    return b


def reduce_plan(nb):
    bits = nb.bit_length() - 1
    plan = []
    for p in range(bits):
        order = [(p + t) % bits for t in range(bits)]
        steps, kept = [], list(range(nb))
        for o in order:
            sent = [m for m in kept if (m >> o) & 1]
            kept = [m for m in kept if not (m >> o) & 1]
            steps.append((o, sent, kept))
        plan.append(steps)
    return plan


def reduce_kernel(
    nb, nr, idx_ref, grad_hbm, out_ref,
    grad, tmp, sib_out, sib_in, pair, hops, z_out, z_in,
    load_sem, sib_send, sib_recv, hop_send, hop_recv, z_send, z_recv,
):
    nz = nr // 2
    own = idx_ref.shape[0] // (nb * nr)
    lines = 4 * own
    unit = 32 if own % 32 == 0 else 8
    plan = reduce_plan(nb)
    parts = len(plan)
    size = lines // parts
    b = lax.axis_index("batch")
    r = lax.axis_index("rows")
    z, c = r // 2, lax.rem(r, 2)
    sibling = (b, r + 1 - 2 * c)
    load = pltpu.make_async_copy(grad_hbm, grad, load_sem)
    load.start()

    barrier = pltpu.get_barrier_semaphore()
    pl.semaphore_signal(barrier, inc=1, device_id=sibling, device_id_type=MESH)
    for k in range(parts):
        pl.semaphore_signal(barrier, inc=1, device_id=(flip(b, 2**k), r), device_id_type=MESH)
    for k in range(1, nz):
        pl.semaphore_signal(barrier, inc=1, device_id=(b, 2 * lax.rem(z + k, nz) + c), device_id_type=MESH)

    def column(i):
        return lax.rem(z + 1 + i, nz)

    def collect(m, zz, cc):
        start = (flip(b, m) * nr + 2 * zz + cc) * own

        @pl.loop(0, own // unit)
        def _(g):
            for u in range(unit):
                tmp[pl.ds(pl.multiple_of((g * unit + u) * 4, 4), 4), :] = grad[idx_ref[start + g * unit + u]]

    load.wait()
    pl.semaphore_wait(barrier, 1 + parts + nz - 1)

    def to_sibling(i, m):
        return pltpu.make_async_remote_copy(
            sib_out.at[i, m], sib_in.at[i, m], sib_send.at[i, m], sib_recv.at[i, m], device_id=sibling, device_id_type=MESH
        )

    @pl.loop(0, nz)
    def _(i):
        for m in range(nb):
            collect(m, column(i), 1 - c)
            sib_out[i, m] = tmp[...].astype(bf16)
            to_sibling(i, m).start()

    def rows_of(p):
        return pl.ds(p * size, size)

    def slots(p, t):
        at = sum(len(plan[p][k][2]) for k in range(t))
        return at, len(plan[p][t][2])

    def hop(i, p, t, m):
        o, sent, kept = plan[p][t]
        at, _ = slots(p, t)
        return pltpu.make_async_remote_copy(
            pair.at[i, m, rows_of(p)], hops.at[i, p, at + kept.index(m ^ (1 << o))], hop_send.at[i, p, t], hop_recv.at[i, p, t],
            device_id=(flip(b, 1 << o), r), device_id_type=MESH,
        )

    def hop_wait(i, p, t, sem):
        at, count = slots(p, t)
        whole = hops.at[i, p, pl.ds(at, count)]
        pltpu.make_async_copy(whole, whole, sem.at[i, p, t]).wait()

    @pl.loop(0, nz)
    def _(i):
        for m in reversed(range(nb)):
            collect(m, column(i), c)
            to_sibling(i, m).wait_recv()
            pair[i, m] = (tmp[...] + sib_in[i, m].astype(f32)).astype(bf16)
            for p in range(parts):
                if m in plan[p][0][1]:
                    hop(i, p, 0, m).start()

    for t in range(parts - 1):

        @pl.loop(0, nz)
        def _(i):
            for p in range(parts):
                hop_wait(i, p, t, hop_recv)
                at, _ = slots(p, t)
                for k, m in enumerate(plan[p][t][2]):
                    pair[i, m, rows_of(p)] = (
                        pair[i, m, rows_of(p)].astype(f32) + hops[i, p, at + k].astype(f32)
                    ).astype(bf16)
                    if m in plan[p][t + 1][1]:
                        hop(i, p, t + 1, m).start()

    def to_owner(i):
        return pltpu.make_async_remote_copy(
            z_out.at[i], z_in.at[i], z_send.at[i], z_recv.at[i], device_id=(b, 2 * column(i) + c), device_id_type=MESH
        )

    @pl.loop(0, nz)
    def _(i):
        for p in range(parts):
            hop_wait(i, p, parts - 1, hop_recv)
            at, _ = slots(p, parts - 1)
            tmp[rows_of(p), :] = pair[i, 0, rows_of(p)].astype(f32) + hops[i, p, at].astype(f32)

        @pl.when(i < nz - 1)
        def _():
            z_out[i] = tmp[...].astype(bf16)
            to_owner(i).start()

    for i in range(nz - 1):
        to_owner(i).wait_recv()
        tmp[...] += z_in[i].astype(f32)
    for j in range(4):
        out_ref[:, j * 128 : (j + 1) * 128] = tmp[pl.ds(j, own, stride=4), :]

    @pl.loop(0, nz)
    def _(i):
        for m in range(nb):
            to_sibling(i, m).wait_send()
        for p in range(parts):
            for t in range(parts):
                hop_wait(i, p, t, hop_send)

    for i in range(nz - 1):
        to_owner(i).wait_send()


def reduce_slots(grads, places, own, nb, nr):
    nz, parts = nr // 2, nb.bit_length() - 1
    lines = 4 * own
    vm = lambda shape, dtype=bf16: pltpu.VMEM(shape, dtype)
    dma = pltpu.SemaphoreType.DMA
    return pl.pallas_call(
        functools.partial(reduce_kernel, nb, nr),
        out_shape=jax.ShapeDtypeStruct((own, C), f32),
        in_specs=[pl.BlockSpec(memory_space=pltpu.SMEM), pl.BlockSpec(memory_space=pl.ANY)],
        out_specs=pl.BlockSpec(memory_space=pltpu.VMEM),
        scratch_shapes=[
            vm((grads.shape[0] // 4, 4, 128), f32),
            vm((lines, 128), f32),
            vm((nz, nb, lines, 128)),
            vm((nz, nb, lines, 128)),
            vm((nz, nb, lines, 128)),
            vm((nz, parts, nb - 1, lines // parts, 128)),
            vm((nz, lines, 128)),
            vm((nz, lines, 128)),
            dma,
            dma((nz, nb)),
            dma((nz, nb)),
            dma((nz, parts, parts)),
            dma((nz, parts, parts)),
            dma((nz,)),
            dma((nz,)),
        ],
        compiler_params=pltpu.CompilerParams(collective_id=2, has_side_effects=True, vmem_limit_bytes=48 * 2**20),
    )(places, grads.reshape(-1, 4, 128))


def table_place(t):
    start = 2 * C + 2 * FF
    k_end = start + KL * KL
    s_end = k_end + KS * KS
    m_gain = s_end + 10
    m_bias = m_gain + FF // C
    m_end = m_bias + FF // C
    up = t - 2 * C
    up = 2 * C + up % (FF // C) * C + up // (FF // C)
    base = start + 976
    unused = t - m_end
    unused = jnp.where(unused < 15, k_end + unused, jnp.where(unused < 18, base + 29 + unused - 15, base + 46 + unused - 18))
    p = jnp.where((t >= 2 * C) & (t < 2 * C + FF), up, t)
    p = jnp.where(t >= k_end, t - k_end + base, p)
    p = jnp.where(t >= s_end, t - s_end + base + 32, p)
    p = jnp.where(t >= m_bias, t - m_bias + base + 25, p)
    return jnp.where(t >= m_end, unused, p)


def body(image_in, cotangent, slot_rows, master, first_moment, second_moment):
    n = image_in.shape[0] * image_in.shape[1] * image_in.shape[2]
    nb, nr = lax.axis_size("batch"), lax.axis_size("rows")
    norm_start = 2 * C + 2 * FF + KL * KL + KS * KS
    places = table_place(slot_rows)
    own_copy = master.astype(bf16)
    gathered = lax.all_gather(own_copy, AXES, axis=0, tiled=True)
    ordered = jnp.zeros_like(gathered).at[places].set(gathered)
    x = image_in.reshape(n, C)
    cot = cotangent.reshape(n, C)
    m = jnp.mean(x, axis=0)
    d = x - m
    all_one = exchange((m, jnp.sum(d * d, axis=0)))
    m_x = jnp.mean(all_one[:, 0], axis=0)
    d = all_one[:, 0] - m_x
    q_x = (jnp.sum(all_one[:, 1], axis=0) + n * jnp.sum(d * d, axis=0)) / (n * nb * nr)
    result, grad_x, grads = core(x, cot, jnp.stack([m_x, q_x]), ordered, nb, nr)
    own_count = master.shape[0]
    reduced = reduce_slots(grads, places, own_count, nb, nr)
    place = lax.axis_index("batch") * nr + lax.axis_index("rows")
    own_rows = lax.dynamic_slice_in_dim(slot_rows, place * own_count, own_count)
    rates = jnp.where(own_rows >= norm_start, norm_rate, matrix_rate)[:, None]
    new_first = beta_one * first_moment + (1.0 - beta_one) * reduced
    new_second = beta_two * second_moment + (1.0 - beta_two) * reduced * reduced
    first_hat = new_first / (1.0 - beta_one**STEP)
    second_hat = new_second / (1.0 - beta_two**STEP)
    new_master = master - rates * (
        first_hat / (jnp.sqrt(second_hat) + adam_eps) + decay_rate * master
    )
    return (
        result.reshape(image_in.shape),
        grad_x.reshape(image_in.shape),
        reduced,
        new_first,
        new_second,
        new_master,
        new_master.astype(bf16),
    )


def solution(mesh):
    image = P("batch", "rows", None, None)
    owner = P(AXES, None)
    return jax.shard_map(
        body,
        mesh=mesh,
        in_specs=(image, image, P(), owner, owner, owner),
        out_specs=(image, image, owner, owner, owner, owner, owner),
        check_vma=False,
    )
```

```python
import functools

import jax
import jax.numpy as jnp
import numpy as np
from jax import lax
from jax.experimental import pallas as pl
from jax.experimental.pallas import tpu as pltpu
from jax.sharding import PartitionSpec as P

C = 512
FF = 2048
KL = 31
KS = 5
STEP = 10

norm_eps = 1e-05
beta_one = 0.9
beta_two = 0.999
adam_eps = 1e-08
decay_rate = 0.05
matrix_rate = 0.05
norm_rate = 0.5

TH = 16
TW = 16
NY = 47
NX = 31
NF = 768
REACH = (KL - 1) // 2
AXES = ("batch", "rows")
f32 = jnp.float32
bf16 = jnp.bfloat16


@functools.lru_cache(None)
def tables():
    freqs = [(ky, 0) for ky in range((NY + 1) // 2)]
    freqs += [(ky, kx) for kx in range(1, (NX + 1) // 2) for ky in range(NY)]
    ky = np.array([f[0] for f in freqs], np.int64)[:, None]
    kx = np.array([f[1] for f in freqs], np.int64)[:, None]
    pad = NF - len(freqs)

    def angle(rows, cols):
        ty = (ky * rows.reshape(1, -1)) % NY
        tx = (kx * cols.reshape(1, -1)) % NX
        return 2 * np.pi * (ty / NY + tx / NX)

    def grid(rows, cols):
        r, c = np.meshgrid(rows, cols, indexing="ij")
        return r.reshape(-1), c.reshape(-1)

    def stack(re, im):
        z = np.zeros((pad, re.shape[1]))
        return np.concatenate([re, z, im, z], axis=0)

    r, c = grid(np.arange(-TH, 2 * TH), np.arange(TW))
    used = ((r + REACH >= 0) & (r + REACH < NY - 1)).astype(np.float64)[None]
    t = angle(r + REACH, c)
    a = stack(np.cos(t) * used, -np.sin(t) * used)
    i, j = grid(np.arange(KL), np.arange(KL))
    t = angle(i, j - REACH)
    b = stack(np.cos(t), -np.sin(t))
    lead = REACH - (KS - 1) // 2
    small = ((i >= lead) & (i < lead + KS) & (j >= lead) & (j < lead + KS)).nonzero()[0]
    bs = np.pad(b[:, small], ((0, 0), (0, 32 - KS * KS)))
    b = np.pad(b, ((0, 0), (0, 2 * C - KL * KL)))
    y, x = grid(np.arange(TH), np.arange(TW))
    t = angle(y, x)
    w = np.full((len(freqs), 1), 2.0)
    w[0] = 1.0
    w /= NY * NX
    ct = stack(w * np.cos(t), -w * np.sin(t))
    return tuple(m.astype(np.float32).astype(bf16) for m in (a, a.T, b, b.T, bs, bs.T, ct.T, ct))


def dot(a, b, dims=(1, 0)):
    return lax.dot_general(a, b, (((dims[0],), (dims[1],)), ((), ())), preferred_element_type=f32)


MESH = pl.DeviceIdType.MESH
WIDTHS = (4, 3, 8, 8, 5, 3, 2)


def chunks(n, fn, init=()):
    return lax.fori_loop(0, n // 32, lambda i, c: fn(pl.ds(pl.multiple_of(i * 32, 32), 32), c), init)


def fold(v):
    return jnp.sum(v.reshape(v.shape[0] // 8, 8, v.shape[1]), axis=0)


def close(v):
    return jnp.sum(v, axis=0, keepdims=True)


def put(ref, start, v):
    for j in range(4):
        ref[pl.ds(start * 4 + j, v.shape[0], stride=4), :] = v[:, j * 128 : (j + 1) * 128]


def gelu_both(v):
    a = np.float32(np.sqrt(2 / np.pi))
    sq = v * v
    t = jnp.tanh(a * (v + 0.044715 * (sq * v)))
    half = 0.5 * (1 + t)
    return v * half, half + 0.5 * v * (1 - t * t) * (a * (1 + 3 * 0.044715 * sq))


def core_kernel(
    nb, nr, x_ref, cot_ref, sx_ref, tab_hbm, a_hbm, at_hbm, b_hbm, bt_hbm, bs_ref, bst_ref, c_hbm, ct_hbm,
    out_ref, gin_ref, grad_hbm,
    tab, ta, tat, tb, tbt, tc, tct, pre_low, wide, dz, spec_u, spec_l, spec_s, prod_l, prod_s, prod_k,
    d_l, d_s, s_val, t_low, p_val, mid, c_low, gy_low, hid, gact, a_low, gh_low, g_f, acc, stage0, stage1, halo_out, halo_in,
    *rest,
):
    first = rest[: len(WIDTHS)]
    second = rest[len(WIDTHS) : 2 * len(WIDTHS)]
    send_sem, recv_sem, halo_send, halo_recv, load_sem, store_sem = rest[2 * len(WIDTHS) :]
    n = x_ref.shape[0]
    every = float(n * nb * nr)
    b = lax.axis_index("batch")
    r = lax.axis_index("rows")

    barrier = pltpu.get_barrier_semaphore()
    for k in range(1, nr):
        pl.semaphore_signal(barrier, inc=1, device_id=(b, lax.rem(r + k, nr)), device_id_type=MESH)
    for k in range(1, nb):
        pl.semaphore_signal(barrier, inc=1, device_id=(lax.rem(b + k, nb), r), device_id_type=MESH)

    pieces = [pl.ds(0, 2 * C), pl.ds(2 * C + 2 * FF, 2 * C), pl.ds(2 * C, 2 * FF)]
    moves = [(tab_hbm.at[p], tab.at[p]) for p in pieces]
    order = [moves[0], moves[1], (b_hbm, tb), (a_hbm, ta), (c_hbm, tc), moves[2], (ct_hbm, tct), (at_hbm, tat), (bt_hbm, tbt)]
    loads = [pltpu.make_async_copy(s, d, load_sem.at[i]) for i, (s, d) in enumerate(order)]
    for c in loads:
        c.start()
    ld_w, ld_k, ld_b, ld_a, ld_c, ld_f, ld_ct, ld_at, ld_bt = loads

    def share(e, v, merge, work=lambda: None):
        count = n
        for stage, (buf, mine, axis, size) in enumerate(((first[e], r, "rows", nr), (second[e], b, "batch", nb))):
            buf[mine] = v
            for k in range(1, size):
                other = lax.rem(mine + k, size)
                where = (b, other) if axis == "rows" else (other, r)
                pltpu.make_async_remote_copy(
                    buf.at[mine], buf.at[mine], send_sem.at[e, stage], recv_sem.at[e, stage],
                    device_id=where, device_id_type=MESH,
                ).start()
            if stage == 0:
                work()
            got = buf.at[pl.ds(0, size - 1)]
            pltpu.make_async_copy(got, got, recv_sem.at[e, stage]).wait()
            v = merge(buf, size, float(count))
            count = count * size
        return v

    def merge_sum(buf, size, count):
        return jnp.sum(buf[...], axis=0)

    def merge_stats(h):
        def merge(buf, size, count):
            v = buf[...]
            means = v[:, :h]
            m = jnp.sum(means, axis=0) * (1.0 / size)
            d = means - m
            parts = [m, jnp.sum(v[:, h : 2 * h], axis=0) + count * jnp.sum(d * d, axis=0)]
            if v.shape[1] > 2 * h:
                parts.append(jnp.sum(v[:, 2 * h :], axis=0))
            return jnp.concatenate(parts, axis=0)

        return merge

    zero = jnp.zeros((8, C), f32)

    m_x, q_x = sx_ref[0:1, :], sx_ref[1:2, :]
    inv_x = lax.rsqrt(q_x + norm_eps)
    ld_w.wait()
    ld_k.wait()
    small = tab[pl.ds(2 * C + 2 * FF + 976, 48), :].astype(f32)
    row = lambda i: small[32 + i : 33 + i, :]
    mid_gain = lambda j: small[42 + j : 43 + j, :]
    mid_bias = lambda j: small[25 + j : 26 + j, :]

    def pre(s, sx):
        d = x_ref[s, :] - m_x
        pre_low[s, :] = (d * (inv_x * row(0)) + row(1)).astype(bf16)
        return sx + fold(d)

    sum_x = close(chunks(n, pre, zero))
    dz[...] = dot(pre_low[...], tab[pl.ds(0, C), :])

    def act(s, c):
        u, d = gelu_both(dz[s, :])
        dz[s, :] = d
        wide[pl.ds(pl.multiple_of(n + s.start, 32), 32), :] = u.astype(bf16)
        return c

    chunks(n, act)

    pl.semaphore_wait(barrier, nr - 1 + nb - 1)
    mine = wide.at[pl.ds(n, n)]
    up = pltpu.make_async_remote_copy(
        mine, wide.at[pl.ds(2 * n, n)], halo_send.at[0], halo_recv.at[0], device_id=(b, lax.rem(r + nr - 1, nr)), device_id_type=MESH
    )
    down = pltpu.make_async_remote_copy(
        mine, wide.at[pl.ds(0, n)], halo_send.at[1], halo_recv.at[1], device_id=(b, lax.rem(r + 1, nr)), device_id_type=MESH
    )
    has_above, has_below = r > 0, r < nr - 1

    @pl.when(has_above)
    def _():
        up.start()

    @pl.when(has_below)
    def _():
        down.start()

    ld_b.wait()
    kernel_rows = pl.ds(2 * C + 2 * FF, 2 * C)
    small_rows = pl.ds(2 * C + 2 * FF + 976, 32)

    @pl.loop(0, 2 * NF // 256)
    def _(t):
        s = pl.ds(pl.multiple_of(t * 256, 256), 256)
        spec_l[s, :] = dot(tb[s, :], tab[kernel_rows, :])
        spec_s[s, :] = dot(bs_ref[s, :], tab[small_rows, :])

    @pl.when(has_below)
    def _():
        up.wait_recv()
        down.wait_send()

    @pl.when(has_above)
    def _():
        down.wait_recv()
        up.wait_send()

    @pl.when(jnp.logical_not(has_above))
    def _():
        wide[pl.ds(0, n), :] = jnp.zeros((n, C), bf16)

    @pl.when(jnp.logical_not(has_below))
    def _():
        wide[pl.ds(2 * n, n), :] = jnp.zeros((n, C), bf16)

    ld_a.wait()

    @pl.loop(0, 2 * NF // 256)
    def _(t):
        s = pl.ds(pl.multiple_of(t * 256, 256), 256)
        spec_u[s, :] = dot(ta[s, :], wide[...])

    def halves(i):
        return pl.ds(pl.multiple_of(i * 32, 32), 32), pl.ds(pl.multiple_of(NF + i * 32, 32), 32)

    @pl.loop(0, NF // 32)
    def _(i):
        re, im = halves(i)
        ur, ui = spec_u[re, :], spec_u[im, :]
        for k, p in ((spec_l, prod_l), (spec_s, prod_s)):
            kr, ki = k[re, :], k[im, :]
            p[re, :] = (ur * kr + ui * ki).astype(bf16)
            p[im, :] = (ui * kr - ur * ki).astype(bf16)

    ld_c.wait()
    d_l[...] = dot(tc[...], prod_l[...])
    d_s[...] = dot(tc[...], prod_s[...])

    def local(ref):
        m = close(chunks(n, lambda s, c: c + fold(ref[s, :]), zero)) * (1.0 / n)

        def sq(s, c):
            d = ref[s, :] - m
            return c + fold(d * d)

        return m, close(chunks(n, sq, zero))

    m_l, v_l = local(d_l)
    m_s, v_s = local(d_s)

    def early():
        def low(s, c):
            gy_low[s, :] = cot_ref[s, :].astype(bf16)
            return c

        chunks(n, low)

    tot = share(0, jnp.concatenate([m_l, m_s, v_l, v_s], axis=0), merge_stats(2), early)
    m_l, m_s = tot[0:1], tot[1:2]
    inv_l, inv_s = lax.rsqrt(tot[2:3] / every + norm_eps), lax.rsqrt(tot[3:4] / every + norm_eps)

    def pair(s, c):
        hl = (d_l[s, :] - m_l) * inv_l
        hs = (d_s[s, :] - m_s) * inv_s
        d_l[s, :] = hl
        d_s[s, :] = hs
        t, d = gelu_both(hl * row(2) + row(3) + hs * row(4) + row(5))
        s_val[s, :] = d
        t_low[s, :] = t.astype(bf16)
        return c

    chunks(n, pair)
    p_val[...] = dot(t_low[...], tab[pl.ds(C, C), :])
    m_p = close(chunks(n, lambda s, c: c + fold(p_val[s, :]), zero)) * (1.0 / n)

    def proj(s, c):
        d = p_val[s, :] - m_p
        return c[0] + fold(d * d), c[1] + fold(d * (x_ref[s, :] - m_x))

    v_p, cross = chunks(n, proj, (zero, zero))
    tot = share(1, jnp.concatenate([m_p, close(v_p), close(cross) + m_p * sum_x], axis=0), merge_stats(1))
    m_p, q_p, cov = tot[0:1], tot[1:2] / every, tot[2:3] / every
    inv_p = lax.rsqrt(q_p + norm_eps)
    slope = row(6) * inv_p
    m_f = m_x + row(7)
    q_f = jnp.maximum(q_x + 2 * slope * cov + slope * slope * q_p, 0.0)
    inv_f = lax.rsqrt(q_f + norm_eps)
    hats = inv_f * inv_p * (cov + slope * q_p)

    def ffn(s, c):
        ph = (p_val[s, :] - m_p) * inv_p
        p_val[s, :] = ph
        m = x_ref[s, :] + (ph * row(6) + row(7))
        mid[s, :] = m
        c_low[s, :] = ((m - m_f) * (inv_f * row(8)) + row(9)).astype(bf16)
        g = cot_ref[s, :]
        return c[0] + fold(g), c[1] + fold(g * ph)

    sum_c, sum_ch = chunks(n, ffn, (zero, zero))
    sum_c, sum_ch = close(sum_c), close(sum_ch)
    ld_f.wait()
    up_rows = lambda j: pl.ds(pl.multiple_of(2 * C + j * C, C), C)
    down_rows = lambda j: pl.ds(pl.multiple_of(2 * C + FF + j * C, C), C)
    blocks = FF // C
    for j in range(blocks):
        hid[j] = dot(c_low[...], tab[up_rows(j), :])
    st = [local(hid.at[j]) for j in range(blocks)]

    def back_first():
        for j in range(blocks):
            gact[j] = dot(gy_low[...], tab[down_rows(j), :], (1, 1))

    tot = share(2, jnp.concatenate([s[0] for s in st] + [s[1] for s in st], axis=0), merge_stats(blocks), back_first)
    m_h = tot[:blocks]
    inv_h = lax.rsqrt(tot[blocks:] / every + norm_eps)
    sums = []
    for j in range(blocks):
        mj, ij, gj, bj = m_h[j : j + 1], inv_h[j : j + 1], mid_gain(j), mid_bias(j)

        def hidden(s, c, j=j, mj=mj, ij=ij, gj=gj, bj=bj):
            hat = (hid[j, s, :] - mj) * ij
            hid[j, s, :] = hat
            a, d = gelu_both(hat * gj + bj)
            a_low[j, s, :] = a.astype(bf16)
            g = gact[j, s, :] * d
            gact[j, s, :] = g
            return c[0] + fold(g), c[1] + fold(g * hat)

        sums.append(tuple(close(v) for v in chunks(n, hidden, (zero, zero))))
    mid_rows = jnp.concatenate([s[0] for s in sums] + [s[1] for s in sums], axis=0)

    def half_cols(h):
        return pl.ds(pl.multiple_of(h * 256, 256), 256)

    def outputs():
        out_ref[...] = mid[...]
        for j in range(blocks):
            out_ref[...] += dot(a_low[j], tab[down_rows(j), :])
            for h in range(C // 256):
                put(stage0, j * C + h * 256, dot(a_low[j, :, half_cols(h)], gy_low[...], (0, 0)))

    tot = share(3, mid_rows, merge_sum, outputs) * (1.0 / every)
    st_down = pltpu.make_async_copy(stage0, grad_hbm.at[pl.ds(4 * (2 * C + FF), 4 * FF)], store_sem.at[0])
    st_down.start()
    for j in range(blocks):
        tb_, tg_, sc = tot[j : j + 1], tot[blocks + j : blocks + j + 1], mid_gain(j) * inv_h[j : j + 1]

        def grad_h(s, c, j=j, tb_=tb_, tg_=tg_, sc=sc):
            gh_low[j, s, :] = (sc * (gact[j, s, :] - tb_ - hid[j, s, :] * tg_)).astype(bf16)
            return c

        chunks(n, grad_h)
    g_f[...] = dot(gh_low[0], tab[up_rows(0), :], (1, 1))
    for j in range(1, blocks):
        g_f[...] += dot(gh_low[j], tab[up_rows(j), :], (1, 1))

    def ffn_sums(s, c):
        g = g_f[s, :]
        hat = (mid[s, :] - m_f) * inv_f
        return c[0] + fold(g), c[1] + fold(g * hat), c[2] + fold(g * p_val[s, :])

    b_ffn, g_ffn, g_fp = (close(v) for v in chunks(n, ffn_sums, (zero, zero, zero)))

    def grad_up():
        for j in range(blocks):
            for h in range(C // 256):
                put(stage1, j * C + h * 256, dot(c_low[:, half_cols(h)], gh_low[j], (0, 0)))

    tot = share(4, jnp.concatenate([b_ffn, g_ffn, g_fp, sum_c, sum_ch], axis=0), merge_sum, grad_up) * (1.0 / every)
    st_up = pltpu.make_async_copy(stage1, grad_hbm.at[pl.ds(4 * 2 * C, 4 * FF)], store_sem.at[1])
    st_up.start()
    scale_f = row(8) * inv_f
    mean_hat = tot[4:5] + scale_f * (tot[2:3] - tot[1:2] * hats)

    def grad_mid(s, c):
        hat = (mid[s, :] - m_f) * inv_f
        g = cot_ref[s, :] + scale_f * (g_f[s, :] - tot[0:1] - hat * tot[1:2])
        g_f[s, :] = g
        ph = p_val[s, :]
        pre_p = slope * (g - tot[3:4] - ph * mean_hat)
        gh_low[0, s, :] = pre_p.astype(bf16)
        return c[0] + fold(g), c[1] + fold(g * ph)

    b_proj, g_proj = (close(v) for v in chunks(n, grad_mid, (zero, zero)))
    p_val[...] = dot(gh_low[0], tab[pl.ds(C, C), :], (1, 1))

    def grad_s(s, c):
        g = p_val[s, :] * s_val[s, :]
        p_val[s, :] = g
        return c[0] + fold(g), c[1] + fold(g * d_l[s, :]), c[2] + fold(g * d_s[s, :])

    b_pair, g_lg, g_sg = (close(v) for v in chunks(n, grad_s, (zero, zero, zero)))
    st_down.wait()

    def grad_out():
        for h in range(C // 256):
            put(stage0, C + h * 256, dot(t_low[:, half_cols(h)], gh_low[0], (0, 0)))

    tot = share(5, jnp.concatenate([b_pair, g_lg, g_sg], axis=0), merge_sum, grad_out) * (1.0 / every)
    sc_l, sc_s = row(2) * inv_l, row(4) * inv_s

    def grad_pair(s, c):
        g = p_val[s, :] - tot[0:1]
        t_low[s, :] = (sc_l * (g - d_l[s, :] * tot[1:2])).astype(bf16)
        gh_low[1, s, :] = (sc_s * (g - d_s[s, :] * tot[2:3])).astype(bf16)
        return c

    chunks(n, grad_pair)
    ld_ct.wait()

    @pl.loop(0, NF // 256)
    def _(t):
        re, im = pl.ds(pl.multiple_of(t * 256, 256), 256), pl.ds(pl.multiple_of(NF + t * 256, 256), 256)
        acc[0] = dot(tct[re, :], t_low[...])
        acc[1] = dot(tct[im, :], t_low[...])
        acc[2] = dot(tct[re, :], gh_low[1])
        acc[3] = dot(tct[im, :], gh_low[1])

        @pl.loop(0, 8)
        def _(i):
            s = pl.ds(pl.multiple_of(i * 32, 32), 32)
            re = pl.ds(pl.multiple_of(t * 256 + i * 32, 32), 32)
            im = pl.ds(pl.multiple_of(NF + t * 256 + i * 32, 32), 32)
            lr, li, sr, si = acc[0, s, :], acc[1, s, :], acc[2, s, :], acc[3, s, :]
            kr, ki = spec_l[re, :], spec_l[im, :]
            hr, hi = spec_s[re, :], spec_s[im, :]
            prod_k[re, :] = (lr * kr - li * ki + sr * hr - si * hi).astype(bf16)
            prod_k[im, :] = (lr * ki + li * kr + sr * hi + si * hr).astype(bf16)
            ur, ui = spec_u[re, :], spec_u[im, :]
            prod_l[re, :] = (lr * ur + li * ui).astype(bf16)
            prod_l[im, :] = (lr * ui - li * ur).astype(bf16)
            prod_s[re, :] = (sr * ur + si * ui).astype(bf16)
            prod_s[im, :] = (sr * ui - si * ur).astype(bf16)

    ld_at.wait()
    halo_out[0] = dot(tat[pl.ds(0, n), :], prod_k[...]).astype(bf16)
    halo_out[1] = dot(tat[pl.ds(2 * n, n), :], prod_k[...]).astype(bf16)
    up2 = pltpu.make_async_remote_copy(
        halo_out.at[0], halo_in.at[1], halo_send.at[2], halo_recv.at[2], device_id=(b, lax.rem(r + nr - 1, nr)), device_id_type=MESH
    )
    down2 = pltpu.make_async_remote_copy(
        halo_out.at[1], halo_in.at[0], halo_send.at[3], halo_recv.at[3], device_id=(b, lax.rem(r + 1, nr)), device_id_type=MESH
    )

    @pl.when(has_above)
    def _():
        up2.start()

    @pl.when(has_below)
    def _():
        down2.start()

    p_val[...] = dot(tat[pl.ds(n, n), :], prod_k[...])
    ld_bt.wait()

    @pl.loop(0, 4)
    def _(t):
        s = pl.ds(pl.multiple_of(t * 256, 256), 256)
        put(stage0, 2 * C + t * 256, dot(tbt[s, :], prod_l[...]))

    put(stage0, 2 * C + 976, dot(bst_ref[...], prod_s[...]))

    @pl.when(has_below)
    def _():
        up2.wait_recv()
        down2.wait_send()

    @pl.when(has_above)
    def _():
        down2.wait_recv()
        up2.wait_send()

    @pl.when(jnp.logical_not(has_above))
    def _():
        halo_in[0] = jnp.zeros((n, C), bf16)

    @pl.when(jnp.logical_not(has_below))
    def _():
        halo_in[1] = jnp.zeros((n, C), bf16)

    def grad_z(s, c):
        g = p_val[s, :] + halo_in[0, s, :].astype(f32) + halo_in[1, s, :].astype(f32)
        t_low[s, :] = (g * dz[s, :]).astype(bf16)
        return c

    chunks(n, grad_z)
    p_val[...] = dot(t_low[...], tab[pl.ds(0, C), :], (1, 1))

    def pre_sums(s, c):
        g = p_val[s, :]
        return c[0] + fold(g), c[1] + fold(g * ((x_ref[s, :] - m_x) * inv_x))

    b_pre, g_pre = (close(v) for v in chunks(n, pre_sums, (zero, zero)))

    def grad_in():
        for h in range(C // 256):
            put(stage0, h * 256, dot(pre_low[:, half_cols(h)], t_low[...], (0, 0)))

    tot = share(6, jnp.concatenate([b_pre, g_pre], axis=0), merge_sum, grad_in) * (1.0 / every)
    scale_x = row(0) * inv_x
    norms = [g_pre, b_pre, g_lg, b_pair, g_sg, b_pair, g_proj, b_proj, g_ffn, b_ffn]
    norms += [mid_rows[blocks + j : blocks + j + 1] for j in range(blocks)]
    base = 2 * C + 976
    put(stage0, base + 32, jnp.concatenate(norms + [jnp.zeros((2, C), f32)], axis=0))
    for j in range(blocks):
        for k in range(4):
            stage0[pl.ds((base + 25 + j) * 4 + k, 1), :] = mid_rows[j : j + 1, k * 128 : (k + 1) * 128]
    stores = [
        pltpu.make_async_copy(stage0.at[pl.ds(0, 8 * C)], grad_hbm.at[pl.ds(0, 8 * C)], store_sem.at[2]),
        pltpu.make_async_copy(stage0.at[pl.ds(8 * C, 8 * C)], grad_hbm.at[pl.ds(4 * (2 * C + 2 * FF), 8 * C)], store_sem.at[3]),
    ]
    for c in stores:
        c.start()

    def last(s, c):
        hat = (x_ref[s, :] - m_x) * inv_x
        gin_ref[s, :] = g_f[s, :] + scale_x * (p_val[s, :] - tot[0:1] - hat * tot[1:2])
        return c

    chunks(n, last)
    for e in range(len(WIDTHS)):
        for stage, (buf, size) in enumerate(((first[e], nr), (second[e], nb))):
            sent = buf.at[pl.ds(0, size - 1)]
            pltpu.make_async_copy(sent, sent, send_sem.at[e, stage]).wait()
    st_up.wait()
    for c in stores:
        c.wait()


def core(x, cot, sx, tab, nb, nr):
    (a, at, b, bt, bs, bst, c, ct) = tables()
    n = x.shape[0]
    vm = lambda shape, dtype=f32: pltpu.VMEM(shape, dtype)
    pix = vm((n, C))
    low = vm((n, C), bf16)
    wide_spec = vm((2 * NF, C))
    low_spec = vm((2 * NF, C), bf16)
    vmem = pl.BlockSpec(memory_space=pltpu.VMEM)
    anywhere = pl.BlockSpec(memory_space=pl.ANY)
    scratch = [vm(tab.shape, bf16)] + [vm(m.shape, bf16) for m in (a, at, b, bt, c, ct)]
    scratch += [low, vm((3 * n, C), bf16), pix, wide_spec, wide_spec, wide_spec, low_spec, low_spec, low_spec]
    scratch += [pix, pix, pix, low, pix, pix, low, low]
    scratch += [vm((FF // C, n, C)), vm((FF // C, n, C)), vm((FF // C, n, C), bf16), vm((FF // C, n, C), bf16), pix, vm((4, 256, C))]
    scratch += [vm((4 * FF, 128)), vm((4 * FF, 128)), vm((2, n, C), bf16), vm((2, n, C), bf16)]
    scratch += [vm((nr, w, C)) for w in WIDTHS] + [vm((nb, w, C)) for w in WIDTHS]
    dma = pltpu.SemaphoreType.DMA
    scratch += [dma((len(WIDTHS), 2)), dma((len(WIDTHS), 2)), dma((4,)), dma((4,)), dma((9,)), dma((4,))]
    return pl.pallas_call(
        functools.partial(core_kernel, nb, nr),
        out_shape=[
            jax.ShapeDtypeStruct((n, C), f32),
            jax.ShapeDtypeStruct((n, C), f32),
            jax.ShapeDtypeStruct((4 * tab.shape[0], 128), f32),
        ],
        in_specs=[vmem] * 3 + [anywhere] * 5 + [vmem] * 2 + [anywhere] * 2,
        out_specs=[vmem, vmem, anywhere],
        scratch_shapes=scratch,
        compiler_params=pltpu.CompilerParams(collective_id=1, has_side_effects=True, vmem_limit_bytes=62 * 2**20),
    )(x, cot, sx, tab, a, at, b, bt, bs, bst, c, ct)


def flip(b, m):
    k = 0
    while m >> k:
        if (m >> k) & 1:
            b = b + (1 - 2 * lax.rem(b // 2**k, 2)) * 2**k
        k += 1
    return b


def reduce_plan(nb):
    bits = nb.bit_length() - 1
    plan = []
    for p in range(bits):
        order = [(p + t) % bits for t in range(bits)]
        steps, kept = [], list(range(nb))
        for o in order:
            sent = [m for m in kept if (m >> o) & 1]
            kept = [m for m in kept if not (m >> o) & 1]
            steps.append((o, sent, kept))
        plan.append(steps)
    return plan


def reduce_kernel(
    nb, nr, idx_ref, grad_hbm, out_ref,
    grad, tmp, sib_out, sib_in, pair, hops, z_out, z_in,
    load_sem, sib_send, sib_recv, hop_send, hop_recv, z_send, z_recv,
):
    nz = nr // 2
    own = idx_ref.shape[0] // (nb * nr)
    lines = 4 * own
    unit = 32 if own % 32 == 0 else 8
    plan = reduce_plan(nb)
    parts = len(plan)
    size = lines // parts
    b = lax.axis_index("batch")
    r = lax.axis_index("rows")
    z, c = r // 2, lax.rem(r, 2)
    sibling = (b, r + 1 - 2 * c)
    load = pltpu.make_async_copy(grad_hbm, grad, load_sem)
    load.start()

    barrier = pltpu.get_barrier_semaphore()
    pl.semaphore_signal(barrier, inc=1, device_id=sibling, device_id_type=MESH)
    for k in range(parts):
        pl.semaphore_signal(barrier, inc=1, device_id=(flip(b, 2**k), r), device_id_type=MESH)
    for k in range(1, nz):
        pl.semaphore_signal(barrier, inc=1, device_id=(b, 2 * lax.rem(z + k, nz) + c), device_id_type=MESH)

    def column(i):
        return lax.rem(z + 1 + i, nz)

    def collect(m, zz, cc):
        start = (flip(b, m) * nr + 2 * zz + cc) * own

        @pl.loop(0, own // unit)
        def _(g):
            for u in range(unit):
                tmp[pl.ds(pl.multiple_of((g * unit + u) * 4, 4), 4), :] = grad[idx_ref[start + g * unit + u]]

    load.wait()
    pl.semaphore_wait(barrier, 1 + parts + nz - 1)

    def to_sibling(i, m):
        return pltpu.make_async_remote_copy(
            sib_out.at[i, m], sib_in.at[i, m], sib_send.at[i, m], sib_recv.at[i, m], device_id=sibling, device_id_type=MESH
        )

    @pl.loop(0, nz)
    def _(i):
        for m in range(nb):
            collect(m, column(i), 1 - c)
            sib_out[i, m] = tmp[...].astype(bf16)
            to_sibling(i, m).start()

    def rows_of(p):
        return pl.ds(p * size, size)

    def slots(p, t):
        at = sum(len(plan[p][k][2]) for k in range(t))
        return at, len(plan[p][t][2])

    def hop(i, p, t, m):
        o, sent, kept = plan[p][t]
        at, _ = slots(p, t)
        return pltpu.make_async_remote_copy(
            pair.at[i, m, rows_of(p)], hops.at[i, p, at + kept.index(m ^ (1 << o))], hop_send.at[i, p, t], hop_recv.at[i, p, t],
            device_id=(flip(b, 1 << o), r), device_id_type=MESH,
        )

    def hop_wait(i, p, t, sem):
        at, count = slots(p, t)
        whole = hops.at[i, p, pl.ds(at, count)]
        pltpu.make_async_copy(whole, whole, sem.at[i, p, t]).wait()

    @pl.loop(0, nz)
    def _(i):
        for m in reversed(range(nb)):
            collect(m, column(i), c)
            to_sibling(i, m).wait_recv()
            pair[i, m] = (tmp[...] + sib_in[i, m].astype(f32)).astype(bf16)
            for p in range(parts):
                if m in plan[p][0][1]:
                    hop(i, p, 0, m).start()

    for t in range(parts - 1):

        @pl.loop(0, nz)
        def _(i):
            for p in range(parts):
                hop_wait(i, p, t, hop_recv)
                at, _ = slots(p, t)
                for k, m in enumerate(plan[p][t][2]):
                    pair[i, m, rows_of(p)] = (
                        pair[i, m, rows_of(p)].astype(f32) + hops[i, p, at + k].astype(f32)
                    ).astype(bf16)
                    if m in plan[p][t + 1][1]:
                        hop(i, p, t + 1, m).start()

    def to_owner(i):
        return pltpu.make_async_remote_copy(
            z_out.at[i], z_in.at[i], z_send.at[i], z_recv.at[i], device_id=(b, 2 * column(i) + c), device_id_type=MESH
        )

    @pl.loop(0, nz)
    def _(i):
        for p in range(parts):
            hop_wait(i, p, parts - 1, hop_recv)
            at, _ = slots(p, parts - 1)
            tmp[rows_of(p), :] = pair[i, 0, rows_of(p)].astype(f32) + hops[i, p, at].astype(f32)

        @pl.when(i < nz - 1)
        def _():
            z_out[i] = tmp[...].astype(bf16)
            to_owner(i).start()

    for i in range(nz - 1):
        to_owner(i).wait_recv()
        tmp[...] += z_in[i].astype(f32)
    for j in range(4):
        out_ref[:, j * 128 : (j + 1) * 128] = tmp[pl.ds(j, own, stride=4), :]

    @pl.loop(0, nz)
    def _(i):
        for m in range(nb):
            to_sibling(i, m).wait_send()
        for p in range(parts):
            for t in range(parts):
                hop_wait(i, p, t, hop_send)

    for i in range(nz - 1):
        to_owner(i).wait_send()


def reduce_slots(grads, places, own, nb, nr):
    nz, parts = nr // 2, nb.bit_length() - 1
    lines = 4 * own
    vm = lambda shape, dtype=bf16: pltpu.VMEM(shape, dtype)
    dma = pltpu.SemaphoreType.DMA
    return pl.pallas_call(
        functools.partial(reduce_kernel, nb, nr),
        out_shape=jax.ShapeDtypeStruct((own, C), f32),
        in_specs=[pl.BlockSpec(memory_space=pltpu.SMEM), pl.BlockSpec(memory_space=pl.ANY)],
        out_specs=pl.BlockSpec(memory_space=pltpu.VMEM),
        scratch_shapes=[
            vm((grads.shape[0] // 4, 4, 128), f32),
            vm((lines, 128), f32),
            vm((nz, nb, lines, 128)),
            vm((nz, nb, lines, 128)),
            vm((nz, nb, lines, 128)),
            vm((nz, parts, nb - 1, lines // parts, 128)),
            vm((nz, lines, 128)),
            vm((nz, lines, 128)),
            dma,
            dma((nz, nb)),
            dma((nz, nb)),
            dma((nz, parts, parts)),
            dma((nz, parts, parts)),
            dma((nz,)),
            dma((nz,)),
        ],
        compiler_params=pltpu.CompilerParams(collective_id=2, has_side_effects=True, vmem_limit_bytes=48 * 2**20),
    )(places, grads.reshape(-1, 4, 128))


def gather_kernel(
    nb, nr, x_ref, master_ref, all_ref, sx_ref,
    lin, stat_one, stat_two,
    stat_send, stat_recv, z_send, z_recv, b_send, b_recv, half_send, half_recv, sib_send, sib_recv,
):
    nz = nr // 2
    own = master_ref.shape[0]
    lines = 4 * own
    n = x_ref.shape[0]
    b = lax.axis_index("batch")
    r = lax.axis_index("rows")
    z, c = r // 2, lax.rem(r, 2)
    sibling = (b, r + 1 - 2 * c)
    square = nb == 4

    barrier = pltpu.get_barrier_semaphore()
    for k in range(1, nr):
        pl.semaphore_signal(barrier, inc=1, device_id=(b, lax.rem(r + k, nr)), device_id_type=MESH)
    for m in range(1, nb):
        pl.semaphore_signal(barrier, inc=1, device_id=(flip(b, m), r), device_id_type=MESH)
    for j in range(4):
        lin[pl.ds(j, own, stride=4), :] = master_ref[:, j * 128 : (j + 1) * 128]

    def place(m, zz, core):
        return flip(b, m) * nr + 2 * zz + core

    all_ref[place(0, z, c)] = lin[...].astype(bf16)
    pl.semaphore_wait(barrier, nr - 1 + nb - 1)

    def along_z(zz, up):
        at = place(0, zz, c)
        return pltpu.make_async_remote_copy(
            all_ref.at[at], all_ref.at[at], z_send.at[zz], z_recv.at[zz],
            device_id=(b, r + 2 if up else r - 2), device_id_type=MESH,
        )

    def to_peer(m, zz):
        at = place(0, zz, c)
        return pltpu.make_async_remote_copy(
            all_ref.at[at], all_ref.at[at], b_send.at[m, zz], b_recv.at[m, zz], device_id=(flip(b, m), r), device_id_type=MESH
        )

    def from_peer(m, zz):
        at = all_ref.at[place(m, zz, c)]
        return pltpu.make_async_copy(at, at, b_recv.at[m, zz])

    def half(m, zz, h, to):
        at = all_ref.at[place(m, zz, c), pl.ds(h * (lines // 2), lines // 2)]
        return pltpu.make_async_remote_copy(
            at, at, half_send.at[h, zz], half_recv.at[h, zz], device_id=(flip(b, to), r), device_id_type=MESH
        )

    def to_sibling(m, zz, core):
        at = place(m, zz, core)
        return pltpu.make_async_remote_copy(
            all_ref.at[at], all_ref.at[at], sib_send.at[m, zz], sib_recv.at[m, zz], device_id=sibling, device_id_type=MESH
        )

    def sends(zz):
        for m in range(1, nb):
            if not (square and m == 3):
                to_peer(m, zz).start()
        to_sibling(0, zz, c).start()

    def own_column(k):
        if k == 0:

            @pl.when(z < nz - 1)
            def _():
                along_z(z, True).start()

            @pl.when(z > 0)
            def _():
                along_z(z, False).start()

            sends(z)
            return

        @pl.when(z >= k)
        def _():
            along_z(z - k, True).wait_recv()

            @pl.when(z < nz - 1)
            def _():
                along_z(z - k, True).start()

            sends(z - k)

        @pl.when(z + k < nz)
        def _():
            along_z(z + k, False).wait_recv()

            @pl.when(z > 0)
            def _():
                along_z(z + k, False).start()

            sends(z + k)

    def each(k, fn):
        if k == 0:
            fn(z)
            return

        @pl.when(z >= k)
        def _():
            fn(z - k)

        @pl.when(z + k < nz)
        def _():
            fn(z + k)

    def pass_on(zz):
        for m in range(1, nb):
            if square and m == 3:
                continue
            from_peer(m, zz).wait()
            if square:
                half(m, zz, 2 - m, 3 - m).start()
            to_sibling(m, zz, c).start()

    def corner(zz):
        if square:
            for h in range(2):
                half(3, zz, h, 0).wait_recv()
            to_sibling(3, zz, c).start()

    zero = jnp.zeros((8, C), f32)

    def share(stage, v, buf, mine, size, where):
        buf[mine] = v
        for k in range(1, size):
            pltpu.make_async_remote_copy(
                buf.at[mine], buf.at[mine], stat_send.at[stage], stat_recv.at[stage], device_id=where(k), device_id_type=MESH
            ).start()

    def shared(stage, buf, size, count):
        got = buf.at[pl.ds(0, size - 1)]
        pltpu.make_async_copy(got, got, stat_recv.at[stage]).wait()
        v = buf[...]
        m = jnp.sum(v[:, :1], axis=0) * (1.0 / size)
        d = v[:, :1] - m
        return jnp.concatenate([m, jnp.sum(v[:, 1:], axis=0) + count * jnp.sum(d * d, axis=0)], axis=0)

    own_column(0)
    m_x = close(chunks(n, lambda s, a: a + fold(x_ref[s, :]), zero)) * (1.0 / n)

    def sq(s, a):
        d = x_ref[s, :] - m_x
        return a + fold(d * d)

    v_x = close(chunks(n, sq, zero))
    share(0, jnp.concatenate([m_x, v_x], axis=0), stat_one, r, nr, lambda k: (b, lax.rem(r + k, nr)))
    for k in range(1, nz):
        own_column(k)
        each(k - 1, pass_on)
        if k > 1:
            each(k - 2, corner)
        if k == 1:
            v = shared(0, stat_one, nr, float(n))
            share(1, v, stat_two, b, nb, lambda m: (flip(b, m), r))
    each(nz - 1, pass_on)
    if nz > 1:
        each(nz - 2, corner)
    each(nz - 1, corner)
    v = shared(1, stat_two, nb, float(n * nr))
    sx_ref[0:1, :] = v[0:1]
    sx_ref[1:2, :] = v[1:2] * (1.0 / (n * nb * nr))
    for m in range(nb):

        @pl.loop(0, nz)
        def _(zz):
            to_sibling(m, zz, 1 - c).wait_recv()
            to_sibling(m, zz, c).wait_send()
            if m and not (square and m == 3):
                to_peer(m, zz).wait_send()
            if square and m in (1, 2):
                half(m, zz, 2 - m, 3 - m).wait_send()

    for k in range(nz):

        @pl.when((z >= k) & (z < nz - 1))
        def _():
            along_z(z - k, True).wait_send()

        @pl.when((z + k < nz) & (z > 0))
        def _():
            along_z(z + k, False).wait_send()

    for stage, (buf, size) in enumerate(((stat_one, nr), (stat_two, nb))):
        sent = buf.at[pl.ds(0, size - 1)]
        pltpu.make_async_copy(sent, sent, stat_send.at[stage]).wait()


def gather_rows(x, master, nb, nr):
    own, n, nz = master.shape[0], x.shape[0], nr // 2
    vm = lambda shape, dtype=f32: pltpu.VMEM(shape, dtype)
    dma = pltpu.SemaphoreType.DMA
    vmem = pl.BlockSpec(memory_space=pltpu.VMEM)
    return pl.pallas_call(
        functools.partial(gather_kernel, nb, nr),
        out_shape=[jax.ShapeDtypeStruct((nb * nr, 4 * own, 128), bf16), jax.ShapeDtypeStruct((2, C), f32)],
        in_specs=[vmem, vmem],
        out_specs=[vmem, vmem],
        scratch_shapes=[vm((4 * own, 128)), vm((nr, 2, C)), vm((nb, 2, C))]
        + [dma((2,))] * 2
        + [dma((nz,))] * 2
        + [dma((nb, nz))] * 2
        + [dma((2, nz))] * 2
        + [dma((nb, nz))] * 2,
        compiler_params=pltpu.CompilerParams(collective_id=0, has_side_effects=True, vmem_limit_bytes=24 * 2**20),
    )(x, master)


def order_kernel(idx_ref, rows_ref, out_hbm, flat, lin, out, store_sem):
    total = idx_ref.shape[0]
    unit = 32

    @pl.loop(0, total // 64)
    def _(g):
        s = pl.ds(pl.multiple_of(g * 256, 256), 256)
        flat[s, :] = rows_ref[s, :].astype(f32)

    @pl.loop(0, total // unit)
    def _(g):
        for u in range(unit):
            s = g * unit + u
            lin[pl.ds(pl.multiple_of(idx_ref[s], 4), 4), :] = flat[pl.ds(pl.multiple_of(s * 4, 4), 4), :]

    parts = store_sem.shape[0]
    part = total // parts
    stores = [pltpu.make_async_copy(out.at[pl.ds(p * part, part)], out_hbm.at[pl.ds(p * part, part)], store_sem.at[p]) for p in range(parts)]
    for p in range(parts):

        @pl.loop(0, part // 64)
        def _(g):
            start = p * part + g * 64
            for j in range(4):
                out[pl.ds(pl.multiple_of(start, 64), 64), j * 128 : (j + 1) * 128] = lin[pl.ds(start * 4 + j, 64, stride=4), :].astype(bf16)

        stores[p].start()
    for c in stores:
        c.wait()


def order_rows(rows, places):
    total = places.shape[0]
    return pl.pallas_call(
        order_kernel,
        out_shape=jax.ShapeDtypeStruct((total, C), bf16),
        in_specs=[pl.BlockSpec(memory_space=pltpu.SMEM), pl.BlockSpec(memory_space=pltpu.VMEM)],
        out_specs=pl.BlockSpec(memory_space=pl.ANY),
        scratch_shapes=[
            pltpu.VMEM((4 * total, 128), f32),
            pltpu.VMEM((4 * total, 128), f32),
            pltpu.VMEM((total, C), bf16),
            pltpu.SemaphoreType.DMA((8,)),
        ],
        compiler_params=pltpu.CompilerParams(vmem_limit_bytes=48 * 2**20),
    )(places * 4, rows.reshape(-1, 128))


def table_place(t):
    start = 2 * C + 2 * FF
    k_end = start + KL * KL
    s_end = k_end + KS * KS
    m_gain = s_end + 10
    m_bias = m_gain + FF // C
    m_end = m_bias + FF // C
    up = t - 2 * C
    up = 2 * C + up % (FF // C) * C + up // (FF // C)
    base = start + 976
    unused = t - m_end
    unused = jnp.where(unused < 15, k_end + unused, jnp.where(unused < 18, base + 29 + unused - 15, base + 46 + unused - 18))
    p = jnp.where((t >= 2 * C) & (t < 2 * C + FF), up, t)
    p = jnp.where(t >= k_end, t - k_end + base, p)
    p = jnp.where(t >= s_end, t - s_end + base + 32, p)
    p = jnp.where(t >= m_bias, t - m_bias + base + 25, p)
    return jnp.where(t >= m_end, unused, p)


def body(image_in, cotangent, slot_rows, master, first_moment, second_moment):
    n = image_in.shape[0] * image_in.shape[1] * image_in.shape[2]
    nb, nr = lax.axis_size("batch"), lax.axis_size("rows")
    norm_start = 2 * C + 2 * FF + KL * KL + KS * KS
    places = table_place(slot_rows)
    x = image_in.reshape(n, C)
    cot = cotangent.reshape(n, C)
    rows, sx = gather_rows(x, master, nb, nr)
    ordered = order_rows(rows, places)
    result, grad_x, grads = core(x, cot, sx, ordered, nb, nr)
    own_count = master.shape[0]
    reduced = reduce_slots(grads, places, own_count, nb, nr)
    place = lax.axis_index("batch") * nr + lax.axis_index("rows")
    own_rows = lax.dynamic_slice_in_dim(slot_rows, place * own_count, own_count)
    rates = jnp.where(own_rows >= norm_start, norm_rate, matrix_rate)[:, None]
    new_first = beta_one * first_moment + (1.0 - beta_one) * reduced
    new_second = beta_two * second_moment + (1.0 - beta_two) * reduced * reduced
    first_hat = new_first / (1.0 - beta_one**STEP)
    second_hat = new_second / (1.0 - beta_two**STEP)
    new_master = master - rates * (
        first_hat / (jnp.sqrt(second_hat) + adam_eps) + decay_rate * master
    )
    return (
        result.reshape(image_in.shape),
        grad_x.reshape(image_in.shape),
        reduced,
        new_first,
        new_second,
        new_master,
        new_master.astype(bf16),
    )


def solution(mesh):
    image = P("batch", "rows", None, None)
    owner = P(AXES, None)
    return jax.shard_map(
        body,
        mesh=mesh,
        in_specs=(image, image, P(), owner, owner, owner),
        out_specs=(image, image, owner, owner, owner, owner, owner),
        check_vma=False,
    )
```

```python
import functools
import types

import jax
import jax.numpy as jnp
import numpy as np
from jax import lax
from jax.experimental import pallas as pl
from jax.experimental.pallas import tpu as pltpu
from jax.sharding import PartitionSpec as P

C = 512
FF = 2048
KL = 31
KS = 5
STEP = 10

norm_eps = 1e-05
beta_one = 0.9
beta_two = 0.999
adam_eps = 1e-08
decay_rate = 0.05
matrix_rate = 0.05
norm_rate = 0.5

TH = 16
TW = 16
NY = 47
NX = 31
NF = 768
REACH = (KL - 1) // 2
AXES = ("batch", "rows")
f32 = jnp.float32
bf16 = jnp.bfloat16


@functools.lru_cache(None)
def tables():
    freqs = [(ky, 0) for ky in range((NY + 1) // 2)]
    freqs += [(ky, kx) for kx in range(1, (NX + 1) // 2) for ky in range(NY)]
    ky = np.array([f[0] for f in freqs], np.int64)[:, None]
    kx = np.array([f[1] for f in freqs], np.int64)[:, None]
    pad = NF - len(freqs)

    def angle(rows, cols):
        ty = (ky * rows.reshape(1, -1)) % NY
        tx = (kx * cols.reshape(1, -1)) % NX
        return 2 * np.pi * (ty / NY + tx / NX)

    def grid(rows, cols):
        r, c = np.meshgrid(rows, cols, indexing="ij")
        return r.reshape(-1), c.reshape(-1)

    def stack(re, im):
        z = np.zeros((pad, re.shape[1]))
        return np.concatenate([re, z, im, z], axis=0)

    r, c = grid(np.arange(-TH, 2 * TH), np.arange(TW))
    used = ((r + REACH >= 0) & (r + REACH < NY - 1)).astype(np.float64)[None]
    t = angle(r + REACH, c)
    a = stack(np.cos(t) * used, -np.sin(t) * used)
    i, j = grid(np.arange(KL), np.arange(KL))
    t = angle(i, j - REACH)
    b = stack(np.cos(t), -np.sin(t))
    lead = REACH - (KS - 1) // 2
    small = ((i >= lead) & (i < lead + KS) & (j >= lead) & (j < lead + KS)).nonzero()[0]
    bs = np.pad(b[:, small], ((0, 0), (0, 32 - KS * KS)))
    b = np.pad(b, ((0, 0), (0, 2 * C - KL * KL)))
    y, x = grid(np.arange(TH), np.arange(TW))
    t = angle(y, x)
    w = np.full((len(freqs), 1), 2.0)
    w[0] = 1.0
    w /= NY * NX
    ct = stack(w * np.cos(t), -w * np.sin(t))
    return tuple(m.astype(np.float32).astype(bf16) for m in (a, a.T, b, b.T, bs, bs.T, ct.T, ct))


def dot(a, b, dims=(1, 0)):
    return lax.dot_general(a, b, (((dims[0],), (dims[1],)), ((), ())), preferred_element_type=f32)


MESH = pl.DeviceIdType.MESH
WIDTHS = (2, 4, 3, 8, 8, 5, 3, 2)
BASE = 2 * C + 2 * FF + 976


def chunks(n, fn, init=()):
    return lax.fori_loop(0, n // 32, lambda i, c: fn(pl.ds(pl.multiple_of(i * 32, 32), 32), c), init)


def fold(v):
    return jnp.sum(v.reshape(v.shape[0] // 8, 8, v.shape[1]), axis=0)


def close(v):
    return jnp.sum(v, axis=0, keepdims=True)


def put(ref, start, v):
    for j in range(4):
        ref[pl.ds(start * 4 + j, v.shape[0], stride=4), :] = v[:, j * 128 : (j + 1) * 128]


def gelu_both(v):
    a = np.float32(np.sqrt(2 / np.pi))
    sq = v * v
    t = jnp.tanh(a * (v + 0.044715 * (sq * v)))
    half = 0.5 * (1 + t)
    return v * half, half + 0.5 * v * (1 - t * t) * (a * (1 + 3 * 0.044715 * sq))


def flip(b, m):
    k = 0
    while m >> k:
        if (m >> k) & 1:
            b = b + (1 - 2 * lax.rem(b // 2**k, 2)) * 2**k
        k += 1
    return b


def reduce_plan(nb):
    bits = nb.bit_length() - 1
    plan = []
    for p in range(bits):
        order = [(p + t) % bits for t in range(bits)]
        steps, kept = [], list(range(nb))
        for o in order:
            sent = [m for m in kept if (m >> o) & 1]
            kept = [m for m in kept if not (m >> o) & 1]
            steps.append((o, sent, kept))
        plan.append(steps)
    return plan


def merge_sum(v, count):
    return jnp.sum(v, axis=0)


def merge_stats(h):
    def merge(v, count):
        means = v[:, :h]
        m = jnp.sum(means, axis=0) * (1.0 / v.shape[0])
        d = means - m
        parts = [m, jnp.sum(v[:, h : 2 * h], axis=0) + count * jnp.sum(d * d, axis=0)]
        if v.shape[1] > 2 * h:
            parts.append(jnp.sum(v[:, 2 * h :], axis=0))
        return jnp.concatenate(parts, axis=0)

    return merge


def local(read, n):
    zero = jnp.zeros((8, C), f32)
    m = close(chunks(n, lambda s, c: c + fold(read(s)), zero)) * (1.0 / n)

    def sq(s, c):
        d = read(s) - m
        return c + fold(d * d)

    return m, close(chunks(n, sq, zero))


def half_cols(h):
    return pl.ds(pl.multiple_of(h * 256, 256), 256)


def up_rows(j):
    return pl.ds(pl.multiple_of(2 * C + j * C, C), C)


def down_rows(j):
    return pl.ds(pl.multiple_of(2 * C + FF + j * C, C), C)


def step_kernel(nb, nr, names, *refs):
    S = types.SimpleNamespace(**dict(zip(names, refs)))
    nz = nr // 2
    nd = nb * nr
    n = S.x.shape[0]
    own = S.master.shape[0]
    lines = 4 * own
    total = S.tab.shape[0]
    every = float(n * nd)
    b = lax.axis_index("batch")
    r = lax.axis_index("rows")
    z, c = r // 2, lax.rem(r, 2)
    sibling = (b, r + 1 - 2 * c)
    square = nb == 4
    blocks = FF // C
    zero = jnp.zeros((8, C), f32)
    rows_in = S.rows_in

    def load(i, src, dst):
        return pltpu.make_async_copy(src, dst, S.load_sem.at[i])

    ld_m, ld_x, ld_c = load(0, S.master_hbm, S.master), load(1, S.x_hbm, S.x), load(2, S.cot_hbm, S.cot)
    for copy in (ld_m, ld_x, ld_c):
        copy.start()
    barrier = pltpu.get_barrier_semaphore()
    for k in range(1, nr):
        pl.semaphore_signal(barrier, inc=1, device_id=(b, lax.rem(r + k, nr)), device_id_type=MESH)
    for m in range(1, nb):
        pl.semaphore_signal(barrier, inc=1, device_id=(flip(b, m), r), device_id_type=MESH)


    def share_stage(e, stage):
        if stage == 0:
            return getattr(S, f"one{e}"), r, nr, [(b, lax.rem(r + k, nr)) for k in range(1, nr)]
        return getattr(S, f"two{e}"), b, nb, [(flip(b, m), r) for m in range(1, nb)]

    def share_send(e, stage, v):
        buf, mine, size, peers = share_stage(e, stage)
        buf[mine] = v
        for peer in peers:
            pltpu.make_async_remote_copy(
                buf.at[mine], buf.at[mine], S.stat_send.at[e, stage], S.stat_recv.at[e, stage], device_id=peer, device_id_type=MESH
            ).start()

    def share_wait(e, stage, merge):
        buf, mine, size, peers = share_stage(e, stage)
        got = buf.at[pl.ds(0, size - 1)]
        pltpu.make_async_copy(got, got, S.stat_recv.at[e, stage]).wait()
        return merge(buf[...], float(n if stage == 0 else n * nr))

    def share(e, v, merge, work=None, more=None):
        share_send(e, 0, v)
        if work:
            work()
        v = share_wait(e, 0, merge)
        share_send(e, 1, v)
        if more:
            more()
        return share_wait(e, 1, merge)


    def place(m, zz, core):
        return flip(b, m) * nr + 2 * zz + core

    def along_z(zz, up):
        at = rows_in.at[place(0, zz, c)]
        return pltpu.make_async_remote_copy(
            at, at, S.z_send.at[zz], S.z_recv.at[zz], device_id=(b, r + 2 if up else r - 2), device_id_type=MESH
        )

    def to_peer(m, zz):
        at = rows_in.at[place(0, zz, c)]
        return pltpu.make_async_remote_copy(
            at, at, S.b_send.at[m, zz], S.b_recv.at[m, zz], device_id=(flip(b, m), r), device_id_type=MESH
        )

    def from_peer(m, zz):
        at = rows_in.at[place(m, zz, c)]
        return pltpu.make_async_copy(at, at, S.b_recv.at[m, zz])

    def half(m, zz, h, to):
        at = rows_in.at[place(m, zz, c), pl.ds(h * (lines // 2), lines // 2)]
        return pltpu.make_async_remote_copy(
            at, at, S.half_send.at[h, zz], S.half_recv.at[h, zz], device_id=(flip(b, to), r), device_id_type=MESH
        )

    def to_other_core(m, zz, core):
        at = rows_in.at[place(m, zz, core)]
        return pltpu.make_async_remote_copy(
            at, at, S.core_send.at[m, zz], S.core_recv.at[m, zz], device_id=sibling, device_id_type=MESH
        )

    def sends(zz):
        for m in range(1, nb):
            if not (square and m == 3):
                to_peer(m, zz).start()
        to_other_core(0, zz, c).start()

    def own_column(k):
        if k == 0:

            @pl.when(z < nz - 1)
            def _():
                along_z(z, True).start()

            @pl.when(z > 0)
            def _():
                along_z(z, False).start()

            sends(z)
            return

        @pl.when(z >= k)
        def _():
            along_z(z - k, True).wait_recv()

            @pl.when(z < nz - 1)
            def _():
                along_z(z - k, True).start()

            sends(z - k)

        @pl.when(z + k < nz)
        def _():
            along_z(z + k, False).wait_recv()

            @pl.when(z > 0)
            def _():
                along_z(z + k, False).start()

            sends(z + k)

    def each(k, fn):
        if k == 0:
            fn(z)
            return

        @pl.when(z >= k)
        def _():
            fn(z - k)

        @pl.when(z + k < nz)
        def _():
            fn(z + k)

    def pass_on(zz):
        for m in range(1, nb):
            if square and m == 3:
                continue
            from_peer(m, zz).wait()
            if square:
                half(m, zz, 2 - m, 3 - m).start()
            to_other_core(m, zz, c).start()

    def corner(zz):
        if square:
            for h in range(2):
                half(3, zz, h, 0).wait_recv()
            to_other_core(3, zz, c).start()

    def find(part, parts):
        tiles = total // 1024
        unit = 16
        spots = [
            lax.broadcasted_iota(jnp.int32, (8, 128), 0) * 128 + lax.broadcasted_iota(jnp.int32, (8, 128), 1) + 1024 * k
            for k in range(tiles)
        ]

        def some(g, acc):
            for u in range(unit):
                s = part * (total // parts) + g * unit + u
                p = S.idx[s]
                acc = [jnp.where(spot == p, s, a) for spot, a in zip(spots, acc)]
            return acc

        acc = [S.inv[k * 8 : k * 8 + 8, :] if part else jnp.zeros((8, 128), jnp.int32) for k in range(tiles)]
        acc = lax.fori_loop(0, total // parts // unit, some, acc)
        for k in range(tiles):
            S.inv[k * 8 : k * 8 + 8, :] = acc[k]

    def order(start, stop):
        flat = S.flat.reshape(total, 4, 128)
        unit = 32

        @pl.loop(start, stop)
        def _(t):
            @pl.loop(0, 128 // unit)
            def _(g):
                for u in range(unit):
                    S.chunk[pl.ds(pl.multiple_of((g * unit + u) * 4, 4), 4), :] = flat[S.inv_at[t, g * unit + u]]

            rows = pl.ds(pl.multiple_of(t * 128, 128), 128)
            for j in range(4):
                S.tab[rows, j * 128 : (j + 1) * 128] = S.chunk[pl.ds(j, 128, stride=4), :].astype(bf16)

    def front(ta, tb, tc):
        ld_a, ld_b, ld_t = load(3, S.a_hbm, ta), load(4, S.b_hbm, tb), load(5, S.c_hbm, tc)
        for copy in (ld_b, ld_a, ld_t):
            copy.start()
        ld_m.wait()
        for j in range(4):
            S.tmp[pl.ds(j, own, stride=4), :] = S.master[:, j * 128 : (j + 1) * 128]
        rows_in[place(0, z, c)] = S.tmp[...].astype(bf16)
        pl.semaphore_wait(barrier, nr - 1 + nb - 1)
        own_column(0)
        ld_x.wait()
        share_send(0, 0, jnp.concatenate(local(lambda s: S.x[s, :], n), axis=0))
        steps = max(nz - 1, 1)
        for k in range(1, nz):
            find(k - 1, steps)
            own_column(k)
            each(k - 1, pass_on)
            if k > 1:
                each(k - 2, corner)
            if k == 1:
                share_send(0, 1, share_wait(0, 0, merge_stats(1)))
        if nz == 1:
            find(0, 1)
            share_send(0, 1, share_wait(0, 0, merge_stats(1)))
        to_scalar = pltpu.make_async_copy(S.inv, S.inv_at, S.load_sem.at[6])
        to_scalar.start()
        each(nz - 1, pass_on)
        if nz > 1:
            each(nz - 2, corner)
        each(nz - 1, corner)
        tot = share_wait(0, 1, merge_stats(1))
        m_x, q_x = tot[0:1], tot[1:2] * (1.0 / every)
        inv_x = lax.rsqrt(q_x + norm_eps)
        to_scalar.wait()
        for m in range(nb):

            @pl.loop(0, nz)
            def _(zz):
                to_other_core(m, zz, 1 - c).wait_recv()

        @pl.loop(0, nd)
        def _(d):
            S.flat[pl.ds(pl.multiple_of(d * lines, lines), lines), :] = rows_in[d].astype(f32)

        tiles = total // 128
        late = (2 * C + 2 * FF) // 128
        order(0, 2 * C // 128)
        order(late, tiles)

        for m in range(nb):

            @pl.loop(0, nz)
            def _(zz):
                to_other_core(m, zz, c).wait_send()
                if m and not (square and m == 3):
                    to_peer(m, zz).wait_send()
                if square and m in (1, 2):
                    half(m, zz, 2 - m, 3 - m).wait_send()

        for k in range(nz):

            @pl.when((z >= k) & (z < nz - 1))
            def _():
                along_z(z - k, True).wait_send()

            @pl.when((z + k < nz) & (z > 0))
            def _():
                along_z(z + k, False).wait_send()

        small = S.tab[pl.ds(BASE, 48), :].astype(f32)
        S.small[...] = small
        row = lambda i: small[32 + i : 33 + i, :]

        def pre(s, sx):
            d = S.x[s, :] - m_x
            S.pre_low[s, :] = (d * (inv_x * row(0)) + row(1)).astype(bf16)
            return sx + fold(d)

        sum_x = close(chunks(n, pre, zero))
        S.dz[...] = dot(S.pre_low[...], S.tab[pl.ds(0, C), :])

        def act(s, a):
            u, d = gelu_both(S.dz[s, :])
            S.dz[s, :] = d
            S.wide[pl.ds(pl.multiple_of(n + s.start, 32), 32), :] = u.astype(bf16)
            return a

        chunks(n, act)
        mine = S.wide.at[pl.ds(n, n)]
        halo_up = halo(0, mine, S.wide.at[pl.ds(2 * n, n)], True)
        halo_down = halo(1, mine, S.wide.at[pl.ds(0, n)], False)
        halo_start(halo_up, halo_down)

        ld_b.wait()

        @pl.loop(0, 2 * NF // 256)
        def _(t):
            s = pl.ds(pl.multiple_of(t * 256, 256), 256)
            S.spec_l[s, :] = dot(tb[s, :], S.tab[pl.ds(2 * C + 2 * FF, 2 * C), :])
            S.spec_s[s, :] = dot(S.bs[s, :], S.tab[pl.ds(BASE, 32), :])

        halo_wait(halo_up, halo_down, S.wide.at[pl.ds(0, n)], S.wide.at[pl.ds(2 * n, n)])
        ld_a.wait()

        @pl.loop(0, 2 * NF // 256)
        def _(t):
            s = pl.ds(pl.multiple_of(t * 256, 256), 256)
            S.spec_u[s, :] = dot(ta[s, :], S.wide[...])

        @pl.loop(0, NF // 32)
        def _(i):
            re, im = pl.ds(pl.multiple_of(i * 32, 32), 32), pl.ds(pl.multiple_of(NF + i * 32, 32), 32)
            ur, ui = S.spec_u[re, :], S.spec_u[im, :]
            for k, p in ((S.spec_l, S.prod_l), (S.spec_s, S.prod_s)):
                kr, ki = k[re, :], k[im, :]
                p[re, :] = (ur * kr + ui * ki).astype(bf16)
                p[im, :] = (ui * kr - ur * ki).astype(bf16)

        ld_t.wait()
        S.d_l[...] = dot(tc[...], S.prod_l[...])
        S.d_s[...] = dot(tc[...], S.prod_s[...])
        return m_x, q_x, sum_x


    has_above, has_below = r > 0, r < nr - 1

    def halo(i, src, dst, up):
        peer = lax.rem(r + nr - 1, nr) if up else lax.rem(r + 1, nr)
        return pltpu.make_async_remote_copy(
            src, dst, S.halo_send.at[i], S.halo_recv.at[i], device_id=(b, peer), device_id_type=MESH
        )

    def halo_start(up, down):
        @pl.when(has_above)
        def _():
            up.start()

        @pl.when(has_below)
        def _():
            down.start()

    def halo_wait(up, down, above, below):
        @pl.when(has_below)
        def _():
            up.wait_recv()
            down.wait_send()

        @pl.when(has_above)
        def _():
            down.wait_recv()
            up.wait_send()

        @pl.when(jnp.logical_not(has_above))
        def _():
            above[...] = jnp.zeros((n, C), bf16)

        @pl.when(jnp.logical_not(has_below))
        def _():
            below[...] = jnp.zeros((n, C), bf16)

    m_x, q_x, sum_x = pl.run_scoped(
        front, pltpu.VMEM(S.a_hbm.shape, bf16), pltpu.VMEM(S.b_hbm.shape, bf16), pltpu.VMEM(S.c_hbm.shape, bf16)
    )
    inv_x = lax.rsqrt(q_x + norm_eps)
    small = S.small[...]
    row = lambda i: small[32 + i : 33 + i, :]
    mid_gain = lambda j: small[42 + j : 43 + j, :]
    mid_bias = lambda j: small[25 + j : 26 + j, :]
    m_l, v_l = local(lambda s: S.d_l[s, :], n)
    m_s, v_s = local(lambda s: S.d_s[s, :], n)
    ld_c.wait()

    def early():
        order(2 * C // 128, (2 * C + FF) // 128)

        def low(s, a):
            S.gy_low[s, :] = S.cot[s, :].astype(bf16)
            return a

        chunks(n, low)

    tot = share(
        1, jnp.concatenate([m_l, m_s, v_l, v_s], axis=0), merge_stats(2), early,
        lambda: order((2 * C + FF) // 128, (2 * C + 2 * FF) // 128),
    )
    m_l, m_s = tot[0:1], tot[1:2]
    inv_l, inv_s = lax.rsqrt(tot[2:3] / every + norm_eps), lax.rsqrt(tot[3:4] / every + norm_eps)

    def pair(s, a):
        hl = (S.d_l[s, :] - m_l) * inv_l
        hs = (S.d_s[s, :] - m_s) * inv_s
        S.d_l[s, :] = hl
        S.d_s[s, :] = hs
        t, d = gelu_both(hl * row(2) + row(3) + hs * row(4) + row(5))
        S.s_val[s, :] = d
        S.t_low[s, :] = t.astype(bf16)
        return a

    chunks(n, pair)
    S.p_val[...] = dot(S.t_low[...], S.tab[pl.ds(C, C), :])
    m_p = close(chunks(n, lambda s, a: a + fold(S.p_val[s, :]), zero)) * (1.0 / n)

    def proj(s, a):
        d = S.p_val[s, :] - m_p
        return a[0] + fold(d * d), a[1] + fold(d * (S.x[s, :] - m_x))

    v_p, cross = chunks(n, proj, (zero, zero))
    tot = share(2, jnp.concatenate([m_p, close(v_p), close(cross) + m_p * sum_x], axis=0), merge_stats(1))
    m_p, q_p, cov = tot[0:1], tot[1:2] / every, tot[2:3] / every
    inv_p = lax.rsqrt(q_p + norm_eps)
    slope = row(6) * inv_p
    m_f = m_x + row(7)
    q_f = jnp.maximum(q_x + 2 * slope * cov + slope * slope * q_p, 0.0)
    inv_f = lax.rsqrt(q_f + norm_eps)
    hats = inv_f * inv_p * (cov + slope * q_p)

    def ffn(s, a):
        ph = (S.p_val[s, :] - m_p) * inv_p
        S.p_val[s, :] = ph
        m = S.x[s, :] + (ph * row(6) + row(7))
        S.mid[s, :] = m
        S.c_low[s, :] = ((m - m_f) * (inv_f * row(8)) + row(9)).astype(bf16)
        g = S.cot[s, :]
        return a[0] + fold(g), a[1] + fold(g * ph)

    sum_c, sum_ch = chunks(n, ffn, (zero, zero))
    sum_c, sum_ch = close(sum_c), close(sum_ch)

    def middle(hid, gact, a_low, gh_low):
        for j in range(blocks):
            hid[j] = dot(S.c_low[...], S.tab[up_rows(j), :])
        st = [local(lambda s, j=j: hid[j, s, :], n) for j in range(blocks)]

        def back_first():
            for j in range(blocks):
                gact[j] = dot(S.gy_low[...], S.tab[down_rows(j), :], (1, 1))

        tot = share(3, jnp.concatenate([s[0] for s in st] + [s[1] for s in st], axis=0), merge_stats(blocks), back_first)
        m_h = tot[:blocks]
        inv_h = lax.rsqrt(tot[blocks:] / every + norm_eps)
        sums = []
        for j in range(blocks):
            mj, ij, gj, bj = m_h[j : j + 1], inv_h[j : j + 1], mid_gain(j), mid_bias(j)

            def hidden(s, a, j=j, mj=mj, ij=ij, gj=gj, bj=bj):
                hat = (hid[j, s, :] - mj) * ij
                hid[j, s, :] = hat
                v, d = gelu_both(hat * gj + bj)
                a_low[j, s, :] = v.astype(bf16)
                g = gact[j, s, :] * d
                gact[j, s, :] = g
                return a[0] + fold(g), a[1] + fold(g * hat)

            sums.append(tuple(close(v) for v in chunks(n, hidden, (zero, zero))))
        mid_rows = jnp.concatenate([s[0] for s in sums] + [s[1] for s in sums], axis=0)

        def down_grads():
            for j in range(blocks):
                for h in range(C // 256):
                    put(S.flat, 2 * C + FF + j * C + h * 256, dot(a_low[j, :, half_cols(h)], S.gy_low[...], (0, 0)))

        def outputs():
            S.out[...] = S.mid[...]
            for j in range(blocks):
                S.out[...] += dot(a_low[j], S.tab[down_rows(j), :])

        tot = share(4, mid_rows, merge_sum, down_grads, outputs) * (1.0 / every)
        out_copy.start()
        for j in range(blocks):
            tb_, tg_, sc = tot[j : j + 1], tot[blocks + j : blocks + j + 1], mid_gain(j) * inv_h[j : j + 1]

            def grad_h(s, a, j=j, tb_=tb_, tg_=tg_, sc=sc):
                gh_low[j, s, :] = (sc * (gact[j, s, :] - tb_ - hid[j, s, :] * tg_)).astype(bf16)
                return a

            chunks(n, grad_h)
        S.g_f[...] = dot(gh_low[0], S.tab[up_rows(0), :], (1, 1))
        for j in range(1, blocks):
            S.g_f[...] += dot(gh_low[j], S.tab[up_rows(j), :], (1, 1))

        def ffn_sums(s, a):
            g = S.g_f[s, :]
            hat = (S.mid[s, :] - m_f) * inv_f
            return a[0] + fold(g), a[1] + fold(g * hat), a[2] + fold(g * S.p_val[s, :])

        b_ffn, g_ffn, g_fp = (close(v) for v in chunks(n, ffn_sums, (zero, zero, zero)))

        def grad_up():
            for j in range(blocks):
                for h in range(C // 256):
                    put(S.flat, 2 * C + j * C + h * 256, dot(S.c_low[:, half_cols(h)], gh_low[j], (0, 0)))

        tot = share(5, jnp.concatenate([b_ffn, g_ffn, g_fp, sum_c, sum_ch], axis=0), merge_sum, grad_up) * (1.0 / every)
        return mid_rows, b_ffn, g_ffn, tot

    out_copy = pltpu.make_async_copy(S.out, S.out_hbm, S.load_sem.at[7])
    hidden_shape = (blocks, n, C)
    mid_rows, b_ffn, g_ffn, tot = pl.run_scoped(
        middle, pltpu.VMEM(hidden_shape, f32), pltpu.VMEM(hidden_shape, f32), pltpu.VMEM(hidden_shape, bf16), pltpu.VMEM(hidden_shape, bf16)
    )

    def back(tat, tbt, tct, acc):
        ld_ct, ld_at, ld_bt = load(3, S.ct_hbm, tct), load(4, S.at_hbm, tat), load(5, S.bt_hbm, tbt)
        for copy in (ld_ct, ld_at, ld_bt):
            copy.start()
        scale_f = row(8) * inv_f
        mean_hat = tot[4:5] + scale_f * (tot[2:3] - tot[1:2] * hats)

        def grad_mid(s, a):
            hat = (S.mid[s, :] - m_f) * inv_f
            g = S.cot[s, :] + scale_f * (S.g_f[s, :] - tot[0:1] - hat * tot[1:2])
            S.g_f[s, :] = g
            ph = S.p_val[s, :]
            S.gp_low[s, :] = (slope * (g - tot[3:4] - ph * mean_hat)).astype(bf16)
            return a[0] + fold(g), a[1] + fold(g * ph)

        b_proj, g_proj = (close(v) for v in chunks(n, grad_mid, (zero, zero)))
        S.p_val[...] = dot(S.gp_low[...], S.tab[pl.ds(C, C), :], (1, 1))

        def grad_s(s, a):
            g = S.p_val[s, :] * S.s_val[s, :]
            S.p_val[s, :] = g
            return a[0] + fold(g), a[1] + fold(g * S.d_l[s, :]), a[2] + fold(g * S.d_s[s, :])

        b_pair, g_lg, g_sg = (close(v) for v in chunks(n, grad_s, (zero, zero, zero)))

        def grad_out():
            for h in range(C // 256):
                put(S.flat, C + h * 256, dot(S.t_low[:, half_cols(h)], S.gp_low[...], (0, 0)))

        sums = share(6, jnp.concatenate([b_pair, g_lg, g_sg], axis=0), merge_sum, grad_out) * (1.0 / every)
        sc_l, sc_s = row(2) * inv_l, row(4) * inv_s
        gl_low, gs_low = S.t_low, S.gp_low

        def grad_pair(s, a):
            g = S.p_val[s, :] - sums[0:1]
            gl_low[s, :] = (sc_l * (g - S.d_l[s, :] * sums[1:2])).astype(bf16)
            gs_low[s, :] = (sc_s * (g - S.d_s[s, :] * sums[2:3])).astype(bf16)
            return a

        chunks(n, grad_pair)
        ld_ct.wait()

        @pl.loop(0, NF // 256)
        def _(t):
            re, im = pl.ds(pl.multiple_of(t * 256, 256), 256), pl.ds(pl.multiple_of(NF + t * 256, 256), 256)
            acc[0] = dot(tct[re, :], gl_low[...])
            acc[1] = dot(tct[im, :], gl_low[...])
            acc[2] = dot(tct[re, :], gs_low[...])
            acc[3] = dot(tct[im, :], gs_low[...])

            @pl.loop(0, 8)
            def _(i):
                s = pl.ds(pl.multiple_of(i * 32, 32), 32)
                re = pl.ds(pl.multiple_of(t * 256 + i * 32, 32), 32)
                im = pl.ds(pl.multiple_of(NF + t * 256 + i * 32, 32), 32)
                lr, li, sr, si = acc[0, s, :], acc[1, s, :], acc[2, s, :], acc[3, s, :]
                kr, ki = S.spec_l[re, :], S.spec_l[im, :]
                hr, hi = S.spec_s[re, :], S.spec_s[im, :]
                S.prod_k[re, :] = (lr * kr - li * ki + sr * hr - si * hi).astype(bf16)
                S.prod_k[im, :] = (lr * ki + li * kr + sr * hi + si * hr).astype(bf16)
                ur, ui = S.spec_u[re, :], S.spec_u[im, :]
                S.prod_l[re, :] = (lr * ur + li * ui).astype(bf16)
                S.prod_l[im, :] = (lr * ui - li * ur).astype(bf16)
                S.prod_s[re, :] = (sr * ur + si * ui).astype(bf16)
                S.prod_s[im, :] = (sr * ui - si * ur).astype(bf16)

        ld_at.wait()
        S.halo_out[0] = dot(tat[pl.ds(0, n), :], S.prod_k[...]).astype(bf16)
        S.halo_out[1] = dot(tat[pl.ds(2 * n, n), :], S.prod_k[...]).astype(bf16)
        halo_up = halo(2, S.halo_out.at[0], S.halo_in.at[1], True)
        halo_down = halo(3, S.halo_out.at[1], S.halo_in.at[0], False)
        halo_start(halo_up, halo_down)
        S.p_val[...] = dot(tat[pl.ds(n, n), :], S.prod_k[...])
        ld_bt.wait()

        @pl.loop(0, 4)
        def _(t):
            s = pl.ds(pl.multiple_of(t * 256, 256), 256)
            put(S.flat, 2 * C + 2 * FF + t * 256, dot(tbt[s, :], S.prod_l[...]))

        put(S.flat, BASE, dot(S.bst[...], S.prod_s[...]))
        halo_wait(halo_up, halo_down, S.halo_in.at[0], S.halo_in.at[1])
        gz_low = S.t_low

        def grad_z(s, a):
            g = S.p_val[s, :] + S.halo_in[0, s, :].astype(f32) + S.halo_in[1, s, :].astype(f32)
            gz_low[s, :] = (g * S.dz[s, :]).astype(bf16)
            return a

        chunks(n, grad_z)
        S.p_val[...] = dot(gz_low[...], S.tab[pl.ds(0, C), :], (1, 1))

        def pre_sums(s, a):
            g = S.p_val[s, :]
            return a[0] + fold(g), a[1] + fold(g * ((S.x[s, :] - m_x) * inv_x))

        b_pre, g_pre = (close(v) for v in chunks(n, pre_sums, (zero, zero)))
        share_send(7, 0, jnp.concatenate([b_pre, g_pre], axis=0))
        for h in range(C // 256):
            put(S.flat, h * 256, dot(S.pre_low[:, half_cols(h)], gz_low[...], (0, 0)))
        norms = [g_pre, b_pre, g_lg, b_pair, g_sg, b_pair, g_proj, b_proj, g_ffn, b_ffn]
        norms += [mid_rows[blocks + j : blocks + j + 1] for j in range(blocks)]
        put(S.flat, BASE + 32, jnp.concatenate(norms + [jnp.zeros((2, C), f32)], axis=0))
        for j in range(blocks):
            for k in range(4):
                S.flat[pl.ds((BASE + 25 + j) * 4 + k, 1), :] = mid_rows[j : j + 1, k * 128 : (k + 1) * 128]

    pl.run_scoped(
        back, pltpu.VMEM(S.at_hbm.shape, bf16), pltpu.VMEM(S.bt_hbm.shape, bf16), pltpu.VMEM(S.ct_hbm.shape, bf16), pltpu.VMEM((4, 256, C), f32)
    )


    plan = reduce_plan(nb)
    parts = len(plan)
    size = lines // parts
    unit = 32 if own % 32 == 0 else 8
    tmp = S.tmp
    hop_base = nz * nb
    z_base = hop_base + nz * (nb - 1)

    def tail(sib_out, pair, z_out):
        grad = S.flat.reshape(total, 4, 128)

        def column(i):
            return lax.rem(z + 1 + i, nz)

        def collect(m, zz, cc):
            start = (flip(b, m) * nr + 2 * zz + cc) * own

            @pl.loop(0, own // unit)
            def _(g):
                for u in range(unit):
                    tmp[pl.ds(pl.multiple_of((g * unit + u) * 4, 4), 4), :] = grad[S.idx[start + g * unit + u]]

        def to_sibling(i, m):
            return pltpu.make_async_remote_copy(
                sib_out.at[i, m], rows_in.at[i * nb + m], S.sib_send.at[i, m], S.sib_recv.at[i, m],
                device_id=sibling, device_id_type=MESH,
            )

        def rows_of(p):
            return pl.ds(p * size, size)

        def slots(p, t):
            at = sum(len(plan[p][k][2]) for k in range(t))
            return at, len(plan[p][t][2])

        def hop_at(i, p, at, count):
            return rows_in.at[pl.ds(hop_base + i * (nb - 1) + at, count), rows_of(p)]

        def hop(i, p, t, m):
            o, sent, kept = plan[p][t]
            at, _ = slots(p, t)
            landing = rows_in.at[hop_base + i * (nb - 1) + at + kept.index(m ^ (1 << o)), rows_of(p)]
            return pltpu.make_async_remote_copy(
                pair.at[i, m, rows_of(p)], landing, S.hop_send.at[i, p, t], S.hop_recv.at[i, p, t],
                device_id=(flip(b, 1 << o), r), device_id_type=MESH,
            )

        def hop_wait(i, p, t, sem):
            whole = hop_at(i, p, *slots(p, t))
            pltpu.make_async_copy(whole, whole, sem.at[i, p, t]).wait()

        def for_sibling(i):
            for m in range(nb):
                collect(m, column(i), 1 - c)
                sib_out[i, m] = tmp[...].astype(bf16)
                to_sibling(i, m).start()

        for_sibling(0)

        @pl.loop(0, nz)
        def _(i):
            @pl.when(i < nz - 1)
            def _():
                for_sibling(i + 1)

            for m in reversed(range(nb)):
                collect(m, column(i), c)
                to_sibling(i, m).wait_recv()
                pair[i, m] = (tmp[...] + rows_in[i * nb + m].astype(f32)).astype(bf16)
                for p in range(parts):
                    if m in plan[p][0][1]:
                        hop(i, p, 0, m).start()

        share_send(7, 1, share_wait(7, 0, merge_sum))

        for t in range(parts - 1):

            @pl.loop(0, nz)
            def _(i):
                for p in range(parts):
                    hop_wait(i, p, t, S.hop_recv)
                    at, _ = slots(p, t)
                    for k, m in enumerate(plan[p][t][2]):
                        pair[i, m, rows_of(p)] = (
                            pair[i, m, rows_of(p)].astype(f32)
                            + rows_in[hop_base + i * (nb - 1) + at + k, rows_of(p)].astype(f32)
                        ).astype(bf16)
                        if m in plan[p][t + 1][1]:
                            hop(i, p, t + 1, m).start()

        sums = share_wait(7, 1, merge_sum) * (1.0 / every)
        scale_x = row(0) * inv_x

        def last(s, a):
            hat = (S.x[s, :] - m_x) * inv_x
            S.g_f[s, :] = S.g_f[s, :] + scale_x * (S.p_val[s, :] - sums[0:1] - hat * sums[1:2])
            return a

        chunks(n, last)
        gin_copy = pltpu.make_async_copy(S.g_f, S.gin_hbm, S.load_sem.at[6])
        gin_copy.start()
        for i in range(own):
            p = S.idx[(b * nr + r) * own + i]
            fast = (p >= 2 * C + 2 * FF + KL * KL) & ((p < BASE) | (p >= BASE + KS * KS))
            S.rate[pl.ds(i, 1), :] = jnp.full((1, 128), jnp.where(fast, np.float32(norm_rate), np.float32(matrix_rate)), f32)

        def to_owner(i):
            return pltpu.make_async_remote_copy(
                z_out.at[i], rows_in.at[z_base + i], S.own_send.at[i], S.own_recv.at[i],
                device_id=(b, 2 * column(i) + c), device_id_type=MESH,
            )

        @pl.loop(0, nz)
        def _(i):
            for p in range(parts):
                hop_wait(i, p, parts - 1, S.hop_recv)
                at, _ = slots(p, parts - 1)
                tmp[rows_of(p), :] = pair[i, 0, rows_of(p)].astype(f32) + rows_in[hop_base + i * (nb - 1) + at, rows_of(p)].astype(f32)

            @pl.when(i < nz - 1)
            def _():
                z_out[i] = tmp[...].astype(bf16)
                to_owner(i).start()

        for i in range(nz - 1):
            to_owner(i).wait_recv()
            tmp[...] += rows_in[z_base + i].astype(f32)
        for j in range(4):
            S.red[:, j * 128 : (j + 1) * 128] = tmp[pl.ds(j, own, stride=4), :]

        @pl.loop(0, nz)
        def _(i):
            for m in range(nb):
                to_sibling(i, m).wait_send()
            for p in range(parts):
                for t in range(parts):
                    hop_wait(i, p, t, S.hop_send)

        for i in range(nz - 1):
            to_owner(i).wait_send()
        gin_copy.wait()

    low_block = lambda *lead: pltpu.VMEM(lead + (lines, 128), bf16)
    pl.run_scoped(tail, low_block(nz, nb), low_block(nz, nb), low_block(nz))
    for e in range(len(WIDTHS)):
        for stage in range(2):
            buf, mine, count, peers = share_stage(e, stage)
            sent = buf.at[pl.ds(0, count - 1)]
            pltpu.make_async_copy(sent, sent, S.stat_send.at[e, stage]).wait()
    out_copy.wait()


def step(x, cot, master, places, nb, nr):
    (a, at, b, bt, bs, bst, c, ct) = tables()
    n, own, nz, parts = x.shape[0], master.shape[0], nr // 2, nb.bit_length() - 1
    total = places.shape[0]
    vm = lambda *shape: pltpu.VMEM(shape, f32)
    low = lambda *shape: pltpu.VMEM(shape, bf16)
    dma = lambda *shape: pltpu.SemaphoreType.DMA(shape)
    vmem, anywhere = pl.BlockSpec(memory_space=pltpu.VMEM), pl.BlockSpec(memory_space=pl.ANY)
    ins = dict(
        idx=(places, pl.BlockSpec(memory_space=pltpu.SMEM)), x_hbm=(x, anywhere), cot_hbm=(cot, anywhere), master_hbm=(master, anywhere),
        a_hbm=(a, anywhere), at_hbm=(at, anywhere), b_hbm=(b, anywhere), bt_hbm=(bt, anywhere), bs=(bs, vmem), bst=(bst, vmem),
        c_hbm=(c, anywhere), ct_hbm=(ct, anywhere),
    )
    image = jax.ShapeDtypeStruct((n, C), f32)
    outs = dict(
        out_hbm=(image, anywhere), gin_hbm=(image, anywhere), red=(jax.ShapeDtypeStruct((own, C), f32), vmem),
        rate=(jax.ShapeDtypeStruct((own, 128), f32), vmem),
    )
    scratch = dict(
        rows_in=low(nb * nr, 4 * own, 128), flat=vm(4 * total, 128), tab=low(total, C), x=vm(n, C), cot=vm(n, C), master=vm(own, C),
        tmp=vm(4 * own, 128), chunk=vm(512, 128), inv=pltpu.VMEM((total // 128, 128), jnp.int32),
        inv_at=pltpu.SMEM((total // 128, 128), jnp.int32), small=vm(48, C),
        pre_low=low(n, C), wide=low(3 * n, C), dz=vm(n, C), spec_u=vm(2 * NF, C), spec_l=vm(2 * NF, C), spec_s=vm(2 * NF, C),
        prod_l=low(2 * NF, C), prod_s=low(2 * NF, C), prod_k=low(2 * NF, C), d_l=vm(n, C), d_s=vm(n, C), s_val=vm(n, C),
        t_low=low(n, C), p_val=vm(n, C), mid=vm(n, C), c_low=low(n, C), gy_low=low(n, C), gp_low=low(n, C), g_f=vm(n, C), out=vm(n, C),
        halo_out=low(2, n, C), halo_in=low(2, n, C),
    )
    for e, w in enumerate(WIDTHS):
        scratch[f"one{e}"] = vm(nr, w, C)
        scratch[f"two{e}"] = vm(nb, w, C)
    scratch.update(
        load_sem=dma(8), stat_send=dma(len(WIDTHS), 2), stat_recv=dma(len(WIDTHS), 2), halo_send=dma(4), halo_recv=dma(4),
        z_send=dma(nz), z_recv=dma(nz), b_send=dma(nb, nz), b_recv=dma(nb, nz), half_send=dma(2, nz), half_recv=dma(2, nz),
        core_send=dma(nb, nz), core_recv=dma(nb, nz), sib_send=dma(nz, nb), sib_recv=dma(nz, nb),
        hop_send=dma(nz, parts, parts), hop_recv=dma(nz, parts, parts), own_send=dma(nz), own_recv=dma(nz),
    )
    return pl.pallas_call(
        functools.partial(step_kernel, nb, nr, [*ins, *outs, *scratch]),
        out_shape=[v[0] for v in outs.values()],
        in_specs=[v[1] for v in ins.values()],
        out_specs=[v[1] for v in outs.values()],
        scratch_shapes=list(scratch.values()),
        compiler_params=pltpu.CompilerParams(collective_id=0, has_side_effects=True, vmem_limit_bytes=62 * 2**20),
    )(*[v[0] for v in ins.values()])


def finish_kernel(
    red_ref, rate_ref, first_hbm, second_hbm, master_hbm, out_hbm, gin_hbm,
    result_hbm, grad_hbm, slots_ref, new_first_ref, new_second_ref, new_master_ref, new_copy_ref,
    first_ref, second_ref, master_ref, out_ref, gin_ref, sem,
):
    ends = ((first_hbm, first_ref), (second_hbm, second_ref), (master_hbm, master_ref), (out_hbm, out_ref), (gin_hbm, gin_ref))
    loads = [pltpu.make_async_copy(src, dst, sem.at[2 + i]) for i, (src, dst) in enumerate(ends)]
    for copy in loads:
        copy.start()
    through = [pltpu.make_async_copy(out_ref, result_hbm, sem.at[0]), pltpu.make_async_copy(gin_ref, grad_hbm, sem.at[1])]
    for copy in loads:
        copy.wait()
    for copy in through:
        copy.start()
    own = red_ref.shape[0]
    size = 32 if own % 32 == 0 else 8
    for s in range(0, own, size):
        s = pl.ds(s, size)
        for j in range(C // 128):
            at = (s, pl.ds(j * 128, 128))
            g = red_ref[at]
            first = beta_one * first_ref[at] + (1.0 - beta_one) * g
            second = beta_two * second_ref[at] + (1.0 - beta_two) * g * g
            slots_ref[at] = g
            new_first_ref[at] = first
            new_second_ref[at] = second
            first_hat = first / (1.0 - beta_one**STEP)
            second_hat = second / (1.0 - beta_two**STEP)
            master = master_ref[at]
            new = master - rate_ref[s, :] * (first_hat / (jnp.sqrt(second_hat) + adam_eps) + decay_rate * master)
            new_master_ref[at] = new
            new_copy_ref[at] = new.astype(bf16)
    for copy in through:
        copy.wait()


def finish(reduced, first, second, master, rates, out, gin):
    vmem, anywhere = pl.BlockSpec(memory_space=pltpu.VMEM), pl.BlockSpec(memory_space=pl.ANY)
    slot = jax.ShapeDtypeStruct(reduced.shape, f32)
    image = jax.ShapeDtypeStruct(out.shape, f32)
    return pl.pallas_call(
        finish_kernel,
        out_shape=[image, image, slot, slot, slot, slot, jax.ShapeDtypeStruct(reduced.shape, bf16)],
        in_specs=[vmem] * 2 + [anywhere] * 5,
        out_specs=[anywhere] * 2 + [vmem] * 5,
        scratch_shapes=[pltpu.VMEM(reduced.shape, f32)] * 3 + [pltpu.VMEM(out.shape, f32)] * 2 + [pltpu.SemaphoreType.DMA((7,))],
        compiler_params=pltpu.CompilerParams(vmem_limit_bytes=62 * 2**20),
    )(reduced, rates, first, second, master, out, gin)


def table_place(t):
    start = 2 * C + 2 * FF
    k_end = start + KL * KL
    s_end = k_end + KS * KS
    m_gain = s_end + 10
    m_bias = m_gain + FF // C
    m_end = m_bias + FF // C
    up = t - 2 * C
    up = 2 * C + up % (FF // C) * C + up // (FF // C)
    base = start + 976
    unused = t - m_end
    unused = jnp.where(unused < 15, k_end + unused, jnp.where(unused < 18, base + 29 + unused - 15, base + 46 + unused - 18))
    p = jnp.where((t >= 2 * C) & (t < 2 * C + FF), up, t)
    p = jnp.where(t >= k_end, t - k_end + base, p)
    p = jnp.where(t >= s_end, t - s_end + base + 32, p)
    p = jnp.where(t >= m_bias, t - m_bias + base + 25, p)
    return jnp.where(t >= m_end, unused, p)


def body(image_in, cotangent, slot_rows, master, first_moment, second_moment):
    n = image_in.shape[0] * image_in.shape[1] * image_in.shape[2]
    nb, nr = lax.axis_size("batch"), lax.axis_size("rows")
    out, grad_in, reduced, rates = step(
        image_in.reshape(n, C), cotangent.reshape(n, C), master, table_place(slot_rows), nb, nr
    )
    result, grad_x, *slots = finish(reduced, first_moment, second_moment, master, rates, out, grad_in)
    return (result.reshape(image_in.shape), grad_x.reshape(image_in.shape), *slots)


def solution(mesh):
    image = P("batch", "rows", None, None)
    owner = P(AXES, None)
    return jax.shard_map(
        body,
        mesh=mesh,
        in_specs=(image, image, P(), owner, owner, owner),
        out_specs=(image, image, owner, owner, owner, owner, owner),
        check_vma=False,
    )
```

```python
import functools
import types

import jax
import jax.numpy as jnp
import numpy as np
from jax import lax
from jax.experimental import pallas as pl
from jax.experimental.pallas import tpu as pltpu
from jax.sharding import PartitionSpec as P

C = 512
FF = 2048
KL = 31
KS = 5
STEP = 10

norm_eps = 1e-05
beta_one = 0.9
beta_two = 0.999
adam_eps = 1e-08
decay_rate = 0.05
matrix_rate = 0.05
norm_rate = 0.5

TH = 16
TW = 16
NY = 47
NX = 31
NF = 768
REACH = (KL - 1) // 2
AXES = ("batch", "rows")
f32 = jnp.float32
bf16 = jnp.bfloat16


@functools.lru_cache(None)
def tables():
    freqs = [(ky, 0) for ky in range((NY + 1) // 2)]
    freqs += [(ky, kx) for kx in range(1, (NX + 1) // 2) for ky in range(NY)]
    ky = np.array([f[0] for f in freqs], np.int64)[:, None]
    kx = np.array([f[1] for f in freqs], np.int64)[:, None]
    pad = NF - len(freqs)

    def angle(rows, cols):
        ty = (ky * rows.reshape(1, -1)) % NY
        tx = (kx * cols.reshape(1, -1)) % NX
        return 2 * np.pi * (ty / NY + tx / NX)

    def grid(rows, cols):
        r, c = np.meshgrid(rows, cols, indexing="ij")
        return r.reshape(-1), c.reshape(-1)

    def stack(re, im):
        z = np.zeros((pad, re.shape[1]))
        return np.concatenate([re, z, im, z], axis=0)

    r, c = grid(np.arange(-TH, 2 * TH), np.arange(TW))
    used = ((r + REACH >= 0) & (r + REACH < NY - 1)).astype(np.float64)[None]
    t = angle(r + REACH, c)
    a = stack(np.cos(t) * used, -np.sin(t) * used)
    i, j = grid(np.arange(KL), np.arange(KL))
    t = angle(i, j - REACH)
    b = stack(np.cos(t), -np.sin(t))
    lead = REACH - (KS - 1) // 2
    small = ((i >= lead) & (i < lead + KS) & (j >= lead) & (j < lead + KS)).nonzero()[0]
    bs = np.pad(b[:, small], ((0, 0), (0, 32 - KS * KS)))
    b = np.pad(b, ((0, 0), (0, 2 * C - KL * KL)))
    y, x = grid(np.arange(TH), np.arange(TW))
    t = angle(y, x)
    w = np.full((len(freqs), 1), 2.0)
    w[0] = 1.0
    w /= NY * NX
    ct = stack(w * np.cos(t), -w * np.sin(t))
    return tuple(m.astype(np.float32).astype(bf16) for m in (a, a.T, b, b.T, bs, bs.T, ct.T, ct))


def dot(a, b, dims=(1, 0)):
    return lax.dot_general(a, b, (((dims[0],), (dims[1],)), ((), ())), preferred_element_type=f32)


MESH = pl.DeviceIdType.MESH
WIDTHS = (2, 4, 3, 8, 8, 5, 3, 2)
BASE = 2 * C + 2 * FF + 976


def chunks(n, fn, init=()):
    return lax.fori_loop(0, n // 32, lambda i, c: fn(pl.ds(pl.multiple_of(i * 32, 32), 32), c), init)


def fold(v):
    return jnp.sum(v.reshape(v.shape[0] // 8, 8, v.shape[1]), axis=0)


def close(v):
    return jnp.sum(v, axis=0, keepdims=True)


def put(ref, start, v):
    for j in range(4):
        ref[pl.ds(start * 4 + j, v.shape[0], stride=4), :] = v[:, j * 128 : (j + 1) * 128]


def gelu_both(v):
    a = np.float32(np.sqrt(2 / np.pi))
    sq = v * v
    t = jnp.tanh(a * (v + 0.044715 * (sq * v)))
    half = 0.5 * (1 + t)
    return v * half, half + 0.5 * v * (1 - t * t) * (a * (1 + 3 * 0.044715 * sq))


def flip(b, m):
    k = 0
    while m >> k:
        if (m >> k) & 1:
            b = b + (1 - 2 * lax.rem(b // 2**k, 2)) * 2**k
        k += 1
    return b


def reduce_plan(nb):
    bits = nb.bit_length() - 1
    plan = []
    for p in range(bits):
        order = [(p + t) % bits for t in range(bits)]
        steps, kept = [], list(range(nb))
        for o in order:
            sent = [m for m in kept if (m >> o) & 1]
            kept = [m for m in kept if not (m >> o) & 1]
            steps.append((o, sent, kept))
        plan.append(steps)
    return plan


def merge_sum(v, count):
    return jnp.sum(v, axis=0)


def merge_stats(h):
    def merge(v, count):
        means = v[:, :h]
        m = jnp.sum(means, axis=0) * (1.0 / v.shape[0])
        d = means - m
        parts = [m, jnp.sum(v[:, h : 2 * h], axis=0) + count * jnp.sum(d * d, axis=0)]
        if v.shape[1] > 2 * h:
            parts.append(jnp.sum(v[:, 2 * h :], axis=0))
        return jnp.concatenate(parts, axis=0)

    return merge


def local(read, n):
    zero = jnp.zeros((8, C), f32)
    m = close(chunks(n, lambda s, c: c + fold(read(s)), zero)) * (1.0 / n)

    def sq(s, c):
        d = read(s) - m
        return c + fold(d * d)

    return m, close(chunks(n, sq, zero))


def half_cols(h):
    return pl.ds(pl.multiple_of(h * 256, 256), 256)


def up_rows(j):
    return pl.ds(pl.multiple_of(2 * C + j * C, C), C)


def down_rows(j):
    return pl.ds(pl.multiple_of(2 * C + FF + j * C, C), C)


def step_kernel(nb, nr, names, *refs):
    S = types.SimpleNamespace(**dict(zip(names, refs)))
    nz = nr // 2
    nd = nb * nr
    n = S.x.shape[0]
    own = S.master.shape[0]
    lines = 4 * own
    total = S.tab.shape[0]
    every = float(n * nd)
    b = lax.axis_index("batch")
    r = lax.axis_index("rows")
    z, c = r // 2, lax.rem(r, 2)
    sibling = (b, r + 1 - 2 * c)
    square = nb == 4
    blocks = FF // C
    zero = jnp.zeros((8, C), f32)
    rows_in = S.rows_in

    def load(i, src, dst):
        return pltpu.make_async_copy(src, dst, S.load_sem.at[i])

    ld_m, ld_x, ld_c = load(0, S.master_hbm, S.master), load(1, S.x_hbm, S.x), load(2, S.cot_hbm, S.cot)
    for copy in (ld_m, ld_x, ld_c):
        copy.start()
    barrier = pltpu.get_barrier_semaphore()
    for k in range(1, nr):
        pl.semaphore_signal(barrier, inc=1, device_id=(b, lax.rem(r + k, nr)), device_id_type=MESH)
    for m in range(1, nb):
        pl.semaphore_signal(barrier, inc=1, device_id=(flip(b, m), r), device_id_type=MESH)


    def share_stage(e, stage):
        if stage == 0:
            return getattr(S, f"one{e}"), r, nr, [(b, lax.rem(r + k, nr)) for k in range(1, nr)]
        return getattr(S, f"two{e}"), b, nb, [(flip(b, m), r) for m in range(1, nb)]

    def share_send(e, stage, v):
        buf, mine, size, peers = share_stage(e, stage)
        buf[mine] = v
        for peer in peers:
            pltpu.make_async_remote_copy(
                buf.at[mine], buf.at[mine], S.stat_send.at[e, stage], S.stat_recv.at[e, stage], device_id=peer, device_id_type=MESH
            ).start()

    def share_wait(e, stage, merge):
        buf, mine, size, peers = share_stage(e, stage)
        got = buf.at[pl.ds(0, size - 1)]
        pltpu.make_async_copy(got, got, S.stat_recv.at[e, stage]).wait()
        return merge(buf[...], float(n if stage == 0 else n * nr))

    def share(e, v, merge, work=None, more=None):
        share_send(e, 0, v)
        if work:
            work()
        v = share_wait(e, 0, merge)
        share_send(e, 1, v)
        if more:
            more()
        return share_wait(e, 1, merge)


    def place(m, zz, core):
        return flip(b, m) * nr + 2 * zz + core

    def along_z(zz, up):
        at = rows_in.at[place(0, zz, c)]
        return pltpu.make_async_remote_copy(
            at, at, S.z_send.at[zz], S.z_recv.at[zz], device_id=(b, r + 2 if up else r - 2), device_id_type=MESH
        )

    def to_peer(m, zz):
        at = rows_in.at[place(0, zz, c)]
        return pltpu.make_async_remote_copy(
            at, at, S.b_send.at[m, zz], S.b_recv.at[m, zz], device_id=(flip(b, m), r), device_id_type=MESH
        )

    def from_peer(m, zz):
        at = rows_in.at[place(m, zz, c)]
        return pltpu.make_async_copy(at, at, S.b_recv.at[m, zz])

    def half(m, zz, h, to):
        at = rows_in.at[place(m, zz, c), pl.ds(h * (lines // 2), lines // 2)]
        return pltpu.make_async_remote_copy(
            at, at, S.half_send.at[h, zz], S.half_recv.at[h, zz], device_id=(flip(b, to), r), device_id_type=MESH
        )

    def to_other_core(m, zz, core):
        at = rows_in.at[place(m, zz, core)]
        return pltpu.make_async_remote_copy(
            at, at, S.core_send.at[m, zz], S.core_recv.at[m, zz], device_id=sibling, device_id_type=MESH
        )

    def cast(m, zz, core):
        d = place(m, zz, core)
        S.flat[pl.ds(pl.multiple_of(d * lines, lines), lines), :] = rows_in[d].astype(f32)

    def sends(zz):
        for m in range(1, nb):
            if not (square and m == 3):
                to_peer(m, zz).start()
        to_other_core(0, zz, c).start()
        cast(0, zz, c)

    def own_column(k):
        if k == 0:

            @pl.when(z < nz - 1)
            def _():
                along_z(z, True).start()

            @pl.when(z > 0)
            def _():
                along_z(z, False).start()

            sends(z)
            return

        @pl.when(z >= k)
        def _():
            along_z(z - k, True).wait_recv()

            @pl.when(z < nz - 1)
            def _():
                along_z(z - k, True).start()

            sends(z - k)

        @pl.when(z + k < nz)
        def _():
            along_z(z + k, False).wait_recv()

            @pl.when(z > 0)
            def _():
                along_z(z + k, False).start()

            sends(z + k)

    def each(k, fn):
        if k == 0:
            fn(z)
            return

        @pl.when(z >= k)
        def _():
            fn(z - k)

        @pl.when(z + k < nz)
        def _():
            fn(z + k)

    def pass_on(zz):
        for m in range(1, nb):
            if square and m == 3:
                continue
            from_peer(m, zz).wait()
            if square:
                half(m, zz, 2 - m, 3 - m).start()
            to_other_core(m, zz, c).start()
            cast(m, zz, c)

    def corner(zz):
        if square:
            for h in range(2):
                half(3, zz, h, 0).wait_recv()
            to_other_core(3, zz, c).start()
            cast(3, zz, c)

    def other_core(zz):
        for m in range(nb):
            to_other_core(m, zz, 1 - c).wait_recv()
            cast(m, zz, 1 - c)

    def find(part, parts):
        tiles = total // 1024
        unit = 16
        spots = [
            lax.broadcasted_iota(jnp.int32, (8, 128), 0) * 128 + lax.broadcasted_iota(jnp.int32, (8, 128), 1) + 1024 * k
            for k in range(tiles)
        ]

        def some(g, acc):
            for u in range(unit):
                s = part * (total // parts) + g * unit + u
                p = S.idx[s]
                acc = [jnp.where(spot == p, s, a) for spot, a in zip(spots, acc)]
            return acc

        acc = [S.inv[k * 8 : k * 8 + 8, :] if part else jnp.zeros((8, 128), jnp.int32) for k in range(tiles)]
        acc = lax.fori_loop(0, total // parts // unit, some, acc)
        for k in range(tiles):
            S.inv[k * 8 : k * 8 + 8, :] = acc[k]

    def order(start, stop):
        flat = S.flat.reshape(total, 4, 128)

        @pl.loop(start, stop)
        def _(t):
            for u in range(128):
                S.chunk[4 * u : 4 * u + 4, :] = flat[S.inv_at[t, u]]

            rows = pl.ds(pl.multiple_of(t * 128, 128), 128)
            for j in range(4):
                S.tab[rows, j * 128 : (j + 1) * 128] = S.chunk[pl.ds(j, 128, stride=4), :].astype(bf16)

    def front(ta, tb, tc):
        ld_a, ld_b, ld_t = load(3, S.a_hbm, ta), load(4, S.b_hbm, tb), load(5, S.c_hbm, tc)
        for copy in (ld_b, ld_a, ld_t):
            copy.start()
        ld_m.wait()
        for j in range(4):
            S.tmp[pl.ds(j, own, stride=4), :] = S.master[:, j * 128 : (j + 1) * 128]
        rows_in[place(0, z, c)] = S.tmp[...].astype(bf16)
        pl.semaphore_wait(barrier, nr - 1 + nb - 1)
        own_column(0)
        ld_x.wait()
        share_send(0, 0, jnp.concatenate(local(lambda s: S.x[s, :], n), axis=0))
        steps = max(nz - 1, 1)
        for k in range(1, nz):
            find(k - 1, steps)
            own_column(k)
            each(k - 1, pass_on)
            if k > 1:
                each(k - 2, corner)
            if k > 2:
                each(k - 3, other_core)
            if k == 1:
                share_send(0, 1, share_wait(0, 0, merge_stats(1)))
        if nz == 1:
            find(0, 1)
            share_send(0, 1, share_wait(0, 0, merge_stats(1)))
        to_scalar = pltpu.make_async_copy(S.inv, S.inv_at, S.load_sem.at[6])
        to_scalar.start()
        each(nz - 1, pass_on)
        if nz > 1:
            each(nz - 2, corner)
        each(nz - 1, corner)
        for k in range(max(nz - 3, 0), nz):
            each(k, other_core)
        tot = share_wait(0, 1, merge_stats(1))
        m_x, q_x = tot[0:1], tot[1:2] * (1.0 / every)
        inv_x = lax.rsqrt(q_x + norm_eps)
        to_scalar.wait()
        tiles = total // 128
        late = (2 * C + 2 * FF) // 128
        order(0, 2 * C // 128)
        order(late, tiles)

        for m in range(nb):

            @pl.loop(0, nz)
            def _(zz):
                to_other_core(m, zz, c).wait_send()
                if m and not (square and m == 3):
                    to_peer(m, zz).wait_send()
                if square and m in (1, 2):
                    half(m, zz, 2 - m, 3 - m).wait_send()

        for k in range(nz):

            @pl.when((z >= k) & (z < nz - 1))
            def _():
                along_z(z - k, True).wait_send()

            @pl.when((z + k < nz) & (z > 0))
            def _():
                along_z(z + k, False).wait_send()

        small = S.tab[pl.ds(BASE, 48), :].astype(f32)
        S.small[...] = small
        row = lambda i: small[32 + i : 33 + i, :]

        def pre(s, sx):
            d = S.x[s, :] - m_x
            S.pre_low[s, :] = (d * (inv_x * row(0)) + row(1)).astype(bf16)
            return sx + fold(d)

        sum_x = close(chunks(n, pre, zero))
        S.dz[...] = dot(S.pre_low[...], S.tab[pl.ds(0, C), :])

        def act(s, a):
            u, d = gelu_both(S.dz[s, :])
            S.dz[s, :] = d
            S.wide[pl.ds(pl.multiple_of(n + s.start, 32), 32), :] = u.astype(bf16)
            return a

        chunks(n, act)
        mine = S.wide.at[pl.ds(n, n)]
        halo_up = halo(0, mine, S.wide.at[pl.ds(2 * n, n)], True)
        halo_down = halo(1, mine, S.wide.at[pl.ds(0, n)], False)
        halo_start(halo_up, halo_down)

        ld_b.wait()

        @pl.loop(0, 2 * NF // 256)
        def _(t):
            s = pl.ds(pl.multiple_of(t * 256, 256), 256)
            S.spec_l[s, :] = dot(tb[s, :], S.tab[pl.ds(2 * C + 2 * FF, 2 * C), :])
            S.spec_s[s, :] = dot(S.bs[s, :], S.tab[pl.ds(BASE, 32), :])

        halo_wait(halo_up, halo_down, S.wide.at[pl.ds(0, n)], S.wide.at[pl.ds(2 * n, n)])
        ld_a.wait()

        @pl.loop(0, 2 * NF // 256)
        def _(t):
            s = pl.ds(pl.multiple_of(t * 256, 256), 256)
            S.spec_u[s, :] = dot(ta[s, :], S.wide[...])

        @pl.loop(0, NF // 32)
        def _(i):
            re, im = pl.ds(pl.multiple_of(i * 32, 32), 32), pl.ds(pl.multiple_of(NF + i * 32, 32), 32)
            ur, ui = S.spec_u[re, :], S.spec_u[im, :]
            for k, p in ((S.spec_l, S.prod_l), (S.spec_s, S.prod_s)):
                kr, ki = k[re, :], k[im, :]
                p[re, :] = (ur * kr + ui * ki).astype(bf16)
                p[im, :] = (ui * kr - ur * ki).astype(bf16)

        ld_t.wait()
        S.d_l[...] = dot(tc[...], S.prod_l[...])
        S.d_s[...] = dot(tc[...], S.prod_s[...])
        return m_x, q_x, sum_x


    has_above, has_below = r > 0, r < nr - 1

    def halo(i, src, dst, up):
        peer = lax.rem(r + nr - 1, nr) if up else lax.rem(r + 1, nr)
        return pltpu.make_async_remote_copy(
            src, dst, S.halo_send.at[i], S.halo_recv.at[i], device_id=(b, peer), device_id_type=MESH
        )

    def halo_start(up, down):
        @pl.when(has_above)
        def _():
            up.start()

        @pl.when(has_below)
        def _():
            down.start()

    def halo_wait(up, down, above, below):
        @pl.when(has_below)
        def _():
            up.wait_recv()
            down.wait_send()

        @pl.when(has_above)
        def _():
            down.wait_recv()
            up.wait_send()

        @pl.when(jnp.logical_not(has_above))
        def _():
            above[...] = jnp.zeros((n, C), bf16)

        @pl.when(jnp.logical_not(has_below))
        def _():
            below[...] = jnp.zeros((n, C), bf16)

    m_x, q_x, sum_x = pl.run_scoped(
        front, pltpu.VMEM(S.a_hbm.shape, bf16), pltpu.VMEM(S.b_hbm.shape, bf16), pltpu.VMEM(S.c_hbm.shape, bf16)
    )
    inv_x = lax.rsqrt(q_x + norm_eps)
    small = S.small[...]
    row = lambda i: small[32 + i : 33 + i, :]
    mid_gain = lambda j: small[42 + j : 43 + j, :]
    mid_bias = lambda j: small[25 + j : 26 + j, :]
    m_l, v_l = local(lambda s: S.d_l[s, :], n)
    m_s, v_s = local(lambda s: S.d_s[s, :], n)
    ld_c.wait()

    def early():
        order(2 * C // 128, (2 * C + FF) // 128)

        def low(s, a):
            S.gy_low[s, :] = S.cot[s, :].astype(bf16)
            return a

        chunks(n, low)

    tot = share(
        1, jnp.concatenate([m_l, m_s, v_l, v_s], axis=0), merge_stats(2), early,
        lambda: order((2 * C + FF) // 128, (2 * C + 2 * FF) // 128),
    )
    m_l, m_s = tot[0:1], tot[1:2]
    inv_l, inv_s = lax.rsqrt(tot[2:3] / every + norm_eps), lax.rsqrt(tot[3:4] / every + norm_eps)

    def pair(s, a):
        hl = (S.d_l[s, :] - m_l) * inv_l
        hs = (S.d_s[s, :] - m_s) * inv_s
        S.d_l[s, :] = hl
        S.d_s[s, :] = hs
        t, d = gelu_both(hl * row(2) + row(3) + hs * row(4) + row(5))
        S.s_val[s, :] = d
        S.t_low[s, :] = t.astype(bf16)
        return a

    chunks(n, pair)
    S.p_val[...] = dot(S.t_low[...], S.tab[pl.ds(C, C), :])
    m_p = close(chunks(n, lambda s, a: a + fold(S.p_val[s, :]), zero)) * (1.0 / n)

    def proj(s, a):
        d = S.p_val[s, :] - m_p
        return a[0] + fold(d * d), a[1] + fold(d * (S.x[s, :] - m_x))

    v_p, cross = chunks(n, proj, (zero, zero))
    tot = share(2, jnp.concatenate([m_p, close(v_p), close(cross) + m_p * sum_x], axis=0), merge_stats(1))
    m_p, q_p, cov = tot[0:1], tot[1:2] / every, tot[2:3] / every
    inv_p = lax.rsqrt(q_p + norm_eps)
    slope = row(6) * inv_p
    m_f = m_x + row(7)
    q_f = jnp.maximum(q_x + 2 * slope * cov + slope * slope * q_p, 0.0)
    inv_f = lax.rsqrt(q_f + norm_eps)
    hats = inv_f * inv_p * (cov + slope * q_p)

    def ffn(s, a):
        ph = (S.p_val[s, :] - m_p) * inv_p
        S.p_val[s, :] = ph
        m = S.x[s, :] + (ph * row(6) + row(7))
        S.mid[s, :] = m
        S.c_low[s, :] = ((m - m_f) * (inv_f * row(8)) + row(9)).astype(bf16)
        g = S.cot[s, :]
        return a[0] + fold(g), a[1] + fold(g * ph)

    sum_c, sum_ch = chunks(n, ffn, (zero, zero))
    sum_c, sum_ch = close(sum_c), close(sum_ch)

    def middle(hid, gact, a_low, gh_low):
        for j in range(blocks):
            hid[j] = dot(S.c_low[...], S.tab[up_rows(j), :])
        st = [local(lambda s, j=j: hid[j, s, :], n) for j in range(blocks)]

        def back_first():
            for j in range(blocks):
                gact[j] = dot(S.gy_low[...], S.tab[down_rows(j), :], (1, 1))

        tot = share(3, jnp.concatenate([s[0] for s in st] + [s[1] for s in st], axis=0), merge_stats(blocks), back_first)
        m_h = tot[:blocks]
        inv_h = lax.rsqrt(tot[blocks:] / every + norm_eps)
        sums = []
        for j in range(blocks):
            mj, ij, gj, bj = m_h[j : j + 1], inv_h[j : j + 1], mid_gain(j), mid_bias(j)

            def hidden(s, a, j=j, mj=mj, ij=ij, gj=gj, bj=bj):
                hat = (hid[j, s, :] - mj) * ij
                hid[j, s, :] = hat
                v, d = gelu_both(hat * gj + bj)
                a_low[j, s, :] = v.astype(bf16)
                g = gact[j, s, :] * d
                gact[j, s, :] = g
                return a[0] + fold(g), a[1] + fold(g * hat)

            sums.append(tuple(close(v) for v in chunks(n, hidden, (zero, zero))))
        mid_rows = jnp.concatenate([s[0] for s in sums] + [s[1] for s in sums], axis=0)

        def down_grads():
            for j in range(blocks):
                for h in range(C // 256):
                    put(S.flat, 2 * C + FF + j * C + h * 256, dot(a_low[j, :, half_cols(h)], S.gy_low[...], (0, 0)))

        def outputs():
            S.out[...] = S.mid[...]
            for j in range(blocks):
                S.out[...] += dot(a_low[j], S.tab[down_rows(j), :])

        tot = share(4, mid_rows, merge_sum, down_grads, outputs) * (1.0 / every)
        out_copy.start()
        for j in range(blocks):
            tb_, tg_, sc = tot[j : j + 1], tot[blocks + j : blocks + j + 1], mid_gain(j) * inv_h[j : j + 1]

            def grad_h(s, a, j=j, tb_=tb_, tg_=tg_, sc=sc):
                gh_low[j, s, :] = (sc * (gact[j, s, :] - tb_ - hid[j, s, :] * tg_)).astype(bf16)
                return a

            chunks(n, grad_h)
        S.g_f[...] = dot(gh_low[0], S.tab[up_rows(0), :], (1, 1))
        for j in range(1, blocks):
            S.g_f[...] += dot(gh_low[j], S.tab[up_rows(j), :], (1, 1))

        def ffn_sums(s, a):
            g = S.g_f[s, :]
            hat = (S.mid[s, :] - m_f) * inv_f
            return a[0] + fold(g), a[1] + fold(g * hat), a[2] + fold(g * S.p_val[s, :])

        b_ffn, g_ffn, g_fp = (close(v) for v in chunks(n, ffn_sums, (zero, zero, zero)))

        def grad_up():
            for j in range(blocks):
                for h in range(C // 256):
                    put(S.flat, 2 * C + j * C + h * 256, dot(S.c_low[:, half_cols(h)], gh_low[j], (0, 0)))

        tot = share(5, jnp.concatenate([b_ffn, g_ffn, g_fp, sum_c, sum_ch], axis=0), merge_sum, grad_up) * (1.0 / every)
        return mid_rows, b_ffn, g_ffn, tot

    out_copy = pltpu.make_async_copy(S.out, S.out_hbm, S.load_sem.at[7])
    hidden_shape = (blocks, n, C)
    mid_rows, b_ffn, g_ffn, tot = pl.run_scoped(
        middle, pltpu.VMEM(hidden_shape, f32), pltpu.VMEM(hidden_shape, f32), pltpu.VMEM(hidden_shape, bf16), pltpu.VMEM(hidden_shape, bf16)
    )

    def back(tat, tbt, tct, acc):
        ld_ct, ld_at, ld_bt = load(3, S.ct_hbm, tct), load(4, S.at_hbm, tat), load(5, S.bt_hbm, tbt)
        for copy in (ld_ct, ld_at, ld_bt):
            copy.start()
        scale_f = row(8) * inv_f
        mean_hat = tot[4:5] + scale_f * (tot[2:3] - tot[1:2] * hats)

        def grad_mid(s, a):
            hat = (S.mid[s, :] - m_f) * inv_f
            g = S.cot[s, :] + scale_f * (S.g_f[s, :] - tot[0:1] - hat * tot[1:2])
            S.g_f[s, :] = g
            ph = S.p_val[s, :]
            S.gp_low[s, :] = (slope * (g - tot[3:4] - ph * mean_hat)).astype(bf16)
            return a[0] + fold(g), a[1] + fold(g * ph)

        b_proj, g_proj = (close(v) for v in chunks(n, grad_mid, (zero, zero)))
        S.p_val[...] = dot(S.gp_low[...], S.tab[pl.ds(C, C), :], (1, 1))

        def grad_s(s, a):
            g = S.p_val[s, :] * S.s_val[s, :]
            S.p_val[s, :] = g
            return a[0] + fold(g), a[1] + fold(g * S.d_l[s, :]), a[2] + fold(g * S.d_s[s, :])

        b_pair, g_lg, g_sg = (close(v) for v in chunks(n, grad_s, (zero, zero, zero)))

        def grad_out():
            for h in range(C // 256):
                put(S.flat, C + h * 256, dot(S.t_low[:, half_cols(h)], S.gp_low[...], (0, 0)))

        sums = share(6, jnp.concatenate([b_pair, g_lg, g_sg], axis=0), merge_sum, grad_out) * (1.0 / every)
        sc_l, sc_s = row(2) * inv_l, row(4) * inv_s
        gl_low, gs_low = S.t_low, S.gp_low

        def grad_pair(s, a):
            g = S.p_val[s, :] - sums[0:1]
            gl_low[s, :] = (sc_l * (g - S.d_l[s, :] * sums[1:2])).astype(bf16)
            gs_low[s, :] = (sc_s * (g - S.d_s[s, :] * sums[2:3])).astype(bf16)
            return a

        chunks(n, grad_pair)
        ld_ct.wait()

        @pl.loop(0, NF // 256)
        def _(t):
            re, im = pl.ds(pl.multiple_of(t * 256, 256), 256), pl.ds(pl.multiple_of(NF + t * 256, 256), 256)
            acc[0] = dot(tct[re, :], gl_low[...])
            acc[1] = dot(tct[im, :], gl_low[...])
            acc[2] = dot(tct[re, :], gs_low[...])
            acc[3] = dot(tct[im, :], gs_low[...])

            @pl.loop(0, 8)
            def _(i):
                s = pl.ds(pl.multiple_of(i * 32, 32), 32)
                re = pl.ds(pl.multiple_of(t * 256 + i * 32, 32), 32)
                im = pl.ds(pl.multiple_of(NF + t * 256 + i * 32, 32), 32)
                lr, li, sr, si = acc[0, s, :], acc[1, s, :], acc[2, s, :], acc[3, s, :]
                kr, ki = S.spec_l[re, :], S.spec_l[im, :]
                hr, hi = S.spec_s[re, :], S.spec_s[im, :]
                S.prod_k[re, :] = (lr * kr - li * ki + sr * hr - si * hi).astype(bf16)
                S.prod_k[im, :] = (lr * ki + li * kr + sr * hi + si * hr).astype(bf16)
                ur, ui = S.spec_u[re, :], S.spec_u[im, :]
                S.prod_l[re, :] = (lr * ur + li * ui).astype(bf16)
                S.prod_l[im, :] = (lr * ui - li * ur).astype(bf16)
                S.prod_s[re, :] = (sr * ur + si * ui).astype(bf16)
                S.prod_s[im, :] = (sr * ui - si * ur).astype(bf16)

        ld_at.wait()
        S.halo_out[0] = dot(tat[pl.ds(0, n), :], S.prod_k[...]).astype(bf16)
        S.halo_out[1] = dot(tat[pl.ds(2 * n, n), :], S.prod_k[...]).astype(bf16)
        halo_up = halo(2, S.halo_out.at[0], S.halo_in.at[1], True)
        halo_down = halo(3, S.halo_out.at[1], S.halo_in.at[0], False)
        halo_start(halo_up, halo_down)
        S.p_val[...] = dot(tat[pl.ds(n, n), :], S.prod_k[...])
        ld_bt.wait()

        @pl.loop(0, 4)
        def _(t):
            s = pl.ds(pl.multiple_of(t * 256, 256), 256)
            put(S.flat, 2 * C + 2 * FF + t * 256, dot(tbt[s, :], S.prod_l[...]))

        put(S.flat, BASE, dot(S.bst[...], S.prod_s[...]))
        halo_wait(halo_up, halo_down, S.halo_in.at[0], S.halo_in.at[1])
        gz_low = S.t_low

        def grad_z(s, a):
            g = S.p_val[s, :] + S.halo_in[0, s, :].astype(f32) + S.halo_in[1, s, :].astype(f32)
            gz_low[s, :] = (g * S.dz[s, :]).astype(bf16)
            return a

        chunks(n, grad_z)
        S.p_val[...] = dot(gz_low[...], S.tab[pl.ds(0, C), :], (1, 1))

        def pre_sums(s, a):
            g = S.p_val[s, :]
            return a[0] + fold(g), a[1] + fold(g * ((S.x[s, :] - m_x) * inv_x))

        b_pre, g_pre = (close(v) for v in chunks(n, pre_sums, (zero, zero)))
        share_send(7, 0, jnp.concatenate([b_pre, g_pre], axis=0))
        for h in range(C // 256):
            put(S.flat, h * 256, dot(S.pre_low[:, half_cols(h)], gz_low[...], (0, 0)))
        norms = [g_pre, b_pre, g_lg, b_pair, g_sg, b_pair, g_proj, b_proj, g_ffn, b_ffn]
        norms += [mid_rows[blocks + j : blocks + j + 1] for j in range(blocks)]
        put(S.flat, BASE + 32, jnp.concatenate(norms + [jnp.zeros((2, C), f32)], axis=0))
        for j in range(blocks):
            for k in range(4):
                S.flat[pl.ds((BASE + 25 + j) * 4 + k, 1), :] = mid_rows[j : j + 1, k * 128 : (k + 1) * 128]

    pl.run_scoped(
        back, pltpu.VMEM(S.at_hbm.shape, bf16), pltpu.VMEM(S.bt_hbm.shape, bf16), pltpu.VMEM(S.ct_hbm.shape, bf16), pltpu.VMEM((4, 256, C), f32)
    )


    plan = reduce_plan(nb)
    parts = len(plan)
    size = lines // parts
    unit = 96 if own % 96 == 0 else 8
    tmp = S.tmp
    hop_base = nz * nb
    z_base = hop_base + nz * (nb - 1)

    def tail(sib_out, pair, z_out):
        grad = S.flat.reshape(total, 4, 128)

        def column(i):
            return lax.rem(z + 1 + i, nz)

        def collect(m, zz, cc):
            start = (flip(b, m) * nr + 2 * zz + cc) * own

            @pl.loop(0, own // unit)
            def _(g):
                for u in range(unit):
                    tmp[pl.ds(pl.multiple_of((g * unit + u) * 4, 4), 4), :] = grad[S.idx[start + g * unit + u]]

        def to_sibling(i, m):
            return pltpu.make_async_remote_copy(
                sib_out.at[i, m], rows_in.at[i * nb + m], S.sib_send.at[i, m], S.sib_recv.at[i, m],
                device_id=sibling, device_id_type=MESH,
            )

        def rows_of(p):
            return pl.ds(p * size, size)

        def slots(p, t):
            at = sum(len(plan[p][k][2]) for k in range(t))
            return at, len(plan[p][t][2])

        def hop_at(i, p, at, count):
            return rows_in.at[pl.ds(hop_base + i * (nb - 1) + at, count), rows_of(p)]

        def hop(i, p, t, m):
            o, sent, kept = plan[p][t]
            at, _ = slots(p, t)
            landing = rows_in.at[hop_base + i * (nb - 1) + at + kept.index(m ^ (1 << o)), rows_of(p)]
            return pltpu.make_async_remote_copy(
                pair.at[i, m, rows_of(p)], landing, S.hop_send.at[i, p, t], S.hop_recv.at[i, p, t],
                device_id=(flip(b, 1 << o), r), device_id_type=MESH,
            )

        def hop_wait(i, p, t, sem):
            whole = hop_at(i, p, *slots(p, t))
            pltpu.make_async_copy(whole, whole, sem.at[i, p, t]).wait()

        def for_sibling(i):
            for m in range(nb):
                collect(m, column(i), 1 - c)
                sib_out[i, m] = tmp[...].astype(bf16)
                to_sibling(i, m).start()

        def to_owner(i):
            return pltpu.make_async_remote_copy(
                z_out.at[i], rows_in.at[z_base + i], S.own_send.at[i], S.own_recv.at[i],
                device_id=(b, 2 * column(i) + c), device_id_type=MESH,
            )

        def first_step(i):
            @pl.when(i < nz - 1)
            def _():
                for_sibling(i + 1)

            for m in reversed(range(nb)):
                collect(m, column(i), c)
                to_sibling(i, m).wait_recv()
                pair[i, m] = (tmp[...] + rows_in[i * nb + m].astype(f32)).astype(bf16)
                for p in range(parts):
                    if m in plan[p][0][1]:
                        hop(i, p, 0, m).start()

        def next_step(i, t):
            for p in range(parts):
                hop_wait(i, p, t, S.hop_recv)
                at, _ = slots(p, t)
                for k, m in enumerate(plan[p][t][2]):
                    pair[i, m, rows_of(p)] = (
                        pair[i, m, rows_of(p)].astype(f32)
                        + rows_in[hop_base + i * (nb - 1) + at + k, rows_of(p)].astype(f32)
                    ).astype(bf16)
                    if m in plan[p][t + 1][1]:
                        hop(i, p, t + 1, m).start()

        def last_step(i):
            for p in range(parts):
                hop_wait(i, p, parts - 1, S.hop_recv)
                at, _ = slots(p, parts - 1)
                tmp[rows_of(p), :] = pair[i, 0, rows_of(p)].astype(f32) + rows_in[hop_base + i * (nb - 1) + at, rows_of(p)].astype(f32)

            @pl.when(i < nz - 1)
            def _():
                z_out[i] = tmp[...].astype(bf16)
                to_owner(i).start()

        def grad_image():
            sums = share_wait(7, 1, merge_sum) * (1.0 / every)
            scale_x = row(0) * inv_x

            def last(s, a):
                hat = (S.x[s, :] - m_x) * inv_x
                S.g_f[s, :] = S.g_f[s, :] + scale_x * (S.p_val[s, :] - sums[0:1] - hat * sums[1:2])
                return a

            chunks(n, last)
            gin_copy.start()
            for i in range(own):
                p = S.idx[(b * nr + r) * own + i]
                fast = (p >= 2 * C + 2 * FF + KL * KL) & ((p < BASE) | (p >= BASE + KS * KS))
                S.rate[pl.ds(i, 1), :] = jnp.full((1, 128), jnp.where(fast, np.float32(norm_rate), np.float32(matrix_rate)), f32)

        gin_copy = pltpu.make_async_copy(S.g_f, S.gin_hbm, S.load_sem.at[6])
        for_sibling(0)

        @pl.loop(0, nz + parts)
        def _(q):
            @pl.when(q < nz)
            def _():
                first_step(q)

            @pl.when(q == 0)
            def _():
                share_send(7, 1, share_wait(7, 0, merge_sum))

            for t in range(parts - 1):

                @pl.when((q >= t + 1) & (q < nz + t + 1))
                def _():
                    next_step(q - t - 1, t)

            @pl.when(q == 1)
            def _():
                grad_image()

            @pl.when(q >= parts)
            def _():
                last_step(q - parts)

        for i in range(nz - 1):
            to_owner(i).wait_recv()
            tmp[...] += rows_in[z_base + i].astype(f32)
        for j in range(4):
            S.red[:, j * 128 : (j + 1) * 128] = tmp[pl.ds(j, own, stride=4), :]

        @pl.loop(0, nz)
        def _(i):
            for m in range(nb):
                to_sibling(i, m).wait_send()
            for p in range(parts):
                for t in range(parts):
                    hop_wait(i, p, t, S.hop_send)

        for i in range(nz - 1):
            to_owner(i).wait_send()
        gin_copy.wait()

    low_block = lambda *lead: pltpu.VMEM(lead + (lines, 128), bf16)
    pl.run_scoped(tail, low_block(nz, nb), low_block(nz, nb), low_block(nz))
    for e in range(len(WIDTHS)):
        for stage in range(2):
            buf, mine, count, peers = share_stage(e, stage)
            sent = buf.at[pl.ds(0, count - 1)]
            pltpu.make_async_copy(sent, sent, S.stat_send.at[e, stage]).wait()
    out_copy.wait()


def step(x, cot, master, places, nb, nr):
    (a, at, b, bt, bs, bst, c, ct) = tables()
    n, own, nz, parts = x.shape[0], master.shape[0], nr // 2, nb.bit_length() - 1
    total = places.shape[0]
    vm = lambda *shape: pltpu.VMEM(shape, f32)
    low = lambda *shape: pltpu.VMEM(shape, bf16)
    dma = lambda *shape: pltpu.SemaphoreType.DMA(shape)
    vmem, anywhere = pl.BlockSpec(memory_space=pltpu.VMEM), pl.BlockSpec(memory_space=pl.ANY)
    ins = dict(
        idx=(places, pl.BlockSpec(memory_space=pltpu.SMEM)), x_hbm=(x, anywhere), cot_hbm=(cot, anywhere), master_hbm=(master, anywhere),
        a_hbm=(a, anywhere), at_hbm=(at, anywhere), b_hbm=(b, anywhere), bt_hbm=(bt, anywhere), bs=(bs, vmem), bst=(bst, vmem),
        c_hbm=(c, anywhere), ct_hbm=(ct, anywhere),
    )
    image = jax.ShapeDtypeStruct((n, C), f32)
    outs = dict(
        out_hbm=(image, anywhere), gin_hbm=(image, anywhere), red=(jax.ShapeDtypeStruct((own, C), f32), vmem),
        rate=(jax.ShapeDtypeStruct((own, 128), f32), vmem),
    )
    scratch = dict(
        rows_in=low(nb * nr, 4 * own, 128), flat=vm(4 * total, 128), tab=low(total, C), x=vm(n, C), cot=vm(n, C), master=vm(own, C),
        tmp=vm(4 * own, 128), chunk=vm(512, 128), inv=pltpu.VMEM((total // 128, 128), jnp.int32),
        inv_at=pltpu.SMEM((total // 128, 128), jnp.int32), small=vm(48, C),
        pre_low=low(n, C), wide=low(3 * n, C), dz=vm(n, C), spec_u=vm(2 * NF, C), spec_l=vm(2 * NF, C), spec_s=vm(2 * NF, C),
        prod_l=low(2 * NF, C), prod_s=low(2 * NF, C), prod_k=low(2 * NF, C), d_l=vm(n, C), d_s=vm(n, C), s_val=vm(n, C),
        t_low=low(n, C), p_val=vm(n, C), mid=vm(n, C), c_low=low(n, C), gy_low=low(n, C), gp_low=low(n, C), g_f=vm(n, C), out=vm(n, C),
        halo_out=low(2, n, C), halo_in=low(2, n, C),
    )
    for e, w in enumerate(WIDTHS):
        scratch[f"one{e}"] = vm(nr, w, C)
        scratch[f"two{e}"] = vm(nb, w, C)
    scratch.update(
        load_sem=dma(8), stat_send=dma(len(WIDTHS), 2), stat_recv=dma(len(WIDTHS), 2), halo_send=dma(4), halo_recv=dma(4),
        z_send=dma(nz), z_recv=dma(nz), b_send=dma(nb, nz), b_recv=dma(nb, nz), half_send=dma(2, nz), half_recv=dma(2, nz),
        core_send=dma(nb, nz), core_recv=dma(nb, nz), sib_send=dma(nz, nb), sib_recv=dma(nz, nb),
        hop_send=dma(nz, parts, parts), hop_recv=dma(nz, parts, parts), own_send=dma(nz), own_recv=dma(nz),
    )
    return pl.pallas_call(
        functools.partial(step_kernel, nb, nr, [*ins, *outs, *scratch]),
        out_shape=[v[0] for v in outs.values()],
        in_specs=[v[1] for v in ins.values()],
        out_specs=[v[1] for v in outs.values()],
        scratch_shapes=list(scratch.values()),
        compiler_params=pltpu.CompilerParams(collective_id=0, has_side_effects=True, vmem_limit_bytes=62 * 2**20),
    )(*[v[0] for v in ins.values()])


def finish_kernel(*refs):
    ins, outs, bufs, (load_sem, store_sem) = refs[:7], refs[7:14], refs[14:25], refs[25:]
    red, rate, first_ref, second_ref, master_ref, out, gin = bufs[:7]
    new_first, new_second, new_master, new_copy = bufs[7:11]
    loads = [pltpu.make_async_copy(src, dst, load_sem.at[i]) for i, (src, dst) in enumerate(zip(ins, bufs[:7]))]
    for copy in loads:
        copy.start()
    own = red.shape[0]
    size = 64 if own % 64 == 0 else own
    for copy in loads[:5]:
        copy.wait()
    stores = [pltpu.make_async_copy(red, outs[2], store_sem.at[2, 0])]
    stores[0].start()
    for part in range(own // size):
        for k in range(0, size, 8):
            s = slice(part * size + k, part * size + k + 8)
            for j in range(C // 128):
                at = (s, slice(j * 128, (j + 1) * 128))
                g = red[at]
                first = beta_one * first_ref[at] + (1.0 - beta_one) * g
                second = beta_two * second_ref[at] + (1.0 - beta_two) * g * g
                new_first[at] = first
                new_second[at] = second
                first_hat = first / (1.0 - beta_one**STEP)
                second_hat = second / (1.0 - beta_two**STEP)
                master = master_ref[at]
                new_master[at] = master - rate[s, :] * (first_hat / (jnp.sqrt(second_hat) + adam_eps) + decay_rate * master)
        s = pl.ds(part * size, size)
        new_copy[s, :] = new_master[s, :].astype(bf16)
        if part == 0:
            for i in (5, 6):
                loads[i].wait()
                stores.append(pltpu.make_async_copy(bufs[i], outs[i - 5], store_sem.at[i - 5, 0]))
                stores[-1].start()
        for i, buf in enumerate((new_first, new_second, new_master, new_copy)):
            stores.append(pltpu.make_async_copy(buf.at[s], outs[3 + i].at[s], store_sem.at[3 + i, part]))
            stores[-1].start()
    for copy in stores:
        copy.wait()


def finish(reduced, first, second, master, rates, out, gin):
    anywhere = pl.BlockSpec(memory_space=pl.ANY)
    slot = jax.ShapeDtypeStruct(reduced.shape, f32)
    image = jax.ShapeDtypeStruct(out.shape, f32)
    low = jax.ShapeDtypeStruct(reduced.shape, bf16)
    ins = (reduced, rates, first, second, master, out, gin)
    outs = [image, image, slot, slot, slot, slot, low]
    return pl.pallas_call(
        finish_kernel,
        out_shape=outs,
        in_specs=[anywhere] * 7,
        out_specs=[anywhere] * 7,
        scratch_shapes=[pltpu.VMEM(v.shape, f32) for v in ins]
        + [pltpu.VMEM(v.shape, v.dtype) for v in (slot, slot, slot, low)]
        + [pltpu.SemaphoreType.DMA((7,)), pltpu.SemaphoreType.DMA((7, 4))],
        compiler_params=pltpu.CompilerParams(vmem_limit_bytes=62 * 2**20),
    )(*ins)


def table_place(t):
    start = 2 * C + 2 * FF
    k_end = start + KL * KL
    s_end = k_end + KS * KS
    m_gain = s_end + 10
    m_bias = m_gain + FF // C
    m_end = m_bias + FF // C
    up = t - 2 * C
    up = 2 * C + up % (FF // C) * C + up // (FF // C)
    base = start + 976
    unused = t - m_end
    unused = jnp.where(unused < 15, k_end + unused, jnp.where(unused < 18, base + 29 + unused - 15, base + 46 + unused - 18))
    p = jnp.where((t >= 2 * C) & (t < 2 * C + FF), up, t)
    p = jnp.where(t >= k_end, t - k_end + base, p)
    p = jnp.where(t >= s_end, t - s_end + base + 32, p)
    p = jnp.where(t >= m_bias, t - m_bias + base + 25, p)
    return jnp.where(t >= m_end, unused, p)


def body(image_in, cotangent, slot_rows, master, first_moment, second_moment):
    n = image_in.shape[0] * image_in.shape[1] * image_in.shape[2]
    nb, nr = lax.axis_size("batch"), lax.axis_size("rows")
    out, grad_in, reduced, rates = step(
        image_in.reshape(n, C), cotangent.reshape(n, C), master, table_place(slot_rows), nb, nr
    )
    result, grad_x, *slots = finish(reduced, first_moment, second_moment, master, rates, out, grad_in)
    return (result.reshape(image_in.shape), grad_x.reshape(image_in.shape), *slots)


def solution(mesh):
    image = P("batch", "rows", None, None)
    owner = P(AXES, None)
    return jax.shard_map(
        body,
        mesh=mesh,
        in_specs=(image, image, P(), owner, owner, owner),
        out_specs=(image, image, owner, owner, owner, owner, owner),
        check_vma=False,
    )
```

```python
import functools
import types

import jax
import jax.numpy as jnp
import numpy as np
from jax import lax
from jax.experimental import pallas as pl
from jax.experimental.pallas import tpu as pltpu
from jax.sharding import PartitionSpec as P

C = 512
FF = 2048
KL = 31
KS = 5
STEP = 10

norm_eps = 1e-05
beta_one = 0.9
beta_two = 0.999
adam_eps = 1e-08
decay_rate = 0.05
matrix_rate = 0.05
norm_rate = 0.5

TH = 16
TW = 16
NY = 47
NX = 31
NF = 768
REACH = (KL - 1) // 2
AXES = ("batch", "rows")
f32 = jnp.float32
bf16 = jnp.bfloat16


@functools.lru_cache(None)
def tables():
    freqs = [(ky, 0) for ky in range((NY + 1) // 2)]
    freqs += [(ky, kx) for kx in range(1, (NX + 1) // 2) for ky in range(NY)]
    ky = np.array([f[0] for f in freqs], np.int64)[:, None]
    kx = np.array([f[1] for f in freqs], np.int64)[:, None]
    pad = NF - len(freqs)

    def angle(rows, cols):
        ty = (ky * rows.reshape(1, -1)) % NY
        tx = (kx * cols.reshape(1, -1)) % NX
        return 2 * np.pi * (ty / NY + tx / NX)

    def grid(rows, cols):
        r, c = np.meshgrid(rows, cols, indexing="ij")
        return r.reshape(-1), c.reshape(-1)

    def stack(re, im):
        z = np.zeros((pad, re.shape[1]))
        return np.concatenate([re, z, im, z], axis=0)

    r, c = grid(np.arange(-TH, 2 * TH), np.arange(TW))
    used = ((r + REACH >= 0) & (r + REACH < NY - 1)).astype(np.float64)[None]
    t = angle(r + REACH, c)
    a = stack(np.cos(t) * used, -np.sin(t) * used)
    i, j = grid(np.arange(KL), np.arange(KL))
    t = angle(i, j - REACH)
    b = stack(np.cos(t), -np.sin(t))
    lead = REACH - (KS - 1) // 2
    small = ((i >= lead) & (i < lead + KS) & (j >= lead) & (j < lead + KS)).nonzero()[0]
    bs = np.pad(b[:, small], ((0, 0), (0, 32 - KS * KS)))
    b = np.pad(b, ((0, 0), (0, 2 * C - KL * KL)))
    y, x = grid(np.arange(TH), np.arange(TW))
    t = angle(y, x)
    w = np.full((len(freqs), 1), 2.0)
    w[0] = 1.0
    w /= NY * NX
    ct = stack(w * np.cos(t), -w * np.sin(t))
    return tuple(m.astype(np.float32).astype(bf16) for m in (a, a.T, b, b.T, bs, bs.T, ct.T, ct))


def dot(a, b, dims=(1, 0)):
    return lax.dot_general(a, b, (((dims[0],), (dims[1],)), ((), ())), preferred_element_type=f32)


MESH = pl.DeviceIdType.MESH
WIDTHS = (2, 4, 3, 8, 8, 5, 3, 2)
BY_CHIP = (1, 2, 5, 6)
BASE = 2 * C + 2 * FF + 976


def chunks(n, fn, init=()):
    return lax.fori_loop(0, n // 32, lambda i, c: fn(pl.ds(pl.multiple_of(i * 32, 32), 32), c), init)


def fold(v):
    return jnp.sum(v.reshape(v.shape[0] // 8, 8, v.shape[1]), axis=0)


def close(v):
    return jnp.sum(v, axis=0, keepdims=True)


def put(ref, start, v):
    for j in range(4):
        ref[pl.ds(start * 4 + j, v.shape[0], stride=4), :] = v[:, j * 128 : (j + 1) * 128]


def gelu_both(v):
    a = np.float32(np.sqrt(2 / np.pi))
    sq = v * v
    t = jnp.tanh(a * (v + 0.044715 * (sq * v)))
    half = 0.5 * (1 + t)
    return v * half, half + 0.5 * v * (1 - t * t) * (a * (1 + 3 * 0.044715 * sq))


def flip(b, m):
    k = 0
    while m >> k:
        if (m >> k) & 1:
            b = b + (1 - 2 * lax.rem(b // 2**k, 2)) * 2**k
        k += 1
    return b


def reduce_plan(nb):
    bits = nb.bit_length() - 1
    plan = []
    for p in range(bits):
        order = [(p + t) % bits for t in range(bits)]
        steps, kept = [], list(range(nb))
        for o in order:
            sent = [m for m in kept if (m >> o) & 1]
            kept = [m for m in kept if not (m >> o) & 1]
            steps.append((o, sent, kept))
        plan.append(steps)
    return plan


def by_chip(e, chips):
    return e in BY_CHIP and chips <= 32


def merge_sum(v, count):
    return jnp.sum(v, axis=0)


def merge_stats(h):
    def merge(v, count):
        means = v[:, :h]
        m = jnp.sum(means, axis=0) * (1.0 / v.shape[0])
        d = means - m
        parts = [m, jnp.sum(v[:, h : 2 * h], axis=0) + count * jnp.sum(d * d, axis=0)]
        if v.shape[1] > 2 * h:
            parts.append(jnp.sum(v[:, 2 * h :], axis=0))
        return jnp.concatenate(parts, axis=0)

    return merge


def local(read, n):
    zero = jnp.zeros((8, C), f32)
    m = close(chunks(n, lambda s, c: c + fold(read(s)), zero)) * (1.0 / n)

    def sq(s, c):
        d = read(s) - m
        return c + fold(d * d)

    return m, close(chunks(n, sq, zero))


def half_cols(h):
    return pl.ds(pl.multiple_of(h * 256, 256), 256)


def up_rows(j):
    return pl.ds(pl.multiple_of(2 * C + j * C, C), C)


def down_rows(j):
    return pl.ds(pl.multiple_of(2 * C + FF + j * C, C), C)


def table_place(t):
    start = 2 * C + 2 * FF
    k_end = start + KL * KL
    s_end = k_end + KS * KS
    m_gain = s_end + 10
    m_bias = m_gain + FF // C
    m_end = m_bias + FF // C
    up = t - 2 * C
    up = 2 * C + (up & (FF // C - 1)) * C + (up >> ((FF // C).bit_length() - 1))
    base = start + 976
    unused = t - m_end
    unused = jnp.where(unused < 15, k_end + unused, jnp.where(unused < 18, base + 29 + unused - 15, base + 46 + unused - 18))
    p = jnp.where((t >= 2 * C) & (t < 2 * C + FF), up, t)
    p = jnp.where(t >= k_end, t - k_end + base, p)
    p = jnp.where(t >= s_end, t - s_end + base + 32, p)
    p = jnp.where(t >= m_bias, t - m_bias + base + 25, p)
    return jnp.where(t >= m_end, unused, p)


def step_kernel(nb, nr, names, *refs):
    S = types.SimpleNamespace(**dict(zip(names, refs)))
    nz = nr // 2
    nd = nb * nr
    n = S.x.shape[0]
    own = S.master.shape[0]
    lines = 4 * own
    total = S.tab.shape[0]
    every = float(n * nd)
    b = lax.axis_index("batch")
    r = lax.axis_index("rows")
    z, c = r // 2, lax.rem(r, 2)
    sibling = (b, r + 1 - 2 * c)
    square = nb == 4
    blocks = FF // C
    zero = jnp.zeros((8, C), f32)
    rows_in = S.rows_in

    def load(i, src, dst):
        return pltpu.make_async_copy(src, dst, S.load_sem.at[i])

    ld_m, ld_x, ld_c = load(0, S.master_hbm, S.master), load(1, S.x_hbm, S.x), load(2, S.cot_hbm, S.cot)
    ld_s = load(8, S.slots_hbm, S.at_v)
    for copy in (ld_s, ld_m, ld_x, ld_c):
        copy.start()
    barrier = pltpu.get_barrier_semaphore()
    for k in range(1, nr):
        pl.semaphore_signal(barrier, inc=1, device_id=(b, lax.rem(r + k, nr)), device_id_type=MESH)
    for m in range(1, nb):
        pl.semaphore_signal(barrier, inc=1, device_id=(flip(b, m), r), device_id_type=MESH)

    @pl.loop(0, (nb - 1) * (nz - 1))
    def _(k):
        at = (lax.rem(b + 1 + k // (nz - 1), nb), 2 * lax.rem(z + 1 + lax.rem(k, nz - 1), nz) + c)
        pl.semaphore_signal(barrier, inc=1, device_id=at, device_id_type=MESH)


    def share_stage(e, stage):
        buf = getattr(S, ("one" if stage == 0 else "two") + str(e))
        if by_chip(e, nb * nz):
            return (buf, c, 2) if stage == 0 else (buf, b * nz + z, nb * nz)
        return (buf, r, nr) if stage == 0 else (buf, b, nb)

    def share_peer(e, stage, k):
        if by_chip(e, nb * nz):
            if stage == 0:
                return sibling
            other = lax.rem(b * nz + z + k, nb * nz)
            return (other // nz, 2 * lax.rem(other, nz) + c)
        return (b, lax.rem(r + k, nr)) if stage == 0 else (lax.rem(b + k, nb), r)

    def share_send(e, stage, v):
        buf, mine, size = share_stage(e, stage)
        buf[mine] = v

        def one(k):
            pltpu.make_async_remote_copy(
                buf.at[mine], buf.at[mine], S.stat_send.at[e, stage], S.stat_recv.at[e, stage],
                device_id=share_peer(e, stage, k), device_id_type=MESH,
            ).start()

        if size > 8:
            pl.loop(1, size)(one)
        else:
            for k in range(1, size):
                one(k)

    def share_wait(e, stage, merge):
        buf, mine, size = share_stage(e, stage)
        got = buf.at[pl.ds(0, size - 1)]
        pltpu.make_async_copy(got, got, S.stat_recv.at[e, stage]).wait()
        return merge(buf[...], float(n if stage == 0 else n * getattr(S, f"one{e}").shape[0]))

    def share(e, v, merge, work=None, more=None):
        share_send(e, 0, v)
        if work and not by_chip(e, nb * nz):
            work()
        v = share_wait(e, 0, merge)
        share_send(e, 1, v)
        if work and by_chip(e, nb * nz):
            work()
        if more:
            more()
        return share_wait(e, 1, merge)


    def place(m, zz, core):
        return flip(b, m) * nr + 2 * zz + core

    def along_z(zz, up):
        at = rows_in.at[place(0, zz, c)]
        return pltpu.make_async_remote_copy(
            at, at, S.z_send.at[zz], S.z_recv.at[zz], device_id=(b, r + 2 if up else r - 2), device_id_type=MESH
        )

    def to_peer(m, zz):
        at = rows_in.at[place(0, zz, c)]
        return pltpu.make_async_remote_copy(
            at, at, S.b_send.at[m, zz], S.b_recv.at[m, zz], device_id=(flip(b, m), r), device_id_type=MESH
        )

    def from_peer(m, zz):
        at = rows_in.at[place(m, zz, c)]
        return pltpu.make_async_copy(at, at, S.b_recv.at[m, zz])

    def half(m, zz, h, to):
        at = rows_in.at[place(m, zz, c), pl.ds(h * (lines // 2), lines // 2)]
        return pltpu.make_async_remote_copy(
            at, at, S.half_send.at[h, zz], S.half_recv.at[h, zz], device_id=(flip(b, to), r), device_id_type=MESH
        )

    def to_other_core(m, zz, core):
        at = rows_in.at[place(m, zz, core)]
        return pltpu.make_async_remote_copy(
            at, at, S.core_send.at[m, zz], S.core_recv.at[m, zz], device_id=sibling, device_id_type=MESH
        )

    def cast(m, zz, core):
        d = place(m, zz, core)
        S.flat[pl.ds(pl.multiple_of(d * lines, lines), lines), :] = rows_in[d].astype(f32)

    def sends(zz):
        for m in range(1, nb):
            if not (square and m == 3):
                to_peer(m, zz).start()
        to_other_core(0, zz, c).start()
        cast(0, zz, c)

    def own_column(k):
        if k == 0:

            @pl.when(z < nz - 1)
            def _():
                along_z(z, True).start()

            @pl.when(z > 0)
            def _():
                along_z(z, False).start()

            sends(z)
            return

        @pl.when(z >= k)
        def _():
            along_z(z - k, True).wait_recv()

            @pl.when(z < nz - 1)
            def _():
                along_z(z - k, True).start()

            sends(z - k)

        @pl.when(z + k < nz)
        def _():
            along_z(z + k, False).wait_recv()

            @pl.when(z > 0)
            def _():
                along_z(z + k, False).start()

            sends(z + k)

    def each(k, fn):
        if k == 0:
            fn(z)
            return

        @pl.when(z >= k)
        def _():
            fn(z - k)

        @pl.when(z + k < nz)
        def _():
            fn(z + k)

    def pass_on(zz):
        for m in range(1, nb):
            if square and m == 3:
                continue
            from_peer(m, zz).wait()
            if square:
                half(m, zz, 2 - m, 3 - m).start()
            to_other_core(m, zz, c).start()
            cast(m, zz, c)

    def corner(zz):
        if square:
            for h in range(2):
                half(3, zz, h, 0).wait_recv()
            to_other_core(3, zz, c).start()
            cast(3, zz, c)

    def other_core(zz):
        for m in range(nb):
            to_other_core(m, zz, 1 - c).wait_recv()
            cast(m, zz, 1 - c)

    def find(part, parts):
        tiles = total // 1024
        unit = 16
        spots = [
            lax.broadcasted_iota(jnp.int32, (8, 128), 0) * 128 + lax.broadcasted_iota(jnp.int32, (8, 128), 1) + 1024 * k
            for k in range(tiles)
        ]

        def some(g, acc):
            for u in range(unit):
                start = part * (total // parts) + g * unit
                s = start + u
                p = S.idx[start // 128, lax.rem(start, 128) + u]
                acc = [jnp.where(spot == p, s, a) for spot, a in zip(spots, acc)]
            return acc

        acc = [S.inv[k * 8 : k * 8 + 8, :] if part else jnp.zeros((8, 128), jnp.int32) for k in range(tiles)]
        acc = lax.fori_loop(0, total // parts // unit, some, acc)
        for k in range(tiles):
            S.inv[k * 8 : k * 8 + 8, :] = acc[k]

    def order(start, stop):
        flat = S.flat.reshape(total, 4, 128)

        @pl.loop(start, stop)
        def _(t):
            for u in range(128):
                S.chunk[4 * u : 4 * u + 4, :] = flat[S.inv_at[t, u]]

            rows = pl.ds(pl.multiple_of(t * 128, 128), 128)
            for j in range(4):
                S.tab[rows, j * 128 : (j + 1) * 128] = S.chunk[pl.ds(j, 128, stride=4), :].astype(bf16)

    def front(ta, tb, tc):
        ld_a, ld_b, ld_t = load(3, S.a_hbm, ta), load(4, S.b_hbm, tb), load(5, S.c_hbm, tc)
        for copy in (ld_b, ld_a, ld_t):
            copy.start()
        ld_s.wait()
        S.at_v[...] = table_place(S.at_v[...])
        to_scalar = pltpu.make_async_copy(S.at_v, S.idx, S.load_sem.at[8])
        to_scalar.start()
        ld_m.wait()
        for j in range(4):
            S.tmp[pl.ds(j, own, stride=4), :] = S.master[:, j * 128 : (j + 1) * 128]
        rows_in[place(0, z, c)] = S.tmp[...].astype(bf16)
        pl.semaphore_wait(barrier, nr - 1 + nb - 1 + (nb - 1) * (nz - 1))
        own_column(0)
        to_scalar.wait()
        ld_x.wait()
        share_send(0, 0, jnp.concatenate(local(lambda s: S.x[s, :], n), axis=0))
        steps = max(nz - 1, 1)
        for k in range(1, nz):
            find(k - 1, steps)
            own_column(k)
            each(k - 1, pass_on)
            if k > 1:
                each(k - 2, corner)
            if k > 2:
                each(k - 3, other_core)
            if k == 1:
                share_send(0, 1, share_wait(0, 0, merge_stats(1)))
        if nz == 1:
            find(0, 1)
            share_send(0, 1, share_wait(0, 0, merge_stats(1)))
        to_scalar = pltpu.make_async_copy(S.inv, S.inv_at, S.load_sem.at[6])
        to_scalar.start()
        each(nz - 1, pass_on)
        if nz > 1:
            each(nz - 2, corner)
        each(nz - 1, corner)
        for k in range(max(nz - 3, 0), nz):
            each(k, other_core)
        tot = share_wait(0, 1, merge_stats(1))
        m_x, q_x = tot[0:1], tot[1:2] * (1.0 / every)
        inv_x = lax.rsqrt(q_x + norm_eps)
        to_scalar.wait()
        tiles = total // 128
        late = (2 * C + 2 * FF) // 128
        order(0, C // 128)
        order(tiles - 2, tiles)

        for m in range(nb):

            @pl.loop(0, nz)
            def _(zz):
                to_other_core(m, zz, c).wait_send()
                if m and not (square and m == 3):
                    to_peer(m, zz).wait_send()
                if square and m in (1, 2):
                    half(m, zz, 2 - m, 3 - m).wait_send()

        for k in range(nz):

            @pl.when((z >= k) & (z < nz - 1))
            def _():
                along_z(z - k, True).wait_send()

            @pl.when((z + k < nz) & (z > 0))
            def _():
                along_z(z + k, False).wait_send()

        small = S.tab[pl.ds(BASE, 48), :].astype(f32)
        S.small[...] = small
        row = lambda i: small[32 + i : 33 + i, :]

        def pre(s, sx):
            d = S.x[s, :] - m_x
            S.pre_low[s, :] = (d * (inv_x * row(0)) + row(1)).astype(bf16)
            return sx + fold(d)

        sum_x = close(chunks(n, pre, zero))
        S.dz[...] = dot(S.pre_low[...], S.tab[pl.ds(0, C), :])

        def act(s, a):
            u, d = gelu_both(S.dz[s, :])
            S.dz[s, :] = d
            S.wide[pl.ds(pl.multiple_of(n + s.start, 32), 32), :] = u.astype(bf16)
            return a

        chunks(n, act)
        mine = S.wide.at[pl.ds(n, n)]
        halo_up = halo(0, mine, S.wide.at[pl.ds(2 * n, n)], True)
        halo_down = halo(1, mine, S.wide.at[pl.ds(0, n)], False)
        halo_start(halo_up, halo_down)
        order(late, tiles - 2)
        order(C // 128, 2 * C // 128)

        ld_b.wait()

        @pl.loop(0, 2 * NF // 256)
        def _(t):
            s = pl.ds(pl.multiple_of(t * 256, 256), 256)
            S.spec_l[s, :] = dot(tb[s, :], S.tab[pl.ds(2 * C + 2 * FF, 2 * C), :])
            S.spec_s[s, :] = dot(S.bs[s, :], S.tab[pl.ds(BASE, 32), :])

        halo_wait(halo_up, halo_down, S.wide.at[pl.ds(0, n)], S.wide.at[pl.ds(2 * n, n)])
        ld_a.wait()

        @pl.loop(0, 2 * NF // 256)
        def _(t):
            s = pl.ds(pl.multiple_of(t * 256, 256), 256)
            S.spec_u[s, :] = dot(ta[s, :], S.wide[...])

        @pl.loop(0, NF // 32)
        def _(i):
            re, im = pl.ds(pl.multiple_of(i * 32, 32), 32), pl.ds(pl.multiple_of(NF + i * 32, 32), 32)
            ur, ui = S.spec_u[re, :], S.spec_u[im, :]
            for k, p in ((S.spec_l, S.prod_l), (S.spec_s, S.prod_s)):
                kr, ki = k[re, :], k[im, :]
                p[re, :] = (ur * kr + ui * ki).astype(bf16)
                p[im, :] = (ui * kr - ur * ki).astype(bf16)

        ld_t.wait()
        S.d_l[...] = dot(tc[...], S.prod_l[...])
        S.d_s[...] = dot(tc[...], S.prod_s[...])
        return m_x, q_x, sum_x


    has_above, has_below = r > 0, r < nr - 1

    def halo(i, src, dst, up):
        peer = lax.rem(r + nr - 1, nr) if up else lax.rem(r + 1, nr)
        return pltpu.make_async_remote_copy(
            src, dst, S.halo_send.at[i], S.halo_recv.at[i], device_id=(b, peer), device_id_type=MESH
        )

    def halo_start(up, down):
        @pl.when(has_above)
        def _():
            up.start()

        @pl.when(has_below)
        def _():
            down.start()

    def halo_wait(up, down, above, below):
        @pl.when(has_below)
        def _():
            up.wait_recv()
            down.wait_send()

        @pl.when(has_above)
        def _():
            down.wait_recv()
            up.wait_send()

        @pl.when(jnp.logical_not(has_above))
        def _():
            above[...] = jnp.zeros((n, C), bf16)

        @pl.when(jnp.logical_not(has_below))
        def _():
            below[...] = jnp.zeros((n, C), bf16)

    m_x, q_x, sum_x = pl.run_scoped(
        front, pltpu.VMEM(S.a_hbm.shape, bf16), pltpu.VMEM(S.b_hbm.shape, bf16), pltpu.VMEM(S.c_hbm.shape, bf16)
    )
    inv_x = lax.rsqrt(q_x + norm_eps)
    small = S.small[...]
    row = lambda i: small[32 + i : 33 + i, :]
    mid_gain = lambda j: small[42 + j : 43 + j, :]
    mid_bias = lambda j: small[25 + j : 26 + j, :]
    m_l, v_l = local(lambda s: S.d_l[s, :], n)
    m_s, v_s = local(lambda s: S.d_s[s, :], n)
    ld_c.wait()

    def early():
        order(2 * C // 128, (2 * C + FF) // 128)

        def low(s, a):
            S.gy_low[s, :] = S.cot[s, :].astype(bf16)
            return a

        chunks(n, low)

    tot = share(
        1, jnp.concatenate([m_l, m_s, v_l, v_s], axis=0), merge_stats(2), early,
        lambda: order((2 * C + FF) // 128, (2 * C + 2 * FF) // 128),
    )
    m_l, m_s = tot[0:1], tot[1:2]
    inv_l, inv_s = lax.rsqrt(tot[2:3] / every + norm_eps), lax.rsqrt(tot[3:4] / every + norm_eps)

    def pair(s, a):
        hl = (S.d_l[s, :] - m_l) * inv_l
        hs = (S.d_s[s, :] - m_s) * inv_s
        S.d_l[s, :] = hl
        S.d_s[s, :] = hs
        t, d = gelu_both(hl * row(2) + row(3) + hs * row(4) + row(5))
        S.s_val[s, :] = d
        S.t_low[s, :] = t.astype(bf16)
        return a

    chunks(n, pair)
    S.p_val[...] = dot(S.t_low[...], S.tab[pl.ds(C, C), :])
    m_p = close(chunks(n, lambda s, a: a + fold(S.p_val[s, :]), zero)) * (1.0 / n)

    def proj(s, a):
        d = S.p_val[s, :] - m_p
        return a[0] + fold(d * d), a[1] + fold(d * (S.x[s, :] - m_x))

    v_p, cross = chunks(n, proj, (zero, zero))
    tot = share(2, jnp.concatenate([m_p, close(v_p), close(cross) + m_p * sum_x], axis=0), merge_stats(1))
    m_p, q_p, cov = tot[0:1], tot[1:2] / every, tot[2:3] / every
    inv_p = lax.rsqrt(q_p + norm_eps)
    slope = row(6) * inv_p
    m_f = m_x + row(7)
    q_f = jnp.maximum(q_x + 2 * slope * cov + slope * slope * q_p, 0.0)
    inv_f = lax.rsqrt(q_f + norm_eps)
    hats = inv_f * inv_p * (cov + slope * q_p)

    def ffn(s, a):
        ph = (S.p_val[s, :] - m_p) * inv_p
        S.p_val[s, :] = ph
        m = S.x[s, :] + (ph * row(6) + row(7))
        S.mid[s, :] = m
        S.c_low[s, :] = ((m - m_f) * (inv_f * row(8)) + row(9)).astype(bf16)
        g = S.cot[s, :]
        return a[0] + fold(g), a[1] + fold(g * ph)

    sum_c, sum_ch = chunks(n, ffn, (zero, zero))
    sum_c, sum_ch = close(sum_c), close(sum_ch)

    def middle(hid, gact, a_low, gh_low):
        for j in range(blocks):
            hid[j] = dot(S.c_low[...], S.tab[up_rows(j), :])
        st = [local(lambda s, j=j: hid[j, s, :], n) for j in range(blocks)]

        def back_first():
            for j in range(blocks):
                gact[j] = dot(S.gy_low[...], S.tab[down_rows(j), :], (1, 1))

        tot = share(3, jnp.concatenate([s[0] for s in st] + [s[1] for s in st], axis=0), merge_stats(blocks), back_first)
        m_h = tot[:blocks]
        inv_h = lax.rsqrt(tot[blocks:] / every + norm_eps)
        sums = []
        for j in range(blocks):
            mj, ij, gj, bj = m_h[j : j + 1], inv_h[j : j + 1], mid_gain(j), mid_bias(j)

            def hidden(s, a, j=j, mj=mj, ij=ij, gj=gj, bj=bj):
                hat = (hid[j, s, :] - mj) * ij
                hid[j, s, :] = hat
                v, d = gelu_both(hat * gj + bj)
                a_low[j, s, :] = v.astype(bf16)
                g = gact[j, s, :] * d
                gact[j, s, :] = g
                return a[0] + fold(g), a[1] + fold(g * hat)

            sums.append(tuple(close(v) for v in chunks(n, hidden, (zero, zero))))
        mid_rows = jnp.concatenate([s[0] for s in sums] + [s[1] for s in sums], axis=0)

        def down_grads():
            for j in range(blocks):
                for h in range(C // 256):
                    put(S.flat, 2 * C + FF + j * C + h * 256, dot(a_low[j, :, half_cols(h)], S.gy_low[...], (0, 0)))

        def outputs():
            S.out[...] = S.mid[...]
            for j in range(blocks):
                S.out[...] += dot(a_low[j], S.tab[down_rows(j), :])

        tot = share(4, mid_rows, merge_sum, down_grads, outputs) * (1.0 / every)
        out_copy.start()
        for j in range(blocks):
            tb_, tg_, sc = tot[j : j + 1], tot[blocks + j : blocks + j + 1], mid_gain(j) * inv_h[j : j + 1]

            def grad_h(s, a, j=j, tb_=tb_, tg_=tg_, sc=sc):
                gh_low[j, s, :] = (sc * (gact[j, s, :] - tb_ - hid[j, s, :] * tg_)).astype(bf16)
                return a

            chunks(n, grad_h)
        S.g_f[...] = dot(gh_low[0], S.tab[up_rows(0), :], (1, 1))
        for j in range(1, blocks):
            S.g_f[...] += dot(gh_low[j], S.tab[up_rows(j), :], (1, 1))

        def ffn_sums(s, a):
            g = S.g_f[s, :]
            hat = (S.mid[s, :] - m_f) * inv_f
            return a[0] + fold(g), a[1] + fold(g * hat), a[2] + fold(g * S.p_val[s, :])

        b_ffn, g_ffn, g_fp = (close(v) for v in chunks(n, ffn_sums, (zero, zero, zero)))

        def grad_up():
            for j in range(blocks):
                for h in range(C // 256):
                    put(S.flat, 2 * C + j * C + h * 256, dot(S.c_low[:, half_cols(h)], gh_low[j], (0, 0)))

        tot = share(5, jnp.concatenate([b_ffn, g_ffn, g_fp, sum_c, sum_ch], axis=0), merge_sum, grad_up) * (1.0 / every)
        return mid_rows, b_ffn, g_ffn, tot

    out_copy = pltpu.make_async_copy(S.out, S.out_hbm, S.load_sem.at[7])
    hidden_shape = (blocks, n, C)
    mid_rows, b_ffn, g_ffn, tot = pl.run_scoped(
        middle, pltpu.VMEM(hidden_shape, f32), pltpu.VMEM(hidden_shape, f32), pltpu.VMEM(hidden_shape, bf16), pltpu.VMEM(hidden_shape, bf16)
    )

    def back(tat, tbt, tct, acc):
        ld_ct, ld_at, ld_bt = load(3, S.ct_hbm, tct), load(4, S.at_hbm, tat), load(5, S.bt_hbm, tbt)
        for copy in (ld_ct, ld_at, ld_bt):
            copy.start()
        scale_f = row(8) * inv_f
        mean_hat = tot[4:5] + scale_f * (tot[2:3] - tot[1:2] * hats)

        def grad_mid(s, a):
            hat = (S.mid[s, :] - m_f) * inv_f
            g = S.cot[s, :] + scale_f * (S.g_f[s, :] - tot[0:1] - hat * tot[1:2])
            S.g_f[s, :] = g
            ph = S.p_val[s, :]
            S.gp_low[s, :] = (slope * (g - tot[3:4] - ph * mean_hat)).astype(bf16)
            return a[0] + fold(g), a[1] + fold(g * ph)

        b_proj, g_proj = (close(v) for v in chunks(n, grad_mid, (zero, zero)))
        S.p_val[...] = dot(S.gp_low[...], S.tab[pl.ds(C, C), :], (1, 1))

        def grad_s(s, a):
            g = S.p_val[s, :] * S.s_val[s, :]
            S.p_val[s, :] = g
            return a[0] + fold(g), a[1] + fold(g * S.d_l[s, :]), a[2] + fold(g * S.d_s[s, :])

        b_pair, g_lg, g_sg = (close(v) for v in chunks(n, grad_s, (zero, zero, zero)))

        def grad_out():
            for h in range(C // 256):
                put(S.flat, C + h * 256, dot(S.t_low[:, half_cols(h)], S.gp_low[...], (0, 0)))

        sums = share(6, jnp.concatenate([b_pair, g_lg, g_sg], axis=0), merge_sum, grad_out) * (1.0 / every)
        sc_l, sc_s = row(2) * inv_l, row(4) * inv_s
        gl_low, gs_low = S.t_low, S.gp_low

        def grad_pair(s, a):
            g = S.p_val[s, :] - sums[0:1]
            gl_low[s, :] = (sc_l * (g - S.d_l[s, :] * sums[1:2])).astype(bf16)
            gs_low[s, :] = (sc_s * (g - S.d_s[s, :] * sums[2:3])).astype(bf16)
            return a

        chunks(n, grad_pair)
        ld_ct.wait()

        @pl.loop(0, NF // 256)
        def _(t):
            re, im = pl.ds(pl.multiple_of(t * 256, 256), 256), pl.ds(pl.multiple_of(NF + t * 256, 256), 256)
            acc[0] = dot(tct[re, :], gl_low[...])
            acc[1] = dot(tct[im, :], gl_low[...])
            acc[2] = dot(tct[re, :], gs_low[...])
            acc[3] = dot(tct[im, :], gs_low[...])

            @pl.loop(0, 8)
            def _(i):
                s = pl.ds(pl.multiple_of(i * 32, 32), 32)
                re = pl.ds(pl.multiple_of(t * 256 + i * 32, 32), 32)
                im = pl.ds(pl.multiple_of(NF + t * 256 + i * 32, 32), 32)
                lr, li, sr, si = acc[0, s, :], acc[1, s, :], acc[2, s, :], acc[3, s, :]
                kr, ki = S.spec_l[re, :], S.spec_l[im, :]
                hr, hi = S.spec_s[re, :], S.spec_s[im, :]
                S.prod_k[re, :] = (lr * kr - li * ki + sr * hr - si * hi).astype(bf16)
                S.prod_k[im, :] = (lr * ki + li * kr + sr * hi + si * hr).astype(bf16)
                ur, ui = S.spec_u[re, :], S.spec_u[im, :]
                S.prod_l[re, :] = (lr * ur + li * ui).astype(bf16)
                S.prod_l[im, :] = (lr * ui - li * ur).astype(bf16)
                S.prod_s[re, :] = (sr * ur + si * ui).astype(bf16)
                S.prod_s[im, :] = (sr * ui - si * ur).astype(bf16)

        ld_at.wait()
        halo_up = halo(2, S.halo_out.at[0], S.halo_in.at[1], True)
        halo_down = halo(3, S.halo_out.at[1], S.halo_in.at[0], False)
        S.halo_out[0] = dot(tat[pl.ds(0, n), :], S.prod_k[...]).astype(bf16)

        @pl.when(has_above)
        def _():
            halo_up.start()

        S.halo_out[1] = dot(tat[pl.ds(2 * n, n), :], S.prod_k[...]).astype(bf16)

        @pl.when(has_below)
        def _():
            halo_down.start()

        S.p_val[...] = dot(tat[pl.ds(n, n), :], S.prod_k[...])
        ld_bt.wait()

        @pl.loop(0, 4)
        def _(t):
            s = pl.ds(pl.multiple_of(t * 256, 256), 256)
            put(S.flat, 2 * C + 2 * FF + t * 256, dot(tbt[s, :], S.prod_l[...]))

        put(S.flat, BASE, dot(S.bst[...], S.prod_s[...]))
        halo_wait(halo_up, halo_down, S.halo_in.at[0], S.halo_in.at[1])
        gz_low = S.t_low

        def grad_z(s, a):
            g = S.p_val[s, :] + S.halo_in[0, s, :].astype(f32) + S.halo_in[1, s, :].astype(f32)
            gz_low[s, :] = (g * S.dz[s, :]).astype(bf16)
            return a

        chunks(n, grad_z)
        S.p_val[...] = dot(gz_low[...], S.tab[pl.ds(0, C), :], (1, 1))

        def pre_sums(s, a):
            g = S.p_val[s, :]
            return a[0] + fold(g), a[1] + fold(g * ((S.x[s, :] - m_x) * inv_x))

        b_pre, g_pre = (close(v) for v in chunks(n, pre_sums, (zero, zero)))
        share_send(7, 0, jnp.concatenate([b_pre, g_pre], axis=0))
        for h in range(C // 256):
            put(S.flat, h * 256, dot(S.pre_low[:, half_cols(h)], gz_low[...], (0, 0)))
        norms = [g_pre, b_pre, g_lg, b_pair, g_sg, b_pair, g_proj, b_proj, g_ffn, b_ffn]
        norms += [mid_rows[blocks + j : blocks + j + 1] for j in range(blocks)]
        put(S.flat, BASE + 32, jnp.concatenate(norms + [jnp.zeros((2, C), f32)], axis=0))
        for j in range(blocks):
            for k in range(4):
                S.flat[pl.ds((BASE + 25 + j) * 4 + k, 1), :] = mid_rows[j : j + 1, k * 128 : (k + 1) * 128]

    pl.run_scoped(
        back, pltpu.VMEM(S.at_hbm.shape, bf16), pltpu.VMEM(S.bt_hbm.shape, bf16), pltpu.VMEM(S.ct_hbm.shape, bf16), pltpu.VMEM((4, 256, C), f32)
    )


    plan = reduce_plan(nb)
    parts = len(plan)
    size = lines // parts
    unit = 64 if own % 64 == 0 else 8
    tmp = S.tmp
    hop_base = nz * nb
    z_base = hop_base + nz * (nb - 1)

    def tail(sib_out, pair, z_out):
        grad = S.flat.reshape(total, 4, 128)

        def column(i):
            return lax.rem(z + 1 + i, nz)

        def collect(m, zz, cc):
            start = (flip(b, m) * nr + 2 * zz + cc) * own

            @pl.loop(0, own // unit)
            def _(g):
                at = start + g * unit
                for u in range(unit):
                    tmp[pl.ds(pl.multiple_of((g * unit + u) * 4, 4), 4), :] = grad[S.idx[at // 128, lax.rem(at, 128) + u]]

        def to_sibling(i, m):
            return pltpu.make_async_remote_copy(
                sib_out.at[i, m], rows_in.at[i * nb + m], S.sib_send.at[i, m], S.sib_recv.at[i, m],
                device_id=sibling, device_id_type=MESH,
            )

        def rows_of(p):
            return pl.ds(p * size, size)

        def slots(p, t):
            at = sum(len(plan[p][k][2]) for k in range(t))
            return at, len(plan[p][t][2])

        def hop_at(i, p, at, count):
            return rows_in.at[pl.ds(hop_base + i * (nb - 1) + at, count), rows_of(p)]

        def hop(i, p, t, m):
            o, sent, kept = plan[p][t]
            at, _ = slots(p, t)
            landing = rows_in.at[hop_base + i * (nb - 1) + at + kept.index(m ^ (1 << o)), rows_of(p)]
            return pltpu.make_async_remote_copy(
                pair.at[i, m, rows_of(p)], landing, S.hop_send.at[i, p, t], S.hop_recv.at[i, p, t],
                device_id=(flip(b, 1 << o), r), device_id_type=MESH,
            )

        def hop_wait(i, p, t, sem):
            whole = hop_at(i, p, *slots(p, t))
            pltpu.make_async_copy(whole, whole, sem.at[i, p, t]).wait()

        def for_sibling(i):
            for m in reversed(range(nb)):
                collect(m, column(i), 1 - c)
                sib_out[i, m] = tmp[...].astype(bf16)
                to_sibling(i, m).start()

        def to_owner(i):
            return pltpu.make_async_remote_copy(
                z_out.at[i], rows_in.at[z_base + i], S.own_send.at[i], S.own_recv.at[i],
                device_id=(b, 2 * column(i) + c), device_id_type=MESH,
            )

        def first_step(i):
            for m in reversed(range(nb)):
                collect(m, column(i), c)
                to_sibling(i, m).wait_recv()
                pair[i, m] = (tmp[...] + rows_in[i * nb + m].astype(f32)).astype(bf16)
                for p in range(parts):
                    if m in plan[p][0][1]:
                        hop(i, p, 0, m).start()

            @pl.when(i < nz - 1)
            def _():
                for_sibling(i + 1)

        def next_step(i, t):
            for p in range(parts):
                hop_wait(i, p, t, S.hop_recv)
                at, _ = slots(p, t)
                for k, m in enumerate(plan[p][t][2]):
                    pair[i, m, rows_of(p)] = (
                        pair[i, m, rows_of(p)].astype(f32)
                        + rows_in[hop_base + i * (nb - 1) + at + k, rows_of(p)].astype(f32)
                    ).astype(bf16)
                    if m in plan[p][t + 1][1]:
                        hop(i, p, t + 1, m).start()

        def last_step(i):
            for p in range(parts):
                hop_wait(i, p, parts - 1, S.hop_recv)
                at, _ = slots(p, parts - 1)
                tmp[rows_of(p), :] = pair[i, 0, rows_of(p)].astype(f32) + rows_in[hop_base + i * (nb - 1) + at, rows_of(p)].astype(f32)

            @pl.when(i < nz - 1)
            def _():
                z_out[i] = tmp[...].astype(bf16)
                to_owner(i).start()

        def grad_image():
            sums = share_wait(7, 1, merge_sum) * (1.0 / every)
            scale_x = row(0) * inv_x

            def last(s, a):
                hat = (S.x[s, :] - m_x) * inv_x
                S.g_f[s, :] = S.g_f[s, :] + scale_x * (S.p_val[s, :] - sums[0:1] - hat * sums[1:2])
                return a

            chunks(n, last)
            gin_copy.start()
            for i in range(own):
                at = (b * nr + r) * own + i // unit * unit
                p = S.idx[at // 128, lax.rem(at, 128) + i % unit]
                fast = (p >= 2 * C + 2 * FF + KL * KL) & ((p < BASE) | (p >= BASE + KS * KS))
                S.rate[pl.ds(i, 1), :] = jnp.full((1, 128), jnp.where(fast, np.float32(norm_rate), np.float32(matrix_rate)), f32)

        gin_copy = pltpu.make_async_copy(S.g_f, S.gin_hbm, S.load_sem.at[6])
        for_sibling(0)

        @pl.loop(0, nz + parts)
        def _(q):
            @pl.when(q < nz)
            def _():
                first_step(q)

            @pl.when(q == 0)
            def _():
                share_send(7, 1, share_wait(7, 0, merge_sum))

            for t in range(parts - 1):

                @pl.when((q >= t + 1) & (q < nz + t + 1))
                def _():
                    next_step(q - t - 1, t)

            @pl.when(q == 1)
            def _():
                grad_image()

            @pl.when(q >= parts)
            def _():
                last_step(q - parts)

        for i in range(nz - 1):
            to_owner(i).wait_recv()
            tmp[...] += rows_in[z_base + i].astype(f32)
        for j in range(4):
            S.red[:, j * 128 : (j + 1) * 128] = tmp[pl.ds(j, own, stride=4), :]

        @pl.loop(0, nz)
        def _(i):
            for m in range(nb):
                to_sibling(i, m).wait_send()
            for p in range(parts):
                for t in range(parts):
                    hop_wait(i, p, t, S.hop_send)

        for i in range(nz - 1):
            to_owner(i).wait_send()
        gin_copy.wait()

    low_block = lambda *lead: pltpu.VMEM(lead + (lines, 128), bf16)
    pl.run_scoped(tail, low_block(nz, nb), low_block(nz, nb), low_block(nz))
    for e in range(len(WIDTHS)):
        for stage in range(2):
            buf, mine, count = share_stage(e, stage)
            sent = buf.at[pl.ds(0, count - 1)]
            pltpu.make_async_copy(sent, sent, S.stat_send.at[e, stage]).wait()
    out_copy.wait()


def step(x, cot, master, slots, nb, nr):
    (a, at, b, bt, bs, bst, c, ct) = tables()
    n, own, nz, parts = x.shape[0], master.shape[0], nr // 2, nb.bit_length() - 1
    total = slots.size
    vm = lambda *shape: pltpu.VMEM(shape, f32)
    low = lambda *shape: pltpu.VMEM(shape, bf16)
    dma = lambda *shape: pltpu.SemaphoreType.DMA(shape)
    vmem, anywhere = pl.BlockSpec(memory_space=pltpu.VMEM), pl.BlockSpec(memory_space=pl.ANY)
    ins = dict(
        slots_hbm=(slots, anywhere), x_hbm=(x, anywhere), cot_hbm=(cot, anywhere), master_hbm=(master, anywhere),
        a_hbm=(a, anywhere), at_hbm=(at, anywhere), b_hbm=(b, anywhere), bt_hbm=(bt, anywhere), bs=(bs, vmem), bst=(bst, vmem),
        c_hbm=(c, anywhere), ct_hbm=(ct, anywhere),
    )
    image = jax.ShapeDtypeStruct((n, C), f32)
    outs = dict(
        out_hbm=(image, anywhere), gin_hbm=(image, anywhere), red=(jax.ShapeDtypeStruct((own, C), f32), vmem),
        rate=(jax.ShapeDtypeStruct((own, 128), f32), vmem),
    )
    scratch = dict(
        rows_in=low(nb * nr, 4 * own, 128), flat=vm(4 * total, 128), tab=low(total, C), x=vm(n, C), cot=vm(n, C), master=vm(own, C),
        tmp=vm(4 * own, 128), chunk=vm(512, 128), inv=pltpu.VMEM((total // 128, 128), jnp.int32), at_v=pltpu.VMEM((total // 128, 128), jnp.int32),
        idx=pltpu.SMEM((total // 128, 128), jnp.int32),
        inv_at=pltpu.SMEM((total // 128, 128), jnp.int32), small=vm(48, C),
        pre_low=low(n, C), wide=low(3 * n, C), dz=vm(n, C), spec_u=vm(2 * NF, C), spec_l=vm(2 * NF, C), spec_s=vm(2 * NF, C),
        prod_l=low(2 * NF, C), prod_s=low(2 * NF, C), prod_k=low(2 * NF, C), d_l=vm(n, C), d_s=vm(n, C), s_val=vm(n, C),
        t_low=low(n, C), p_val=vm(n, C), mid=vm(n, C), c_low=low(n, C), gy_low=low(n, C), gp_low=low(n, C), g_f=vm(n, C), out=vm(n, C),
        halo_out=low(2, n, C), halo_in=low(2, n, C),
    )
    for e, w in enumerate(WIDTHS):
        one, two = (2, nb * nz) if by_chip(e, nb * nz) else (nr, nb)
        scratch[f"one{e}"] = vm(one, w, C)
        scratch[f"two{e}"] = vm(two, w, C)
    scratch.update(
        load_sem=dma(9), stat_send=dma(len(WIDTHS), 2), stat_recv=dma(len(WIDTHS), 2), halo_send=dma(4), halo_recv=dma(4),
        z_send=dma(nz), z_recv=dma(nz), b_send=dma(nb, nz), b_recv=dma(nb, nz), half_send=dma(2, nz), half_recv=dma(2, nz),
        core_send=dma(nb, nz), core_recv=dma(nb, nz), sib_send=dma(nz, nb), sib_recv=dma(nz, nb),
        hop_send=dma(nz, parts, parts), hop_recv=dma(nz, parts, parts), own_send=dma(nz), own_recv=dma(nz),
    )
    return pl.pallas_call(
        functools.partial(step_kernel, nb, nr, [*ins, *outs, *scratch]),
        out_shape=[v[0] for v in outs.values()],
        in_specs=[v[1] for v in ins.values()],
        out_specs=[v[1] for v in outs.values()],
        scratch_shapes=list(scratch.values()),
        compiler_params=pltpu.CompilerParams(collective_id=0, has_side_effects=True, vmem_limit_bytes=62 * 2**20),
    )(*[v[0] for v in ins.values()])


def finish_kernel(*refs):
    ins, outs, bufs, (load_sem, store_sem) = refs[:7], refs[7:14], refs[14:25], refs[25:]
    red, rate, first_ref, second_ref, master_ref, out, gin = bufs[:7]
    new_first, new_second, new_master, new_copy = bufs[7:11]
    loads = [pltpu.make_async_copy(src, dst, load_sem.at[i]) for i, (src, dst) in enumerate(zip(ins, bufs[:7]))]
    for copy in loads:
        copy.start()
    own = red.shape[0]
    size = 64 if own % 64 == 0 else own
    for copy in loads[:5]:
        copy.wait()
    stores = [pltpu.make_async_copy(red, outs[2], store_sem.at[2, 0])]
    stores[0].start()
    for part in range(own // size):
        for k in range(0, size, 8):
            s = slice(part * size + k, part * size + k + 8)
            for j in range(C // 128):
                at = (s, slice(j * 128, (j + 1) * 128))
                g = red[at]
                first = beta_one * first_ref[at] + (1.0 - beta_one) * g
                second = beta_two * second_ref[at] + (1.0 - beta_two) * g * g
                new_first[at] = first
                new_second[at] = second
                first_hat = first / (1.0 - beta_one**STEP)
                second_hat = second / (1.0 - beta_two**STEP)
                master = master_ref[at]
                new_master[at] = master - rate[s, :] * (first_hat / (jnp.sqrt(second_hat) + adam_eps) + decay_rate * master)
        s = pl.ds(part * size, size)
        new_copy[s, :] = new_master[s, :].astype(bf16)
        if part == 0:
            for i in (5, 6):
                loads[i].wait()
                stores.append(pltpu.make_async_copy(bufs[i], outs[i - 5], store_sem.at[i - 5, 0]))
                stores[-1].start()
        for i, buf in enumerate((new_first, new_second, new_master, new_copy)):
            stores.append(pltpu.make_async_copy(buf.at[s], outs[3 + i].at[s], store_sem.at[3 + i, part]))
            stores[-1].start()
    for copy in stores:
        copy.wait()


def finish(reduced, first, second, master, rates, out, gin):
    anywhere = pl.BlockSpec(memory_space=pl.ANY)
    slot = jax.ShapeDtypeStruct(reduced.shape, f32)
    image = jax.ShapeDtypeStruct(out.shape, f32)
    low = jax.ShapeDtypeStruct(reduced.shape, bf16)
    ins = (reduced, rates, first, second, master, out, gin)
    outs = [image, image, slot, slot, slot, slot, low]
    return pl.pallas_call(
        finish_kernel,
        out_shape=outs,
        in_specs=[anywhere] * 7,
        out_specs=[anywhere] * 7,
        scratch_shapes=[pltpu.VMEM(v.shape, f32) for v in ins]
        + [pltpu.VMEM(v.shape, v.dtype) for v in (slot, slot, slot, low)]
        + [pltpu.SemaphoreType.DMA((7,)), pltpu.SemaphoreType.DMA((7, 4))],
        compiler_params=pltpu.CompilerParams(vmem_limit_bytes=62 * 2**20),
    )(*ins)


def body(image_in, cotangent, slot_rows, master, first_moment, second_moment):
    n = image_in.shape[0] * image_in.shape[1] * image_in.shape[2]
    nb, nr = lax.axis_size("batch"), lax.axis_size("rows")
    out, grad_in, reduced, rates = step(
        image_in.reshape(n, C), cotangent.reshape(n, C), master, slot_rows.reshape(-1, 128), nb, nr
    )
    result, grad_x, *slots = finish(reduced, first_moment, second_moment, master, rates, out, grad_in)
    return (result.reshape(image_in.shape), grad_x.reshape(image_in.shape), *slots)


def solution(mesh):
    image = P("batch", "rows", None, None)
    owner = P(AXES, None)
    return jax.shard_map(
        body,
        mesh=mesh,
        in_specs=(image, image, P(), owner, owner, owner),
        out_specs=(image, image, owner, owner, owner, owner, owner),
        check_vma=False,
    )
```

```python
import functools
import types

import jax
import jax.numpy as jnp
import numpy as np
from jax import lax
from jax.experimental import pallas as pl
from jax.experimental.pallas import tpu as pltpu
from jax.sharding import PartitionSpec as P

C = 512
FF = 2048
KL = 31
KS = 5
STEP = 10

norm_eps = 1e-05
beta_one = 0.9
beta_two = 0.999
adam_eps = 1e-08
decay_rate = 0.05
matrix_rate = 0.05
norm_rate = 0.5

TH = 16
TW = 16
NY = 47
NX = 31
NF = 768
REACH = (KL - 1) // 2
AXES = ("batch", "rows")
f32 = jnp.float32
bf16 = jnp.bfloat16


@functools.lru_cache(None)
def tables():
    freqs = [(ky, 0) for ky in range((NY + 1) // 2)]
    freqs += [(ky, kx) for kx in range(1, (NX + 1) // 2) for ky in range(NY)]
    ky = np.array([f[0] for f in freqs], np.int64)[:, None]
    kx = np.array([f[1] for f in freqs], np.int64)[:, None]
    pad = NF - len(freqs)

    def angle(rows, cols):
        ty = (ky * rows.reshape(1, -1)) % NY
        tx = (kx * cols.reshape(1, -1)) % NX
        return 2 * np.pi * (ty / NY + tx / NX)

    def grid(rows, cols):
        r, c = np.meshgrid(rows, cols, indexing="ij")
        return r.reshape(-1), c.reshape(-1)

    def stack(re, im):
        z = np.zeros((pad, re.shape[1]))
        return np.concatenate([re, z, im, z], axis=0)

    r, c = grid(np.arange(-TH, 2 * TH), np.arange(TW))
    used = ((r + REACH >= 0) & (r + REACH < NY - 1)).astype(np.float64)[None]
    t = angle(r + REACH, c)
    a = stack(np.cos(t) * used, -np.sin(t) * used)
    i, j = grid(np.arange(KL), np.arange(KL))
    t = angle(i, j - REACH)
    b = stack(np.cos(t), -np.sin(t))
    lead = REACH - (KS - 1) // 2
    small = ((i >= lead) & (i < lead + KS) & (j >= lead) & (j < lead + KS)).nonzero()[0]
    bs = np.pad(b[:, small], ((0, 0), (0, 32 - KS * KS)))
    b = np.pad(b, ((0, 0), (0, 2 * C - KL * KL)))
    y, x = grid(np.arange(TH), np.arange(TW))
    t = angle(y, x)
    w = np.full((len(freqs), 1), 2.0)
    w[0] = 1.0
    w /= NY * NX
    ct = stack(w * np.cos(t), -w * np.sin(t))
    return tuple(m.astype(np.float32).astype(bf16) for m in (a, a.T, b, b.T, bs, bs.T, ct.T, ct))


def dot(a, b, dims=(1, 0)):
    return lax.dot_general(a, b, (((dims[0],), (dims[1],)), ((), ())), preferred_element_type=f32)


MESH = pl.DeviceIdType.MESH
WIDTHS = (2, 4, 3, 8, 8, 5, 3, 2)
BY_CHIP = (1, 2, 5, 6)
BASE = 2 * C + 2 * FF + 976


def chunks(n, fn, init=()):
    return lax.fori_loop(0, n // 32, lambda i, c: fn(pl.ds(pl.multiple_of(i * 32, 32), 32), c), init)


def fold(v):
    return jnp.sum(v.reshape(v.shape[0] // 8, 8, v.shape[1]), axis=0)


def close(v):
    return jnp.sum(v, axis=0, keepdims=True)


def put(ref, start, v):
    for j in range(4):
        ref[pl.ds(start * 4 + j, v.shape[0], stride=4), :] = v[:, j * 128 : (j + 1) * 128]


def gelu_both(v):
    a = np.float32(np.sqrt(2 / np.pi))
    sq = v * v
    t = jnp.tanh(a * (v + 0.044715 * (sq * v)))
    half = 0.5 * (1 + t)
    return v * half, half + 0.5 * v * (1 - t * t) * (a * (1 + 3 * 0.044715 * sq))


def flip(b, m):
    k = 0
    while m >> k:
        if (m >> k) & 1:
            b = b + (1 - 2 * lax.rem(b // 2**k, 2)) * 2**k
        k += 1
    return b


def reduce_plan(nb):
    bits = nb.bit_length() - 1
    plan = []
    for p in range(bits):
        order = [(p + t) % bits for t in range(bits)]
        steps, kept = [], list(range(nb))
        for o in order:
            sent = [m for m in kept if (m >> o) & 1]
            kept = [m for m in kept if not (m >> o) & 1]
            steps.append((o, sent, kept))
        plan.append(steps)
    return plan


def first_along_z(nb, lines):
    return lines // 6 if nb == 4 and lines % 192 == 0 else 0


def by_chip(e, chips):
    return e in BY_CHIP and chips <= 32


def merge_sum(v, count):
    return jnp.sum(v, axis=0)


def merge_stats(h):
    def merge(v, count):
        means = v[:, :h]
        m = jnp.sum(means, axis=0) * (1.0 / v.shape[0])
        d = means - m
        parts = [m, jnp.sum(v[:, h : 2 * h], axis=0) + count * jnp.sum(d * d, axis=0)]
        if v.shape[1] > 2 * h:
            parts.append(jnp.sum(v[:, 2 * h :], axis=0))
        return jnp.concatenate(parts, axis=0)

    return merge


def local(read, n):
    zero = jnp.zeros((8, C), f32)
    m = close(chunks(n, lambda s, c: c + fold(read(s)), zero)) * (1.0 / n)

    def sq(s, c):
        d = read(s) - m
        return c + fold(d * d)

    return m, close(chunks(n, sq, zero))


def half_cols(h):
    return pl.ds(pl.multiple_of(h * 256, 256), 256)


def up_rows(j):
    return pl.ds(pl.multiple_of(2 * C + j * C, C), C)


def down_rows(j):
    return pl.ds(pl.multiple_of(2 * C + FF + j * C, C), C)


def table_place(t):
    start = 2 * C + 2 * FF
    k_end = start + KL * KL
    s_end = k_end + KS * KS
    m_gain = s_end + 10
    m_bias = m_gain + FF // C
    m_end = m_bias + FF // C
    up = t - 2 * C
    up = 2 * C + (up & (FF // C - 1)) * C + (up >> ((FF // C).bit_length() - 1))
    base = start + 976
    unused = t - m_end
    unused = jnp.where(unused < 15, k_end + unused, jnp.where(unused < 18, base + 29 + unused - 15, base + 46 + unused - 18))
    p = jnp.where((t >= 2 * C) & (t < 2 * C + FF), up, t)
    p = jnp.where(t >= k_end, t - k_end + base, p)
    p = jnp.where(t >= s_end, t - s_end + base + 32, p)
    p = jnp.where(t >= m_bias, t - m_bias + base + 25, p)
    return jnp.where(t >= m_end, unused, p)


def step_kernel(nb, nr, names, *refs):
    S = types.SimpleNamespace(**dict(zip(names, refs)))
    nz = nr // 2
    nd = nb * nr
    n = S.x.shape[0]
    own = S.master.shape[0]
    lines = 4 * own
    total = S.tab.shape[0]
    every = float(n * nd)
    b = lax.axis_index("batch")
    r = lax.axis_index("rows")
    z, c = r // 2, lax.rem(r, 2)
    sibling = (b, r + 1 - 2 * c)
    square = nb == 4
    blocks = FF // C
    zero = jnp.zeros((8, C), f32)
    rows_in = S.rows_in

    def load(i, src, dst):
        return pltpu.make_async_copy(src, dst, S.load_sem.at[i])

    ld_m, ld_x, ld_c = load(0, S.master_hbm, S.master), load(1, S.x_hbm, S.x), load(2, S.cot_hbm, S.cot)
    ld_s = load(8, S.slots_hbm, S.at_v)
    for copy in (ld_s, ld_m, ld_x, ld_c):
        copy.start()
    barrier = pltpu.get_barrier_semaphore()
    for k in range(1, nr):
        pl.semaphore_signal(barrier, inc=1, device_id=(b, lax.rem(r + k, nr)), device_id_type=MESH)
    for m in range(1, nb):
        pl.semaphore_signal(barrier, inc=1, device_id=(flip(b, m), r), device_id_type=MESH)

    @pl.loop(0, (nb - 1) * (nz - 1))
    def _(k):
        at = (lax.rem(b + 1 + k // (nz - 1), nb), 2 * lax.rem(z + 1 + lax.rem(k, nz - 1), nz) + c)
        pl.semaphore_signal(barrier, inc=1, device_id=at, device_id_type=MESH)


    def share_stage(e, stage):
        buf = getattr(S, ("one" if stage == 0 else "two") + str(e))
        if by_chip(e, nb * nz):
            return (buf, c, 2) if stage == 0 else (buf, b * nz + z, nb * nz)
        return (buf, r, nr) if stage == 0 else (buf, b, nb)

    def share_peer(e, stage, k):
        if by_chip(e, nb * nz):
            if stage == 0:
                return sibling
            other = lax.rem(b * nz + z + k, nb * nz)
            return (other // nz, 2 * lax.rem(other, nz) + c)
        return (b, lax.rem(r + k, nr)) if stage == 0 else (lax.rem(b + k, nb), r)

    def share_send(e, stage, v):
        buf, mine, size = share_stage(e, stage)
        buf[mine] = v

        def one(k):
            pltpu.make_async_remote_copy(
                buf.at[mine], buf.at[mine], S.stat_send.at[e, stage], S.stat_recv.at[e, stage],
                device_id=share_peer(e, stage, k), device_id_type=MESH,
            ).start()

        if size > 8:
            pl.loop(1, size)(one)
        else:
            for k in range(1, size):
                one(k)

    def share_wait(e, stage, merge):
        buf, mine, size = share_stage(e, stage)
        got = buf.at[pl.ds(0, size - 1)]
        pltpu.make_async_copy(got, got, S.stat_recv.at[e, stage]).wait()
        return merge(buf[...], float(n if stage == 0 else n * getattr(S, f"one{e}").shape[0]))

    def share(e, v, merge, work=None, more=None):
        share_send(e, 0, v)
        if work and not by_chip(e, nb * nz):
            work()
        v = share_wait(e, 0, merge)
        share_send(e, 1, v)
        if work and by_chip(e, nb * nz):
            work()
        if more:
            more()
        return share_wait(e, 1, merge)


    def place(m, zz, core):
        return flip(b, m) * nr + 2 * zz + core

    def along_z(zz, up):
        at = rows_in.at[place(0, zz, c)]
        return pltpu.make_async_remote_copy(
            at, at, S.z_send.at[zz], S.z_recv.at[zz], device_id=(b, r + 2 if up else r - 2), device_id_type=MESH
        )

    def to_peer(m, zz):
        at = rows_in.at[place(0, zz, c)]
        return pltpu.make_async_remote_copy(
            at, at, S.b_send.at[m, zz], S.b_recv.at[m, zz], device_id=(flip(b, m), r), device_id_type=MESH
        )

    def from_peer(m, zz):
        at = rows_in.at[place(m, zz, c)]
        return pltpu.make_async_copy(at, at, S.b_recv.at[m, zz])

    def half(m, zz, h, to):
        at = rows_in.at[place(m, zz, c), pl.ds(h * (lines // 2), lines // 2)]
        return pltpu.make_async_remote_copy(
            at, at, S.half_send.at[h, zz], S.half_recv.at[h, zz], device_id=(flip(b, to), r), device_id_type=MESH
        )

    def to_other_core(m, zz, core):
        at = rows_in.at[place(m, zz, core)]
        return pltpu.make_async_remote_copy(
            at, at, S.core_send.at[m, zz], S.core_recv.at[m, zz], device_id=sibling, device_id_type=MESH
        )

    def cast(m, zz, core):
        d = place(m, zz, core)
        S.flat[pl.ds(pl.multiple_of(d * lines, lines), lines), :] = rows_in[d].astype(f32)

    def sends(zz):
        for m in range(1, nb):
            if not (square and m == 3):
                to_peer(m, zz).start()
        to_other_core(0, zz, c).start()
        cast(0, zz, c)

    def own_column(k):
        if k == 0:

            @pl.when(z < nz - 1)
            def _():
                along_z(z, True).start()

            @pl.when(z > 0)
            def _():
                along_z(z, False).start()

            sends(z)
            return

        @pl.when(z >= k)
        def _():
            along_z(z - k, True).wait_recv()

            @pl.when(z < nz - 1)
            def _():
                along_z(z - k, True).start()

            sends(z - k)

        @pl.when(z + k < nz)
        def _():
            along_z(z + k, False).wait_recv()

            @pl.when(z > 0)
            def _():
                along_z(z + k, False).start()

            sends(z + k)

    def each(k, fn):
        if k == 0:
            fn(z)
            return

        @pl.when(z >= k)
        def _():
            fn(z - k)

        @pl.when(z + k < nz)
        def _():
            fn(z + k)

    def pass_on(zz):
        for m in range(1, nb):
            if square and m == 3:
                continue
            from_peer(m, zz).wait()
            if square:
                half(m, zz, 2 - m, 3 - m).start()
            to_other_core(m, zz, c).start()
            cast(m, zz, c)

    def corner(zz):
        if square:
            for h in range(2):
                half(3, zz, h, 0).wait_recv()
            to_other_core(3, zz, c).start()
            cast(3, zz, c)

    def other_core(zz):
        for m in range(nb):
            to_other_core(m, zz, 1 - c).wait_recv()
            cast(m, zz, 1 - c)

    def find(part, parts):
        tiles = total // 1024
        unit = 16
        spots = [
            lax.broadcasted_iota(jnp.int32, (8, 128), 0) * 128 + lax.broadcasted_iota(jnp.int32, (8, 128), 1) + 1024 * k
            for k in range(tiles)
        ]

        def some(g, acc):
            for u in range(unit):
                start = part * (total // parts) + g * unit
                s = start + u
                p = S.idx[start // 128, lax.rem(start, 128) + u]
                acc = [jnp.where(spot == p, s, a) for spot, a in zip(spots, acc)]
            return acc

        acc = [S.inv[k * 8 : k * 8 + 8, :] if part else jnp.zeros((8, 128), jnp.int32) for k in range(tiles)]
        acc = lax.fori_loop(0, total // parts // unit, some, acc)
        for k in range(tiles):
            S.inv[k * 8 : k * 8 + 8, :] = acc[k]

    def order(start, stop):
        flat = S.flat.reshape(total, 4, 128)

        @pl.loop(start, stop)
        def _(t):
            for u in range(128):
                S.chunk[4 * u : 4 * u + 4, :] = flat[S.inv_at[t, u]]

            rows = pl.ds(pl.multiple_of(t * 128, 128), 128)
            for j in range(4):
                S.tab[rows, j * 128 : (j + 1) * 128] = S.chunk[pl.ds(j, 128, stride=4), :].astype(bf16)

    def front(ta, tb, tc):
        ld_a, ld_b, ld_t = load(3, S.a_hbm, ta), load(4, S.b_hbm, tb), load(5, S.c_hbm, tc)
        for copy in (ld_b, ld_a, ld_t):
            copy.start()
        ld_s.wait()
        S.at_v[...] = table_place(S.at_v[...])
        to_scalar = pltpu.make_async_copy(S.at_v, S.idx, S.load_sem.at[8])
        to_scalar.start()
        ld_m.wait()
        for j in range(4):
            S.tmp[pl.ds(j, own, stride=4), :] = S.master[:, j * 128 : (j + 1) * 128]
        rows_in[place(0, z, c)] = S.tmp[...].astype(bf16)
        pl.semaphore_wait(barrier, nr - 1 + nb - 1 + (nb - 1) * (nz - 1))
        own_column(0)
        to_scalar.wait()
        ld_x.wait()
        share_send(0, 0, jnp.concatenate(local(lambda s: S.x[s, :], n), axis=0))
        steps = max(nz - 1, 1)
        for k in range(1, nz):
            find(k - 1, steps)
            own_column(k)
            each(k - 1, pass_on)
            if k > 1:
                each(k - 2, corner)
            if k > 2:
                each(k - 3, other_core)
            if k == 1:
                share_send(0, 1, share_wait(0, 0, merge_stats(1)))
        if nz == 1:
            find(0, 1)
            share_send(0, 1, share_wait(0, 0, merge_stats(1)))
        to_scalar = pltpu.make_async_copy(S.inv, S.inv_at, S.load_sem.at[6])
        to_scalar.start()
        each(nz - 1, pass_on)
        if nz > 1:
            each(nz - 2, corner)
        each(nz - 1, corner)
        for k in range(max(nz - 3, 0), nz):
            each(k, other_core)
        tot = share_wait(0, 1, merge_stats(1))
        m_x, q_x = tot[0:1], tot[1:2] * (1.0 / every)
        inv_x = lax.rsqrt(q_x + norm_eps)
        to_scalar.wait()
        tiles = total // 128
        late = (2 * C + 2 * FF) // 128
        order(0, C // 128)
        order(tiles - 2, tiles)

        for m in range(nb):

            @pl.loop(0, nz)
            def _(zz):
                to_other_core(m, zz, c).wait_send()
                if m and not (square and m == 3):
                    to_peer(m, zz).wait_send()
                if square and m in (1, 2):
                    half(m, zz, 2 - m, 3 - m).wait_send()

        for k in range(nz):

            @pl.when((z >= k) & (z < nz - 1))
            def _():
                along_z(z - k, True).wait_send()

            @pl.when((z + k < nz) & (z > 0))
            def _():
                along_z(z + k, False).wait_send()

        small = S.tab[pl.ds(BASE, 48), :].astype(f32)
        S.small[...] = small
        row = lambda i: small[32 + i : 33 + i, :]

        def pre(s, sx):
            d = S.x[s, :] - m_x
            S.pre_low[s, :] = (d * (inv_x * row(0)) + row(1)).astype(bf16)
            return sx + fold(d)

        sum_x = close(chunks(n, pre, zero))
        S.dz[...] = dot(S.pre_low[...], S.tab[pl.ds(0, C), :])

        def act(s, a):
            u, d = gelu_both(S.dz[s, :])
            S.dz[s, :] = d
            S.wide[pl.ds(pl.multiple_of(n + s.start, 32), 32), :] = u.astype(bf16)
            return a

        chunks(n, act)
        mine = S.wide.at[pl.ds(n, n)]
        halo_up = halo(0, mine, S.wide.at[pl.ds(2 * n, n)], True)
        halo_down = halo(1, mine, S.wide.at[pl.ds(0, n)], False)
        halo_start(halo_up, halo_down)
        order(late, tiles - 2)
        order(C // 128, 2 * C // 128)

        ld_b.wait()

        @pl.loop(0, 2 * NF // 256)
        def _(t):
            s = pl.ds(pl.multiple_of(t * 256, 256), 256)
            S.spec_l[s, :] = dot(tb[s, :], S.tab[pl.ds(2 * C + 2 * FF, 2 * C), :])
            S.spec_s[s, :] = dot(S.bs[s, :], S.tab[pl.ds(BASE, 32), :])

        halo_wait(halo_up, halo_down, S.wide.at[pl.ds(0, n)], S.wide.at[pl.ds(2 * n, n)])
        ld_a.wait()

        @pl.loop(0, 2 * NF // 256)
        def _(t):
            s = pl.ds(pl.multiple_of(t * 256, 256), 256)
            S.spec_u[s, :] = dot(ta[s, :], S.wide[...])

        @pl.loop(0, NF // 32)
        def _(i):
            re, im = pl.ds(pl.multiple_of(i * 32, 32), 32), pl.ds(pl.multiple_of(NF + i * 32, 32), 32)
            ur, ui = S.spec_u[re, :], S.spec_u[im, :]
            for k, p in ((S.spec_l, S.prod_l), (S.spec_s, S.prod_s)):
                kr, ki = k[re, :], k[im, :]
                p[re, :] = (ur * kr + ui * ki).astype(bf16)
                p[im, :] = (ui * kr - ur * ki).astype(bf16)

        ld_t.wait()
        S.d_l[...] = dot(tc[...], S.prod_l[...])
        S.d_s[...] = dot(tc[...], S.prod_s[...])
        return m_x, q_x, sum_x


    has_above, has_below = r > 0, r < nr - 1

    def halo(i, src, dst, up):
        peer = lax.rem(r + nr - 1, nr) if up else lax.rem(r + 1, nr)
        return pltpu.make_async_remote_copy(
            src, dst, S.halo_send.at[i], S.halo_recv.at[i], device_id=(b, peer), device_id_type=MESH
        )

    def halo_start(up, down):
        @pl.when(has_above)
        def _():
            up.start()

        @pl.when(has_below)
        def _():
            down.start()

    def halo_wait(up, down, above, below):
        @pl.when(has_below)
        def _():
            up.wait_recv()
            down.wait_send()

        @pl.when(has_above)
        def _():
            down.wait_recv()
            up.wait_send()

        @pl.when(jnp.logical_not(has_above))
        def _():
            above[...] = jnp.zeros((n, C), bf16)

        @pl.when(jnp.logical_not(has_below))
        def _():
            below[...] = jnp.zeros((n, C), bf16)

    m_x, q_x, sum_x = pl.run_scoped(
        front, pltpu.VMEM(S.a_hbm.shape, bf16), pltpu.VMEM(S.b_hbm.shape, bf16), pltpu.VMEM(S.c_hbm.shape, bf16)
    )
    inv_x = lax.rsqrt(q_x + norm_eps)
    small = S.small[...]
    row = lambda i: small[32 + i : 33 + i, :]
    mid_gain = lambda j: small[42 + j : 43 + j, :]
    mid_bias = lambda j: small[25 + j : 26 + j, :]
    m_l, v_l = local(lambda s: S.d_l[s, :], n)
    m_s, v_s = local(lambda s: S.d_s[s, :], n)
    ld_c.wait()

    def early():
        order(2 * C // 128, (2 * C + FF) // 128)

        def low(s, a):
            S.gy_low[s, :] = S.cot[s, :].astype(bf16)
            return a

        chunks(n, low)

    tot = share(
        1, jnp.concatenate([m_l, m_s, v_l, v_s], axis=0), merge_stats(2), early,
        lambda: order((2 * C + FF) // 128, (2 * C + 2 * FF) // 128),
    )
    m_l, m_s = tot[0:1], tot[1:2]
    inv_l, inv_s = lax.rsqrt(tot[2:3] / every + norm_eps), lax.rsqrt(tot[3:4] / every + norm_eps)

    def pair(s, a):
        hl = (S.d_l[s, :] - m_l) * inv_l
        hs = (S.d_s[s, :] - m_s) * inv_s
        S.d_l[s, :] = hl
        S.d_s[s, :] = hs
        t, d = gelu_both(hl * row(2) + row(3) + hs * row(4) + row(5))
        S.s_val[s, :] = d
        S.t_low[s, :] = t.astype(bf16)
        return a

    chunks(n, pair)
    S.p_val[...] = dot(S.t_low[...], S.tab[pl.ds(C, C), :])
    m_p = close(chunks(n, lambda s, a: a + fold(S.p_val[s, :]), zero)) * (1.0 / n)

    def proj(s, a):
        d = S.p_val[s, :] - m_p
        return a[0] + fold(d * d), a[1] + fold(d * (S.x[s, :] - m_x))

    v_p, cross = chunks(n, proj, (zero, zero))
    tot = share(2, jnp.concatenate([m_p, close(v_p), close(cross) + m_p * sum_x], axis=0), merge_stats(1))
    m_p, q_p, cov = tot[0:1], tot[1:2] / every, tot[2:3] / every
    inv_p = lax.rsqrt(q_p + norm_eps)
    slope = row(6) * inv_p
    m_f = m_x + row(7)
    q_f = jnp.maximum(q_x + 2 * slope * cov + slope * slope * q_p, 0.0)
    inv_f = lax.rsqrt(q_f + norm_eps)
    hats = inv_f * inv_p * (cov + slope * q_p)

    def ffn(s, a):
        ph = (S.p_val[s, :] - m_p) * inv_p
        S.p_val[s, :] = ph
        m = S.x[s, :] + (ph * row(6) + row(7))
        S.mid[s, :] = m
        S.c_low[s, :] = ((m - m_f) * (inv_f * row(8)) + row(9)).astype(bf16)
        g = S.cot[s, :]
        return a[0] + fold(g), a[1] + fold(g * ph)

    sum_c, sum_ch = chunks(n, ffn, (zero, zero))
    sum_c, sum_ch = close(sum_c), close(sum_ch)

    def middle(hid, gact, a_low, gh_low):
        for j in range(blocks):
            hid[j] = dot(S.c_low[...], S.tab[up_rows(j), :])
        st = [local(lambda s, j=j: hid[j, s, :], n) for j in range(blocks)]

        def back_first():
            for j in range(blocks):
                gact[j] = dot(S.gy_low[...], S.tab[down_rows(j), :], (1, 1))

        tot = share(3, jnp.concatenate([s[0] for s in st] + [s[1] for s in st], axis=0), merge_stats(blocks), back_first)
        m_h = tot[:blocks]
        inv_h = lax.rsqrt(tot[blocks:] / every + norm_eps)
        sums = []
        for j in range(blocks):
            mj, ij, gj, bj = m_h[j : j + 1], inv_h[j : j + 1], mid_gain(j), mid_bias(j)

            def hidden(s, a, j=j, mj=mj, ij=ij, gj=gj, bj=bj):
                hat = (hid[j, s, :] - mj) * ij
                hid[j, s, :] = hat
                v, d = gelu_both(hat * gj + bj)
                a_low[j, s, :] = v.astype(bf16)
                g = gact[j, s, :] * d
                gact[j, s, :] = g
                return a[0] + fold(g), a[1] + fold(g * hat)

            sums.append(tuple(close(v) for v in chunks(n, hidden, (zero, zero))))
        mid_rows = jnp.concatenate([s[0] for s in sums] + [s[1] for s in sums], axis=0)

        def down_grads():
            for j in range(blocks):
                for h in range(C // 256):
                    put(S.flat, 2 * C + FF + j * C + h * 256, dot(a_low[j, :, half_cols(h)], S.gy_low[...], (0, 0)))

        def outputs():
            S.out[...] = S.mid[...]
            for j in range(blocks):
                S.out[...] += dot(a_low[j], S.tab[down_rows(j), :])

        tot = share(4, mid_rows, merge_sum, down_grads, outputs) * (1.0 / every)
        out_copy.start()
        for j in range(blocks):
            tb_, tg_, sc = tot[j : j + 1], tot[blocks + j : blocks + j + 1], mid_gain(j) * inv_h[j : j + 1]

            def grad_h(s, a, j=j, tb_=tb_, tg_=tg_, sc=sc):
                gh_low[j, s, :] = (sc * (gact[j, s, :] - tb_ - hid[j, s, :] * tg_)).astype(bf16)
                return a

            chunks(n, grad_h)
        S.g_f[...] = dot(gh_low[0], S.tab[up_rows(0), :], (1, 1))
        for j in range(1, blocks):
            S.g_f[...] += dot(gh_low[j], S.tab[up_rows(j), :], (1, 1))

        def ffn_sums(s, a):
            g = S.g_f[s, :]
            hat = (S.mid[s, :] - m_f) * inv_f
            return a[0] + fold(g), a[1] + fold(g * hat), a[2] + fold(g * S.p_val[s, :])

        b_ffn, g_ffn, g_fp = (close(v) for v in chunks(n, ffn_sums, (zero, zero, zero)))

        def grad_up():
            for j in range(blocks):
                for h in range(C // 256):
                    put(S.flat, 2 * C + j * C + h * 256, dot(S.c_low[:, half_cols(h)], gh_low[j], (0, 0)))

        tot = share(5, jnp.concatenate([b_ffn, g_ffn, g_fp, sum_c, sum_ch], axis=0), merge_sum, grad_up) * (1.0 / every)
        return mid_rows, b_ffn, g_ffn, tot

    out_copy = pltpu.make_async_copy(S.out, S.out_hbm, S.load_sem.at[7])
    hidden_shape = (blocks, n, C)
    mid_rows, b_ffn, g_ffn, tot = pl.run_scoped(
        middle, pltpu.VMEM(hidden_shape, f32), pltpu.VMEM(hidden_shape, f32), pltpu.VMEM(hidden_shape, bf16), pltpu.VMEM(hidden_shape, bf16)
    )

    def back(tat, tbt, tct, acc):
        ld_ct, ld_at, ld_bt = load(3, S.ct_hbm, tct), load(4, S.at_hbm, tat), load(5, S.bt_hbm, tbt)
        for copy in (ld_ct, ld_at, ld_bt):
            copy.start()
        scale_f = row(8) * inv_f
        mean_hat = tot[4:5] + scale_f * (tot[2:3] - tot[1:2] * hats)

        def grad_mid(s, a):
            hat = (S.mid[s, :] - m_f) * inv_f
            g = S.cot[s, :] + scale_f * (S.g_f[s, :] - tot[0:1] - hat * tot[1:2])
            S.g_f[s, :] = g
            ph = S.p_val[s, :]
            S.gp_low[s, :] = (slope * (g - tot[3:4] - ph * mean_hat)).astype(bf16)
            return a[0] + fold(g), a[1] + fold(g * ph)

        b_proj, g_proj = (close(v) for v in chunks(n, grad_mid, (zero, zero)))
        S.p_val[...] = dot(S.gp_low[...], S.tab[pl.ds(C, C), :], (1, 1))

        def grad_s(s, a):
            g = S.p_val[s, :] * S.s_val[s, :]
            S.p_val[s, :] = g
            return a[0] + fold(g), a[1] + fold(g * S.d_l[s, :]), a[2] + fold(g * S.d_s[s, :])

        b_pair, g_lg, g_sg = (close(v) for v in chunks(n, grad_s, (zero, zero, zero)))

        def grad_out():
            for h in range(C // 256):
                put(S.flat, C + h * 256, dot(S.t_low[:, half_cols(h)], S.gp_low[...], (0, 0)))

        sums = share(6, jnp.concatenate([b_pair, g_lg, g_sg], axis=0), merge_sum, grad_out) * (1.0 / every)
        sc_l, sc_s = row(2) * inv_l, row(4) * inv_s
        gl_low, gs_low = S.t_low, S.gp_low

        def grad_pair(s, a):
            g = S.p_val[s, :] - sums[0:1]
            gl_low[s, :] = (sc_l * (g - S.d_l[s, :] * sums[1:2])).astype(bf16)
            gs_low[s, :] = (sc_s * (g - S.d_s[s, :] * sums[2:3])).astype(bf16)
            return a

        chunks(n, grad_pair)
        ld_ct.wait()

        @pl.loop(0, NF // 256)
        def _(t):
            re, im = pl.ds(pl.multiple_of(t * 256, 256), 256), pl.ds(pl.multiple_of(NF + t * 256, 256), 256)
            acc[0] = dot(tct[re, :], gl_low[...])
            acc[1] = dot(tct[im, :], gl_low[...])
            acc[2] = dot(tct[re, :], gs_low[...])
            acc[3] = dot(tct[im, :], gs_low[...])

            @pl.loop(0, 8)
            def _(i):
                s = pl.ds(pl.multiple_of(i * 32, 32), 32)
                re = pl.ds(pl.multiple_of(t * 256 + i * 32, 32), 32)
                im = pl.ds(pl.multiple_of(NF + t * 256 + i * 32, 32), 32)
                lr, li, sr, si = acc[0, s, :], acc[1, s, :], acc[2, s, :], acc[3, s, :]
                kr, ki = S.spec_l[re, :], S.spec_l[im, :]
                hr, hi = S.spec_s[re, :], S.spec_s[im, :]
                S.prod_k[re, :] = (lr * kr - li * ki + sr * hr - si * hi).astype(bf16)
                S.prod_k[im, :] = (lr * ki + li * kr + sr * hi + si * hr).astype(bf16)
                ur, ui = S.spec_u[re, :], S.spec_u[im, :]
                S.prod_l[re, :] = (lr * ur + li * ui).astype(bf16)
                S.prod_l[im, :] = (lr * ui - li * ur).astype(bf16)
                S.prod_s[re, :] = (sr * ur + si * ui).astype(bf16)
                S.prod_s[im, :] = (sr * ui - si * ur).astype(bf16)

        ld_at.wait()
        halo_up = halo(2, S.halo_out.at[0], S.halo_in.at[1], True)
        halo_down = halo(3, S.halo_out.at[1], S.halo_in.at[0], False)
        S.halo_out[0] = dot(tat[pl.ds(0, n), :], S.prod_k[...]).astype(bf16)

        @pl.when(has_above)
        def _():
            halo_up.start()

        S.halo_out[1] = dot(tat[pl.ds(2 * n, n), :], S.prod_k[...]).astype(bf16)

        @pl.when(has_below)
        def _():
            halo_down.start()

        S.p_val[...] = dot(tat[pl.ds(n, n), :], S.prod_k[...])
        ld_bt.wait()

        @pl.loop(0, 4)
        def _(t):
            s = pl.ds(pl.multiple_of(t * 256, 256), 256)
            put(S.flat, 2 * C + 2 * FF + t * 256, dot(tbt[s, :], S.prod_l[...]))

        put(S.flat, BASE, dot(S.bst[...], S.prod_s[...]))
        halo_wait(halo_up, halo_down, S.halo_in.at[0], S.halo_in.at[1])
        gz_low = S.t_low

        def grad_z(s, a):
            g = S.p_val[s, :] + S.halo_in[0, s, :].astype(f32) + S.halo_in[1, s, :].astype(f32)
            gz_low[s, :] = (g * S.dz[s, :]).astype(bf16)
            return a

        chunks(n, grad_z)
        S.p_val[...] = dot(gz_low[...], S.tab[pl.ds(0, C), :], (1, 1))

        def pre_sums(s, a):
            g = S.p_val[s, :]
            return a[0] + fold(g), a[1] + fold(g * ((S.x[s, :] - m_x) * inv_x))

        b_pre, g_pre = (close(v) for v in chunks(n, pre_sums, (zero, zero)))
        share_send(7, 0, jnp.concatenate([b_pre, g_pre], axis=0))
        for h in range(C // 256):
            put(S.flat, h * 256, dot(S.pre_low[:, half_cols(h)], gz_low[...], (0, 0)))
        norms = [g_pre, b_pre, g_lg, b_pair, g_sg, b_pair, g_proj, b_proj, g_ffn, b_ffn]
        norms += [mid_rows[blocks + j : blocks + j + 1] for j in range(blocks)]
        put(S.flat, BASE + 32, jnp.concatenate(norms + [jnp.zeros((2, C), f32)], axis=0))
        for j in range(blocks):
            for k in range(4):
                S.flat[pl.ds((BASE + 25 + j) * 4 + k, 1), :] = mid_rows[j : j + 1, k * 128 : (k + 1) * 128]

    pl.run_scoped(
        back, pltpu.VMEM(S.at_hbm.shape, bf16), pltpu.VMEM(S.bt_hbm.shape, bf16), pltpu.VMEM(S.ct_hbm.shape, bf16), pltpu.VMEM((4, 256, C), f32)
    )


    plan = reduce_plan(nb)
    parts = len(plan)
    by_z = first_along_z(nb, lines)
    main = lines - by_z
    size = main // parts
    z_size = by_z // parts
    unit = 64 if own % 64 == 0 else 8
    tmp = S.tmp
    hop_base = nz * nb
    z_base = hop_base + nz * (nb - 1)

    def tail(sib_out, pair, z_out):
        grad = S.flat.reshape(total, 4, 128)

        def column(i):
            return lax.rem(z + 1 + i, nz)

        def collect(m, zz, cc):
            start = (flip(b, m) * nr + 2 * zz + cc) * own

            @pl.loop(0, own // unit)
            def _(g):
                at = start + g * unit
                for u in range(unit):
                    tmp[pl.ds(pl.multiple_of((g * unit + u) * 4, 4), 4), :] = grad[S.idx[at // 128, lax.rem(at, 128) + u]]

        def to_sibling(i, m):
            return pltpu.make_async_remote_copy(
                sib_out.at[i, m], rows_in.at[i * nb + m], S.sib_send.at[i, m], S.sib_recv.at[i, m],
                device_id=sibling, device_id_type=MESH,
            )

        def rows_of(p):
            return pl.ds(p * size, size)

        def slots(p, t):
            at = sum(len(plan[p][k][2]) for k in range(t))
            return at, len(plan[p][t][2])

        def hop_at(i, p, at, count):
            return rows_in.at[pl.ds(hop_base + i * (nb - 1) + at, count), rows_of(p)]

        def hop(i, p, t, m):
            o, sent, kept = plan[p][t]
            at, _ = slots(p, t)
            landing = rows_in.at[hop_base + i * (nb - 1) + at + kept.index(m ^ (1 << o)), rows_of(p)]
            return pltpu.make_async_remote_copy(
                pair.at[i, m, rows_of(p)], landing, S.hop_send.at[i, p, t], S.hop_recv.at[i, p, t],
                device_id=(flip(b, 1 << o), r), device_id_type=MESH,
            )

        def hop_wait(i, p, t, sem):
            whole = hop_at(i, p, *slots(p, t))
            pltpu.make_async_copy(whole, whole, sem.at[i, p, t]).wait()

        def for_sibling(i):
            for m in reversed(range(nb)):
                collect(m, column(i), 1 - c)
                sib_out[i, m] = tmp[...].astype(bf16)
                to_sibling(i, m).start()

        def to_owner(i):
            return pltpu.make_async_remote_copy(
                z_out.at[i], rows_in.at[z_base + i, pl.ds(0, main)], S.own_send.at[i], S.own_recv.at[i],
                device_id=(b, 2 * column(i) + c), device_id_type=MESH,
            )

        def to_layer(i, m):
            return pltpu.make_async_remote_copy(
                pair.at[i, m, pl.ds(main, by_z)], S.layer_in.at[i, m], S.layer_send.at[i], S.layer_recv.at[i],
                device_id=(b, 2 * column(i) + c), device_id_type=MESH,
            )

        def layer_wait(i, sem):
            pltpu.make_async_copy(S.layer_in.at[i], S.layer_in.at[i], sem.at[i]).wait()

        def z_rows(p):
            return pl.ds(main + p * z_size, z_size)

        def z_hop(p, t, m):
            o, sent, kept = plan[p][t]
            at, _ = slots(p, t)
            return pltpu.make_async_remote_copy(
                pair.at[nz - 1, m, z_rows(p)], S.z_hops.at[p, at + kept.index(m ^ (1 << o))], S.z_hop_send.at[p, t], S.z_hop_recv.at[p, t],
                device_id=(flip(b, 1 << o), r), device_id_type=MESH,
            )

        def z_hop_wait(p, t, sem):
            at, count = slots(p, t)
            whole = S.z_hops.at[p, pl.ds(at, count)]
            pltpu.make_async_copy(whole, whole, sem.at[p, t]).wait()

        def z_start():
            for i in range(nz - 1):
                layer_wait(i, S.layer_recv)
            for m in reversed(range(nb)):
                v = pair[nz - 1, m, pl.ds(main, by_z)].astype(f32)
                for i in range(nz - 1):
                    v = v + S.layer_in[i, m].astype(f32)
                pair[nz - 1, m, pl.ds(main, by_z)] = v.astype(bf16)
                for p in range(parts):
                    if m in plan[p][0][1]:
                        z_hop(p, 0, m).start()

        def z_next(t):
            for p in range(parts):
                z_hop_wait(p, t, S.z_hop_recv)
                at, _ = slots(p, t)
                for k, m in enumerate(plan[p][t][2]):
                    v = pair[nz - 1, m, z_rows(p)].astype(f32) + S.z_hops[p, at + k].astype(f32)
                    if t == parts - 1:
                        tmp[z_rows(p), :] = v
                        continue
                    pair[nz - 1, m, z_rows(p)] = v.astype(bf16)
                    if m in plan[p][t + 1][1]:
                        z_hop(p, t + 1, m).start()

        def first_step(i):
            for m in reversed(range(nb)):
                collect(m, column(i), c)
                to_sibling(i, m).wait_recv()
                pair[i, m] = (tmp[...] + rows_in[i * nb + m].astype(f32)).astype(bf16)
                for p in range(parts):
                    if m in plan[p][0][1]:
                        hop(i, p, 0, m).start()
                if by_z:

                    @pl.when(i < nz - 1)
                    def _():
                        to_layer(i, m).start()

            @pl.when(i < nz - 1)
            def _():
                for_sibling(i + 1)

        def next_step(i, t):
            for p in range(parts):
                hop_wait(i, p, t, S.hop_recv)
                at, _ = slots(p, t)
                for k, m in enumerate(plan[p][t][2]):
                    pair[i, m, rows_of(p)] = (
                        pair[i, m, rows_of(p)].astype(f32)
                        + rows_in[hop_base + i * (nb - 1) + at + k, rows_of(p)].astype(f32)
                    ).astype(bf16)
                    if m in plan[p][t + 1][1]:
                        hop(i, p, t + 1, m).start()

        def last_step(i):
            for p in range(parts):
                hop_wait(i, p, parts - 1, S.hop_recv)
                at, _ = slots(p, parts - 1)
                tmp[rows_of(p), :] = pair[i, 0, rows_of(p)].astype(f32) + rows_in[hop_base + i * (nb - 1) + at, rows_of(p)].astype(f32)

            @pl.when(i < nz - 1)
            def _():
                z_out[i] = tmp[pl.ds(0, main), :].astype(bf16)
                to_owner(i).start()

        def grad_image():
            sums = share_wait(7, 1, merge_sum) * (1.0 / every)
            scale_x = row(0) * inv_x

            def last(s, a):
                hat = (S.x[s, :] - m_x) * inv_x
                S.g_f[s, :] = S.g_f[s, :] + scale_x * (S.p_val[s, :] - sums[0:1] - hat * sums[1:2])
                return a

            chunks(n, last)
            gin_copy.start()
            for i in range(own):
                at = (b * nr + r) * own + i // unit * unit
                p = S.idx[at // 128, lax.rem(at, 128) + i % unit]
                fast = (p >= 2 * C + 2 * FF + KL * KL) & ((p < BASE) | (p >= BASE + KS * KS))
                S.rate[pl.ds(i, 1), :] = jnp.full((1, 128), jnp.where(fast, np.float32(norm_rate), np.float32(matrix_rate)), f32)

        gin_copy = pltpu.make_async_copy(S.g_f, S.gin_hbm, S.load_sem.at[6])
        for_sibling(0)

        @pl.loop(0, nz + parts)
        def _(q):
            @pl.when(q < nz)
            def _():
                first_step(q)

            @pl.when(q == 0)
            def _():
                share_send(7, 1, share_wait(7, 0, merge_sum))

            if by_z:

                @pl.when(q == nz - 1)
                def _():
                    z_start()

            for t in range(parts - 1):

                @pl.when((q >= t + 1) & (q < nz + t + 1))
                def _():
                    next_step(q - t - 1, t)

            @pl.when(q == 1)
            def _():
                grad_image()

            if by_z:

                @pl.when(q == nz)
                def _():
                    for t in range(parts - 1):
                        z_next(t)

            @pl.when(q >= parts)
            def _():
                last_step(q - parts)

        for i in range(nz - 1):
            to_owner(i).wait_recv()
            tmp[pl.ds(0, main), :] += rows_in[z_base + i, pl.ds(0, main)].astype(f32)
        if by_z:
            z_next(parts - 1)
        for j in range(4):
            S.red[:, j * 128 : (j + 1) * 128] = tmp[pl.ds(j, own, stride=4), :]

        @pl.loop(0, nz)
        def _(i):
            for m in range(nb):
                to_sibling(i, m).wait_send()
            for p in range(parts):
                for t in range(parts):
                    hop_wait(i, p, t, S.hop_send)

        for i in range(nz - 1):
            to_owner(i).wait_send()
            if by_z:
                layer_wait(i, S.layer_send)
        if by_z:
            for p in range(parts):
                for t in range(parts):
                    z_hop_wait(p, t, S.z_hop_send)
        gin_copy.wait()

    low_block = lambda *lead: pltpu.VMEM(lead + (lines, 128), bf16)
    pl.run_scoped(tail, low_block(nz, nb), low_block(nz, nb), pltpu.VMEM((nz, main, 128), bf16))
    for e in range(len(WIDTHS)):
        for stage in range(2):
            buf, mine, count = share_stage(e, stage)
            sent = buf.at[pl.ds(0, count - 1)]
            pltpu.make_async_copy(sent, sent, S.stat_send.at[e, stage]).wait()
    out_copy.wait()


def step(x, cot, master, slots, nb, nr):
    (a, at, b, bt, bs, bst, c, ct) = tables()
    n, own, nz, parts = x.shape[0], master.shape[0], nr // 2, nb.bit_length() - 1
    total = slots.size
    vm = lambda *shape: pltpu.VMEM(shape, f32)
    low = lambda *shape: pltpu.VMEM(shape, bf16)
    dma = lambda *shape: pltpu.SemaphoreType.DMA(shape)
    vmem, anywhere = pl.BlockSpec(memory_space=pltpu.VMEM), pl.BlockSpec(memory_space=pl.ANY)
    ins = dict(
        slots_hbm=(slots, anywhere), x_hbm=(x, anywhere), cot_hbm=(cot, anywhere), master_hbm=(master, anywhere),
        a_hbm=(a, anywhere), at_hbm=(at, anywhere), b_hbm=(b, anywhere), bt_hbm=(bt, anywhere), bs=(bs, vmem), bst=(bst, vmem),
        c_hbm=(c, anywhere), ct_hbm=(ct, anywhere),
    )
    image = jax.ShapeDtypeStruct((n, C), f32)
    outs = dict(
        out_hbm=(image, anywhere), gin_hbm=(image, anywhere), red=(jax.ShapeDtypeStruct((own, C), f32), vmem),
        rate=(jax.ShapeDtypeStruct((own, 128), f32), vmem),
    )
    scratch = dict(
        rows_in=low(nb * nr, 4 * own, 128), flat=vm(4 * total, 128), tab=low(total, C), x=vm(n, C), cot=vm(n, C), master=vm(own, C),
        tmp=vm(4 * own, 128), chunk=vm(512, 128), inv=pltpu.VMEM((total // 128, 128), jnp.int32), at_v=pltpu.VMEM((total // 128, 128), jnp.int32),
        idx=pltpu.SMEM((total // 128, 128), jnp.int32),
        inv_at=pltpu.SMEM((total // 128, 128), jnp.int32), small=vm(48, C),
        pre_low=low(n, C), wide=low(3 * n, C), dz=vm(n, C), spec_u=vm(2 * NF, C), spec_l=vm(2 * NF, C), spec_s=vm(2 * NF, C),
        prod_l=low(2 * NF, C), prod_s=low(2 * NF, C), prod_k=low(2 * NF, C), d_l=vm(n, C), d_s=vm(n, C), s_val=vm(n, C),
        t_low=low(n, C), p_val=vm(n, C), mid=vm(n, C), c_low=low(n, C), gy_low=low(n, C), gp_low=low(n, C), g_f=vm(n, C), out=vm(n, C),
        halo_out=low(2, n, C), halo_in=low(2, n, C),
    )
    by_z = first_along_z(nb, 4 * own)
    if by_z:
        scratch.update(
            layer_in=low(nz - 1, nb, by_z, 128), z_hops=low(parts, nb - 1, by_z // parts, 128), layer_send=dma(nz), layer_recv=dma(nz),
            z_hop_send=dma(parts, parts), z_hop_recv=dma(parts, parts),
        )
    for e, w in enumerate(WIDTHS):
        one, two = (2, nb * nz) if by_chip(e, nb * nz) else (nr, nb)
        scratch[f"one{e}"] = vm(one, w, C)
        scratch[f"two{e}"] = vm(two, w, C)
    scratch.update(
        load_sem=dma(9), stat_send=dma(len(WIDTHS), 2), stat_recv=dma(len(WIDTHS), 2), halo_send=dma(4), halo_recv=dma(4),
        z_send=dma(nz), z_recv=dma(nz), b_send=dma(nb, nz), b_recv=dma(nb, nz), half_send=dma(2, nz), half_recv=dma(2, nz),
        core_send=dma(nb, nz), core_recv=dma(nb, nz), sib_send=dma(nz, nb), sib_recv=dma(nz, nb),
        hop_send=dma(nz, parts, parts), hop_recv=dma(nz, parts, parts), own_send=dma(nz), own_recv=dma(nz),
    )
    return pl.pallas_call(
        functools.partial(step_kernel, nb, nr, [*ins, *outs, *scratch]),
        out_shape=[v[0] for v in outs.values()],
        in_specs=[v[1] for v in ins.values()],
        out_specs=[v[1] for v in outs.values()],
        scratch_shapes=list(scratch.values()),
        compiler_params=pltpu.CompilerParams(collective_id=0, has_side_effects=True, vmem_limit_bytes=62 * 2**20),
    )(*[v[0] for v in ins.values()])


def finish_kernel(*refs):
    ins, outs, bufs, (load_sem, store_sem) = refs[:7], refs[7:14], refs[14:25], refs[25:]
    red, rate, first_ref, second_ref, master_ref, out, gin = bufs[:7]
    new_first, new_second, new_master, new_copy = bufs[7:11]
    loads = [pltpu.make_async_copy(src, dst, load_sem.at[i]) for i, (src, dst) in enumerate(zip(ins, bufs[:7]))]
    for copy in loads:
        copy.start()
    own = red.shape[0]
    size = 64 if own % 64 == 0 else own
    for copy in loads[:5]:
        copy.wait()
    stores = [pltpu.make_async_copy(red, outs[2], store_sem.at[2, 0])]
    stores[0].start()
    for part in range(own // size):
        for k in range(0, size, 8):
            s = slice(part * size + k, part * size + k + 8)
            for j in range(C // 128):
                at = (s, slice(j * 128, (j + 1) * 128))
                g = red[at]
                first = beta_one * first_ref[at] + (1.0 - beta_one) * g
                second = beta_two * second_ref[at] + (1.0 - beta_two) * g * g
                new_first[at] = first
                new_second[at] = second
                first_hat = first / (1.0 - beta_one**STEP)
                second_hat = second / (1.0 - beta_two**STEP)
                master = master_ref[at]
                new_master[at] = master - rate[s, :] * (first_hat / (jnp.sqrt(second_hat) + adam_eps) + decay_rate * master)
        s = pl.ds(part * size, size)
        new_copy[s, :] = new_master[s, :].astype(bf16)
        if part == 0:
            for i in (5, 6):
                loads[i].wait()
                stores.append(pltpu.make_async_copy(bufs[i], outs[i - 5], store_sem.at[i - 5, 0]))
                stores[-1].start()
        for i, buf in enumerate((new_first, new_second, new_master, new_copy)):
            stores.append(pltpu.make_async_copy(buf.at[s], outs[3 + i].at[s], store_sem.at[3 + i, part]))
            stores[-1].start()
    for copy in stores:
        copy.wait()


def finish(reduced, first, second, master, rates, out, gin):
    anywhere = pl.BlockSpec(memory_space=pl.ANY)
    slot = jax.ShapeDtypeStruct(reduced.shape, f32)
    image = jax.ShapeDtypeStruct(out.shape, f32)
    low = jax.ShapeDtypeStruct(reduced.shape, bf16)
    ins = (reduced, rates, first, second, master, out, gin)
    outs = [image, image, slot, slot, slot, slot, low]
    return pl.pallas_call(
        finish_kernel,
        out_shape=outs,
        in_specs=[anywhere] * 7,
        out_specs=[anywhere] * 7,
        scratch_shapes=[pltpu.VMEM(v.shape, f32) for v in ins]
        + [pltpu.VMEM(v.shape, v.dtype) for v in (slot, slot, slot, low)]
        + [pltpu.SemaphoreType.DMA((7,)), pltpu.SemaphoreType.DMA((7, 4))],
        compiler_params=pltpu.CompilerParams(vmem_limit_bytes=62 * 2**20),
    )(*ins)


def body(image_in, cotangent, slot_rows, master, first_moment, second_moment):
    n = image_in.shape[0] * image_in.shape[1] * image_in.shape[2]
    nb, nr = lax.axis_size("batch"), lax.axis_size("rows")
    out, grad_in, reduced, rates = step(
        image_in.reshape(n, C), cotangent.reshape(n, C), master, slot_rows.reshape(-1, 128), nb, nr
    )
    result, grad_x, *slots = finish(reduced, first_moment, second_moment, master, rates, out, grad_in)
    return (result.reshape(image_in.shape), grad_x.reshape(image_in.shape), *slots)


def solution(mesh):
    image = P("batch", "rows", None, None)
    owner = P(AXES, None)
    return jax.shard_map(
        body,
        mesh=mesh,
        in_specs=(image, image, P(), owner, owner, owner),
        out_specs=(image, image, owner, owner, owner, owner, owner),
        check_vma=False,
    )
```

```python
import functools
import types

import jax
import jax.numpy as jnp
import numpy as np
from jax import lax
from jax.experimental import pallas as pl
from jax.experimental.pallas import tpu as pltpu
from jax.sharding import PartitionSpec as P

C = 512
FF = 2048
KL = 31
KS = 5
STEP = 10

norm_eps = 1e-05
beta_one = 0.9
beta_two = 0.999
adam_eps = 1e-08
decay_rate = 0.05
matrix_rate = 0.05
norm_rate = 0.5

TH = 16
TW = 16
NY = 47
NX = 31
NF = 768
REACH = (KL - 1) // 2
AXES = ("batch", "rows")
f32 = jnp.float32
bf16 = jnp.bfloat16


@functools.lru_cache(None)
def tables():
    freqs = [(ky, 0) for ky in range((NY + 1) // 2)]
    freqs += [(ky, kx) for kx in range(1, (NX + 1) // 2) for ky in range(NY)]
    ky = np.array([f[0] for f in freqs], np.int64)[:, None]
    kx = np.array([f[1] for f in freqs], np.int64)[:, None]
    pad = NF - len(freqs)

    def angle(rows, cols):
        ty = (ky * rows.reshape(1, -1)) % NY
        tx = (kx * cols.reshape(1, -1)) % NX
        return 2 * np.pi * (ty / NY + tx / NX)

    def grid(rows, cols):
        r, c = np.meshgrid(rows, cols, indexing="ij")
        return r.reshape(-1), c.reshape(-1)

    def stack(re, im):
        z = np.zeros((pad, re.shape[1]))
        return np.concatenate([re, z, im, z], axis=0)

    r, c = grid(np.arange(-TH, 2 * TH), np.arange(TW))
    used = ((r + REACH >= 0) & (r + REACH < NY - 1)).astype(np.float64)[None]
    t = angle(r + REACH, c)
    a = stack(np.cos(t) * used, -np.sin(t) * used)
    i, j = grid(np.arange(KL), np.arange(KL))
    t = angle(i, j - REACH)
    b = stack(np.cos(t), -np.sin(t))
    lead = REACH - (KS - 1) // 2
    small = ((i >= lead) & (i < lead + KS) & (j >= lead) & (j < lead + KS)).nonzero()[0]
    bs = np.pad(b[:, small], ((0, 0), (0, 32 - KS * KS)))
    b = np.pad(b, ((0, 0), (0, 2 * C - KL * KL)))
    y, x = grid(np.arange(TH), np.arange(TW))
    t = angle(y, x)
    w = np.full((len(freqs), 1), 2.0)
    w[0] = 1.0
    w /= NY * NX
    ct = stack(w * np.cos(t), -w * np.sin(t))
    return tuple(m.astype(np.float32).astype(bf16) for m in (a, a.T, b, b.T, bs, bs.T, ct.T, ct))


def dot(a, b, dims=(1, 0)):
    return lax.dot_general(a, b, (((dims[0],), (dims[1],)), ((), ())), preferred_element_type=f32)


MESH = pl.DeviceIdType.MESH
WIDTHS = (2, 4, 3, 8, 8, 5, 3, 2)
BY_CHIP = (1, 2, 5, 6)
BASE = 2 * C + 2 * FF + 976


def chunks(n, fn, init=()):
    return lax.fori_loop(0, n // 32, lambda i, c: fn(pl.ds(pl.multiple_of(i * 32, 32), 32), c), init)


def fold(v):
    return jnp.sum(v.reshape(v.shape[0] // 8, 8, v.shape[1]), axis=0)


def close(v):
    return jnp.sum(v, axis=0, keepdims=True)


def put(ref, start, v):
    for j in range(4):
        ref[pl.ds(start * 4 + j, v.shape[0], stride=4), :] = v[:, j * 128 : (j + 1) * 128]


def gelu_both(v):
    a = np.float32(np.sqrt(2 / np.pi))
    sq = v * v
    t = jnp.tanh(a * (v + 0.044715 * (sq * v)))
    half = 0.5 * (1 + t)
    return v * half, half + 0.5 * v * (1 - t * t) * (a * (1 + 3 * 0.044715 * sq))


def flip(b, m):
    k = 0
    while m >> k:
        if (m >> k) & 1:
            b = b + (1 - 2 * lax.rem(b // 2**k, 2)) * 2**k
        k += 1
    return b


def reduce_plan(nb):
    bits = nb.bit_length() - 1
    plan = []
    for p in range(bits):
        order = [(p + t) % bits for t in range(bits)]
        steps, kept = [], list(range(nb))
        for o in order:
            sent = [m for m in kept if (m >> o) & 1]
            kept = [m for m in kept if not (m >> o) & 1]
            steps.append((o, sent, kept))
        plan.append(steps)
    return plan


def first_along_z(nb, lines):
    return lines // 6 if nb == 4 and lines % 192 == 0 else 0


def by_chip(e, chips):
    return e in BY_CHIP and chips <= 32


def merge_sum(v, count):
    return jnp.sum(v, axis=0)


def merge_stats(h):
    def merge(v, count):
        means = v[:, :h]
        m = jnp.sum(means, axis=0) * (1.0 / v.shape[0])
        d = means - m
        parts = [m, jnp.sum(v[:, h : 2 * h], axis=0) + count * jnp.sum(d * d, axis=0)]
        if v.shape[1] > 2 * h:
            parts.append(jnp.sum(v[:, 2 * h :], axis=0))
        return jnp.concatenate(parts, axis=0)

    return merge


def local(read, n):
    zero = jnp.zeros((8, C), f32)
    m = close(chunks(n, lambda s, c: c + fold(read(s)), zero)) * (1.0 / n)

    def sq(s, c):
        d = read(s) - m
        return c + fold(d * d)

    return m, close(chunks(n, sq, zero))


def half_cols(h):
    return pl.ds(pl.multiple_of(h * 256, 256), 256)


def up_rows(j):
    return pl.ds(pl.multiple_of(2 * C + j * C, C), C)


def down_rows(j):
    return pl.ds(pl.multiple_of(2 * C + FF + j * C, C), C)


def table_place(t):
    start = 2 * C + 2 * FF
    k_end = start + KL * KL
    s_end = k_end + KS * KS
    m_gain = s_end + 10
    m_bias = m_gain + FF // C
    m_end = m_bias + FF // C
    up = t - 2 * C
    up = 2 * C + (up & (FF // C - 1)) * C + (up >> ((FF // C).bit_length() - 1))
    base = start + 976
    unused = t - m_end
    unused = jnp.where(unused < 15, k_end + unused, jnp.where(unused < 18, base + 29 + unused - 15, base + 46 + unused - 18))
    p = jnp.where((t >= 2 * C) & (t < 2 * C + FF), up, t)
    p = jnp.where(t >= k_end, t - k_end + base, p)
    p = jnp.where(t >= s_end, t - s_end + base + 32, p)
    p = jnp.where(t >= m_bias, t - m_bias + base + 25, p)
    return jnp.where(t >= m_end, unused, p)


def step_kernel(nb, nr, names, *refs):
    S = types.SimpleNamespace(**dict(zip(names, refs)))
    nz = nr // 2
    nd = nb * nr
    n = S.x.shape[0]
    own = S.master.shape[0]
    lines = 4 * own
    total = S.tab.shape[0]
    every = float(n * nd)
    b = lax.axis_index("batch")
    r = lax.axis_index("rows")
    z, c = r // 2, lax.rem(r, 2)
    sibling = (b, r + 1 - 2 * c)
    square = nb == 4
    blocks = FF // C
    zero = jnp.zeros((8, C), f32)
    rows_in = S.rows_in

    def load(i, src, dst):
        return pltpu.make_async_copy(src, dst, S.load_sem.at[i])

    ld_m, ld_x, ld_c = load(0, S.master_hbm, S.master), load(1, S.x_hbm, S.x), load(2, S.cot_hbm, S.cot)
    ld_s = load(8, S.slots_hbm, S.at_v)
    for copy in (ld_s, ld_m, ld_x, ld_c):
        copy.start()
    barrier = pltpu.get_barrier_semaphore()
    for k in range(1, nr):
        pl.semaphore_signal(barrier, inc=1, device_id=(b, lax.rem(r + k, nr)), device_id_type=MESH)
    for m in range(1, nb):
        pl.semaphore_signal(barrier, inc=1, device_id=(flip(b, m), r), device_id_type=MESH)

    @pl.loop(0, (nb - 1) * (nz - 1))
    def _(k):
        at = (lax.rem(b + 1 + k // (nz - 1), nb), 2 * lax.rem(z + 1 + lax.rem(k, nz - 1), nz) + c)
        pl.semaphore_signal(barrier, inc=1, device_id=at, device_id_type=MESH)


    def share_stage(e, stage):
        buf = getattr(S, ("one" if stage == 0 else "two") + str(e))
        if by_chip(e, nb * nz):
            return (buf, c, 2) if stage == 0 else (buf, b * nz + z, nb * nz)
        return (buf, r, nr) if stage == 0 else (buf, b, nb)

    def share_peer(e, stage, k):
        if by_chip(e, nb * nz):
            if stage == 0:
                return sibling
            other = lax.rem(b * nz + z + k, nb * nz)
            return (other // nz, 2 * lax.rem(other, nz) + c)
        return (b, lax.rem(r + k, nr)) if stage == 0 else (lax.rem(b + k, nb), r)

    def share_send(e, stage, v):
        buf, mine, size = share_stage(e, stage)
        buf[mine] = v

        def one(k):
            pltpu.make_async_remote_copy(
                buf.at[mine], buf.at[mine], S.stat_send.at[e, stage], S.stat_recv.at[e, stage],
                device_id=share_peer(e, stage, k), device_id_type=MESH,
            ).start()

        if size > 8:
            pl.loop(1, size)(one)
        else:
            for k in range(1, size):
                one(k)

    def share_wait(e, stage, merge):
        buf, mine, size = share_stage(e, stage)
        got = buf.at[pl.ds(0, size - 1)]
        pltpu.make_async_copy(got, got, S.stat_recv.at[e, stage]).wait()
        return merge(buf[...], float(n if stage == 0 else n * getattr(S, f"one{e}").shape[0]))

    def share(e, v, merge, work=None, more=None):
        share_send(e, 0, v)
        if work and not by_chip(e, nb * nz):
            work()
        v = share_wait(e, 0, merge)
        share_send(e, 1, v)
        if work and by_chip(e, nb * nz):
            work()
        if more:
            more()
        return share_wait(e, 1, merge)


    def place(m, zz, core):
        return flip(b, m) * nr + 2 * zz + core

    spread = first_along_z(nb, lines)
    rest = pl.ds(lines - spread, spread)

    def lines_of(k):
        return lines if k == 0 else lines - spread

    def part(m, zz, core, k):
        return rows_in.at[place(m, zz, core), pl.ds(0, lines_of(k))]

    def along_z(zz, up):
        at = part(0, zz, c, 1)
        return pltpu.make_async_remote_copy(
            at, at, S.z_send.at[zz], S.z_recv.at[zz], device_id=(b, r + 2 if up else r - 2), device_id_type=MESH
        )

    def to_peer(m, zz, k):
        at = part(0, zz, c, k)
        return pltpu.make_async_remote_copy(
            at, at, S.b_send.at[m, zz], S.b_recv.at[m, zz], device_id=(flip(b, m), r), device_id_type=MESH
        )

    def from_peer(m, zz, k):
        at = part(m, zz, c, k)
        return pltpu.make_async_copy(at, at, S.b_recv.at[m, zz])

    def half(m, zz, h, to, k):
        size = lines_of(k) // 2
        at = rows_in.at[place(m, zz, c), pl.ds(h * size, size)]
        return pltpu.make_async_remote_copy(
            at, at, S.half_send.at[h, zz], S.half_recv.at[h, zz], device_id=(flip(b, to), r), device_id_type=MESH
        )

    def to_other_core(m, zz, core, k):
        at = part(m, zz, core, k)
        return pltpu.make_async_remote_copy(
            at, at, S.core_send.at[m, zz], S.core_recv.at[m, zz], device_id=sibling, device_id_type=MESH
        )

    def cast(m, zz, core, k):
        d = place(m, zz, core)
        S.flat[pl.ds(pl.multiple_of(d * lines, lines), lines_of(k)), :] = rows_in[d, pl.ds(0, lines_of(k))].astype(f32)

    def rest_out(m, zz):
        at = rows_in.at[place(m, z, c), rest]
        return pltpu.make_async_remote_copy(
            at, at, S.rest_send.at[m, zz], S.rest_recv.at[m, z], device_id=(b, 2 * zz + c), device_id_type=MESH
        )

    def rest_in(m, zz):
        at = rows_in.at[place(m, zz, c), rest]
        return pltpu.make_async_copy(at, at, S.rest_recv.at[m, zz])

    def rest_to_core(m, zz, core):
        at = rows_in.at[place(m, zz, core), rest]
        return pltpu.make_async_remote_copy(
            at, at, S.rest_core_send.at[m, zz], S.rest_core_recv.at[m, zz], device_id=sibling, device_id_type=MESH
        )

    def rest_cast(m, zz, core):
        d = place(m, zz, core)
        S.flat[pl.ds(pl.multiple_of(d * lines + lines - spread, 64), spread), :] = rows_in[d, rest].astype(f32)

    direct = [m for m in range(1, nb) if not (square and m == 3)]

    def each(k, fn):
        if k == 0:
            fn(z, True, True)
            return

        @pl.when(z >= k)
        def _():
            fn(z - k, True, False)

        @pl.when(z + k < nz)
        def _():
            fn(z + k, False, True)

    def onward(zz, below, above, act):
        if below:

            @pl.when(z < nz - 1)
            def _():
                act(along_z(zz, True))

        if above:

            @pl.when(z > 0)
            def _():
                act(along_z(zz, False))

    def own_column(k):
        def go(zz, below, above):
            if k:
                along_z(zz, below).wait_recv()
            onward(zz, below, above, lambda copy: copy.start())
            for m in direct:
                to_peer(m, zz, k).start()
            to_other_core(0, zz, c, k).start()
            cast(0, zz, c, k)

        each(k, go)

    def pass_on(k):
        def go(zz, below, above):
            for m in direct:
                from_peer(m, zz, k).wait()
                if square:
                    half(m, zz, 2 - m, 3 - m, k).start()
                to_other_core(m, zz, c, k).start()
                cast(m, zz, c, k)

        each(k, go)

    def corner(k):
        def go(zz, below, above):
            for h in range(2):
                half(3, zz, h, 0, k).wait_recv()
            if k == 0 and spread:
                for d in range(1, nz):
                    for m in range(nb):
                        rest_out(m, lax.rem(z + d, nz)).start()
            to_other_core(3, zz, c, k).start()
            cast(3, zz, c, k)

        if square:
            each(k, go)

    def other_core(k):
        def go(zz, below, above):
            for m in range(nb):
                to_other_core(m, zz, 1 - c, k).wait_recv()
                cast(m, zz, 1 - c, k)

        each(k, go)

    def rest_here(k):
        def go(zz, below, above):
            for m in range(nb):
                rest_in(m, zz).wait()
                rest_to_core(m, zz, c).start()
                rest_cast(m, zz, c)

        if spread:
            each(k, go)

    def rest_there(k):
        def go(zz, below, above):
            for m in range(nb):
                rest_to_core(m, zz, 1 - c).wait_recv()
                rest_cast(m, zz, 1 - c)

        if spread:
            each(k, go)

    def gather_sent(k):
        def go(zz, below, above):
            onward(zz, below, above, lambda copy: copy.wait_send())
            for m in direct:
                to_peer(m, zz, k).wait_send()
                if square:
                    half(m, zz, 2 - m, 3 - m, k).wait_send()
            for m in range(nb):
                to_other_core(m, zz, c, k).wait_send()
                if spread and k:
                    rest_out(m, zz).wait_send()
                    rest_to_core(m, zz, c).wait_send()

        each(k, go)

    def find(part, parts):
        tiles = total // 1024
        unit = 16
        spots = [
            lax.broadcasted_iota(jnp.int32, (8, 128), 0) * 128 + lax.broadcasted_iota(jnp.int32, (8, 128), 1) + 1024 * k
            for k in range(tiles)
        ]

        def some(g, acc):
            for u in range(unit):
                start = g * unit
                s = start + u
                p = S.idx[start // 128, lax.rem(start, 128) + u]
                acc = [jnp.where(spot == p, s, a) for spot, a in zip(spots, acc)]
            return acc

        acc = [S.inv[k * 8 : k * 8 + 8, :] if part else jnp.zeros((8, 128), jnp.int32) for k in range(tiles)]
        groups = total // unit
        acc = lax.fori_loop(groups * part // parts, groups * (part + 1) // parts, some, acc)
        for k in range(tiles):
            S.inv[k * 8 : k * 8 + 8, :] = acc[k]

    def order(start, stop):
        flat = S.flat.reshape(total, 4, 128)

        @pl.loop(start, stop)
        def _(t):
            for u in range(128):
                S.chunk[4 * u : 4 * u + 4, :] = flat[S.inv_at[t, u]]

            rows = pl.ds(pl.multiple_of(t * 128, 128), 128)
            for j in range(4):
                S.tab[rows, j * 128 : (j + 1) * 128] = S.chunk[pl.ds(j, 128, stride=4), :].astype(bf16)

    def front(ta, tb, tc):
        ld_a, ld_b, ld_t = load(3, S.a_hbm, ta), load(4, S.b_hbm, tb), load(5, S.c_hbm, tc)
        for copy in (ld_b, ld_a, ld_t):
            copy.start()
        ld_s.wait()
        S.at_v[...] = table_place(S.at_v[...])
        to_scalar = pltpu.make_async_copy(S.at_v, S.idx, S.load_sem.at[8])
        to_scalar.start()
        ld_m.wait()
        for j in range(4):
            S.tmp[pl.ds(j, own, stride=4), :] = S.master[:, j * 128 : (j + 1) * 128]
        rows_in[place(0, z, c)] = S.tmp[...].astype(bf16)
        pl.semaphore_wait(barrier, nr - 1 + nb - 1 + (nb - 1) * (nz - 1))
        own_column(0)
        to_scalar.wait()
        ld_x.wait()
        share_send(0, 0, jnp.concatenate(local(lambda s: S.x[s, :], n), axis=0))
        steps = 3 * max(nz - 1, 1)
        for k in range(1, nz):
            find(3 * k - 3, steps)
            own_column(k)
            find(3 * k - 2, steps)
            pass_on(k - 1)
            find(3 * k - 1, steps)
            if k > 1:
                corner(k - 2)
            if k > 2:
                other_core(k - 3)
            if k == 1:
                share_send(0, 1, share_wait(0, 0, merge_stats(1)))
        if nz == 1:
            for part in range(3):
                find(part, 3)
            share_send(0, 1, share_wait(0, 0, merge_stats(1)))
        to_scalar = pltpu.make_async_copy(S.inv, S.inv_at, S.load_sem.at[6])
        to_scalar.start()
        pass_on(nz - 1)
        for k in range(max(nz - 2, 0), nz - 1):
            corner(k)
        for k in range(1, nz):
            rest_here(k)
        corner(nz - 1)
        for k in range(max(nz - 3, 0), nz):
            other_core(k)
        for k in range(1, nz):
            rest_there(k)
        tot = share_wait(0, 1, merge_stats(1))
        m_x, q_x = tot[0:1], tot[1:2] * (1.0 / every)
        inv_x = lax.rsqrt(q_x + norm_eps)
        to_scalar.wait()
        tiles = total // 128
        late = (2 * C + 2 * FF) // 128
        order(0, C // 128)
        order(tiles - 2, tiles)

        for k in range(nz):
            gather_sent(k)

        small = S.tab[pl.ds(BASE, 48), :].astype(f32)
        S.small[...] = small
        row = lambda i: small[32 + i : 33 + i, :]

        def pre(s, sx):
            d = S.x[s, :] - m_x
            S.pre_low[s, :] = (d * (inv_x * row(0)) + row(1)).astype(bf16)
            return sx + fold(d)

        sum_x = close(chunks(n, pre, zero))
        S.dz[...] = dot(S.pre_low[...], S.tab[pl.ds(0, C), :])

        def act(s, a):
            u, d = gelu_both(S.dz[s, :])
            S.dz[s, :] = d
            S.wide[pl.ds(pl.multiple_of(n + s.start, 32), 32), :] = u.astype(bf16)
            return a

        chunks(n, act)
        mine = S.wide.at[pl.ds(n, n)]
        halo_up = halo(0, mine, S.wide.at[pl.ds(2 * n, n)], True)
        halo_down = halo(1, mine, S.wide.at[pl.ds(0, n)], False)
        halo_start(halo_up, halo_down)
        order(late, tiles - 2)
        order(C // 128, 2 * C // 128)

        ld_b.wait()

        @pl.loop(0, 2 * NF // 256)
        def _(t):
            s = pl.ds(pl.multiple_of(t * 256, 256), 256)
            S.spec_l[s, :] = dot(tb[s, :], S.tab[pl.ds(2 * C + 2 * FF, 2 * C), :])
            S.spec_s[s, :] = dot(S.bs[s, :], S.tab[pl.ds(BASE, 32), :])

        halo_wait(halo_up, halo_down, S.wide.at[pl.ds(0, n)], S.wide.at[pl.ds(2 * n, n)])
        ld_a.wait()

        @pl.loop(0, 2 * NF // 256)
        def _(t):
            s = pl.ds(pl.multiple_of(t * 256, 256), 256)
            S.spec_u[s, :] = dot(ta[s, :], S.wide[...])

        @pl.loop(0, NF // 32)
        def _(i):
            re, im = pl.ds(pl.multiple_of(i * 32, 32), 32), pl.ds(pl.multiple_of(NF + i * 32, 32), 32)
            ur, ui = S.spec_u[re, :], S.spec_u[im, :]
            for k, p in ((S.spec_l, S.prod_l), (S.spec_s, S.prod_s)):
                kr, ki = k[re, :], k[im, :]
                p[re, :] = (ur * kr + ui * ki).astype(bf16)
                p[im, :] = (ui * kr - ur * ki).astype(bf16)

        ld_t.wait()
        S.d_l[...] = dot(tc[...], S.prod_l[...])
        S.d_s[...] = dot(tc[...], S.prod_s[...])
        return m_x, q_x, sum_x


    has_above, has_below = r > 0, r < nr - 1

    def halo(i, src, dst, up):
        peer = lax.rem(r + nr - 1, nr) if up else lax.rem(r + 1, nr)
        return pltpu.make_async_remote_copy(
            src, dst, S.halo_send.at[i], S.halo_recv.at[i], device_id=(b, peer), device_id_type=MESH
        )

    def halo_start(up, down):
        @pl.when(has_above)
        def _():
            up.start()

        @pl.when(has_below)
        def _():
            down.start()

    def halo_wait(up, down, above, below):
        @pl.when(has_below)
        def _():
            up.wait_recv()
            down.wait_send()

        @pl.when(has_above)
        def _():
            down.wait_recv()
            up.wait_send()

        @pl.when(jnp.logical_not(has_above))
        def _():
            above[...] = jnp.zeros((n, C), bf16)

        @pl.when(jnp.logical_not(has_below))
        def _():
            below[...] = jnp.zeros((n, C), bf16)

    m_x, q_x, sum_x = pl.run_scoped(
        front, pltpu.VMEM(S.a_hbm.shape, bf16), pltpu.VMEM(S.b_hbm.shape, bf16), pltpu.VMEM(S.c_hbm.shape, bf16)
    )
    inv_x = lax.rsqrt(q_x + norm_eps)
    small = S.small[...]
    row = lambda i: small[32 + i : 33 + i, :]
    mid_gain = lambda j: small[42 + j : 43 + j, :]
    mid_bias = lambda j: small[25 + j : 26 + j, :]
    m_l, v_l = local(lambda s: S.d_l[s, :], n)
    m_s, v_s = local(lambda s: S.d_s[s, :], n)
    ld_c.wait()

    def early():
        order(2 * C // 128, (2 * C + FF) // 128)

        def low(s, a):
            S.gy_low[s, :] = S.cot[s, :].astype(bf16)
            return a

        chunks(n, low)

    tot = share(
        1, jnp.concatenate([m_l, m_s, v_l, v_s], axis=0), merge_stats(2), early,
        lambda: order((2 * C + FF) // 128, (2 * C + 2 * FF) // 128),
    )
    m_l, m_s = tot[0:1], tot[1:2]
    inv_l, inv_s = lax.rsqrt(tot[2:3] / every + norm_eps), lax.rsqrt(tot[3:4] / every + norm_eps)

    def pair(s, a):
        hl = (S.d_l[s, :] - m_l) * inv_l
        hs = (S.d_s[s, :] - m_s) * inv_s
        S.d_l[s, :] = hl
        S.d_s[s, :] = hs
        t, d = gelu_both(hl * row(2) + row(3) + hs * row(4) + row(5))
        S.s_val[s, :] = d
        S.t_low[s, :] = t.astype(bf16)
        return a

    chunks(n, pair)
    S.p_val[...] = dot(S.t_low[...], S.tab[pl.ds(C, C), :])
    m_p = close(chunks(n, lambda s, a: a + fold(S.p_val[s, :]), zero)) * (1.0 / n)

    def proj(s, a):
        d = S.p_val[s, :] - m_p
        return a[0] + fold(d * d), a[1] + fold(d * (S.x[s, :] - m_x))

    v_p, cross = chunks(n, proj, (zero, zero))
    tot = share(2, jnp.concatenate([m_p, close(v_p), close(cross) + m_p * sum_x], axis=0), merge_stats(1))
    m_p, q_p, cov = tot[0:1], tot[1:2] / every, tot[2:3] / every
    inv_p = lax.rsqrt(q_p + norm_eps)
    slope = row(6) * inv_p
    m_f = m_x + row(7)
    q_f = jnp.maximum(q_x + 2 * slope * cov + slope * slope * q_p, 0.0)
    inv_f = lax.rsqrt(q_f + norm_eps)
    hats = inv_f * inv_p * (cov + slope * q_p)

    def ffn(s, a):
        ph = (S.p_val[s, :] - m_p) * inv_p
        S.p_val[s, :] = ph
        m = S.x[s, :] + (ph * row(6) + row(7))
        S.mid[s, :] = m
        S.c_low[s, :] = ((m - m_f) * (inv_f * row(8)) + row(9)).astype(bf16)
        g = S.cot[s, :]
        return a[0] + fold(g), a[1] + fold(g * ph)

    sum_c, sum_ch = chunks(n, ffn, (zero, zero))
    sum_c, sum_ch = close(sum_c), close(sum_ch)

    def middle(hid, gact, a_low, gh_low):
        for j in range(blocks):
            hid[j] = dot(S.c_low[...], S.tab[up_rows(j), :])
        st = [local(lambda s, j=j: hid[j, s, :], n) for j in range(blocks)]

        def back_first():
            for j in range(blocks):
                gact[j] = dot(S.gy_low[...], S.tab[down_rows(j), :], (1, 1))

        tot = share(3, jnp.concatenate([s[0] for s in st] + [s[1] for s in st], axis=0), merge_stats(blocks), back_first)
        m_h = tot[:blocks]
        inv_h = lax.rsqrt(tot[blocks:] / every + norm_eps)
        sums = []
        for j in range(blocks):
            mj, ij, gj, bj = m_h[j : j + 1], inv_h[j : j + 1], mid_gain(j), mid_bias(j)

            def hidden(s, a, j=j, mj=mj, ij=ij, gj=gj, bj=bj):
                hat = (hid[j, s, :] - mj) * ij
                hid[j, s, :] = hat
                v, d = gelu_both(hat * gj + bj)
                a_low[j, s, :] = v.astype(bf16)
                g = gact[j, s, :] * d
                gact[j, s, :] = g
                return a[0] + fold(g), a[1] + fold(g * hat)

            sums.append(tuple(close(v) for v in chunks(n, hidden, (zero, zero))))
        mid_rows = jnp.concatenate([s[0] for s in sums] + [s[1] for s in sums], axis=0)

        def down_grads():
            for j in range(blocks):
                for h in range(C // 256):
                    put(S.flat, 2 * C + FF + j * C + h * 256, dot(a_low[j, :, half_cols(h)], S.gy_low[...], (0, 0)))

        def outputs():
            S.out[...] = S.mid[...]
            for j in range(blocks):
                S.out[...] += dot(a_low[j], S.tab[down_rows(j), :])

        tot = share(4, mid_rows, merge_sum, down_grads, outputs) * (1.0 / every)
        out_copy.start()
        for j in range(blocks):
            tb_, tg_, sc = tot[j : j + 1], tot[blocks + j : blocks + j + 1], mid_gain(j) * inv_h[j : j + 1]

            def grad_h(s, a, j=j, tb_=tb_, tg_=tg_, sc=sc):
                gh_low[j, s, :] = (sc * (gact[j, s, :] - tb_ - hid[j, s, :] * tg_)).astype(bf16)
                return a

            chunks(n, grad_h)
        S.g_f[...] = dot(gh_low[0], S.tab[up_rows(0), :], (1, 1))
        for j in range(1, blocks):
            S.g_f[...] += dot(gh_low[j], S.tab[up_rows(j), :], (1, 1))

        def ffn_sums(s, a):
            g = S.g_f[s, :]
            hat = (S.mid[s, :] - m_f) * inv_f
            return a[0] + fold(g), a[1] + fold(g * hat), a[2] + fold(g * S.p_val[s, :])

        b_ffn, g_ffn, g_fp = (close(v) for v in chunks(n, ffn_sums, (zero, zero, zero)))

        def grad_up():
            for j in range(blocks):
                for h in range(C // 256):
                    put(S.flat, 2 * C + j * C + h * 256, dot(S.c_low[:, half_cols(h)], gh_low[j], (0, 0)))

        tot = share(5, jnp.concatenate([b_ffn, g_ffn, g_fp, sum_c, sum_ch], axis=0), merge_sum, grad_up) * (1.0 / every)
        return mid_rows, b_ffn, g_ffn, tot

    out_copy = pltpu.make_async_copy(S.out, S.out_hbm, S.load_sem.at[7])
    hidden_shape = (blocks, n, C)
    mid_rows, b_ffn, g_ffn, tot = pl.run_scoped(
        middle, pltpu.VMEM(hidden_shape, f32), pltpu.VMEM(hidden_shape, f32), pltpu.VMEM(hidden_shape, bf16), pltpu.VMEM(hidden_shape, bf16)
    )

    def back(tat, tbt, tct, acc):
        ld_ct, ld_at, ld_bt = load(3, S.ct_hbm, tct), load(4, S.at_hbm, tat), load(5, S.bt_hbm, tbt)
        for copy in (ld_ct, ld_at, ld_bt):
            copy.start()
        scale_f = row(8) * inv_f
        mean_hat = tot[4:5] + scale_f * (tot[2:3] - tot[1:2] * hats)

        def grad_mid(s, a):
            hat = (S.mid[s, :] - m_f) * inv_f
            g = S.cot[s, :] + scale_f * (S.g_f[s, :] - tot[0:1] - hat * tot[1:2])
            S.g_f[s, :] = g
            ph = S.p_val[s, :]
            S.gp_low[s, :] = (slope * (g - tot[3:4] - ph * mean_hat)).astype(bf16)
            return a[0] + fold(g), a[1] + fold(g * ph)

        b_proj, g_proj = (close(v) for v in chunks(n, grad_mid, (zero, zero)))
        S.p_val[...] = dot(S.gp_low[...], S.tab[pl.ds(C, C), :], (1, 1))

        def grad_s(s, a):
            g = S.p_val[s, :] * S.s_val[s, :]
            S.p_val[s, :] = g
            return a[0] + fold(g), a[1] + fold(g * S.d_l[s, :]), a[2] + fold(g * S.d_s[s, :])

        b_pair, g_lg, g_sg = (close(v) for v in chunks(n, grad_s, (zero, zero, zero)))

        def grad_out():
            for h in range(C // 256):
                put(S.flat, C + h * 256, dot(S.t_low[:, half_cols(h)], S.gp_low[...], (0, 0)))

        sums = share(6, jnp.concatenate([b_pair, g_lg, g_sg], axis=0), merge_sum, grad_out) * (1.0 / every)
        sc_l, sc_s = row(2) * inv_l, row(4) * inv_s
        gl_low, gs_low = S.t_low, S.gp_low

        def grad_pair(s, a):
            g = S.p_val[s, :] - sums[0:1]
            gl_low[s, :] = (sc_l * (g - S.d_l[s, :] * sums[1:2])).astype(bf16)
            gs_low[s, :] = (sc_s * (g - S.d_s[s, :] * sums[2:3])).astype(bf16)
            return a

        chunks(n, grad_pair)
        ld_ct.wait()

        @pl.loop(0, NF // 256)
        def _(t):
            re, im = pl.ds(pl.multiple_of(t * 256, 256), 256), pl.ds(pl.multiple_of(NF + t * 256, 256), 256)
            acc[0] = dot(tct[re, :], gl_low[...])
            acc[1] = dot(tct[im, :], gl_low[...])
            acc[2] = dot(tct[re, :], gs_low[...])
            acc[3] = dot(tct[im, :], gs_low[...])

            @pl.loop(0, 8)
            def _(i):
                s = pl.ds(pl.multiple_of(i * 32, 32), 32)
                re = pl.ds(pl.multiple_of(t * 256 + i * 32, 32), 32)
                im = pl.ds(pl.multiple_of(NF + t * 256 + i * 32, 32), 32)
                lr, li, sr, si = acc[0, s, :], acc[1, s, :], acc[2, s, :], acc[3, s, :]
                kr, ki = S.spec_l[re, :], S.spec_l[im, :]
                hr, hi = S.spec_s[re, :], S.spec_s[im, :]
                S.prod_k[re, :] = (lr * kr - li * ki + sr * hr - si * hi).astype(bf16)
                S.prod_k[im, :] = (lr * ki + li * kr + sr * hi + si * hr).astype(bf16)
                ur, ui = S.spec_u[re, :], S.spec_u[im, :]
                S.prod_l[re, :] = (lr * ur + li * ui).astype(bf16)
                S.prod_l[im, :] = (lr * ui - li * ur).astype(bf16)
                S.prod_s[re, :] = (sr * ur + si * ui).astype(bf16)
                S.prod_s[im, :] = (sr * ui - si * ur).astype(bf16)

        ld_at.wait()
        halo_up = halo(2, S.halo_out.at[0], S.halo_in.at[1], True)
        halo_down = halo(3, S.halo_out.at[1], S.halo_in.at[0], False)
        S.halo_out[0] = dot(tat[pl.ds(0, n), :], S.prod_k[...]).astype(bf16)

        @pl.when(has_above)
        def _():
            halo_up.start()

        S.halo_out[1] = dot(tat[pl.ds(2 * n, n), :], S.prod_k[...]).astype(bf16)

        @pl.when(has_below)
        def _():
            halo_down.start()

        S.p_val[...] = dot(tat[pl.ds(n, n), :], S.prod_k[...])
        ld_bt.wait()

        @pl.loop(0, 4)
        def _(t):
            s = pl.ds(pl.multiple_of(t * 256, 256), 256)
            put(S.flat, 2 * C + 2 * FF + t * 256, dot(tbt[s, :], S.prod_l[...]))

        put(S.flat, BASE, dot(S.bst[...], S.prod_s[...]))
        halo_wait(halo_up, halo_down, S.halo_in.at[0], S.halo_in.at[1])
        gz_low = S.t_low

        def grad_z(s, a):
            g = S.p_val[s, :] + S.halo_in[0, s, :].astype(f32) + S.halo_in[1, s, :].astype(f32)
            gz_low[s, :] = (g * S.dz[s, :]).astype(bf16)
            return a

        chunks(n, grad_z)
        S.p_val[...] = dot(gz_low[...], S.tab[pl.ds(0, C), :], (1, 1))

        def pre_sums(s, a):
            g = S.p_val[s, :]
            return a[0] + fold(g), a[1] + fold(g * ((S.x[s, :] - m_x) * inv_x))

        b_pre, g_pre = (close(v) for v in chunks(n, pre_sums, (zero, zero)))
        share_send(7, 0, jnp.concatenate([b_pre, g_pre], axis=0))
        for h in range(C // 256):
            put(S.flat, h * 256, dot(S.pre_low[:, half_cols(h)], gz_low[...], (0, 0)))
        norms = [g_pre, b_pre, g_lg, b_pair, g_sg, b_pair, g_proj, b_proj, g_ffn, b_ffn]
        norms += [mid_rows[blocks + j : blocks + j + 1] for j in range(blocks)]
        put(S.flat, BASE + 32, jnp.concatenate(norms + [jnp.zeros((2, C), f32)], axis=0))
        for j in range(blocks):
            for k in range(4):
                S.flat[pl.ds((BASE + 25 + j) * 4 + k, 1), :] = mid_rows[j : j + 1, k * 128 : (k + 1) * 128]

    pl.run_scoped(
        back, pltpu.VMEM(S.at_hbm.shape, bf16), pltpu.VMEM(S.bt_hbm.shape, bf16), pltpu.VMEM(S.ct_hbm.shape, bf16), pltpu.VMEM((4, 256, C), f32)
    )


    plan = reduce_plan(nb)
    parts = len(plan)
    by_z = first_along_z(nb, lines)
    main = lines - by_z
    size = main // parts
    z_size = by_z // parts
    unit = 64 if own % 64 == 0 else 8
    tmp = S.tmp
    hop_base = nz * nb
    z_base = hop_base + nz * (nb - 1)

    def tail(sib_out, pair, z_out):
        grad = S.flat.reshape(total, 4, 128)

        def column(i):
            return lax.rem(z + 1 + i, nz)

        def collect(m, zz, cc):
            start = (flip(b, m) * nr + 2 * zz + cc) * own

            @pl.loop(0, own // unit)
            def _(g):
                at = start + g * unit
                for u in range(unit):
                    tmp[pl.ds(pl.multiple_of((g * unit + u) * 4, 4), 4), :] = grad[S.idx[at // 128, lax.rem(at, 128) + u]]

        def to_sibling(i, m):
            return pltpu.make_async_remote_copy(
                sib_out.at[i, m], rows_in.at[i * nb + m], S.sib_send.at[i, m], S.sib_recv.at[i, m],
                device_id=sibling, device_id_type=MESH,
            )

        def rows_of(p):
            return pl.ds(p * size, size)

        def slots(p, t):
            at = sum(len(plan[p][k][2]) for k in range(t))
            return at, len(plan[p][t][2])

        def hop_at(i, p, at, count):
            return rows_in.at[pl.ds(hop_base + i * (nb - 1) + at, count), rows_of(p)]

        def hop(i, p, t, m):
            o, sent, kept = plan[p][t]
            at, _ = slots(p, t)
            landing = rows_in.at[hop_base + i * (nb - 1) + at + kept.index(m ^ (1 << o)), rows_of(p)]
            return pltpu.make_async_remote_copy(
                pair.at[i, m, rows_of(p)], landing, S.hop_send.at[i, p, t], S.hop_recv.at[i, p, t],
                device_id=(flip(b, 1 << o), r), device_id_type=MESH,
            )

        def hop_wait(i, p, t, sem):
            whole = hop_at(i, p, *slots(p, t))
            pltpu.make_async_copy(whole, whole, sem.at[i, p, t]).wait()

        def for_sibling(i):
            for m in reversed(range(nb)):
                collect(m, column(i), 1 - c)
                sib_out[i, m] = tmp[...].astype(bf16)
                to_sibling(i, m).start()

        def to_owner(i):
            return pltpu.make_async_remote_copy(
                z_out.at[i], rows_in.at[z_base + i, pl.ds(0, main)], S.own_send.at[i], S.own_recv.at[i],
                device_id=(b, 2 * column(i) + c), device_id_type=MESH,
            )

        def to_layer(i, m):
            return pltpu.make_async_remote_copy(
                pair.at[i, m, pl.ds(main, by_z)], S.layer_in.at[i, m], S.layer_send.at[i], S.layer_recv.at[i],
                device_id=(b, 2 * column(i) + c), device_id_type=MESH,
            )

        def layer_wait(i, sem):
            pltpu.make_async_copy(S.layer_in.at[i], S.layer_in.at[i], sem.at[i]).wait()

        def z_rows(p):
            return pl.ds(main + p * z_size, z_size)

        def z_hop(p, t, m):
            o, sent, kept = plan[p][t]
            at, _ = slots(p, t)
            return pltpu.make_async_remote_copy(
                pair.at[nz - 1, m, z_rows(p)], S.z_hops.at[p, at + kept.index(m ^ (1 << o))], S.z_hop_send.at[p, t], S.z_hop_recv.at[p, t],
                device_id=(flip(b, 1 << o), r), device_id_type=MESH,
            )

        def z_hop_wait(p, t, sem):
            at, count = slots(p, t)
            whole = S.z_hops.at[p, pl.ds(at, count)]
            pltpu.make_async_copy(whole, whole, sem.at[p, t]).wait()

        def z_start():
            for i in range(nz - 1):
                layer_wait(i, S.layer_recv)
            for m in reversed(range(nb)):
                v = pair[nz - 1, m, pl.ds(main, by_z)].astype(f32)
                for i in range(nz - 1):
                    v = v + S.layer_in[i, m].astype(f32)
                pair[nz - 1, m, pl.ds(main, by_z)] = v.astype(bf16)
                for p in range(parts):
                    if m in plan[p][0][1]:
                        z_hop(p, 0, m).start()

        def z_next(t):
            for p in range(parts):
                z_hop_wait(p, t, S.z_hop_recv)
                at, _ = slots(p, t)
                for k, m in enumerate(plan[p][t][2]):
                    v = pair[nz - 1, m, z_rows(p)].astype(f32) + S.z_hops[p, at + k].astype(f32)
                    if t == parts - 1:
                        tmp[z_rows(p), :] = v
                        continue
                    pair[nz - 1, m, z_rows(p)] = v.astype(bf16)
                    if m in plan[p][t + 1][1]:
                        z_hop(p, t + 1, m).start()

        def first_step(i):
            for m in reversed(range(nb)):
                collect(m, column(i), c)
                to_sibling(i, m).wait_recv()
                pair[i, m] = (tmp[...] + rows_in[i * nb + m].astype(f32)).astype(bf16)
                for p in range(parts):
                    if m in plan[p][0][1]:
                        hop(i, p, 0, m).start()
                if by_z:

                    @pl.when(i < nz - 1)
                    def _():
                        to_layer(i, m).start()

            @pl.when(i < nz - 1)
            def _():
                for_sibling(i + 1)

        def next_step(i, t):
            for p in range(parts):
                hop_wait(i, p, t, S.hop_recv)
                at, _ = slots(p, t)
                for k, m in enumerate(plan[p][t][2]):
                    pair[i, m, rows_of(p)] = (
                        pair[i, m, rows_of(p)].astype(f32)
                        + rows_in[hop_base + i * (nb - 1) + at + k, rows_of(p)].astype(f32)
                    ).astype(bf16)
                    if m in plan[p][t + 1][1]:
                        hop(i, p, t + 1, m).start()

        def last_step(i):
            for p in range(parts):
                hop_wait(i, p, parts - 1, S.hop_recv)
                at, _ = slots(p, parts - 1)
                tmp[rows_of(p), :] = pair[i, 0, rows_of(p)].astype(f32) + rows_in[hop_base + i * (nb - 1) + at, rows_of(p)].astype(f32)

            @pl.when(i < nz - 1)
            def _():
                z_out[i] = tmp[pl.ds(0, main), :].astype(bf16)
                to_owner(i).start()

        def grad_image():
            sums = share_wait(7, 1, merge_sum) * (1.0 / every)
            scale_x = row(0) * inv_x

            def last(s, a):
                hat = (S.x[s, :] - m_x) * inv_x
                S.g_f[s, :] = S.g_f[s, :] + scale_x * (S.p_val[s, :] - sums[0:1] - hat * sums[1:2])
                return a

            chunks(n, last)
            gin_copy.start()
            for i in range(own):
                at = (b * nr + r) * own + i // unit * unit
                p = S.idx[at // 128, lax.rem(at, 128) + i % unit]
                fast = (p >= 2 * C + 2 * FF + KL * KL) & ((p < BASE) | (p >= BASE + KS * KS))
                S.rate[pl.ds(i, 1), :] = jnp.full((1, 128), jnp.where(fast, np.float32(norm_rate), np.float32(matrix_rate)), f32)

        gin_copy = pltpu.make_async_copy(S.g_f, S.gin_hbm, S.load_sem.at[6])
        for_sibling(0)

        @pl.loop(0, nz + parts)
        def _(q):
            @pl.when(q < nz)
            def _():
                first_step(q)

            @pl.when(q == 0)
            def _():
                share_send(7, 1, share_wait(7, 0, merge_sum))

            if by_z:

                @pl.when(q == nz - 1)
                def _():
                    z_start()

            for t in range(parts - 1):

                @pl.when((q >= t + 1) & (q < nz + t + 1))
                def _():
                    next_step(q - t - 1, t)

            @pl.when(q == 1)
            def _():
                grad_image()

            if by_z:

                @pl.when(q == nz)
                def _():
                    for t in range(parts - 1):
                        z_next(t)

            @pl.when(q >= parts)
            def _():
                last_step(q - parts)

        for i in range(nz - 1):
            to_owner(i).wait_recv()
            tmp[pl.ds(0, main), :] += rows_in[z_base + i, pl.ds(0, main)].astype(f32)
        if by_z:
            z_next(parts - 1)
        for j in range(4):
            S.red[:, j * 128 : (j + 1) * 128] = tmp[pl.ds(j, own, stride=4), :]

        @pl.loop(0, nz)
        def _(i):
            for m in range(nb):
                to_sibling(i, m).wait_send()
            for p in range(parts):
                for t in range(parts):
                    hop_wait(i, p, t, S.hop_send)

        for i in range(nz - 1):
            to_owner(i).wait_send()
            if by_z:
                layer_wait(i, S.layer_send)
        if by_z:
            for p in range(parts):
                for t in range(parts):
                    z_hop_wait(p, t, S.z_hop_send)
        gin_copy.wait()

    low_block = lambda *lead: pltpu.VMEM(lead + (lines, 128), bf16)
    pl.run_scoped(tail, low_block(nz, nb), low_block(nz, nb), pltpu.VMEM((nz, main, 128), bf16))
    for e in range(len(WIDTHS)):
        for stage in range(2):
            buf, mine, count = share_stage(e, stage)
            sent = buf.at[pl.ds(0, count - 1)]
            pltpu.make_async_copy(sent, sent, S.stat_send.at[e, stage]).wait()
    out_copy.wait()


def step(x, cot, master, slots, nb, nr):
    (a, at, b, bt, bs, bst, c, ct) = tables()
    n, own, nz, parts = x.shape[0], master.shape[0], nr // 2, nb.bit_length() - 1
    total = slots.size
    vm = lambda *shape: pltpu.VMEM(shape, f32)
    low = lambda *shape: pltpu.VMEM(shape, bf16)
    dma = lambda *shape: pltpu.SemaphoreType.DMA(shape)
    vmem, anywhere = pl.BlockSpec(memory_space=pltpu.VMEM), pl.BlockSpec(memory_space=pl.ANY)
    ins = dict(
        slots_hbm=(slots, anywhere), x_hbm=(x, anywhere), cot_hbm=(cot, anywhere), master_hbm=(master, anywhere),
        a_hbm=(a, anywhere), at_hbm=(at, anywhere), b_hbm=(b, anywhere), bt_hbm=(bt, anywhere), bs=(bs, vmem), bst=(bst, vmem),
        c_hbm=(c, anywhere), ct_hbm=(ct, anywhere),
    )
    image = jax.ShapeDtypeStruct((n, C), f32)
    outs = dict(
        out_hbm=(image, anywhere), gin_hbm=(image, anywhere), red=(jax.ShapeDtypeStruct((own, C), f32), vmem),
        rate=(jax.ShapeDtypeStruct((own, 128), f32), vmem),
    )
    scratch = dict(
        rows_in=low(nb * nr, 4 * own, 128), flat=vm(4 * total, 128), tab=low(total, C), x=vm(n, C), cot=vm(n, C), master=vm(own, C),
        tmp=vm(4 * own, 128), chunk=vm(512, 128), inv=pltpu.VMEM((total // 128, 128), jnp.int32), at_v=pltpu.VMEM((total // 128, 128), jnp.int32),
        idx=pltpu.SMEM((total // 128, 128), jnp.int32),
        inv_at=pltpu.SMEM((total // 128, 128), jnp.int32), small=vm(48, C),
        pre_low=low(n, C), wide=low(3 * n, C), dz=vm(n, C), spec_u=vm(2 * NF, C), spec_l=vm(2 * NF, C), spec_s=vm(2 * NF, C),
        prod_l=low(2 * NF, C), prod_s=low(2 * NF, C), prod_k=low(2 * NF, C), d_l=vm(n, C), d_s=vm(n, C), s_val=vm(n, C),
        t_low=low(n, C), p_val=vm(n, C), mid=vm(n, C), c_low=low(n, C), gy_low=low(n, C), gp_low=low(n, C), g_f=vm(n, C), out=vm(n, C),
        halo_out=low(2, n, C), halo_in=low(2, n, C),
    )
    by_z = first_along_z(nb, 4 * own)
    if by_z:
        scratch.update(
            layer_in=low(nz - 1, nb, by_z, 128), z_hops=low(parts, nb - 1, by_z // parts, 128), layer_send=dma(nz), layer_recv=dma(nz),
            z_hop_send=dma(parts, parts), z_hop_recv=dma(parts, parts),
        )
    for e, w in enumerate(WIDTHS):
        one, two = (2, nb * nz) if by_chip(e, nb * nz) else (nr, nb)
        scratch[f"one{e}"] = vm(one, w, C)
        scratch[f"two{e}"] = vm(two, w, C)
    scratch.update(
        load_sem=dma(9), stat_send=dma(len(WIDTHS), 2), stat_recv=dma(len(WIDTHS), 2), halo_send=dma(4), halo_recv=dma(4),
        z_send=dma(nz), z_recv=dma(nz), b_send=dma(nb, nz), b_recv=dma(nb, nz), half_send=dma(2, nz), half_recv=dma(2, nz),
        core_send=dma(nb, nz), core_recv=dma(nb, nz), rest_send=dma(nb, nz), rest_recv=dma(nb, nz),
        rest_core_send=dma(nb, nz), rest_core_recv=dma(nb, nz), sib_send=dma(nz, nb), sib_recv=dma(nz, nb),
        hop_send=dma(nz, parts, parts), hop_recv=dma(nz, parts, parts), own_send=dma(nz), own_recv=dma(nz),
    )
    return pl.pallas_call(
        functools.partial(step_kernel, nb, nr, [*ins, *outs, *scratch]),
        out_shape=[v[0] for v in outs.values()],
        in_specs=[v[1] for v in ins.values()],
        out_specs=[v[1] for v in outs.values()],
        scratch_shapes=list(scratch.values()),
        compiler_params=pltpu.CompilerParams(collective_id=0, has_side_effects=True, vmem_limit_bytes=62 * 2**20),
    )(*[v[0] for v in ins.values()])


def finish_kernel(*refs):
    ins, outs, bufs, (load_sem, store_sem) = refs[:7], refs[7:14], refs[14:25], refs[25:]
    red, rate, first_ref, second_ref, master_ref, out, gin = bufs[:7]
    new_first, new_second, new_master, new_copy = bufs[7:11]
    loads = [pltpu.make_async_copy(src, dst, load_sem.at[i]) for i, (src, dst) in enumerate(zip(ins, bufs[:7]))]
    for copy in loads:
        copy.start()
    own = red.shape[0]
    size = 64 if own % 64 == 0 else own
    for copy in loads[:5]:
        copy.wait()
    stores = [pltpu.make_async_copy(red, outs[2], store_sem.at[2, 0])]
    stores[0].start()
    for part in range(own // size):
        for k in range(0, size, 8):
            s = slice(part * size + k, part * size + k + 8)
            for j in range(C // 128):
                at = (s, slice(j * 128, (j + 1) * 128))
                g = red[at]
                first = beta_one * first_ref[at] + (1.0 - beta_one) * g
                second = beta_two * second_ref[at] + (1.0 - beta_two) * g * g
                new_first[at] = first
                new_second[at] = second
                first_hat = first / (1.0 - beta_one**STEP)
                second_hat = second / (1.0 - beta_two**STEP)
                master = master_ref[at]
                new_master[at] = master - rate[s, :] * (first_hat / (jnp.sqrt(second_hat) + adam_eps) + decay_rate * master)
        s = pl.ds(part * size, size)
        new_copy[s, :] = new_master[s, :].astype(bf16)
        if part == 0:
            for i in (5, 6):
                loads[i].wait()
                stores.append(pltpu.make_async_copy(bufs[i], outs[i - 5], store_sem.at[i - 5, 0]))
                stores[-1].start()
        for i, buf in enumerate((new_first, new_second, new_master, new_copy)):
            stores.append(pltpu.make_async_copy(buf.at[s], outs[3 + i].at[s], store_sem.at[3 + i, part]))
            stores[-1].start()
    for copy in stores:
        copy.wait()


def finish(reduced, first, second, master, rates, out, gin):
    anywhere = pl.BlockSpec(memory_space=pl.ANY)
    slot = jax.ShapeDtypeStruct(reduced.shape, f32)
    image = jax.ShapeDtypeStruct(out.shape, f32)
    low = jax.ShapeDtypeStruct(reduced.shape, bf16)
    ins = (reduced, rates, first, second, master, out, gin)
    outs = [image, image, slot, slot, slot, slot, low]
    return pl.pallas_call(
        finish_kernel,
        out_shape=outs,
        in_specs=[anywhere] * 7,
        out_specs=[anywhere] * 7,
        scratch_shapes=[pltpu.VMEM(v.shape, f32) for v in ins]
        + [pltpu.VMEM(v.shape, v.dtype) for v in (slot, slot, slot, low)]
        + [pltpu.SemaphoreType.DMA((7,)), pltpu.SemaphoreType.DMA((7, 4))],
        compiler_params=pltpu.CompilerParams(vmem_limit_bytes=62 * 2**20),
    )(*ins)


def body(image_in, cotangent, slot_rows, master, first_moment, second_moment):
    n = image_in.shape[0] * image_in.shape[1] * image_in.shape[2]
    nb, nr = lax.axis_size("batch"), lax.axis_size("rows")
    out, grad_in, reduced, rates = step(
        image_in.reshape(n, C), cotangent.reshape(n, C), master, slot_rows.reshape(-1, 128), nb, nr
    )
    result, grad_x, *slots = finish(reduced, first_moment, second_moment, master, rates, out, grad_in)
    return (result.reshape(image_in.shape), grad_x.reshape(image_in.shape), *slots)


def solution(mesh):
    image = P("batch", "rows", None, None)
    owner = P(AXES, None)
    return jax.shard_map(
        body,
        mesh=mesh,
        in_specs=(image, image, P(), owner, owner, owner),
        out_specs=(image, image, owner, owner, owner, owner, owner),
        check_vma=False,
    )
```

```python
import functools
import types

import jax
import jax.numpy as jnp
import numpy as np
from jax import lax
from jax.experimental import pallas as pl
from jax.experimental.pallas import tpu as pltpu
from jax.sharding import PartitionSpec as P

C = 512
FF = 2048
KL = 31
KS = 5
STEP = 10

norm_eps = 1e-05
beta_one = 0.9
beta_two = 0.999
adam_eps = 1e-08
decay_rate = 0.05
matrix_rate = 0.05
norm_rate = 0.5

TH = 16
TW = 16
NY = 47
NX = 31
NF = 768
REACH = (KL - 1) // 2
AXES = ("batch", "rows")
f32 = jnp.float32
bf16 = jnp.bfloat16


@functools.lru_cache(None)
def tables():
    freqs = [(ky, 0) for ky in range((NY + 1) // 2)]
    freqs += [(ky, kx) for kx in range(1, (NX + 1) // 2) for ky in range(NY)]
    ky = np.array([f[0] for f in freqs], np.int64)[:, None]
    kx = np.array([f[1] for f in freqs], np.int64)[:, None]
    pad = NF - len(freqs)

    def angle(rows, cols):
        ty = (ky * rows.reshape(1, -1)) % NY
        tx = (kx * cols.reshape(1, -1)) % NX
        return 2 * np.pi * (ty / NY + tx / NX)

    def grid(rows, cols):
        r, c = np.meshgrid(rows, cols, indexing="ij")
        return r.reshape(-1), c.reshape(-1)

    def stack(re, im):
        z = np.zeros((pad, re.shape[1]))
        return np.concatenate([re, z, im, z], axis=0)

    r, c = grid(np.arange(-TH, 2 * TH), np.arange(TW))
    used = ((r + REACH >= 0) & (r + REACH < NY - 1)).astype(np.float64)[None]
    t = angle(r + REACH, c)
    a = stack(np.cos(t) * used, -np.sin(t) * used)
    i, j = grid(np.arange(KL), np.arange(KL))
    t = angle(i, j - REACH)
    b = stack(np.cos(t), -np.sin(t))
    lead = REACH - (KS - 1) // 2
    small = ((i >= lead) & (i < lead + KS) & (j >= lead) & (j < lead + KS)).nonzero()[0]
    bs = np.pad(b[:, small], ((0, 0), (0, 32 - KS * KS)))
    b = np.pad(b, ((0, 0), (0, 2 * C - KL * KL)))
    y, x = grid(np.arange(TH), np.arange(TW))
    t = angle(y, x)
    w = np.full((len(freqs), 1), 2.0)
    w[0] = 1.0
    w /= NY * NX
    ct = stack(w * np.cos(t), -w * np.sin(t))
    return tuple(m.astype(np.float32).astype(bf16) for m in (a, a.T, b, b.T, bs, bs.T, ct.T, ct))


def dot(a, b, dims=(1, 0)):
    return lax.dot_general(a, b, (((dims[0],), (dims[1],)), ((), ())), preferred_element_type=f32)


MESH = pl.DeviceIdType.MESH
WIDTHS = (2, 4, 3, 8, 8, 5, 3, 2)
BY_CHIP = (1, 2, 5, 6)
BASE = 2 * C + 2 * FF + 976


def chunks(n, fn, init=()):
    return lax.fori_loop(0, n // 32, lambda i, c: fn(pl.ds(pl.multiple_of(i * 32, 32), 32), c), init)


def fold(v):
    return jnp.sum(v.reshape(v.shape[0] // 8, 8, v.shape[1]), axis=0)


def close(v):
    return jnp.sum(v, axis=0, keepdims=True)


def put(ref, start, v):
    for j in range(4):
        ref[pl.ds(start * 4 + j, v.shape[0], stride=4), :] = v[:, j * 128 : (j + 1) * 128]


def gelu_both(v):
    a = np.float32(np.sqrt(2 / np.pi))
    sq = v * v
    t = jnp.tanh(a * (v + 0.044715 * (sq * v)))
    half = 0.5 * (1 + t)
    return v * half, half + 0.5 * v * (1 - t * t) * (a * (1 + 3 * 0.044715 * sq))


def flip(b, m):
    k = 0
    while m >> k:
        if (m >> k) & 1:
            b = b + (1 - 2 * lax.rem(b // 2**k, 2)) * 2**k
        k += 1
    return b


def reduce_plan(nb):
    bits = nb.bit_length() - 1
    plan = []
    for p in range(bits):
        order = [(p + t) % bits for t in range(bits)]
        steps, kept = [], list(range(nb))
        for o in order:
            sent = [m for m in kept if (m >> o) & 1]
            kept = [m for m in kept if not (m >> o) & 1]
            steps.append((o, sent, kept))
        plan.append(steps)
    return plan


def first_along_z(nb, lines):
    return lines // 6 if nb == 4 and lines % 192 == 0 else 0


def by_chip(e, chips):
    return e in BY_CHIP and chips <= 32


def merge_sum(v, count):
    return jnp.sum(v, axis=0)


def merge_stats(h):
    def merge(v, count):
        means = v[:, :h]
        m = jnp.sum(means, axis=0) * (1.0 / v.shape[0])
        d = means - m
        parts = [m, jnp.sum(v[:, h : 2 * h], axis=0) + count * jnp.sum(d * d, axis=0)]
        if v.shape[1] > 2 * h:
            parts.append(jnp.sum(v[:, 2 * h :], axis=0))
        return jnp.concatenate(parts, axis=0)

    return merge


def local(read, n):
    zero = jnp.zeros((8, C), f32)
    m = close(chunks(n, lambda s, c: c + fold(read(s)), zero)) * (1.0 / n)

    def sq(s, c):
        d = read(s) - m
        return c + fold(d * d)

    return m, close(chunks(n, sq, zero))


def half_cols(h):
    return pl.ds(pl.multiple_of(h * 256, 256), 256)


def up_rows(j):
    return pl.ds(pl.multiple_of(2 * C + j * C, C), C)


def down_rows(j):
    return pl.ds(pl.multiple_of(2 * C + FF + j * C, C), C)


def table_place(t):
    start = 2 * C + 2 * FF
    k_end = start + KL * KL
    s_end = k_end + KS * KS
    m_gain = s_end + 10
    m_bias = m_gain + FF // C
    m_end = m_bias + FF // C
    up = t - 2 * C
    up = 2 * C + (up & (FF // C - 1)) * C + (up >> ((FF // C).bit_length() - 1))
    base = start + 976
    unused = t - m_end
    unused = jnp.where(unused < 15, k_end + unused, jnp.where(unused < 18, base + 29 + unused - 15, base + 46 + unused - 18))
    p = jnp.where((t >= 2 * C) & (t < 2 * C + FF), up, t)
    p = jnp.where(t >= k_end, t - k_end + base, p)
    p = jnp.where(t >= s_end, t - s_end + base + 32, p)
    p = jnp.where(t >= m_bias, t - m_bias + base + 25, p)
    return jnp.where(t >= m_end, unused, p)


def step_kernel(nb, nr, names, *refs):
    S = types.SimpleNamespace(**dict(zip(names, refs)))
    nz = nr // 2
    nd = nb * nr
    n = S.x.shape[0]
    own = S.master.shape[0]
    lines = 4 * own
    total = S.tab.shape[0]
    every = float(n * nd)
    b = lax.axis_index("batch")
    r = lax.axis_index("rows")
    z, c = r // 2, lax.rem(r, 2)
    sibling = (b, r + 1 - 2 * c)
    square = nb == 4
    blocks = FF // C
    zero = jnp.zeros((8, C), f32)
    rows_in = S.rows_in

    def load(i, src, dst):
        return pltpu.make_async_copy(src, dst, S.load_sem.at[i])

    ld_m, ld_x, ld_c = load(0, S.master_hbm, S.master), load(1, S.x_hbm, S.x), load(2, S.cot_hbm, S.cot)
    ld_s = load(8, S.slots_hbm, S.at_v)
    for copy in (ld_s, ld_m, ld_x, ld_c):
        copy.start()
    barrier = pltpu.get_barrier_semaphore()
    for k in range(1, nr):
        pl.semaphore_signal(barrier, inc=1, device_id=(b, lax.rem(r + k, nr)), device_id_type=MESH)
    for m in range(1, nb):
        pl.semaphore_signal(barrier, inc=1, device_id=(flip(b, m), r), device_id_type=MESH)

    @pl.loop(0, (nb - 1) * (nz - 1))
    def _(k):
        at = (lax.rem(b + 1 + k // (nz - 1), nb), 2 * lax.rem(z + 1 + lax.rem(k, nz - 1), nz) + c)
        pl.semaphore_signal(barrier, inc=1, device_id=at, device_id_type=MESH)


    def share_stage(e, stage):
        buf = getattr(S, ("one" if stage == 0 else "two") + str(e))
        if by_chip(e, nb * nz):
            return (buf, c, 2) if stage == 0 else (buf, b * nz + z, nb * nz)
        return (buf, r, nr) if stage == 0 else (buf, b, nb)

    def share_peer(e, stage, k):
        if by_chip(e, nb * nz):
            if stage == 0:
                return sibling
            other = lax.rem(b * nz + z + k, nb * nz)
            return (other // nz, 2 * lax.rem(other, nz) + c)
        return (b, lax.rem(r + k, nr)) if stage == 0 else (lax.rem(b + k, nb), r)

    def share_send(e, stage, v):
        buf, mine, size = share_stage(e, stage)
        buf[mine] = v

        def one(k):
            pltpu.make_async_remote_copy(
                buf.at[mine], buf.at[mine], S.stat_send.at[e, stage], S.stat_recv.at[e, stage],
                device_id=share_peer(e, stage, k), device_id_type=MESH,
            ).start()

        if size > 8:
            pl.loop(1, size)(one)
        else:
            for k in range(1, size):
                one(k)

    def share_wait(e, stage, merge):
        buf, mine, size = share_stage(e, stage)
        got = buf.at[pl.ds(0, size - 1)]
        pltpu.make_async_copy(got, got, S.stat_recv.at[e, stage]).wait()
        return merge(buf[...], float(n if stage == 0 else n * getattr(S, f"one{e}").shape[0]))

    def share(e, v, merge, work=None, more=None):
        share_send(e, 0, v)
        if work and not by_chip(e, nb * nz):
            work()
        v = share_wait(e, 0, merge)
        share_send(e, 1, v)
        if work and by_chip(e, nb * nz):
            work()
        if more:
            more()
        return share_wait(e, 1, merge)


    def place(m, zz, core):
        return flip(b, m) * nr + 2 * zz + core

    spread = first_along_z(nb, lines)
    rest = pl.ds(lines - spread, spread)

    def lines_of(k):
        return lines if k == 0 else lines - spread

    def part(m, zz, core, k):
        return rows_in.at[place(m, zz, core), pl.ds(0, lines_of(k))]

    def along_z(zz, up):
        at = part(0, zz, c, 1)
        return pltpu.make_async_remote_copy(
            at, at, S.z_send.at[zz], S.z_recv.at[zz], device_id=(b, r + 2 if up else r - 2), device_id_type=MESH
        )

    def to_peer(m, zz, k):
        at = part(0, zz, c, k)
        return pltpu.make_async_remote_copy(
            at, at, S.b_send.at[m, zz], S.b_recv.at[m, zz], device_id=(flip(b, m), r), device_id_type=MESH
        )

    def from_peer(m, zz, k):
        at = part(m, zz, c, k)
        return pltpu.make_async_copy(at, at, S.b_recv.at[m, zz])

    def half(m, zz, h, to, k):
        size = lines_of(k) // 2
        at = rows_in.at[place(m, zz, c), pl.ds(h * size, size)]
        return pltpu.make_async_remote_copy(
            at, at, S.half_send.at[h, zz], S.half_recv.at[h, zz], device_id=(flip(b, to), r), device_id_type=MESH
        )

    def to_other_core(m, zz, core, k):
        at = part(m, zz, core, k)
        return pltpu.make_async_remote_copy(
            at, at, S.core_send.at[m, zz], S.core_recv.at[m, zz], device_id=sibling, device_id_type=MESH
        )

    def cast(m, zz, core, k):
        d = place(m, zz, core)
        S.flat[pl.ds(pl.multiple_of(d * lines, lines), lines_of(k)), :] = rows_in[d, pl.ds(0, lines_of(k))].astype(f32)

    def rest_out(m, zz):
        at = rows_in.at[place(m, z, c), rest]
        return pltpu.make_async_remote_copy(
            at, at, S.rest_send.at[m, zz], S.rest_recv.at[m, z], device_id=(b, 2 * zz + c), device_id_type=MESH
        )

    def rest_in(m, zz):
        at = rows_in.at[place(m, zz, c), rest]
        return pltpu.make_async_copy(at, at, S.rest_recv.at[m, zz])

    def rest_to_core(m, zz, core):
        at = rows_in.at[place(m, zz, core), rest]
        return pltpu.make_async_remote_copy(
            at, at, S.rest_core_send.at[m, zz], S.rest_core_recv.at[m, zz], device_id=sibling, device_id_type=MESH
        )

    def rest_cast(m, zz, core):
        d = place(m, zz, core)
        S.flat[pl.ds(pl.multiple_of(d * lines + lines - spread, 64), spread), :] = rows_in[d, rest].astype(f32)

    direct = [m for m in range(1, nb) if not (square and m == 3)]

    def each(k, fn):
        if k == 0:
            fn(z, True, True)
            return

        @pl.when(z >= k)
        def _():
            fn(z - k, True, False)

        @pl.when(z + k < nz)
        def _():
            fn(z + k, False, True)

    def onward(zz, below, above, act):
        if below:

            @pl.when(z < nz - 1)
            def _():
                act(along_z(zz, True))

        if above:

            @pl.when(z > 0)
            def _():
                act(along_z(zz, False))

    def own_column(k):
        def go(zz, below, above):
            if k:
                along_z(zz, below).wait_recv()
            onward(zz, below, above, lambda copy: copy.start())
            for m in direct:
                to_peer(m, zz, k).start()
            to_other_core(0, zz, c, k).start()
            cast(0, zz, c, k)

        each(k, go)

    def pass_on(k):
        def go(zz, below, above):
            for m in direct:
                from_peer(m, zz, k).wait()
                if square:
                    half(m, zz, 2 - m, 3 - m, k).start()
                to_other_core(m, zz, c, k).start()
                cast(m, zz, c, k)

        each(k, go)

    def corner(k):
        def go(zz, below, above):
            for h in range(2):
                half(3, zz, h, 0, k).wait_recv()
            if k == 0 and spread:
                for d in range(1, nz):
                    for m in range(nb):
                        rest_out(m, lax.rem(z + d, nz)).start()
            to_other_core(3, zz, c, k).start()
            cast(3, zz, c, k)

        if square:
            each(k, go)

    def other_core(k):
        def go(zz, below, above):
            for m in range(nb):
                to_other_core(m, zz, 1 - c, k).wait_recv()
                cast(m, zz, 1 - c, k)

        each(k, go)

    def rest_here(k):
        def go(zz, below, above):
            for m in range(nb):
                rest_in(m, zz).wait()
                rest_to_core(m, zz, c).start()
                rest_cast(m, zz, c)

        if spread:
            each(k, go)

    def rest_there(k):
        def go(zz, below, above):
            for m in range(nb):
                rest_to_core(m, zz, 1 - c).wait_recv()
                rest_cast(m, zz, 1 - c)

        if spread:
            each(k, go)

    def gather_sent(k):
        def go(zz, below, above):
            onward(zz, below, above, lambda copy: copy.wait_send())
            for m in direct:
                to_peer(m, zz, k).wait_send()
                if square:
                    half(m, zz, 2 - m, 3 - m, k).wait_send()
            for m in range(nb):
                to_other_core(m, zz, c, k).wait_send()
                if spread and k:
                    rest_out(m, zz).wait_send()
                    rest_to_core(m, zz, c).wait_send()

        each(k, go)

    def find(part, parts):
        tiles = total // 1024
        unit = 16
        spots = [
            lax.broadcasted_iota(jnp.int32, (8, 128), 0) * 128 + lax.broadcasted_iota(jnp.int32, (8, 128), 1) + 1024 * k
            for k in range(tiles)
        ]

        def some(g, acc):
            for u in range(unit):
                start = g * unit
                s = start + u
                p = S.idx[start // 128, lax.rem(start, 128) + u]
                acc = [jnp.where(spot == p, s, a) for spot, a in zip(spots, acc)]
            return acc

        acc = [S.inv[k * 8 : k * 8 + 8, :] if part else jnp.zeros((8, 128), jnp.int32) for k in range(tiles)]
        groups = total // unit
        acc = lax.fori_loop(groups * part // parts, groups * (part + 1) // parts, some, acc)
        for k in range(tiles):
            S.inv[k * 8 : k * 8 + 8, :] = acc[k]

    def order(start, stop):
        flat = S.flat.reshape(total, 4, 128)

        @pl.loop(start, stop)
        def _(t):
            for u in range(128):
                S.chunk[4 * u : 4 * u + 4, :] = flat[S.inv_at[t, u]]

            rows = pl.ds(pl.multiple_of(t * 128, 128), 128)
            for j in range(4):
                S.tab[rows, j * 128 : (j + 1) * 128] = S.chunk[pl.ds(j, 128, stride=4), :].astype(bf16)

    def front(ta, tb, tc):
        ld_a, ld_b, ld_t = load(3, S.a_hbm, ta), load(4, S.b_hbm, tb), load(5, S.c_hbm, tc)
        for copy in (ld_b, ld_a, ld_t):
            copy.start()
        ld_s.wait()
        S.at_v[...] = table_place(S.at_v[...])
        to_scalar = pltpu.make_async_copy(S.at_v, S.idx, S.load_sem.at[8])
        to_scalar.start()
        ld_m.wait()
        for j in range(4):
            S.tmp[pl.ds(j, own, stride=4), :] = S.master[:, j * 128 : (j + 1) * 128]
        rows_in[place(0, z, c)] = S.tmp[...].astype(bf16)
        pl.semaphore_wait(barrier, nr - 1 + nb - 1 + (nb - 1) * (nz - 1))
        own_column(0)
        to_scalar.wait()
        ld_x.wait()
        share_send(0, 0, jnp.concatenate(local(lambda s: S.x[s, :], n), axis=0))
        steps = 3 * max(nz - 1, 1)
        for k in range(1, nz):
            find(3 * k - 3, steps)
            own_column(k)
            find(3 * k - 2, steps)
            pass_on(k - 1)
            find(3 * k - 1, steps)
            if k == 2:
                corner(0)
            if k > 2:
                other_core(k - 3)
            if k == 1:
                share_send(0, 1, share_wait(0, 0, merge_stats(1)))
        if nz == 1:
            for part in range(3):
                find(part, 3)
            share_send(0, 1, share_wait(0, 0, merge_stats(1)))
        to_scalar = pltpu.make_async_copy(S.inv, S.inv_at, S.load_sem.at[6])
        to_scalar.start()
        pass_on(nz - 1)
        for k in range(1 if nz > 2 else 0, nz - 1):
            corner(k)
        for k in range(1, nz):
            rest_here(k)
        corner(nz - 1)
        for k in range(max(nz - 3, 0), nz):
            other_core(k)
        for k in range(1, nz):
            rest_there(k)
        tot = share_wait(0, 1, merge_stats(1))
        m_x, q_x = tot[0:1], tot[1:2] * (1.0 / every)
        inv_x = lax.rsqrt(q_x + norm_eps)
        to_scalar.wait()
        tiles = total // 128
        late = (2 * C + 2 * FF) // 128
        order(0, C // 128)
        order(tiles - 2, tiles)

        for k in range(nz):
            gather_sent(k)

        small = S.tab[pl.ds(BASE, 48), :].astype(f32)
        S.small[...] = small
        row = lambda i: small[32 + i : 33 + i, :]

        def pre(s, sx):
            d = S.x[s, :] - m_x
            S.pre_low[s, :] = (d * (inv_x * row(0)) + row(1)).astype(bf16)
            return sx + fold(d)

        sum_x = close(chunks(n, pre, zero))
        S.dz[...] = dot(S.pre_low[...], S.tab[pl.ds(0, C), :])

        def act(s, a):
            u, d = gelu_both(S.dz[s, :])
            S.dz[s, :] = d
            S.wide[pl.ds(pl.multiple_of(n + s.start, 32), 32), :] = u.astype(bf16)
            return a

        chunks(n, act)
        mine = S.wide.at[pl.ds(n, n)]
        halo_up = halo(0, mine, S.wide.at[pl.ds(2 * n, n)], True)
        halo_down = halo(1, mine, S.wide.at[pl.ds(0, n)], False)
        halo_start(halo_up, halo_down)
        order(late, tiles - 2)
        order(C // 128, 2 * C // 128)

        ld_b.wait()

        @pl.loop(0, 2 * NF // 256)
        def _(t):
            s = pl.ds(pl.multiple_of(t * 256, 256), 256)
            S.spec_l[s, :] = dot(tb[s, :], S.tab[pl.ds(2 * C + 2 * FF, 2 * C), :])
            S.spec_s[s, :] = dot(S.bs[s, :], S.tab[pl.ds(BASE, 32), :])

        halo_wait(halo_up, halo_down, S.wide.at[pl.ds(0, n)], S.wide.at[pl.ds(2 * n, n)])
        ld_a.wait()

        @pl.loop(0, 2 * NF // 256)
        def _(t):
            s = pl.ds(pl.multiple_of(t * 256, 256), 256)
            S.spec_u[s, :] = dot(ta[s, :], S.wide[...])

        @pl.loop(0, NF // 32)
        def _(i):
            re, im = pl.ds(pl.multiple_of(i * 32, 32), 32), pl.ds(pl.multiple_of(NF + i * 32, 32), 32)
            ur, ui = S.spec_u[re, :], S.spec_u[im, :]
            for k, p in ((S.spec_l, S.prod_l), (S.spec_s, S.prod_s)):
                kr, ki = k[re, :], k[im, :]
                p[re, :] = (ur * kr + ui * ki).astype(bf16)
                p[im, :] = (ui * kr - ur * ki).astype(bf16)

        ld_t.wait()
        S.d_l[...] = dot(tc[...], S.prod_l[...])
        S.d_s[...] = dot(tc[...], S.prod_s[...])
        return m_x, q_x, sum_x


    has_above, has_below = r > 0, r < nr - 1

    def halo(i, src, dst, up):
        peer = lax.rem(r + nr - 1, nr) if up else lax.rem(r + 1, nr)
        return pltpu.make_async_remote_copy(
            src, dst, S.halo_send.at[i], S.halo_recv.at[i], device_id=(b, peer), device_id_type=MESH
        )

    def halo_start(up, down):
        @pl.when(has_above)
        def _():
            up.start()

        @pl.when(has_below)
        def _():
            down.start()

    def halo_wait(up, down, above, below):
        @pl.when(has_below)
        def _():
            up.wait_recv()
            down.wait_send()

        @pl.when(has_above)
        def _():
            down.wait_recv()
            up.wait_send()

        @pl.when(jnp.logical_not(has_above))
        def _():
            above[...] = jnp.zeros((n, C), bf16)

        @pl.when(jnp.logical_not(has_below))
        def _():
            below[...] = jnp.zeros((n, C), bf16)

    m_x, q_x, sum_x = pl.run_scoped(
        front, pltpu.VMEM(S.a_hbm.shape, bf16), pltpu.VMEM(S.b_hbm.shape, bf16), pltpu.VMEM(S.c_hbm.shape, bf16)
    )
    inv_x = lax.rsqrt(q_x + norm_eps)
    small = S.small[...]
    row = lambda i: small[32 + i : 33 + i, :]
    mid_gain = lambda j: small[42 + j : 43 + j, :]
    mid_bias = lambda j: small[25 + j : 26 + j, :]
    m_l, v_l = local(lambda s: S.d_l[s, :], n)
    m_s, v_s = local(lambda s: S.d_s[s, :], n)
    ld_c.wait()

    def early():
        order(2 * C // 128, (2 * C + FF) // 128)

        def low(s, a):
            S.gy_low[s, :] = S.cot[s, :].astype(bf16)
            return a

        chunks(n, low)

    tot = share(
        1, jnp.concatenate([m_l, m_s, v_l, v_s], axis=0), merge_stats(2), early,
        lambda: order((2 * C + FF) // 128, (2 * C + 2 * FF) // 128),
    )
    m_l, m_s = tot[0:1], tot[1:2]
    inv_l, inv_s = lax.rsqrt(tot[2:3] / every + norm_eps), lax.rsqrt(tot[3:4] / every + norm_eps)

    def pair(s, a):
        hl = (S.d_l[s, :] - m_l) * inv_l
        hs = (S.d_s[s, :] - m_s) * inv_s
        S.d_l[s, :] = hl
        S.d_s[s, :] = hs
        t, d = gelu_both(hl * row(2) + row(3) + hs * row(4) + row(5))
        S.s_val[s, :] = d
        S.t_low[s, :] = t.astype(bf16)
        return a

    chunks(n, pair)
    S.p_val[...] = dot(S.t_low[...], S.tab[pl.ds(C, C), :])
    m_p = close(chunks(n, lambda s, a: a + fold(S.p_val[s, :]), zero)) * (1.0 / n)

    def proj(s, a):
        d = S.p_val[s, :] - m_p
        return a[0] + fold(d * d), a[1] + fold(d * (S.x[s, :] - m_x))

    v_p, cross = chunks(n, proj, (zero, zero))
    tot = share(2, jnp.concatenate([m_p, close(v_p), close(cross) + m_p * sum_x], axis=0), merge_stats(1))
    m_p, q_p, cov = tot[0:1], tot[1:2] / every, tot[2:3] / every
    inv_p = lax.rsqrt(q_p + norm_eps)
    slope = row(6) * inv_p
    m_f = m_x + row(7)
    q_f = jnp.maximum(q_x + 2 * slope * cov + slope * slope * q_p, 0.0)
    inv_f = lax.rsqrt(q_f + norm_eps)
    hats = inv_f * inv_p * (cov + slope * q_p)

    def ffn(s, a):
        ph = (S.p_val[s, :] - m_p) * inv_p
        S.p_val[s, :] = ph
        m = S.x[s, :] + (ph * row(6) + row(7))
        S.mid[s, :] = m
        S.c_low[s, :] = ((m - m_f) * (inv_f * row(8)) + row(9)).astype(bf16)
        g = S.cot[s, :]
        return a[0] + fold(g), a[1] + fold(g * ph)

    sum_c, sum_ch = chunks(n, ffn, (zero, zero))
    sum_c, sum_ch = close(sum_c), close(sum_ch)

    def middle(hid, gact, a_low, gh_low):
        for j in range(blocks):
            hid[j] = dot(S.c_low[...], S.tab[up_rows(j), :])
        st = [local(lambda s, j=j: hid[j, s, :], n) for j in range(blocks)]

        def back_first():
            for j in range(blocks):
                gact[j] = dot(S.gy_low[...], S.tab[down_rows(j), :], (1, 1))

        tot = share(3, jnp.concatenate([s[0] for s in st] + [s[1] for s in st], axis=0), merge_stats(blocks), back_first)
        m_h = tot[:blocks]
        inv_h = lax.rsqrt(tot[blocks:] / every + norm_eps)
        sums = []
        for j in range(blocks):
            mj, ij, gj, bj = m_h[j : j + 1], inv_h[j : j + 1], mid_gain(j), mid_bias(j)

            def hidden(s, a, j=j, mj=mj, ij=ij, gj=gj, bj=bj):
                hat = (hid[j, s, :] - mj) * ij
                hid[j, s, :] = hat
                v, d = gelu_both(hat * gj + bj)
                a_low[j, s, :] = v.astype(bf16)
                g = gact[j, s, :] * d
                gact[j, s, :] = g
                return a[0] + fold(g), a[1] + fold(g * hat)

            sums.append(tuple(close(v) for v in chunks(n, hidden, (zero, zero))))
        mid_rows = jnp.concatenate([s[0] for s in sums] + [s[1] for s in sums], axis=0)

        def down_grads():
            for j in range(blocks):
                for h in range(C // 256):
                    put(S.flat, 2 * C + FF + j * C + h * 256, dot(a_low[j, :, half_cols(h)], S.gy_low[...], (0, 0)))

        def outputs():
            S.out[...] = S.mid[...]
            for j in range(blocks):
                S.out[...] += dot(a_low[j], S.tab[down_rows(j), :])

        tot = share(4, mid_rows, merge_sum, down_grads, outputs) * (1.0 / every)
        out_copy.start()
        for j in range(blocks):
            tb_, tg_, sc = tot[j : j + 1], tot[blocks + j : blocks + j + 1], mid_gain(j) * inv_h[j : j + 1]

            def grad_h(s, a, j=j, tb_=tb_, tg_=tg_, sc=sc):
                gh_low[j, s, :] = (sc * (gact[j, s, :] - tb_ - hid[j, s, :] * tg_)).astype(bf16)
                return a

            chunks(n, grad_h)
        S.g_f[...] = dot(gh_low[0], S.tab[up_rows(0), :], (1, 1))
        for j in range(1, blocks):
            S.g_f[...] += dot(gh_low[j], S.tab[up_rows(j), :], (1, 1))

        def ffn_sums(s, a):
            g = S.g_f[s, :]
            hat = (S.mid[s, :] - m_f) * inv_f
            return a[0] + fold(g), a[1] + fold(g * hat), a[2] + fold(g * S.p_val[s, :])

        b_ffn, g_ffn, g_fp = (close(v) for v in chunks(n, ffn_sums, (zero, zero, zero)))

        def grad_up():
            for j in range(blocks):
                for h in range(C // 256):
                    put(S.flat, 2 * C + j * C + h * 256, dot(S.c_low[:, half_cols(h)], gh_low[j], (0, 0)))

        tot = share(5, jnp.concatenate([b_ffn, g_ffn, g_fp, sum_c, sum_ch], axis=0), merge_sum, grad_up) * (1.0 / every)
        return mid_rows, b_ffn, g_ffn, tot

    out_copy = pltpu.make_async_copy(S.out, S.out_hbm, S.load_sem.at[7])
    hidden_shape = (blocks, n, C)
    mid_rows, b_ffn, g_ffn, tot = pl.run_scoped(
        middle, pltpu.VMEM(hidden_shape, f32), pltpu.VMEM(hidden_shape, f32), pltpu.VMEM(hidden_shape, bf16), pltpu.VMEM(hidden_shape, bf16)
    )

    def back(tat, tbt, tct, acc):
        ld_ct, ld_at, ld_bt = load(3, S.ct_hbm, tct), load(4, S.at_hbm, tat), load(5, S.bt_hbm, tbt)
        for copy in (ld_ct, ld_at, ld_bt):
            copy.start()
        scale_f = row(8) * inv_f
        mean_hat = tot[4:5] + scale_f * (tot[2:3] - tot[1:2] * hats)

        def grad_mid(s, a):
            hat = (S.mid[s, :] - m_f) * inv_f
            g = S.cot[s, :] + scale_f * (S.g_f[s, :] - tot[0:1] - hat * tot[1:2])
            S.g_f[s, :] = g
            ph = S.p_val[s, :]
            S.gp_low[s, :] = (slope * (g - tot[3:4] - ph * mean_hat)).astype(bf16)
            return a[0] + fold(g), a[1] + fold(g * ph)

        b_proj, g_proj = (close(v) for v in chunks(n, grad_mid, (zero, zero)))
        S.p_val[...] = dot(S.gp_low[...], S.tab[pl.ds(C, C), :], (1, 1))

        def grad_s(s, a):
            g = S.p_val[s, :] * S.s_val[s, :]
            S.p_val[s, :] = g
            return a[0] + fold(g), a[1] + fold(g * S.d_l[s, :]), a[2] + fold(g * S.d_s[s, :])

        b_pair, g_lg, g_sg = (close(v) for v in chunks(n, grad_s, (zero, zero, zero)))

        def grad_out():
            for h in range(C // 256):
                put(S.flat, C + h * 256, dot(S.t_low[:, half_cols(h)], S.gp_low[...], (0, 0)))

        sums = share(6, jnp.concatenate([b_pair, g_lg, g_sg], axis=0), merge_sum, grad_out) * (1.0 / every)
        sc_l, sc_s = row(2) * inv_l, row(4) * inv_s
        gl_low, gs_low = S.t_low, S.gp_low

        def grad_pair(s, a):
            g = S.p_val[s, :] - sums[0:1]
            gl_low[s, :] = (sc_l * (g - S.d_l[s, :] * sums[1:2])).astype(bf16)
            gs_low[s, :] = (sc_s * (g - S.d_s[s, :] * sums[2:3])).astype(bf16)
            return a

        chunks(n, grad_pair)
        ld_ct.wait()

        @pl.loop(0, NF // 256)
        def _(t):
            re, im = pl.ds(pl.multiple_of(t * 256, 256), 256), pl.ds(pl.multiple_of(NF + t * 256, 256), 256)
            acc[0] = dot(tct[re, :], gl_low[...])
            acc[1] = dot(tct[im, :], gl_low[...])
            acc[2] = dot(tct[re, :], gs_low[...])
            acc[3] = dot(tct[im, :], gs_low[...])

            @pl.loop(0, 8)
            def _(i):
                s = pl.ds(pl.multiple_of(i * 32, 32), 32)
                re = pl.ds(pl.multiple_of(t * 256 + i * 32, 32), 32)
                im = pl.ds(pl.multiple_of(NF + t * 256 + i * 32, 32), 32)
                lr, li, sr, si = acc[0, s, :], acc[1, s, :], acc[2, s, :], acc[3, s, :]
                kr, ki = S.spec_l[re, :], S.spec_l[im, :]
                hr, hi = S.spec_s[re, :], S.spec_s[im, :]
                S.prod_k[re, :] = (lr * kr - li * ki + sr * hr - si * hi).astype(bf16)
                S.prod_k[im, :] = (lr * ki + li * kr + sr * hi + si * hr).astype(bf16)
                ur, ui = S.spec_u[re, :], S.spec_u[im, :]
                S.prod_l[re, :] = (lr * ur + li * ui).astype(bf16)
                S.prod_l[im, :] = (lr * ui - li * ur).astype(bf16)
                S.prod_s[re, :] = (sr * ur + si * ui).astype(bf16)
                S.prod_s[im, :] = (sr * ui - si * ur).astype(bf16)

        ld_at.wait()
        halo_up = halo(2, S.halo_out.at[0], S.halo_in.at[1], True)
        halo_down = halo(3, S.halo_out.at[1], S.halo_in.at[0], False)
        S.halo_out[0] = dot(tat[pl.ds(0, n), :], S.prod_k[...]).astype(bf16)

        @pl.when(has_above)
        def _():
            halo_up.start()

        S.halo_out[1] = dot(tat[pl.ds(2 * n, n), :], S.prod_k[...]).astype(bf16)

        @pl.when(has_below)
        def _():
            halo_down.start()

        S.p_val[...] = dot(tat[pl.ds(n, n), :], S.prod_k[...])
        ld_bt.wait()

        @pl.loop(0, 4)
        def _(t):
            s = pl.ds(pl.multiple_of(t * 256, 256), 256)
            put(S.flat, 2 * C + 2 * FF + t * 256, dot(tbt[s, :], S.prod_l[...]))

        put(S.flat, BASE, dot(S.bst[...], S.prod_s[...]))
        halo_wait(halo_up, halo_down, S.halo_in.at[0], S.halo_in.at[1])
        gz_low = S.t_low

        def grad_z(s, a):
            g = S.p_val[s, :] + S.halo_in[0, s, :].astype(f32) + S.halo_in[1, s, :].astype(f32)
            gz_low[s, :] = (g * S.dz[s, :]).astype(bf16)
            return a

        chunks(n, grad_z)
        S.p_val[...] = dot(gz_low[...], S.tab[pl.ds(0, C), :], (1, 1))

        def pre_sums(s, a):
            g = S.p_val[s, :]
            return a[0] + fold(g), a[1] + fold(g * ((S.x[s, :] - m_x) * inv_x))

        b_pre, g_pre = (close(v) for v in chunks(n, pre_sums, (zero, zero)))
        share_send(7, 0, jnp.concatenate([b_pre, g_pre], axis=0))
        for h in range(C // 256):
            put(S.flat, h * 256, dot(S.pre_low[:, half_cols(h)], gz_low[...], (0, 0)))
        norms = [g_pre, b_pre, g_lg, b_pair, g_sg, b_pair, g_proj, b_proj, g_ffn, b_ffn]
        norms += [mid_rows[blocks + j : blocks + j + 1] for j in range(blocks)]
        put(S.flat, BASE + 32, jnp.concatenate(norms + [jnp.zeros((2, C), f32)], axis=0))
        for j in range(blocks):
            for k in range(4):
                S.flat[pl.ds((BASE + 25 + j) * 4 + k, 1), :] = mid_rows[j : j + 1, k * 128 : (k + 1) * 128]

    pl.run_scoped(
        back, pltpu.VMEM(S.at_hbm.shape, bf16), pltpu.VMEM(S.bt_hbm.shape, bf16), pltpu.VMEM(S.ct_hbm.shape, bf16), pltpu.VMEM((4, 256, C), f32)
    )


    plan = reduce_plan(nb)
    parts = len(plan)
    by_z = first_along_z(nb, lines)
    main = lines - by_z
    size = main // parts
    z_size = by_z // parts
    unit = 64 if own % 64 == 0 else 8
    tmp = S.tmp
    hop_base = nz * nb
    z_base = hop_base + nz * (nb - 1)

    def tail(sib_out, pair, z_out):
        grad = S.flat.reshape(total, 4, 128)

        def column(i):
            return lax.rem(z + 1 + i, nz)

        def collect(m, zz, cc):
            start = (flip(b, m) * nr + 2 * zz + cc) * own

            @pl.loop(0, own // unit)
            def _(g):
                at = start + g * unit
                for u in range(unit):
                    tmp[pl.ds(pl.multiple_of((g * unit + u) * 4, 4), 4), :] = grad[S.idx[at // 128, lax.rem(at, 128) + u]]

        def to_sibling(i, m):
            return pltpu.make_async_remote_copy(
                sib_out.at[i, m], rows_in.at[i * nb + m], S.sib_send.at[i, m], S.sib_recv.at[i, m],
                device_id=sibling, device_id_type=MESH,
            )

        def rows_of(p):
            return pl.ds(p * size, size)

        def slots(p, t):
            at = sum(len(plan[p][k][2]) for k in range(t))
            return at, len(plan[p][t][2])

        def hop_at(i, p, at, count):
            return rows_in.at[pl.ds(hop_base + i * (nb - 1) + at, count), rows_of(p)]

        def hop(i, p, t, m):
            o, sent, kept = plan[p][t]
            at, _ = slots(p, t)
            landing = rows_in.at[hop_base + i * (nb - 1) + at + kept.index(m ^ (1 << o)), rows_of(p)]
            return pltpu.make_async_remote_copy(
                pair.at[i, m, rows_of(p)], landing, S.hop_send.at[i, p, t], S.hop_recv.at[i, p, t],
                device_id=(flip(b, 1 << o), r), device_id_type=MESH,
            )

        def hop_wait(i, p, t, sem):
            whole = hop_at(i, p, *slots(p, t))
            pltpu.make_async_copy(whole, whole, sem.at[i, p, t]).wait()

        def for_sibling(i):
            for m in reversed(range(nb)):
                collect(m, column(i), 1 - c)
                sib_out[i, m] = tmp[...].astype(bf16)
                to_sibling(i, m).start()

        def to_owner(i):
            return pltpu.make_async_remote_copy(
                z_out.at[i], rows_in.at[z_base + i, pl.ds(0, main)], S.own_send.at[i], S.own_recv.at[i],
                device_id=(b, 2 * column(i) + c), device_id_type=MESH,
            )

        def to_layer(i, m):
            return pltpu.make_async_remote_copy(
                pair.at[i, m, pl.ds(main, by_z)], S.layer_in.at[i, m], S.layer_send.at[i], S.layer_recv.at[i],
                device_id=(b, 2 * column(i) + c), device_id_type=MESH,
            )

        def layer_wait(i, sem):
            pltpu.make_async_copy(S.layer_in.at[i], S.layer_in.at[i], sem.at[i]).wait()

        def z_rows(p):
            return pl.ds(main + p * z_size, z_size)

        def z_hop(p, t, m):
            o, sent, kept = plan[p][t]
            at, _ = slots(p, t)
            return pltpu.make_async_remote_copy(
                pair.at[nz - 1, m, z_rows(p)], S.z_hops.at[p, at + kept.index(m ^ (1 << o))], S.z_hop_send.at[p, t], S.z_hop_recv.at[p, t],
                device_id=(flip(b, 1 << o), r), device_id_type=MESH,
            )

        def z_hop_wait(p, t, sem):
            at, count = slots(p, t)
            whole = S.z_hops.at[p, pl.ds(at, count)]
            pltpu.make_async_copy(whole, whole, sem.at[p, t]).wait()

        def z_start():
            for i in range(nz - 1):
                layer_wait(i, S.layer_recv)
            for m in reversed(range(nb)):
                v = pair[nz - 1, m, pl.ds(main, by_z)].astype(f32)
                for i in range(nz - 1):
                    v = v + S.layer_in[i, m].astype(f32)
                pair[nz - 1, m, pl.ds(main, by_z)] = v.astype(bf16)
                for p in range(parts):
                    if m in plan[p][0][1]:
                        z_hop(p, 0, m).start()

        def z_next(t):
            for p in range(parts):
                z_hop_wait(p, t, S.z_hop_recv)
                at, _ = slots(p, t)
                for k, m in enumerate(plan[p][t][2]):
                    v = pair[nz - 1, m, z_rows(p)].astype(f32) + S.z_hops[p, at + k].astype(f32)
                    if t == parts - 1:
                        tmp[z_rows(p), :] = v
                        continue
                    pair[nz - 1, m, z_rows(p)] = v.astype(bf16)
                    if m in plan[p][t + 1][1]:
                        z_hop(p, t + 1, m).start()

        def first_step(i):
            for m in reversed(range(nb)):
                collect(m, column(i), c)
                to_sibling(i, m).wait_recv()
                pair[i, m] = (tmp[...] + rows_in[i * nb + m].astype(f32)).astype(bf16)
                for p in range(parts):
                    if m in plan[p][0][1]:
                        hop(i, p, 0, m).start()
                if by_z:

                    @pl.when(i < nz - 1)
                    def _():
                        to_layer(i, m).start()

            @pl.when(i < nz - 1)
            def _():
                for_sibling(i + 1)

        def next_step(i, t):
            for p in range(parts):
                hop_wait(i, p, t, S.hop_recv)
                at, _ = slots(p, t)
                for k, m in enumerate(plan[p][t][2]):
                    pair[i, m, rows_of(p)] = (
                        pair[i, m, rows_of(p)].astype(f32)
                        + rows_in[hop_base + i * (nb - 1) + at + k, rows_of(p)].astype(f32)
                    ).astype(bf16)
                    if m in plan[p][t + 1][1]:
                        hop(i, p, t + 1, m).start()

        def last_step(i):
            for p in range(parts):
                hop_wait(i, p, parts - 1, S.hop_recv)
                at, _ = slots(p, parts - 1)
                tmp[rows_of(p), :] = pair[i, 0, rows_of(p)].astype(f32) + rows_in[hop_base + i * (nb - 1) + at, rows_of(p)].astype(f32)

            @pl.when(i < nz - 1)
            def _():
                z_out[i] = tmp[pl.ds(0, main), :].astype(bf16)
                to_owner(i).start()

        def grad_image():
            sums = share_wait(7, 1, merge_sum) * (1.0 / every)
            scale_x = row(0) * inv_x

            def last(s, a):
                hat = (S.x[s, :] - m_x) * inv_x
                S.g_f[s, :] = S.g_f[s, :] + scale_x * (S.p_val[s, :] - sums[0:1] - hat * sums[1:2])
                return a

            chunks(n, last)
            gin_copy.start()
            for i in range(own):
                at = (b * nr + r) * own + i // unit * unit
                p = S.idx[at // 128, lax.rem(at, 128) + i % unit]
                fast = (p >= 2 * C + 2 * FF + KL * KL) & ((p < BASE) | (p >= BASE + KS * KS))
                S.rate[pl.ds(i, 1), :] = jnp.full((1, 128), jnp.where(fast, np.float32(norm_rate), np.float32(matrix_rate)), f32)

        gin_copy = pltpu.make_async_copy(S.g_f, S.gin_hbm, S.load_sem.at[6])
        for_sibling(0)

        @pl.loop(0, nz + parts)
        def _(q):
            @pl.when(q < nz)
            def _():
                first_step(q)

            @pl.when(q == 0)
            def _():
                share_send(7, 1, share_wait(7, 0, merge_sum))

            if by_z:

                @pl.when(q == nz - 1)
                def _():
                    z_start()

            for t in range(parts - 1):

                @pl.when((q >= t + 1) & (q < nz + t + 1))
                def _():
                    next_step(q - t - 1, t)

            @pl.when(q == 1)
            def _():
                grad_image()

            if by_z:

                @pl.when(q == nz)
                def _():
                    for t in range(parts - 1):
                        z_next(t)

            @pl.when(q >= parts)
            def _():
                last_step(q - parts)

        for i in range(nz - 1):
            to_owner(i).wait_recv()
            tmp[pl.ds(0, main), :] += rows_in[z_base + i, pl.ds(0, main)].astype(f32)
        if by_z:
            z_next(parts - 1)
        for j in range(4):
            S.red[:, j * 128 : (j + 1) * 128] = tmp[pl.ds(j, own, stride=4), :]

        @pl.loop(0, nz)
        def _(i):
            for m in range(nb):
                to_sibling(i, m).wait_send()
            for p in range(parts):
                for t in range(parts):
                    hop_wait(i, p, t, S.hop_send)

        for i in range(nz - 1):
            to_owner(i).wait_send()
            if by_z:
                layer_wait(i, S.layer_send)
        if by_z:
            for p in range(parts):
                for t in range(parts):
                    z_hop_wait(p, t, S.z_hop_send)
        gin_copy.wait()

    low_block = lambda *lead: pltpu.VMEM(lead + (lines, 128), bf16)
    pl.run_scoped(tail, low_block(nz, nb), low_block(nz, nb), pltpu.VMEM((nz, main, 128), bf16))
    for e in range(len(WIDTHS)):
        for stage in range(2):
            buf, mine, count = share_stage(e, stage)
            sent = buf.at[pl.ds(0, count - 1)]
            pltpu.make_async_copy(sent, sent, S.stat_send.at[e, stage]).wait()
    out_copy.wait()


def step(x, cot, master, slots, nb, nr):
    (a, at, b, bt, bs, bst, c, ct) = tables()
    n, own, nz, parts = x.shape[0], master.shape[0], nr // 2, nb.bit_length() - 1
    total = slots.size
    vm = lambda *shape: pltpu.VMEM(shape, f32)
    low = lambda *shape: pltpu.VMEM(shape, bf16)
    dma = lambda *shape: pltpu.SemaphoreType.DMA(shape)
    vmem, anywhere = pl.BlockSpec(memory_space=pltpu.VMEM), pl.BlockSpec(memory_space=pl.ANY)
    ins = dict(
        slots_hbm=(slots, anywhere), x_hbm=(x, anywhere), cot_hbm=(cot, anywhere), master_hbm=(master, anywhere),
        a_hbm=(a, anywhere), at_hbm=(at, anywhere), b_hbm=(b, anywhere), bt_hbm=(bt, anywhere), bs=(bs, vmem), bst=(bst, vmem),
        c_hbm=(c, anywhere), ct_hbm=(ct, anywhere),
    )
    image = jax.ShapeDtypeStruct((n, C), f32)
    outs = dict(
        out_hbm=(image, anywhere), gin_hbm=(image, anywhere), red=(jax.ShapeDtypeStruct((own, C), f32), vmem),
        rate=(jax.ShapeDtypeStruct((own, 128), f32), vmem),
    )
    scratch = dict(
        rows_in=low(nb * nr, 4 * own, 128), flat=vm(4 * total, 128), tab=low(total, C), x=vm(n, C), cot=vm(n, C), master=vm(own, C),
        tmp=vm(4 * own, 128), chunk=vm(512, 128), inv=pltpu.VMEM((total // 128, 128), jnp.int32), at_v=pltpu.VMEM((total // 128, 128), jnp.int32),
        idx=pltpu.SMEM((total // 128, 128), jnp.int32),
        inv_at=pltpu.SMEM((total // 128, 128), jnp.int32), small=vm(48, C),
        pre_low=low(n, C), wide=low(3 * n, C), dz=vm(n, C), spec_u=vm(2 * NF, C), spec_l=vm(2 * NF, C), spec_s=vm(2 * NF, C),
        prod_l=low(2 * NF, C), prod_s=low(2 * NF, C), prod_k=low(2 * NF, C), d_l=vm(n, C), d_s=vm(n, C), s_val=vm(n, C),
        t_low=low(n, C), p_val=vm(n, C), mid=vm(n, C), c_low=low(n, C), gy_low=low(n, C), gp_low=low(n, C), g_f=vm(n, C), out=vm(n, C),
        halo_out=low(2, n, C), halo_in=low(2, n, C),
    )
    by_z = first_along_z(nb, 4 * own)
    if by_z:
        scratch.update(
            layer_in=low(nz - 1, nb, by_z, 128), z_hops=low(parts, nb - 1, by_z // parts, 128), layer_send=dma(nz), layer_recv=dma(nz),
            z_hop_send=dma(parts, parts), z_hop_recv=dma(parts, parts),
        )
    for e, w in enumerate(WIDTHS):
        one, two = (2, nb * nz) if by_chip(e, nb * nz) else (nr, nb)
        scratch[f"one{e}"] = vm(one, w, C)
        scratch[f"two{e}"] = vm(two, w, C)
    scratch.update(
        load_sem=dma(9), stat_send=dma(len(WIDTHS), 2), stat_recv=dma(len(WIDTHS), 2), halo_send=dma(4), halo_recv=dma(4),
        z_send=dma(nz), z_recv=dma(nz), b_send=dma(nb, nz), b_recv=dma(nb, nz), half_send=dma(2, nz), half_recv=dma(2, nz),
        core_send=dma(nb, nz), core_recv=dma(nb, nz), rest_send=dma(nb, nz), rest_recv=dma(nb, nz),
        rest_core_send=dma(nb, nz), rest_core_recv=dma(nb, nz), sib_send=dma(nz, nb), sib_recv=dma(nz, nb),
        hop_send=dma(nz, parts, parts), hop_recv=dma(nz, parts, parts), own_send=dma(nz), own_recv=dma(nz),
    )
    return pl.pallas_call(
        functools.partial(step_kernel, nb, nr, [*ins, *outs, *scratch]),
        out_shape=[v[0] for v in outs.values()],
        in_specs=[v[1] for v in ins.values()],
        out_specs=[v[1] for v in outs.values()],
        scratch_shapes=list(scratch.values()),
        compiler_params=pltpu.CompilerParams(collective_id=0, has_side_effects=True, vmem_limit_bytes=62 * 2**20),
    )(*[v[0] for v in ins.values()])


def finish_kernel(*refs):
    ins, outs, bufs, (load_sem, store_sem) = refs[:7], refs[7:14], refs[14:25], refs[25:]
    red, rate, first_ref, second_ref, master_ref, out, gin = bufs[:7]
    new_first, new_second, new_master, new_copy = bufs[7:11]
    loads = [pltpu.make_async_copy(src, dst, load_sem.at[i]) for i, (src, dst) in enumerate(zip(ins, bufs[:7]))]
    for copy in loads:
        copy.start()
    own = red.shape[0]
    size = 64 if own % 64 == 0 else own
    for copy in loads[:5]:
        copy.wait()
    stores = [pltpu.make_async_copy(red, outs[2], store_sem.at[2, 0])]
    stores[0].start()
    for part in range(own // size):
        for k in range(0, size, 8):
            s = slice(part * size + k, part * size + k + 8)
            for j in range(C // 128):
                at = (s, slice(j * 128, (j + 1) * 128))
                g = red[at]
                first = beta_one * first_ref[at] + (1.0 - beta_one) * g
                second = beta_two * second_ref[at] + (1.0 - beta_two) * g * g
                new_first[at] = first
                new_second[at] = second
                first_hat = first / (1.0 - beta_one**STEP)
                second_hat = second / (1.0 - beta_two**STEP)
                master = master_ref[at]
                new_master[at] = master - rate[s, :] * (first_hat / (jnp.sqrt(second_hat) + adam_eps) + decay_rate * master)
        s = pl.ds(part * size, size)
        new_copy[s, :] = new_master[s, :].astype(bf16)
        if part == 0:
            for i in (5, 6):
                loads[i].wait()
                stores.append(pltpu.make_async_copy(bufs[i], outs[i - 5], store_sem.at[i - 5, 0]))
                stores[-1].start()
        for i, buf in enumerate((new_first, new_second, new_master, new_copy)):
            stores.append(pltpu.make_async_copy(buf.at[s], outs[3 + i].at[s], store_sem.at[3 + i, part]))
            stores[-1].start()
    for copy in stores:
        copy.wait()


def finish(reduced, first, second, master, rates, out, gin):
    anywhere = pl.BlockSpec(memory_space=pl.ANY)
    slot = jax.ShapeDtypeStruct(reduced.shape, f32)
    image = jax.ShapeDtypeStruct(out.shape, f32)
    low = jax.ShapeDtypeStruct(reduced.shape, bf16)
    ins = (reduced, rates, first, second, master, out, gin)
    outs = [image, image, slot, slot, slot, slot, low]
    return pl.pallas_call(
        finish_kernel,
        out_shape=outs,
        in_specs=[anywhere] * 7,
        out_specs=[anywhere] * 7,
        scratch_shapes=[pltpu.VMEM(v.shape, f32) for v in ins]
        + [pltpu.VMEM(v.shape, v.dtype) for v in (slot, slot, slot, low)]
        + [pltpu.SemaphoreType.DMA((7,)), pltpu.SemaphoreType.DMA((7, 4))],
        compiler_params=pltpu.CompilerParams(vmem_limit_bytes=62 * 2**20),
    )(*ins)


def body(image_in, cotangent, slot_rows, master, first_moment, second_moment):
    n = image_in.shape[0] * image_in.shape[1] * image_in.shape[2]
    nb, nr = lax.axis_size("batch"), lax.axis_size("rows")
    out, grad_in, reduced, rates = step(
        image_in.reshape(n, C), cotangent.reshape(n, C), master, slot_rows.reshape(-1, 128), nb, nr
    )
    result, grad_x, *slots = finish(reduced, first_moment, second_moment, master, rates, out, grad_in)
    return (result.reshape(image_in.shape), grad_x.reshape(image_in.shape), *slots)


def solution(mesh):
    image = P("batch", "rows", None, None)
    owner = P(AXES, None)
    return jax.shard_map(
        body,
        mesh=mesh,
        in_specs=(image, image, P(), owner, owner, owner),
        out_specs=(image, image, owner, owner, owner, owner, owner),
        check_vma=False,
    )
```

```python
import functools
import types

import jax
import jax.numpy as jnp
import numpy as np
from jax import lax
from jax.experimental import pallas as pl
from jax.experimental.pallas import tpu as pltpu
from jax.sharding import PartitionSpec as P

C = 512
FF = 2048
KL = 31
KS = 5
STEP = 10

norm_eps = 1e-05
beta_one = 0.9
beta_two = 0.999
adam_eps = 1e-08
decay_rate = 0.05
matrix_rate = 0.05
norm_rate = 0.5

TH = 16
TW = 16
NY = 47
NX = 31
NF = 768
REACH = (KL - 1) // 2
AXES = ("batch", "rows")
f32 = jnp.float32
bf16 = jnp.bfloat16


@functools.lru_cache(None)
def tables():
    freqs = [(ky, 0) for ky in range((NY + 1) // 2)]
    freqs += [(ky, kx) for kx in range(1, (NX + 1) // 2) for ky in range(NY)]
    ky = np.array([f[0] for f in freqs], np.int64)[:, None]
    kx = np.array([f[1] for f in freqs], np.int64)[:, None]
    pad = NF - len(freqs)

    def angle(rows, cols):
        ty = (ky * rows.reshape(1, -1)) % NY
        tx = (kx * cols.reshape(1, -1)) % NX
        return 2 * np.pi * (ty / NY + tx / NX)

    def grid(rows, cols):
        r, c = np.meshgrid(rows, cols, indexing="ij")
        return r.reshape(-1), c.reshape(-1)

    def stack(re, im):
        z = np.zeros((pad, re.shape[1]))
        return np.concatenate([re, z, im, z], axis=0)

    r, c = grid(np.arange(-TH, 2 * TH), np.arange(TW))
    used = ((r + REACH >= 0) & (r + REACH < NY - 1)).astype(np.float64)[None]
    t = angle(r + REACH, c)
    a = stack(np.cos(t) * used, -np.sin(t) * used)
    i, j = grid(np.arange(KL), np.arange(KL))
    t = angle(i, j - REACH)
    b = stack(np.cos(t), -np.sin(t))
    lead = REACH - (KS - 1) // 2
    small = ((i >= lead) & (i < lead + KS) & (j >= lead) & (j < lead + KS)).nonzero()[0]
    bs = np.pad(b[:, small], ((0, 0), (0, 32 - KS * KS)))
    b = np.pad(b, ((0, 0), (0, 2 * C - KL * KL)))
    y, x = grid(np.arange(TH), np.arange(TW))
    t = angle(y, x)
    w = np.full((len(freqs), 1), 2.0)
    w[0] = 1.0
    w /= NY * NX
    ct = stack(w * np.cos(t), -w * np.sin(t))
    return tuple(m.astype(np.float32).astype(bf16) for m in (a, a.T, b, b.T, bs, bs.T, ct.T, ct))


def dot(a, b, dims=(1, 0)):
    return lax.dot_general(a, b, (((dims[0],), (dims[1],)), ((), ())), preferred_element_type=f32)


MESH = pl.DeviceIdType.MESH
WIDTHS = (2, 4, 3, 8, 8, 5, 3, 2)
BY_CHIP = (1, 2, 5, 6)
BASE = 2 * C + 2 * FF + 976


def chunks(n, fn, init=()):
    return lax.fori_loop(0, n // 32, lambda i, c: fn(pl.ds(pl.multiple_of(i * 32, 32), 32), c), init)


def fold(v):
    return jnp.sum(v.reshape(v.shape[0] // 8, 8, v.shape[1]), axis=0)


def close(v):
    return jnp.sum(v, axis=0, keepdims=True)


def put(ref, start, v):
    for j in range(4):
        ref[pl.ds(start * 4 + j, v.shape[0], stride=4), :] = v[:, j * 128 : (j + 1) * 128]


def gelu_both(v):
    a = np.float32(np.sqrt(2 / np.pi))
    sq = v * v
    t = jnp.tanh(a * (v + 0.044715 * (sq * v)))
    half = 0.5 * (1 + t)
    return v * half, half + 0.5 * v * (1 - t * t) * (a * (1 + 3 * 0.044715 * sq))


def flip(b, m):
    k = 0
    while m >> k:
        if (m >> k) & 1:
            b = b + (1 - 2 * lax.rem(b // 2**k, 2)) * 2**k
        k += 1
    return b


def reduce_plan(nb):
    bits = nb.bit_length() - 1
    plan = []
    for p in range(bits):
        order = [(p + t) % bits for t in range(bits)]
        steps, kept = [], list(range(nb))
        for o in order:
            sent = [m for m in kept if (m >> o) & 1]
            kept = [m for m in kept if not (m >> o) & 1]
            steps.append((o, sent, kept))
        plan.append(steps)
    return plan


def first_along_z(nb, lines):
    return lines // 6 if nb == 4 and lines % 192 == 0 else 0


def by_chip(e, chips):
    return e in BY_CHIP and chips <= 32


def merge_sum(v, count):
    return jnp.sum(v, axis=0)


def merge_stats(h):
    def merge(v, count):
        means = v[:, :h]
        m = jnp.sum(means, axis=0) * (1.0 / v.shape[0])
        d = means - m
        parts = [m, jnp.sum(v[:, h : 2 * h], axis=0) + count * jnp.sum(d * d, axis=0)]
        if v.shape[1] > 2 * h:
            parts.append(jnp.sum(v[:, 2 * h :], axis=0))
        return jnp.concatenate(parts, axis=0)

    return merge


def local(read, n):
    zero = jnp.zeros((8, C), f32)
    m = close(chunks(n, lambda s, c: c + fold(read(s)), zero)) * (1.0 / n)

    def sq(s, c):
        d = read(s) - m
        return c + fold(d * d)

    return m, close(chunks(n, sq, zero))


def half_cols(h):
    return pl.ds(pl.multiple_of(h * 256, 256), 256)


def up_rows(j):
    return pl.ds(pl.multiple_of(2 * C + j * C, C), C)


def down_rows(j):
    return pl.ds(pl.multiple_of(2 * C + FF + j * C, C), C)


def table_place(t):
    start = 2 * C + 2 * FF
    k_end = start + KL * KL
    s_end = k_end + KS * KS
    m_gain = s_end + 10
    m_bias = m_gain + FF // C
    m_end = m_bias + FF // C
    up = t - 2 * C
    up = 2 * C + (up & (FF // C - 1)) * C + (up >> ((FF // C).bit_length() - 1))
    base = start + 976
    unused = t - m_end
    unused = jnp.where(unused < 15, k_end + unused, jnp.where(unused < 18, base + 29 + unused - 15, base + 46 + unused - 18))
    p = jnp.where((t >= 2 * C) & (t < 2 * C + FF), up, t)
    p = jnp.where(t >= k_end, t - k_end + base, p)
    p = jnp.where(t >= s_end, t - s_end + base + 32, p)
    p = jnp.where(t >= m_bias, t - m_bias + base + 25, p)
    return jnp.where(t >= m_end, unused, p)


def step_kernel(nb, nr, names, *refs):
    S = types.SimpleNamespace(**dict(zip(names, refs)))
    nz = nr // 2
    nd = nb * nr
    n = S.x.shape[0]
    own = S.master.shape[0]
    lines = 4 * own
    total = S.tab.shape[0]
    every = float(n * nd)
    b = lax.axis_index("batch")
    r = lax.axis_index("rows")
    z, c = r // 2, lax.rem(r, 2)
    sibling = (b, r + 1 - 2 * c)
    square = nb == 4
    blocks = FF // C
    zero = jnp.zeros((8, C), f32)
    rows_in = S.rows_in

    def load(i, src, dst):
        return pltpu.make_async_copy(src, dst, S.load_sem.at[i])

    ld_m, ld_x, ld_c = load(0, S.master_hbm, S.master), load(1, S.x_hbm, S.x), load(2, S.cot_hbm, S.cot)
    ld_s = load(8, S.slots_hbm, S.at_v)
    for copy in (ld_s, ld_m, ld_x, ld_c):
        copy.start()
    barrier = pltpu.get_barrier_semaphore()
    for k in range(1, nr):
        pl.semaphore_signal(barrier, inc=1, device_id=(b, lax.rem(r + k, nr)), device_id_type=MESH)
    for m in range(1, nb):
        pl.semaphore_signal(barrier, inc=1, device_id=(flip(b, m), r), device_id_type=MESH)

    @pl.loop(0, (nb - 1) * (nz - 1))
    def _(k):
        at = (lax.rem(b + 1 + k // (nz - 1), nb), 2 * lax.rem(z + 1 + lax.rem(k, nz - 1), nz) + c)
        pl.semaphore_signal(barrier, inc=1, device_id=at, device_id_type=MESH)


    def share_stage(e, stage):
        buf = getattr(S, ("one" if stage == 0 else "two") + str(e))
        if by_chip(e, nb * nz):
            return (buf, c, 2) if stage == 0 else (buf, b * nz + z, nb * nz)
        return (buf, r, nr) if stage == 0 else (buf, b, nb)

    def share_peer(e, stage, k):
        if by_chip(e, nb * nz):
            if stage == 0:
                return sibling
            other = lax.rem(b * nz + z + k, nb * nz)
            return (other // nz, 2 * lax.rem(other, nz) + c)
        return (b, lax.rem(r + k, nr)) if stage == 0 else (lax.rem(b + k, nb), r)

    def share_send(e, stage, v):
        buf, mine, size = share_stage(e, stage)
        buf[mine] = v

        def one(k):
            pltpu.make_async_remote_copy(
                buf.at[mine], buf.at[mine], S.stat_send.at[e, stage], S.stat_recv.at[e, stage],
                device_id=share_peer(e, stage, k), device_id_type=MESH,
            ).start()

        if size > 8:
            pl.loop(1, size)(one)
        else:
            for k in range(1, size):
                one(k)

    def share_wait(e, stage, merge):
        buf, mine, size = share_stage(e, stage)
        got = buf.at[pl.ds(0, size - 1)]
        pltpu.make_async_copy(got, got, S.stat_recv.at[e, stage]).wait()
        return merge(buf[...], float(n if stage == 0 else n * getattr(S, f"one{e}").shape[0]))

    def share(e, v, merge, work=None, more=None):
        share_send(e, 0, v)
        if work and not by_chip(e, nb * nz):
            work()
        v = share_wait(e, 0, merge)
        share_send(e, 1, v)
        if work and by_chip(e, nb * nz):
            work()
        if more:
            more()
        return share_wait(e, 1, merge)


    def place(m, zz, core):
        return flip(b, m) * nr + 2 * zz + core

    spread = first_along_z(nb, lines) * 3 // 4
    rest = pl.ds(lines - spread, spread)

    def lines_of(k):
        return lines if k == 0 else lines - spread

    def part(m, zz, core, k):
        return rows_in.at[place(m, zz, core), pl.ds(0, lines_of(k))]

    def along_z(zz, up):
        at = part(0, zz, c, 1)
        return pltpu.make_async_remote_copy(
            at, at, S.z_send.at[zz], S.z_recv.at[zz], device_id=(b, r + 2 if up else r - 2), device_id_type=MESH
        )

    def to_peer(m, zz, k):
        at = part(0, zz, c, k)
        return pltpu.make_async_remote_copy(
            at, at, S.b_send.at[m, zz], S.b_recv.at[m, zz], device_id=(flip(b, m), r), device_id_type=MESH
        )

    def from_peer(m, zz, k):
        at = part(m, zz, c, k)
        return pltpu.make_async_copy(at, at, S.b_recv.at[m, zz])

    def half(m, zz, h, to, k):
        size = lines_of(k) // 2
        at = rows_in.at[place(m, zz, c), pl.ds(h * size, size)]
        return pltpu.make_async_remote_copy(
            at, at, S.half_send.at[h, zz], S.half_recv.at[h, zz], device_id=(flip(b, to), r), device_id_type=MESH
        )

    def to_other_core(m, zz, core, k):
        at = part(m, zz, core, k)
        return pltpu.make_async_remote_copy(
            at, at, S.core_send.at[m, zz], S.core_recv.at[m, zz], device_id=sibling, device_id_type=MESH
        )

    def cast(m, zz, core, k):
        d = place(m, zz, core)
        S.flat[pl.ds(pl.multiple_of(d * lines, lines), lines_of(k)), :] = rows_in[d, pl.ds(0, lines_of(k))].astype(f32)

    def rest_out(m, zz):
        at = rows_in.at[place(m, z, c), rest]
        return pltpu.make_async_remote_copy(
            at, at, S.rest_send.at[m, zz], S.rest_recv.at[m, z], device_id=(b, 2 * zz + c), device_id_type=MESH
        )

    def rest_in(m, zz):
        at = rows_in.at[place(m, zz, c), rest]
        return pltpu.make_async_copy(at, at, S.rest_recv.at[m, zz])

    def rest_to_core(m, zz, core):
        at = rows_in.at[place(m, zz, core), rest]
        return pltpu.make_async_remote_copy(
            at, at, S.rest_core_send.at[m, zz], S.rest_core_recv.at[m, zz], device_id=sibling, device_id_type=MESH
        )

    def rest_cast(m, zz, core):
        d = place(m, zz, core)
        S.flat[pl.ds(pl.multiple_of(d * lines + lines - spread, 32), spread), :] = rows_in[d, rest].astype(f32)

    direct = [m for m in range(1, nb) if not (square and m == 3)]

    def each(k, fn):
        if k == 0:
            fn(z, True, True)
            return

        @pl.when(z >= k)
        def _():
            fn(z - k, True, False)

        @pl.when(z + k < nz)
        def _():
            fn(z + k, False, True)

    def onward(zz, below, above, act):
        if below:

            @pl.when(z < nz - 1)
            def _():
                act(along_z(zz, True))

        if above:

            @pl.when(z > 0)
            def _():
                act(along_z(zz, False))

    def own_column(k):
        def go(zz, below, above):
            if k:
                along_z(zz, below).wait_recv()
            onward(zz, below, above, lambda copy: copy.start())
            for m in direct:
                to_peer(m, zz, k).start()
            to_other_core(0, zz, c, k).start()
            cast(0, zz, c, k)

        each(k, go)

    def pass_on(k):
        def go(zz, below, above):
            for m in direct:
                from_peer(m, zz, k).wait()
                if square:
                    half(m, zz, 2 - m, 3 - m, k).start()
                to_other_core(m, zz, c, k).start()
                cast(m, zz, c, k)

        each(k, go)

    def corner(k):
        def go(zz, below, above):
            for h in range(2):
                half(3, zz, h, 0, k).wait_recv()
            if k == 0 and spread:
                for d in range(1, nz):
                    for m in range(nb):
                        rest_out(m, lax.rem(z + d, nz)).start()
            to_other_core(3, zz, c, k).start()
            cast(3, zz, c, k)

        if square:
            each(k, go)

    def other_core(k):
        def go(zz, below, above):
            for m in range(nb):
                to_other_core(m, zz, 1 - c, k).wait_recv()
                cast(m, zz, 1 - c, k)

        each(k, go)

    def rest_here(k):
        def go(zz, below, above):
            for m in range(nb):
                rest_in(m, zz).wait()
                rest_to_core(m, zz, c).start()
                rest_cast(m, zz, c)

        if spread:
            each(k, go)

    def rest_there(k):
        def go(zz, below, above):
            for m in range(nb):
                rest_to_core(m, zz, 1 - c).wait_recv()
                rest_cast(m, zz, 1 - c)

        if spread:
            each(k, go)

    def gather_sent(k):
        def go(zz, below, above):
            onward(zz, below, above, lambda copy: copy.wait_send())
            for m in direct:
                to_peer(m, zz, k).wait_send()
                if square:
                    half(m, zz, 2 - m, 3 - m, k).wait_send()
            for m in range(nb):
                to_other_core(m, zz, c, k).wait_send()
                if spread and k:
                    rest_out(m, zz).wait_send()
                    rest_to_core(m, zz, c).wait_send()

        each(k, go)

    def find(part, parts):
        tiles = total // 1024
        unit = 16
        spots = [
            lax.broadcasted_iota(jnp.int32, (8, 128), 0) * 128 + lax.broadcasted_iota(jnp.int32, (8, 128), 1) + 1024 * k
            for k in range(tiles)
        ]

        def some(g, acc):
            for u in range(unit):
                start = g * unit
                s = start + u
                p = S.idx[start // 128, lax.rem(start, 128) + u]
                acc = [jnp.where(spot == p, s, a) for spot, a in zip(spots, acc)]
            return acc

        acc = [S.inv[k * 8 : k * 8 + 8, :] if part else jnp.zeros((8, 128), jnp.int32) for k in range(tiles)]
        groups = total // unit
        acc = lax.fori_loop(groups * part // parts, groups * (part + 1) // parts, some, acc)
        for k in range(tiles):
            S.inv[k * 8 : k * 8 + 8, :] = acc[k]

    def order(start, stop):
        flat = S.flat.reshape(total, 4, 128)

        @pl.loop(start, stop)
        def _(t):
            for u in range(128):
                S.chunk[4 * u : 4 * u + 4, :] = flat[S.inv_at[t, u]]

            rows = pl.ds(pl.multiple_of(t * 128, 128), 128)
            for j in range(4):
                S.tab[rows, j * 128 : (j + 1) * 128] = S.chunk[pl.ds(j, 128, stride=4), :].astype(bf16)

    def front(ta, tb, tc):
        ld_a, ld_b, ld_t = load(3, S.a_hbm, ta), load(4, S.b_hbm, tb), load(5, S.c_hbm, tc)
        for copy in (ld_b, ld_a, ld_t):
            copy.start()
        ld_s.wait()
        S.at_v[...] = table_place(S.at_v[...])
        to_scalar = pltpu.make_async_copy(S.at_v, S.idx, S.load_sem.at[8])
        to_scalar.start()
        ld_m.wait()
        for j in range(4):
            S.tmp[pl.ds(j, own, stride=4), :] = S.master[:, j * 128 : (j + 1) * 128]
        rows_in[place(0, z, c)] = S.tmp[...].astype(bf16)
        pl.semaphore_wait(barrier, nr - 1 + nb - 1 + (nb - 1) * (nz - 1))
        own_column(0)
        to_scalar.wait()
        ld_x.wait()
        share_send(0, 0, jnp.concatenate(local(lambda s: S.x[s, :], n), axis=0))
        steps = 3 * max(nz - 1, 1)
        for k in range(1, nz):
            find(3 * k - 3, steps)
            own_column(k)
            find(3 * k - 2, steps)
            pass_on(k - 1)
            find(3 * k - 1, steps)
            if k == 2:
                corner(0)
            if k > 2:
                other_core(k - 3)
            if k == 1:
                share_send(0, 1, share_wait(0, 0, merge_stats(1)))
        if nz == 1:
            for part in range(3):
                find(part, 3)
            share_send(0, 1, share_wait(0, 0, merge_stats(1)))
        to_scalar = pltpu.make_async_copy(S.inv, S.inv_at, S.load_sem.at[6])
        to_scalar.start()
        pass_on(nz - 1)
        for k in range(1 if nz > 2 else 0, nz - 1):
            corner(k)
        for k in range(1, nz):
            rest_here(k)
        corner(nz - 1)
        for k in range(max(nz - 3, 0), nz):
            other_core(k)
        for k in range(1, nz):
            rest_there(k)
        tot = share_wait(0, 1, merge_stats(1))
        m_x, q_x = tot[0:1], tot[1:2] * (1.0 / every)
        inv_x = lax.rsqrt(q_x + norm_eps)
        to_scalar.wait()
        tiles = total // 128
        late = (2 * C + 2 * FF) // 128
        order(0, C // 128)
        order(tiles - 2, tiles)

        for k in range(nz):
            gather_sent(k)

        small = S.tab[pl.ds(BASE, 48), :].astype(f32)
        S.small[...] = small
        row = lambda i: small[32 + i : 33 + i, :]

        def pre(s, sx):
            d = S.x[s, :] - m_x
            S.pre_low[s, :] = (d * (inv_x * row(0)) + row(1)).astype(bf16)
            return sx + fold(d)

        sum_x = close(chunks(n, pre, zero))
        S.dz[...] = dot(S.pre_low[...], S.tab[pl.ds(0, C), :])

        def act(s, a):
            u, d = gelu_both(S.dz[s, :])
            S.dz[s, :] = d
            S.wide[pl.ds(pl.multiple_of(n + s.start, 32), 32), :] = u.astype(bf16)
            return a

        chunks(n, act)
        mine = S.wide.at[pl.ds(n, n)]
        halo_up = halo(0, mine, S.wide.at[pl.ds(2 * n, n)], True)
        halo_down = halo(1, mine, S.wide.at[pl.ds(0, n)], False)
        halo_start(halo_up, halo_down)
        order(late, tiles - 2)
        order(C // 128, 2 * C // 128)

        ld_b.wait()

        @pl.loop(0, 2 * NF // 256)
        def _(t):
            s = pl.ds(pl.multiple_of(t * 256, 256), 256)
            S.spec_l[s, :] = dot(tb[s, :], S.tab[pl.ds(2 * C + 2 * FF, 2 * C), :])
            S.spec_s[s, :] = dot(S.bs[s, :], S.tab[pl.ds(BASE, 32), :])

        halo_wait(halo_up, halo_down, S.wide.at[pl.ds(0, n)], S.wide.at[pl.ds(2 * n, n)])
        ld_a.wait()

        @pl.loop(0, 2 * NF // 256)
        def _(t):
            s = pl.ds(pl.multiple_of(t * 256, 256), 256)
            S.spec_u[s, :] = dot(ta[s, :], S.wide[...])

        @pl.loop(0, NF // 32)
        def _(i):
            re, im = pl.ds(pl.multiple_of(i * 32, 32), 32), pl.ds(pl.multiple_of(NF + i * 32, 32), 32)
            ur, ui = S.spec_u[re, :], S.spec_u[im, :]
            for k, p in ((S.spec_l, S.prod_l), (S.spec_s, S.prod_s)):
                kr, ki = k[re, :], k[im, :]
                p[re, :] = (ur * kr + ui * ki).astype(bf16)
                p[im, :] = (ui * kr - ur * ki).astype(bf16)

        ld_t.wait()
        S.d_l[...] = dot(tc[...], S.prod_l[...])
        S.d_s[...] = dot(tc[...], S.prod_s[...])
        return m_x, q_x, sum_x


    has_above, has_below = r > 0, r < nr - 1

    def halo(i, src, dst, up):
        peer = lax.rem(r + nr - 1, nr) if up else lax.rem(r + 1, nr)
        return pltpu.make_async_remote_copy(
            src, dst, S.halo_send.at[i], S.halo_recv.at[i], device_id=(b, peer), device_id_type=MESH
        )

    def halo_start(up, down):
        @pl.when(has_above)
        def _():
            up.start()

        @pl.when(has_below)
        def _():
            down.start()

    def halo_wait(up, down, above, below):
        @pl.when(has_below)
        def _():
            up.wait_recv()
            down.wait_send()

        @pl.when(has_above)
        def _():
            down.wait_recv()
            up.wait_send()

        @pl.when(jnp.logical_not(has_above))
        def _():
            above[...] = jnp.zeros((n, C), bf16)

        @pl.when(jnp.logical_not(has_below))
        def _():
            below[...] = jnp.zeros((n, C), bf16)

    m_x, q_x, sum_x = pl.run_scoped(
        front, pltpu.VMEM(S.a_hbm.shape, bf16), pltpu.VMEM(S.b_hbm.shape, bf16), pltpu.VMEM(S.c_hbm.shape, bf16)
    )
    inv_x = lax.rsqrt(q_x + norm_eps)
    small = S.small[...]
    row = lambda i: small[32 + i : 33 + i, :]
    mid_gain = lambda j: small[42 + j : 43 + j, :]
    mid_bias = lambda j: small[25 + j : 26 + j, :]
    m_l, v_l = local(lambda s: S.d_l[s, :], n)
    m_s, v_s = local(lambda s: S.d_s[s, :], n)
    ld_c.wait()

    def early():
        order(2 * C // 128, (2 * C + FF) // 128)

        def low(s, a):
            S.gy_low[s, :] = S.cot[s, :].astype(bf16)
            return a

        chunks(n, low)

    tot = share(
        1, jnp.concatenate([m_l, m_s, v_l, v_s], axis=0), merge_stats(2), early,
        lambda: order((2 * C + FF) // 128, (2 * C + 2 * FF) // 128),
    )
    m_l, m_s = tot[0:1], tot[1:2]
    inv_l, inv_s = lax.rsqrt(tot[2:3] / every + norm_eps), lax.rsqrt(tot[3:4] / every + norm_eps)

    def pair(s, a):
        hl = (S.d_l[s, :] - m_l) * inv_l
        hs = (S.d_s[s, :] - m_s) * inv_s
        S.d_l[s, :] = hl
        S.d_s[s, :] = hs
        t, d = gelu_both(hl * row(2) + row(3) + hs * row(4) + row(5))
        S.s_val[s, :] = d
        S.t_low[s, :] = t.astype(bf16)
        return a

    chunks(n, pair)
    S.p_val[...] = dot(S.t_low[...], S.tab[pl.ds(C, C), :])
    m_p = close(chunks(n, lambda s, a: a + fold(S.p_val[s, :]), zero)) * (1.0 / n)

    def proj(s, a):
        d = S.p_val[s, :] - m_p
        return a[0] + fold(d * d), a[1] + fold(d * (S.x[s, :] - m_x))

    v_p, cross = chunks(n, proj, (zero, zero))
    tot = share(2, jnp.concatenate([m_p, close(v_p), close(cross) + m_p * sum_x], axis=0), merge_stats(1))
    m_p, q_p, cov = tot[0:1], tot[1:2] / every, tot[2:3] / every
    inv_p = lax.rsqrt(q_p + norm_eps)
    slope = row(6) * inv_p
    m_f = m_x + row(7)
    q_f = jnp.maximum(q_x + 2 * slope * cov + slope * slope * q_p, 0.0)
    inv_f = lax.rsqrt(q_f + norm_eps)
    hats = inv_f * inv_p * (cov + slope * q_p)

    def ffn(s, a):
        ph = (S.p_val[s, :] - m_p) * inv_p
        S.p_val[s, :] = ph
        m = S.x[s, :] + (ph * row(6) + row(7))
        S.mid[s, :] = m
        S.c_low[s, :] = ((m - m_f) * (inv_f * row(8)) + row(9)).astype(bf16)
        g = S.cot[s, :]
        return a[0] + fold(g), a[1] + fold(g * ph)

    sum_c, sum_ch = chunks(n, ffn, (zero, zero))
    sum_c, sum_ch = close(sum_c), close(sum_ch)

    def middle(hid, gact, a_low, gh_low):
        for j in range(blocks):
            hid[j] = dot(S.c_low[...], S.tab[up_rows(j), :])
        st = [local(lambda s, j=j: hid[j, s, :], n) for j in range(blocks)]

        def back_first():
            for j in range(blocks):
                gact[j] = dot(S.gy_low[...], S.tab[down_rows(j), :], (1, 1))

        tot = share(3, jnp.concatenate([s[0] for s in st] + [s[1] for s in st], axis=0), merge_stats(blocks), back_first)
        m_h = tot[:blocks]
        inv_h = lax.rsqrt(tot[blocks:] / every + norm_eps)
        sums = []
        for j in range(blocks):
            mj, ij, gj, bj = m_h[j : j + 1], inv_h[j : j + 1], mid_gain(j), mid_bias(j)

            def hidden(s, a, j=j, mj=mj, ij=ij, gj=gj, bj=bj):
                hat = (hid[j, s, :] - mj) * ij
                hid[j, s, :] = hat
                v, d = gelu_both(hat * gj + bj)
                a_low[j, s, :] = v.astype(bf16)
                g = gact[j, s, :] * d
                gact[j, s, :] = g
                return a[0] + fold(g), a[1] + fold(g * hat)

            sums.append(tuple(close(v) for v in chunks(n, hidden, (zero, zero))))
        mid_rows = jnp.concatenate([s[0] for s in sums] + [s[1] for s in sums], axis=0)

        def down_grads():
            for j in range(blocks):
                for h in range(C // 256):
                    put(S.flat, 2 * C + FF + j * C + h * 256, dot(a_low[j, :, half_cols(h)], S.gy_low[...], (0, 0)))

        def outputs():
            S.out[...] = S.mid[...]
            for j in range(blocks):
                S.out[...] += dot(a_low[j], S.tab[down_rows(j), :])

        tot = share(4, mid_rows, merge_sum, down_grads, outputs) * (1.0 / every)
        out_copy.start()
        for j in range(blocks):
            tb_, tg_, sc = tot[j : j + 1], tot[blocks + j : blocks + j + 1], mid_gain(j) * inv_h[j : j + 1]

            def grad_h(s, a, j=j, tb_=tb_, tg_=tg_, sc=sc):
                gh_low[j, s, :] = (sc * (gact[j, s, :] - tb_ - hid[j, s, :] * tg_)).astype(bf16)
                return a

            chunks(n, grad_h)
        S.g_f[...] = dot(gh_low[0], S.tab[up_rows(0), :], (1, 1))
        for j in range(1, blocks):
            S.g_f[...] += dot(gh_low[j], S.tab[up_rows(j), :], (1, 1))

        def ffn_sums(s, a):
            g = S.g_f[s, :]
            hat = (S.mid[s, :] - m_f) * inv_f
            return a[0] + fold(g), a[1] + fold(g * hat), a[2] + fold(g * S.p_val[s, :])

        b_ffn, g_ffn, g_fp = (close(v) for v in chunks(n, ffn_sums, (zero, zero, zero)))

        def grad_up():
            for j in range(blocks):
                for h in range(C // 256):
                    put(S.flat, 2 * C + j * C + h * 256, dot(S.c_low[:, half_cols(h)], gh_low[j], (0, 0)))

        tot = share(5, jnp.concatenate([b_ffn, g_ffn, g_fp, sum_c, sum_ch], axis=0), merge_sum, grad_up) * (1.0 / every)
        return mid_rows, b_ffn, g_ffn, tot

    out_copy = pltpu.make_async_copy(S.out, S.out_hbm, S.load_sem.at[7])
    hidden_shape = (blocks, n, C)
    mid_rows, b_ffn, g_ffn, tot = pl.run_scoped(
        middle, pltpu.VMEM(hidden_shape, f32), pltpu.VMEM(hidden_shape, f32), pltpu.VMEM(hidden_shape, bf16), pltpu.VMEM(hidden_shape, bf16)
    )

    def back(tat, tbt, tct, acc):
        ld_ct, ld_at, ld_bt = load(3, S.ct_hbm, tct), load(4, S.at_hbm, tat), load(5, S.bt_hbm, tbt)
        for copy in (ld_ct, ld_at, ld_bt):
            copy.start()
        scale_f = row(8) * inv_f
        mean_hat = tot[4:5] + scale_f * (tot[2:3] - tot[1:2] * hats)

        def grad_mid(s, a):
            hat = (S.mid[s, :] - m_f) * inv_f
            g = S.cot[s, :] + scale_f * (S.g_f[s, :] - tot[0:1] - hat * tot[1:2])
            S.g_f[s, :] = g
            ph = S.p_val[s, :]
            S.gp_low[s, :] = (slope * (g - tot[3:4] - ph * mean_hat)).astype(bf16)
            return a[0] + fold(g), a[1] + fold(g * ph)

        b_proj, g_proj = (close(v) for v in chunks(n, grad_mid, (zero, zero)))
        S.p_val[...] = dot(S.gp_low[...], S.tab[pl.ds(C, C), :], (1, 1))

        def grad_s(s, a):
            g = S.p_val[s, :] * S.s_val[s, :]
            S.p_val[s, :] = g
            return a[0] + fold(g), a[1] + fold(g * S.d_l[s, :]), a[2] + fold(g * S.d_s[s, :])

        b_pair, g_lg, g_sg = (close(v) for v in chunks(n, grad_s, (zero, zero, zero)))

        def grad_out():
            for h in range(C // 256):
                put(S.flat, C + h * 256, dot(S.t_low[:, half_cols(h)], S.gp_low[...], (0, 0)))

        sums = share(6, jnp.concatenate([b_pair, g_lg, g_sg], axis=0), merge_sum, grad_out) * (1.0 / every)
        sc_l, sc_s = row(2) * inv_l, row(4) * inv_s
        gl_low, gs_low = S.t_low, S.gp_low

        def grad_pair(s, a):
            g = S.p_val[s, :] - sums[0:1]
            gl_low[s, :] = (sc_l * (g - S.d_l[s, :] * sums[1:2])).astype(bf16)
            gs_low[s, :] = (sc_s * (g - S.d_s[s, :] * sums[2:3])).astype(bf16)
            return a

        chunks(n, grad_pair)
        ld_ct.wait()

        @pl.loop(0, NF // 256)
        def _(t):
            re, im = pl.ds(pl.multiple_of(t * 256, 256), 256), pl.ds(pl.multiple_of(NF + t * 256, 256), 256)
            acc[0] = dot(tct[re, :], gl_low[...])
            acc[1] = dot(tct[im, :], gl_low[...])
            acc[2] = dot(tct[re, :], gs_low[...])
            acc[3] = dot(tct[im, :], gs_low[...])

            @pl.loop(0, 8)
            def _(i):
                s = pl.ds(pl.multiple_of(i * 32, 32), 32)
                re = pl.ds(pl.multiple_of(t * 256 + i * 32, 32), 32)
                im = pl.ds(pl.multiple_of(NF + t * 256 + i * 32, 32), 32)
                lr, li, sr, si = acc[0, s, :], acc[1, s, :], acc[2, s, :], acc[3, s, :]
                kr, ki = S.spec_l[re, :], S.spec_l[im, :]
                hr, hi = S.spec_s[re, :], S.spec_s[im, :]
                S.prod_k[re, :] = (lr * kr - li * ki + sr * hr - si * hi).astype(bf16)
                S.prod_k[im, :] = (lr * ki + li * kr + sr * hi + si * hr).astype(bf16)
                ur, ui = S.spec_u[re, :], S.spec_u[im, :]
                S.prod_l[re, :] = (lr * ur + li * ui).astype(bf16)
                S.prod_l[im, :] = (lr * ui - li * ur).astype(bf16)
                S.prod_s[re, :] = (sr * ur + si * ui).astype(bf16)
                S.prod_s[im, :] = (sr * ui - si * ur).astype(bf16)

        ld_at.wait()
        halo_up = halo(2, S.halo_out.at[0], S.halo_in.at[1], True)
        halo_down = halo(3, S.halo_out.at[1], S.halo_in.at[0], False)
        S.halo_out[0] = dot(tat[pl.ds(0, n), :], S.prod_k[...]).astype(bf16)

        @pl.when(has_above)
        def _():
            halo_up.start()

        S.halo_out[1] = dot(tat[pl.ds(2 * n, n), :], S.prod_k[...]).astype(bf16)

        @pl.when(has_below)
        def _():
            halo_down.start()

        S.p_val[...] = dot(tat[pl.ds(n, n), :], S.prod_k[...])
        ld_bt.wait()

        @pl.loop(0, 4)
        def _(t):
            s = pl.ds(pl.multiple_of(t * 256, 256), 256)
            put(S.flat, 2 * C + 2 * FF + t * 256, dot(tbt[s, :], S.prod_l[...]))

        put(S.flat, BASE, dot(S.bst[...], S.prod_s[...]))
        halo_wait(halo_up, halo_down, S.halo_in.at[0], S.halo_in.at[1])
        gz_low = S.t_low

        def grad_z(s, a):
            g = S.p_val[s, :] + S.halo_in[0, s, :].astype(f32) + S.halo_in[1, s, :].astype(f32)
            gz_low[s, :] = (g * S.dz[s, :]).astype(bf16)
            return a

        chunks(n, grad_z)
        S.p_val[...] = dot(gz_low[...], S.tab[pl.ds(0, C), :], (1, 1))

        def pre_sums(s, a):
            g = S.p_val[s, :]
            return a[0] + fold(g), a[1] + fold(g * ((S.x[s, :] - m_x) * inv_x))

        b_pre, g_pre = (close(v) for v in chunks(n, pre_sums, (zero, zero)))
        share_send(7, 0, jnp.concatenate([b_pre, g_pre], axis=0))
        for h in range(C // 256):
            put(S.flat, h * 256, dot(S.pre_low[:, half_cols(h)], gz_low[...], (0, 0)))
        norms = [g_pre, b_pre, g_lg, b_pair, g_sg, b_pair, g_proj, b_proj, g_ffn, b_ffn]
        norms += [mid_rows[blocks + j : blocks + j + 1] for j in range(blocks)]
        put(S.flat, BASE + 32, jnp.concatenate(norms + [jnp.zeros((2, C), f32)], axis=0))
        for j in range(blocks):
            for k in range(4):
                S.flat[pl.ds((BASE + 25 + j) * 4 + k, 1), :] = mid_rows[j : j + 1, k * 128 : (k + 1) * 128]

    pl.run_scoped(
        back, pltpu.VMEM(S.at_hbm.shape, bf16), pltpu.VMEM(S.bt_hbm.shape, bf16), pltpu.VMEM(S.ct_hbm.shape, bf16), pltpu.VMEM((4, 256, C), f32)
    )


    plan = reduce_plan(nb)
    parts = len(plan)
    by_z = first_along_z(nb, lines)
    main = lines - by_z
    size = main // parts
    z_size = by_z // parts
    unit = 64 if own % 64 == 0 else 8
    tmp = S.tmp
    hop_base = nz * nb
    z_base = hop_base + nz * (nb - 1)

    def tail(sib_out, pair, z_out):
        grad = S.flat.reshape(total, 4, 128)

        def column(i):
            return lax.rem(z + 1 + i, nz)

        def collect(m, zz, cc):
            start = (flip(b, m) * nr + 2 * zz + cc) * own

            @pl.loop(0, own // unit)
            def _(g):
                at = start + g * unit
                for u in range(unit):
                    tmp[pl.ds(pl.multiple_of((g * unit + u) * 4, 4), 4), :] = grad[S.idx[at // 128, lax.rem(at, 128) + u]]

        def to_sibling(i, m):
            return pltpu.make_async_remote_copy(
                sib_out.at[i, m], rows_in.at[i * nb + m], S.sib_send.at[i, m], S.sib_recv.at[i, m],
                device_id=sibling, device_id_type=MESH,
            )

        def rows_of(p):
            return pl.ds(p * size, size)

        def slots(p, t):
            at = sum(len(plan[p][k][2]) for k in range(t))
            return at, len(plan[p][t][2])

        def hop_at(i, p, at, count):
            return rows_in.at[pl.ds(hop_base + i * (nb - 1) + at, count), rows_of(p)]

        def hop(i, p, t, m):
            o, sent, kept = plan[p][t]
            at, _ = slots(p, t)
            landing = rows_in.at[hop_base + i * (nb - 1) + at + kept.index(m ^ (1 << o)), rows_of(p)]
            return pltpu.make_async_remote_copy(
                pair.at[i, m, rows_of(p)], landing, S.hop_send.at[i, p, t], S.hop_recv.at[i, p, t],
                device_id=(flip(b, 1 << o), r), device_id_type=MESH,
            )

        def hop_wait(i, p, t, sem):
            whole = hop_at(i, p, *slots(p, t))
            pltpu.make_async_copy(whole, whole, sem.at[i, p, t]).wait()

        def for_sibling(i):
            for m in reversed(range(nb)):
                collect(m, column(i), 1 - c)
                sib_out[i, m] = tmp[...].astype(bf16)
                to_sibling(i, m).start()

        def to_owner(i):
            return pltpu.make_async_remote_copy(
                z_out.at[i], rows_in.at[z_base + i, pl.ds(0, main)], S.own_send.at[i], S.own_recv.at[i],
                device_id=(b, 2 * column(i) + c), device_id_type=MESH,
            )

        def to_layer(i, m):
            return pltpu.make_async_remote_copy(
                pair.at[i, m, pl.ds(main, by_z)], S.layer_in.at[i, m], S.layer_send.at[i], S.layer_recv.at[i],
                device_id=(b, 2 * column(i) + c), device_id_type=MESH,
            )

        def layer_wait(i, sem):
            pltpu.make_async_copy(S.layer_in.at[i], S.layer_in.at[i], sem.at[i]).wait()

        def z_rows(p):
            return pl.ds(main + p * z_size, z_size)

        def z_hop(p, t, m):
            o, sent, kept = plan[p][t]
            at, _ = slots(p, t)
            return pltpu.make_async_remote_copy(
                pair.at[nz - 1, m, z_rows(p)], S.z_hops.at[p, at + kept.index(m ^ (1 << o))], S.z_hop_send.at[p, t], S.z_hop_recv.at[p, t],
                device_id=(flip(b, 1 << o), r), device_id_type=MESH,
            )

        def z_hop_wait(p, t, sem):
            at, count = slots(p, t)
            whole = S.z_hops.at[p, pl.ds(at, count)]
            pltpu.make_async_copy(whole, whole, sem.at[p, t]).wait()

        def z_start():
            for i in range(nz - 1):
                layer_wait(i, S.layer_recv)
            for m in reversed(range(nb)):
                v = pair[nz - 1, m, pl.ds(main, by_z)].astype(f32)
                for i in range(nz - 1):
                    v = v + S.layer_in[i, m].astype(f32)
                pair[nz - 1, m, pl.ds(main, by_z)] = v.astype(bf16)
                for p in range(parts):
                    if m in plan[p][0][1]:
                        z_hop(p, 0, m).start()

        def z_next(t):
            for p in range(parts):
                z_hop_wait(p, t, S.z_hop_recv)
                at, _ = slots(p, t)
                for k, m in enumerate(plan[p][t][2]):
                    v = pair[nz - 1, m, z_rows(p)].astype(f32) + S.z_hops[p, at + k].astype(f32)
                    if t == parts - 1:
                        tmp[z_rows(p), :] = v
                        continue
                    pair[nz - 1, m, z_rows(p)] = v.astype(bf16)
                    if m in plan[p][t + 1][1]:
                        z_hop(p, t + 1, m).start()

        def first_step(i):
            for m in reversed(range(nb)):
                collect(m, column(i), c)
                to_sibling(i, m).wait_recv()
                pair[i, m] = (tmp[...] + rows_in[i * nb + m].astype(f32)).astype(bf16)
                for p in range(parts):
                    if m in plan[p][0][1]:
                        hop(i, p, 0, m).start()
                if by_z:

                    @pl.when(i < nz - 1)
                    def _():
                        to_layer(i, m).start()

            @pl.when(i < nz - 1)
            def _():
                for_sibling(i + 1)

        def next_step(i, t):
            for p in range(parts):
                hop_wait(i, p, t, S.hop_recv)
                at, _ = slots(p, t)
                for k, m in enumerate(plan[p][t][2]):
                    pair[i, m, rows_of(p)] = (
                        pair[i, m, rows_of(p)].astype(f32)
                        + rows_in[hop_base + i * (nb - 1) + at + k, rows_of(p)].astype(f32)
                    ).astype(bf16)
                    if m in plan[p][t + 1][1]:
                        hop(i, p, t + 1, m).start()

        def last_step(i):
            for p in range(parts):
                hop_wait(i, p, parts - 1, S.hop_recv)
                at, _ = slots(p, parts - 1)
                tmp[rows_of(p), :] = pair[i, 0, rows_of(p)].astype(f32) + rows_in[hop_base + i * (nb - 1) + at, rows_of(p)].astype(f32)

            @pl.when(i < nz - 1)
            def _():
                z_out[i] = tmp[pl.ds(0, main), :].astype(bf16)
                to_owner(i).start()

        def grad_image():
            sums = share_wait(7, 1, merge_sum) * (1.0 / every)
            scale_x = row(0) * inv_x

            def last(s, a):
                hat = (S.x[s, :] - m_x) * inv_x
                S.g_f[s, :] = S.g_f[s, :] + scale_x * (S.p_val[s, :] - sums[0:1] - hat * sums[1:2])
                return a

            chunks(n, last)
            gin_copy.start()
            for i in range(own):
                at = (b * nr + r) * own + i // unit * unit
                p = S.idx[at // 128, lax.rem(at, 128) + i % unit]
                fast = (p >= 2 * C + 2 * FF + KL * KL) & ((p < BASE) | (p >= BASE + KS * KS))
                S.rate[pl.ds(i, 1), :] = jnp.full((1, 128), jnp.where(fast, np.float32(norm_rate), np.float32(matrix_rate)), f32)

        gin_copy = pltpu.make_async_copy(S.g_f, S.gin_hbm, S.load_sem.at[6])
        for_sibling(0)

        @pl.loop(0, nz + parts)
        def _(q):
            @pl.when(q < nz)
            def _():
                first_step(q)

            @pl.when(q == 0)
            def _():
                share_send(7, 1, share_wait(7, 0, merge_sum))

            if by_z:

                @pl.when(q == nz - 1)
                def _():
                    z_start()

            for t in range(parts - 1):

                @pl.when((q >= t + 1) & (q < nz + t + 1))
                def _():
                    next_step(q - t - 1, t)

            @pl.when(q == 1)
            def _():
                grad_image()

            if by_z:

                @pl.when(q == nz)
                def _():
                    for t in range(parts - 1):
                        z_next(t)

            @pl.when(q >= parts)
            def _():
                last_step(q - parts)

        for i in range(nz - 1):
            to_owner(i).wait_recv()
            tmp[pl.ds(0, main), :] += rows_in[z_base + i, pl.ds(0, main)].astype(f32)
        if by_z:
            z_next(parts - 1)
        for j in range(4):
            S.red[:, j * 128 : (j + 1) * 128] = tmp[pl.ds(j, own, stride=4), :]

        @pl.loop(0, nz)
        def _(i):
            for m in range(nb):
                to_sibling(i, m).wait_send()
            for p in range(parts):
                for t in range(parts):
                    hop_wait(i, p, t, S.hop_send)

        for i in range(nz - 1):
            to_owner(i).wait_send()
            if by_z:
                layer_wait(i, S.layer_send)
        if by_z:
            for p in range(parts):
                for t in range(parts):
                    z_hop_wait(p, t, S.z_hop_send)
        gin_copy.wait()

    low_block = lambda *lead: pltpu.VMEM(lead + (lines, 128), bf16)
    pl.run_scoped(tail, low_block(nz, nb), low_block(nz, nb), pltpu.VMEM((nz, main, 128), bf16))
    for e in range(len(WIDTHS)):
        for stage in range(2):
            buf, mine, count = share_stage(e, stage)
            sent = buf.at[pl.ds(0, count - 1)]
            pltpu.make_async_copy(sent, sent, S.stat_send.at[e, stage]).wait()
    out_copy.wait()


def step(x, cot, master, slots, nb, nr):
    (a, at, b, bt, bs, bst, c, ct) = tables()
    n, own, nz, parts = x.shape[0], master.shape[0], nr // 2, nb.bit_length() - 1
    total = slots.size
    vm = lambda *shape: pltpu.VMEM(shape, f32)
    low = lambda *shape: pltpu.VMEM(shape, bf16)
    dma = lambda *shape: pltpu.SemaphoreType.DMA(shape)
    vmem, anywhere = pl.BlockSpec(memory_space=pltpu.VMEM), pl.BlockSpec(memory_space=pl.ANY)
    ins = dict(
        slots_hbm=(slots, anywhere), x_hbm=(x, anywhere), cot_hbm=(cot, anywhere), master_hbm=(master, anywhere),
        a_hbm=(a, anywhere), at_hbm=(at, anywhere), b_hbm=(b, anywhere), bt_hbm=(bt, anywhere), bs=(bs, vmem), bst=(bst, vmem),
        c_hbm=(c, anywhere), ct_hbm=(ct, anywhere),
    )
    image = jax.ShapeDtypeStruct((n, C), f32)
    outs = dict(
        out_hbm=(image, anywhere), gin_hbm=(image, anywhere), red=(jax.ShapeDtypeStruct((own, C), f32), vmem),
        rate=(jax.ShapeDtypeStruct((own, 128), f32), vmem),
    )
    scratch = dict(
        rows_in=low(nb * nr, 4 * own, 128), flat=vm(4 * total, 128), tab=low(total, C), x=vm(n, C), cot=vm(n, C), master=vm(own, C),
        tmp=vm(4 * own, 128), chunk=vm(512, 128), inv=pltpu.VMEM((total // 128, 128), jnp.int32), at_v=pltpu.VMEM((total // 128, 128), jnp.int32),
        idx=pltpu.SMEM((total // 128, 128), jnp.int32),
        inv_at=pltpu.SMEM((total // 128, 128), jnp.int32), small=vm(48, C),
        pre_low=low(n, C), wide=low(3 * n, C), dz=vm(n, C), spec_u=vm(2 * NF, C), spec_l=vm(2 * NF, C), spec_s=vm(2 * NF, C),
        prod_l=low(2 * NF, C), prod_s=low(2 * NF, C), prod_k=low(2 * NF, C), d_l=vm(n, C), d_s=vm(n, C), s_val=vm(n, C),
        t_low=low(n, C), p_val=vm(n, C), mid=vm(n, C), c_low=low(n, C), gy_low=low(n, C), gp_low=low(n, C), g_f=vm(n, C), out=vm(n, C),
        halo_out=low(2, n, C), halo_in=low(2, n, C),
    )
    by_z = first_along_z(nb, 4 * own)
    if by_z:
        scratch.update(
            layer_in=low(nz - 1, nb, by_z, 128), z_hops=low(parts, nb - 1, by_z // parts, 128), layer_send=dma(nz), layer_recv=dma(nz),
            z_hop_send=dma(parts, parts), z_hop_recv=dma(parts, parts),
        )
    for e, w in enumerate(WIDTHS):
        one, two = (2, nb * nz) if by_chip(e, nb * nz) else (nr, nb)
        scratch[f"one{e}"] = vm(one, w, C)
        scratch[f"two{e}"] = vm(two, w, C)
    scratch.update(
        load_sem=dma(9), stat_send=dma(len(WIDTHS), 2), stat_recv=dma(len(WIDTHS), 2), halo_send=dma(4), halo_recv=dma(4),
        z_send=dma(nz), z_recv=dma(nz), b_send=dma(nb, nz), b_recv=dma(nb, nz), half_send=dma(2, nz), half_recv=dma(2, nz),
        core_send=dma(nb, nz), core_recv=dma(nb, nz), rest_send=dma(nb, nz), rest_recv=dma(nb, nz),
        rest_core_send=dma(nb, nz), rest_core_recv=dma(nb, nz), sib_send=dma(nz, nb), sib_recv=dma(nz, nb),
        hop_send=dma(nz, parts, parts), hop_recv=dma(nz, parts, parts), own_send=dma(nz), own_recv=dma(nz),
    )
    return pl.pallas_call(
        functools.partial(step_kernel, nb, nr, [*ins, *outs, *scratch]),
        out_shape=[v[0] for v in outs.values()],
        in_specs=[v[1] for v in ins.values()],
        out_specs=[v[1] for v in outs.values()],
        scratch_shapes=list(scratch.values()),
        compiler_params=pltpu.CompilerParams(collective_id=0, has_side_effects=True, vmem_limit_bytes=62 * 2**20),
    )(*[v[0] for v in ins.values()])


def finish_kernel(*refs):
    ins, outs, bufs, (load_sem, store_sem) = refs[:7], refs[7:14], refs[14:25], refs[25:]
    red, rate, first_ref, second_ref, master_ref, out, gin = bufs[:7]
    new_first, new_second, new_master, new_copy = bufs[7:11]
    loads = [pltpu.make_async_copy(src, dst, load_sem.at[i]) for i, (src, dst) in enumerate(zip(ins, bufs[:7]))]
    for copy in loads:
        copy.start()
    own = red.shape[0]
    size = 64 if own % 64 == 0 else own
    for copy in loads[:5]:
        copy.wait()
    stores = [pltpu.make_async_copy(red, outs[2], store_sem.at[2, 0])]
    stores[0].start()
    for part in range(own // size):
        for k in range(0, size, 8):
            s = slice(part * size + k, part * size + k + 8)
            for j in range(C // 128):
                at = (s, slice(j * 128, (j + 1) * 128))
                g = red[at]
                first = beta_one * first_ref[at] + (1.0 - beta_one) * g
                second = beta_two * second_ref[at] + (1.0 - beta_two) * g * g
                new_first[at] = first
                new_second[at] = second
                first_hat = first / (1.0 - beta_one**STEP)
                second_hat = second / (1.0 - beta_two**STEP)
                master = master_ref[at]
                new_master[at] = master - rate[s, :] * (first_hat / (jnp.sqrt(second_hat) + adam_eps) + decay_rate * master)
        s = pl.ds(part * size, size)
        new_copy[s, :] = new_master[s, :].astype(bf16)
        if part == 0:
            for i in (5, 6):
                loads[i].wait()
                stores.append(pltpu.make_async_copy(bufs[i], outs[i - 5], store_sem.at[i - 5, 0]))
                stores[-1].start()
        for i, buf in enumerate((new_first, new_second, new_master, new_copy)):
            stores.append(pltpu.make_async_copy(buf.at[s], outs[3 + i].at[s], store_sem.at[3 + i, part]))
            stores[-1].start()
    for copy in stores:
        copy.wait()


def finish(reduced, first, second, master, rates, out, gin):
    anywhere = pl.BlockSpec(memory_space=pl.ANY)
    slot = jax.ShapeDtypeStruct(reduced.shape, f32)
    image = jax.ShapeDtypeStruct(out.shape, f32)
    low = jax.ShapeDtypeStruct(reduced.shape, bf16)
    ins = (reduced, rates, first, second, master, out, gin)
    outs = [image, image, slot, slot, slot, slot, low]
    return pl.pallas_call(
        finish_kernel,
        out_shape=outs,
        in_specs=[anywhere] * 7,
        out_specs=[anywhere] * 7,
        scratch_shapes=[pltpu.VMEM(v.shape, f32) for v in ins]
        + [pltpu.VMEM(v.shape, v.dtype) for v in (slot, slot, slot, low)]
        + [pltpu.SemaphoreType.DMA((7,)), pltpu.SemaphoreType.DMA((7, 4))],
        compiler_params=pltpu.CompilerParams(vmem_limit_bytes=62 * 2**20),
    )(*ins)


def body(image_in, cotangent, slot_rows, master, first_moment, second_moment):
    n = image_in.shape[0] * image_in.shape[1] * image_in.shape[2]
    nb, nr = lax.axis_size("batch"), lax.axis_size("rows")
    out, grad_in, reduced, rates = step(
        image_in.reshape(n, C), cotangent.reshape(n, C), master, slot_rows.reshape(-1, 128), nb, nr
    )
    result, grad_x, *slots = finish(reduced, first_moment, second_moment, master, rates, out, grad_in)
    return (result.reshape(image_in.shape), grad_x.reshape(image_in.shape), *slots)


def solution(mesh):
    image = P("batch", "rows", None, None)
    owner = P(AXES, None)
    return jax.shard_map(
        body,
        mesh=mesh,
        in_specs=(image, image, P(), owner, owner, owner),
        out_specs=(image, image, owner, owner, owner, owner, owner),
        check_vma=False,
    )
```
